32 devices in a mesh: seq: 8 (over y, x, core), wt: 4 (over z).
Axes of the slice: x: 2, y: 2, z: 4, core: 2. Of those that a mesh axis runs over, the one named last changes fastest.
Arguments:
- inputs: bfloat16 [4, 1024, 2560], P('wt', 'seq'), may hold values from -6 to 6
- segment: int32 [4, 1024], P('wt', 'seq'), may hold values from 0 to 32, as said below
- mixer_gain: float32 [2560], replicated, may hold values from 0.5 to 1.5
- input_weight: bfloat16 [2560, 2560], P(None, 'wt'), may hold values from -0.125 to 0.125
- branch_weight: bfloat16 [2560, 2560], P(None, 'wt'), may hold values from -0.125 to 0.125
- conv_weight: float32 [2560, 4], replicated, may hold values from -3 to 3
- recur_gate: bfloat16 [2560, 256], replicated, may hold values from -0.375 to 0.375
- input_gate: bfloat16 [2560, 256], replicated, may hold values from -0.375 to 0.375
- recur_bias: float32 [2560], replicated, may hold values from -6 to 6
- input_bias: float32 [2560], replicated, may hold values from -6 to 6
- decay_rate: float32 [2560], replicated, may hold values from -14 to -4
- output_weight: bfloat16 [2560, 2560], P(None, 'wt'), may hold values from -0.3125 to 0.3125
- second_gain: float32 [2560], replicated, may hold values from 0.5 to 1.5
- gate_weight: bfloat16 [2560, 7680], P(None, 'wt'), may hold values from -0.125 to 0.125
- up_weight: bfloat16 [2560, 7680], P(None, 'wt'), may hold values from -0.125 to 0.125
- down_weight: bfloat16 [2560, 7680], P(None, 'wt'), may hold values from -0.125 to 0.125
- cotangent: float32 [4, 1024, 2560], P('wt', 'seq'), may hold values from -6 to 6
Outputs:
- block_out: bfloat16 [4, 1024, 2560], P('wt', 'seq')
- input_grad: float32 [4, 1024, 2560], P('wt', 'seq')
- mixer_gain_grad: float32 [2560], P(('seq', 'wt'))
- input_weight_grad: float32 [2560, 2560], P(('seq', 'wt'))
- branch_weight_grad: float32 [2560, 2560], P(('seq', 'wt'))
- conv_weight_grad: float32 [2560, 4], P(('seq', 'wt'))
- recur_gate_grad: float32 [2560, 256], P(('seq', 'wt'))
- input_gate_grad: float32 [2560, 256], P(('seq', 'wt'))
- recur_bias_grad: float32 [2560], P(('seq', 'wt'))
- input_bias_grad: float32 [2560], P(('seq', 'wt'))
- decay_rate_grad: float32 [2560], P(('seq', 'wt'))
- output_weight_grad: float32 [2560, 2560], P(('seq', 'wt'))
- second_gain_grad: float32 [2560], P(('seq', 'wt'))
- gate_weight_grad: float32 [2560, 7680], P(('seq', 'wt'))
- up_weight_grad: float32 [2560, 7680], P(('seq', 'wt'))
- down_weight_grad: float32 [2560, 7680], P(('seq', 'wt'))
The draws below stay inside these ranges and needn't reach their ends.
Inputs may be any that keep to these rules, and one draw needn't show every extreme that they name: `segment`: in every sequence the numbers start at 0 and rise by 0 or 1 from one position to the next. In each group of 1 sequence of one index of wt, one sequence, drawn from the seed, keeps document 0 up to its last 64 positions and starts exactly 32 new documents among those positions; every other sequence holds exactly 129 documents.
All inputs are finite; a program needn't handle non-finite values.
Results may differ from the reference program's by a relative error of at most 0.02.
Values may be sent and summed in bfloat16 or wider, within the bound.
A program may use at most 768 MiB of HBM per device.

```python
import math
import jax
import jax.numpy as jnp
from jax import lax

D = 2560
HEAD = 256
CONV = 4
F = 7680
SEQ_PART = 128
SEQS = 1
L = 2560
LENGTH = 1024
SEQ_ALL = 4
N_WT = 4


def draw_segment(key, part):
    key = jax.random.fold_in(key, 11)
    pick_key, start_key, tail_key = jax.random.split(key, 3)
    start_count = LENGTH // 8
    tail_span = SEQ_PART // 2
    tail_count = SEQ_PART // 4
    row_keys = jax.random.split(start_key, SEQ_ALL)
    tail_keys = jax.random.split(tail_key, SEQ_ALL)

    def one_row(row_key):
        order = jax.random.permutation(row_key, LENGTH - 1) + 1
        chosen_spots = order[:start_count]
        return jnp.zeros((LENGTH,), jnp.int32).at[chosen_spots].set(1)

    def tail_row(row_key):
        order = jax.random.permutation(row_key, tail_span) + (LENGTH - tail_span)
        chosen_spots = order[:tail_count]
        return jnp.zeros((LENGTH,), jnp.int32).at[chosen_spots].set(1)
    starts = jax.vmap(one_row)(row_keys)
    tails = jax.vmap(tail_row)(tail_keys)
    chosen = jax.random.randint(pick_key, (N_WT,), 0, SEQS)
    row_ids = jnp.arange(SEQ_ALL)
    long_doc = (row_ids % SEQS == chosen[row_ids // SEQS])[:, None]
    starts = jnp.where(long_doc, tails, starts)
    return jnp.cumsum(starts, axis=1).astype(jnp.int32)


def draw_decay_rate(key, part):
    key = jax.random.fold_in(key, 23)
    kind_key, fast_key, slow_key = jax.random.split(key, 3)
    fast_share = 5
    fast_mask = jax.random.randint(kind_key, (L,), 0, 10) < fast_share
    fast_rate = jnp.exp(jax.random.uniform(fast_key, (L,), jnp.float32, math.log(1.0 / 50.0), math.log(1.0 / 30.0)))
    slow_rate = jnp.exp(jax.random.uniform(slow_key, (L,), jnp.float32, math.log(0.2 / LENGTH), math.log(1.0 / LENGTH)))
    per_step = jnp.where(fast_mask, fast_rate, slow_rate) / 4.0
    return jnp.log(jnp.expm1(per_step)).astype(jnp.float32)


def level_of(key, shape, pieces, least, largest):
    gain = 1.0
    for dim, shards_of in pieces:
        draws = jax.random.uniform(jax.random.fold_in(jax.random.fold_in(key, 6), dim), (shards_of,), jnp.float32, least / len(pieces), largest / len(pieces))
        gain = gain * jnp.repeat(jnp.exp(draws), shape[dim] // shards_of).reshape((-1,) + (1,) * (len(shape) - 1 - dim))
    return gain


def centred(own_key, shape, width, most, shards=(), held_as=jnp.bfloat16):
    loudness = level_of(own_key, shape, shards, -0.22, 0.18) if shards else 1.0
    array = jax.random.normal(own_key, shape, jnp.float32) * width * loudness
    return jnp.minimum(jnp.maximum(array, -most), most).astype(held_as)


def setup_inputs(seed: int = 0) -> dict:
    key_list = jax.random.split(jax.random.key(seed), 18)
    inputs = centred(key_list[0], (SEQ_ALL, LENGTH, D), 1.0, 6.0, ((0, 4), (1, 8)))
    segment = draw_segment(jax.random.fold_in(key_list[17], 71), 0)
    mixer_gain = jnp.clip(1.0 + 0.1 * jax.random.normal(key_list[2], (D,), jnp.float32), 0.5, 1.5)
    input_weight = centred(key_list[3], (D, L), D ** -0.5, 0.125, ((1, 4),))
    branch_weight = centred(key_list[4], (D, L), D ** -0.5, 0.125, ((1, 4),))
    conv_weight = centred(key_list[5], (L, CONV), 0.5, 3.0, (), jnp.float32)
    recur_gate = centred(key_list[6], (L, HEAD), HEAD ** -0.5, 0.375)
    input_gate = centred(key_list[7], (L, HEAD), HEAD ** -0.5, 0.375)
    recur_bias = centred(key_list[8], (L,), 1.0, 6.0, (), jnp.float32)
    input_bias = centred(key_list[9], (L,), 1.0, 6.0, (), jnp.float32)
    decay_rate = draw_decay_rate(jax.random.fold_in(key_list[17], 71), 0)
    output_weight = centred(key_list[11], (D, L), (L // 8) ** -0.5, 0.3125, ((1, 4),))
    second_gain = jnp.clip(1.0 + 0.1 * jax.random.normal(key_list[12], (D,), jnp.float32), 0.5, 1.5)
    gate_weight = centred(key_list[13], (D, F), D ** -0.5, 0.125, ((1, 4),))
    up_weight = centred(key_list[14], (D, F), D ** -0.5, 0.125, ((1, 4),))
    down_weight = centred(key_list[15], (D, F), (F // 4) ** -0.5, 0.125, ((1, 4),))
    cotangent = centred(key_list[16], (SEQ_ALL, LENGTH, D), 1.0, 6.0, ((0, 4), (1, 8)), jnp.float32)
    return dict(inputs=inputs, segment=segment, mixer_gain=mixer_gain, input_weight=input_weight, branch_weight=branch_weight, conv_weight=conv_weight, recur_gate=recur_gate, input_gate=input_gate, recur_bias=recur_bias, input_bias=input_bias, decay_rate=decay_rate, output_weight=output_weight, second_gain=second_gain, gate_weight=gate_weight, up_weight=up_weight, down_weight=down_weight, cotangent=cotangent)


@jax.custom_vjp
def low(v):
    return lax.optimization_barrier(v.astype(jnp.bfloat16)).astype(jnp.float32)

@jax.custom_vjp
def low_back(v):
    return v

def low_keep(v):
    return (low(v), None)

def low_pass(kept, grad):
    return (grad,)

def back_keep(v):
    return (v, None)

def back_low(kept, grad):
    return (low(grad),)
low.defvjp(low_keep, low_pass)
low_back.defvjp(back_keep, back_low)
EPSILON = 1e-06
PRECISE = lax.Precision.HIGHEST

def gelu_tanh(values):
    return jax.nn.gelu(values, approximate=True)

def rms_scale(values, gain_row):
    return values * lax.rsqrt(lax.optimization_barrier(jnp.mean(values * values, axis=-1, keepdims=True)) + EPSILON) * gain_row

def project(values, weight_rows):
    return jnp.einsum('gnd,dk->gnk', values, weight_rows, precision=PRECISE)

def project_back(values, weight_rows):
    return jnp.einsum('gnk,dk->gnd', values, weight_rows, precision=PRECISE)

def block_gate(values, gate_rows):
    head_size = gate_rows.shape[1]
    head_count = gate_rows.shape[0] // head_size
    blocks = values.reshape(values.shape[0], values.shape[1], head_count, head_size)
    mixed_heads = jnp.einsum('gnhi,hij->gnhj', blocks, gate_rows.reshape(head_count, head_size, head_size), precision=PRECISE)
    return mixed_heads.reshape(values.shape)

def previous(values, offset, fill_value):
    pad_spec = [(0, 0)] * values.ndim
    pad_spec[1] = (offset, 0)
    return jnp.pad(values, pad_spec, constant_values=fill_value)[:, :values.shape[1]]

def combine(earlier_pair, later_pair):
    return (earlier_pair[0] * later_pair[0], later_pair[0] * earlier_pair[1] + later_pair[1])

def forward(values, doc_group, mixer_gain, input_weight, branch_weight, conv_weight, recur_gate, input_gate, recur_bias, input_bias, decay_rate, output_weight, second_gain, gate_weight, up_weight, down_weight):
    normed = low(rms_scale(values, mixer_gain))
    u_value = low(low_back(project(normed, input_weight)))
    y_value = low_back(project(normed, branch_weight))
    conv_sum = u_value * conv_weight[:, 0]
    for offset in range(1, conv_weight.shape[1]):
        same_doc = (previous(doc_group, offset, -1) == doc_group).astype(values.dtype)[..., None]
        conv_sum = conv_sum + previous(u_value, offset, 0.0) * same_doc * conv_weight[:, offset]
    c_value = low(conv_sum)
    reset_mask = (previous(doc_group, 1, -1) != doc_group)[..., None]
    keep_state = (previous(doc_group, 1, -1) == doc_group).astype(values.dtype)[..., None]
    recur_act = jax.nn.sigmoid(low_back(block_gate(c_value, recur_gate)) + recur_bias)
    input_act = jax.nn.sigmoid(low_back(block_gate(c_value, input_gate)) + input_bias)
    log_coef = -8.0 * jax.nn.softplus(decay_rate) * recur_act
    in_scale = jnp.where(reset_mask, 1.0, jnp.sqrt(-jnp.expm1(2.0 * log_coef)))
    b_value = in_scale * c_value * input_act
    coef_all = jnp.exp(low(low_back(log_coef))) * keep_state
    state_seq = lax.associative_scan(combine, (coef_all, low(low_back(b_value))), axis=1)[1]
    h_value = low(low_back(state_seq))
    o_value = low(h_value * gelu_tanh(y_value))
    mid_resid = values + low_back(project_back(o_value, output_weight))
    second_normed = low(rms_scale(mid_resid, second_gain))
    g_value = low_back(project(second_normed, gate_weight))
    v_value = low_back(project(second_normed, up_weight))
    hidden = low(gelu_tanh(g_value) * v_value)
    return mid_resid + low_back(project_back(hidden, down_weight))

def reference(inputs, segment, mixer_gain, input_weight, branch_weight, conv_weight, recur_gate, input_gate, recur_bias, input_bias, decay_rate, output_weight, second_gain, gate_weight, up_weight, down_weight, cotangent):
    params = tuple((weight_item.astype(jnp.float32) for weight_item in (mixer_gain, input_weight, branch_weight, conv_weight, recur_gate, input_gate, recur_bias, input_bias, decay_rate, output_weight, second_gain, gate_weight, up_weight, down_weight)))
    group_size = math.gcd(SEQ_ALL, max(1, 4096 // LENGTH))
    group_count = SEQ_ALL // group_size

    def one_group(totals, group_index):
        group_start = (group_index * group_size).astype(jnp.int32)
        values = lax.dynamic_slice_in_dim(inputs, group_start, group_size, 0).astype(jnp.float32)
        doc_group = lax.dynamic_slice_in_dim(segment, group_start, group_size, 0)
        cot_group = lax.dynamic_slice_in_dim(cotangent, group_start, group_size, 0).astype(jnp.float32)

        def run_block(values_in, *weights):
            return forward(values_in, doc_group, *weights)
        result, block_pull = jax.vjp(run_block, values, *params)
        grad_list = block_pull(cot_group)
        totals = tuple((left_term + right_term for left_term, right_term in zip(totals, grad_list[1:])))
        return (totals, (result.astype(jnp.bfloat16), grad_list[0]))
    initial = tuple((jnp.zeros_like(weight_item) for weight_item in params))
    totals, (out_groups, slope_groups) = lax.scan(one_group, initial, jnp.arange(group_count, dtype=jnp.int32))
    block_out = out_groups.reshape(SEQ_ALL, LENGTH, D)
    input_grad = slope_groups.reshape(SEQ_ALL, LENGTH, D)
    return (block_out, input_grad, totals[0], totals[1], totals[2], totals[3], totals[4], totals[5], totals[6], totals[7], totals[8], totals[9], totals[10], totals[11], totals[12], totals[13])
```

```python
import jax
import jax.numpy as jnp
from jax import lax
from jax.experimental import pallas as pl
from jax.experimental.pallas import tpu as pltpu
from jax.sharding import Mesh
from jax.sharding import PartitionSpec as P

EPSILON = 1e-06
LOW = jnp.bfloat16
FULL = jnp.float32


def dot(left, right, left_dim=1, right_dim=0):
    return lax.dot_general(
        left, right, (((left_dim,), (right_dim,)), ((), ())), preferred_element_type=FULL
    )


def gelu_both(values):
    slope = jnp.sqrt(2.0 / jnp.pi).astype(FULL)
    inner = jnp.tanh(slope * (values + 0.044715 * values * values * values))
    gelu = 0.5 * values * (1.0 + inner)
    grad = 0.5 * (1.0 + inner) + 0.5 * values * (1.0 - inner * inner) * slope * (
        1.0 + 3.0 * 0.044715 * values * values
    )
    return gelu, grad


def shard_weight(weight, shards, inner):
    rows, width = weight.shape
    part = rows // (shards * inner)
    me = lax.axis_index("si") * inner + lax.axis_index("sj")
    mine = lax.dynamic_slice_in_dim(weight, me * part, part, 0)
    every = lax.all_gather(mine, "wt", axis=0)
    here = lax.all_to_all(every, "si", split_axis=0, concat_axis=0, tiled=True)
    both = lax.all_gather(here, "sj", axis=1)
    return both.reshape(rows, width)


def head_rows(gate_rows, shards):
    head = gate_rows.shape[1]
    width = gate_rows.shape[0] // shards
    heads = -(-width // head)
    first = (lax.axis_index("si") * width) // head
    table = gate_rows.reshape(-1, head, head)
    return lax.dynamic_slice_in_dim(table, first, heads, 0)


def edge_swap(values, edge):
    me = lax.axis_index("si")
    shards = lax.axis_size("si")
    odd = me % 2 == 1
    mine = jnp.where(odd, values[:, :edge], values[:, -edge:])
    other = lax.ppermute(mine, "si", [(i, i ^ 1) for i in range(shards)])
    return jnp.where(
        odd,
        jnp.concatenate([other, values], axis=1),
        jnp.concatenate([values, other], axis=1),
    )


def own_part(values, edge):
    odd = lax.axis_index("si") % 2 == 1
    return jnp.where(odd, values[:, edge:], values[:, :-edge])


def heads_dot(values, table, transposed=False):
    heads, head, _ = table.shape
    return jnp.concatenate(
        [
            dot(values[:, n * head : (n + 1) * head], table[n], 1, 1 if transposed else 0)
            for n in range(heads)
        ],
        axis=1,
    )


def heads_grad(values, slopes, head):
    return jnp.concatenate(
        [
            dot(values[:, n * head : (n + 1) * head], slopes[:, n * head : (n + 1) * head], 0, 0)
            for n in range(values.shape[1] // head)
        ],
        axis=0,
    )


def scan_rows(coef, value, reverse):
    rows = coef.shape[0]
    place = lax.broadcasted_iota(jnp.int32, coef.shape, 0)
    step = 1
    while step < rows:
        if reverse:
            inside = place < rows - step
            by = rows - step
        else:
            inside = place >= step
            by = step
        far_coef = jnp.where(inside, pltpu.roll(coef, by, 0), 1.0)
        far_value = jnp.where(inside, pltpu.roll(value, by, 0), 0.0)
        value = coef * far_value + value
        coef = coef * far_coef
        step *= 2
    return coef, value


def gates_kernel(odd, c_ref, c_own, table_r, table_i, rows_ref, mask_ref, r_ref, ii_ref, a_ref, h_ref):
    c_head = c_ref[...]
    ra = jnp.dot(c_head, table_r[0], preferred_element_type=FULL)
    ia = jnp.dot(c_head, table_i[0], preferred_element_type=FULL)
    r = jax.nn.sigmoid(ra + rows_ref[0:1, :])
    ii = jax.nn.sigmoid(ia + rows_ref[1:2, :])
    keep = mask_ref[:, 0:1]
    log_a = rows_ref[2:3, :] * r
    decay = jnp.exp(2.0 * log_a)
    gap = jnp.where(2.0 * log_a > -0.01, -expm1_small(2.0 * log_a), 1.0 - decay)
    mult = jnp.where(keep == 0.0, 1.0, jnp.sqrt(gap))
    b = (mult * c_own[...].astype(FULL) * ii).astype(LOW).astype(FULL)
    a = jnp.exp(log_a.astype(LOW).astype(FULL)) * keep
    cum_a, h_loc = scan_rows(a, b, False)
    r_ref[...] = r
    ii_ref[...] = ii
    a_ref[...] = cum_a
    h_ref[...] = h_loc


def expm1_small(values):
    return values * (
        1.0 + values * (0.5 + values * (1.0 / 6.0 + values * (1.0 / 24.0 + values / 120.0)))
    )


def gates_scan(c_ext, table_r, table_i, rows8, mask, odd, part_len, width):
    rows = c_ext.shape[0]
    head = table_r.shape[1]
    half = 128
    per = head // half
    grid = (rows // part_len, width // half)
    spec = pltpu.PrefetchScalarGridSpec(
        num_scalar_prefetch=1,
        grid=grid,
        in_specs=[
            pl.BlockSpec((part_len, head), lambda m, n, s: (m, (n + s[0]) // per)),
            pl.BlockSpec((part_len, half), lambda m, n, s: (m, n + s[0])),
            pl.BlockSpec((1, head, half), lambda m, n, s: ((n + s[0]) // per, 0, (n + s[0]) % per)),
            pl.BlockSpec((1, head, half), lambda m, n, s: ((n + s[0]) // per, 0, (n + s[0]) % per)),
            pl.BlockSpec((8, half), lambda m, n, s: (0, n)),
            pl.BlockSpec((part_len, mask.shape[1]), lambda m, n, s: (m, 0)),
        ],
        out_specs=[pl.BlockSpec((part_len, half), lambda m, n, s: (m, n))] * 4,
    )
    return pl.pallas_call(
        gates_kernel,
        grid_spec=spec,
        out_shape=[jax.ShapeDtypeStruct((rows, width), FULL)] * 4,
    )(odd, c_ext, c_ext, table_r, table_i, rows8, mask)


def back_kernel(dh_ref, a_ref, rem_ref, e_ref):
    rows = dh_ref.shape[0]
    place = lax.broadcasted_iota(jnp.int32, dh_ref.shape, 0)
    a_next = jnp.where(place < rows - 1, pltpu.roll(a_ref[...], rows - 1, 0), 1.0)
    rem, e_loc = scan_rows(a_next, dh_ref[...].astype(FULL), True)
    rem_ref[...] = rem
    e_ref[...] = e_loc


def back_scan(dh, a, part_len):
    rows, width = a.shape
    half = 128
    block = pl.BlockSpec((part_len, half), lambda m, n: (m, n))
    return pl.pallas_call(
        back_kernel,
        grid=(rows // part_len, width // half),
        in_specs=[block, block],
        out_specs=[block, block],
        out_shape=[jax.ShapeDtypeStruct((rows, width), FULL)] * 2,
    )(dh, a)


def on_device(
    inputs,
    segment,
    mixer_gain,
    input_weight,
    branch_weight,
    conv_weight,
    recur_gate,
    input_gate,
    recur_bias,
    input_bias,
    decay_rate,
    output_weight,
    second_gain,
    gate_weight,
    up_weight,
    down_weight,
    cotangent,
):
    shards = lax.axis_size("si")
    inner = lax.axis_size("sj")
    me_i = lax.axis_index("si")
    me_j = lax.axis_index("sj")
    part_len, model = inputs.shape[1:]
    lru = conv_weight.shape[0]
    taps = conv_weight.shape[1]
    width = lru // shards
    head = recur_gate.shape[1]
    edge = width % head
    rows = shards * part_len

    def mine(vector):
        return lax.dynamic_slice_in_dim(vector, me_i * width, width, 0)

    doc_all = lax.all_gather(segment[0], ("si", "sj"), axis=0, tiled=True)
    length = doc_all.shape[0]
    same_all = jnp.stack(
        [
            jnp.concatenate([jnp.full((k,), -1, jnp.int32), doc_all[: length - k]]) == doc_all
            for k in range(taps)
        ],
        axis=-1,
    ).astype(FULL)

    def chunks_of(j):
        cut = same_all.reshape(shards, inner, part_len, taps)
        return lax.dynamic_index_in_dim(cut, j, 1, keepdims=False)

    same = chunks_of(me_j)
    keep = same[:, :, 1].reshape(rows, 1)
    reset = keep == 0.0

    flat = inputs[0].astype(FULL)
    scale1 = lax.rsqrt(jnp.mean(flat * flat, axis=-1, keepdims=True) + EPSILON)
    normed = (flat * scale1 * mixer_gain).astype(LOW)
    win = shard_weight(input_weight, shards, inner)
    wbr = shard_weight(branch_weight, shards, inner)
    wout = shard_weight(output_weight, shards, inner)
    xn = lax.all_gather(normed, "si", axis=0, tiled=True)
    slope = cotangent[0]
    dm_all = lax.all_gather(slope.astype(LOW), "wt", axis=0, tiled=True)

    u = dot(xn, win).astype(LOW)
    y = dot(xn, wbr)
    u3 = u.reshape(shards, part_len, width)
    tail = u3[:, part_len - (taps - 1) :, :]
    before = lax.ppermute(tail, "sj", [(j, (j + 1) % inner) for j in range(inner)])
    shifted = jnp.concatenate([jnp.zeros_like(before[:1]), before[:-1]], axis=0)
    before = jnp.where(me_j == 0, shifted, before)
    extended = jnp.concatenate([before, u3], axis=1).astype(FULL)
    conv_mine = mine(conv_weight)
    windows = [
        extended[:, taps - 1 - k : taps - 1 - k + part_len, :] * same[:, :, k : k + 1]
        for k in range(taps)
    ]
    conv = sum(windows[k] * conv_mine[:, k] for k in range(taps))
    c_low = conv.reshape(rows, width).astype(LOW)
    c_ext = edge_swap(c_low, edge)
    recur_table = head_rows(recur_gate, shards)
    input_table = head_rows(input_gate, shards)
    c = c_low.astype(FULL)
    rate = mine(decay_rate)
    soft = -8.0 * jax.nn.softplus(rate)
    odd = (me_i % 2).astype(jnp.int32).reshape(1) * (edge // 128)
    rows8 = jnp.concatenate(
        [jnp.stack([mine(recur_bias), mine(input_bias), soft]), jnp.zeros((5, width), FULL)]
    )
    r, ii, cum_a, h_loc = gates_scan(
        c_ext, recur_table, input_table, rows8, keep, odd, part_len, width
    )
    log_a = soft * r
    mult = jnp.where(reset, 1.0, jnp.sqrt(-jnp.expm1(2.0 * log_a)))
    a = jnp.exp(log_a.astype(LOW).astype(FULL)) * keep
    a3 = a.reshape(shards, part_len, width)
    cum_a = cum_a.reshape(a3.shape)
    h_loc = h_loc.reshape(a3.shape)
    ends = lax.all_gather(jnp.stack([cum_a[:, -1], h_loc[:, -1]]), "sj", axis=2)
    ends = ends.reshape(2, shards * inner, width)
    carry = jnp.zeros((width,), FULL)
    starts = []
    for n in range(shards * inner):
        starts.append(carry)
        carry = ends[0, n] * carry + ends[1, n]
    h_in = lax.dynamic_index_in_dim(
        jnp.stack(starts).reshape(shards, inner, width), me_j, 1, keepdims=True
    )
    h = h_loc + cum_a * h_in
    h_prev = jnp.concatenate([h_in, h[:, :-1]], axis=1).reshape(rows, width)
    hr = h.reshape(rows, width).astype(LOW).astype(FULL)
    gelu_y, grad_y = gelu_both(y)
    o = (hr * gelu_y).astype(LOW)
    z_part = dot(o, wout, 1, 1).astype(LOW)
    z = lax.psum_scatter(z_part, "si", scatter_dimension=0, tiled=True)
    x1 = flat + z.astype(FULL)
    scale2 = lax.rsqrt(jnp.mean(x1 * x1, axis=-1, keepdims=True) + EPSILON)
    xn2 = lax.all_gather((x1 * scale2 * second_gain).astype(LOW), "wt", axis=0, tiled=True)

    g = dot(xn2, gate_weight)
    v = dot(xn2, up_weight)
    gelu_g, grad_g = gelu_both(g)
    hidden = (gelu_g * v).astype(LOW)
    ffn_part = dot(hidden, down_weight, 1, 1).astype(LOW)
    ffn = lax.psum_scatter(ffn_part, "wt", scatter_dimension=0, tiled=True)
    block_out = (x1 + ffn.astype(FULL)).astype(LOW)[None]
    dhidden = dot(dm_all, down_weight)
    dg = (dhidden * v * grad_g).astype(LOW)
    dv = (dhidden * gelu_g).astype(LOW)
    dxn2_part = (dot(dg, gate_weight, 1, 1) + dot(dv, up_weight, 1, 1)).astype(LOW)
    dxn2 = lax.psum_scatter(dxn2_part, "wt", scatter_dimension=0, tiled=True).astype(FULL)

    def ffn_reduce(term):
        kept = lax.psum_scatter(term.astype(LOW), ("si", "sj"), scatter_dimension=0, tiled=True)
        wide = lax.all_to_all(kept, "wt", split_axis=0, concat_axis=1, tiled=True)
        return wide.astype(FULL)

    down_grad = ffn_reduce(dot(dm_all, hidden, 0, 0))
    gate_grad = ffn_reduce(dot(xn2, dg, 0, 0))
    up_grad = ffn_reduce(dot(xn2, dv, 0, 0))

    q2 = dxn2 * second_gain
    dx1 = slope + scale2 * (q2 - x1 * scale2 * scale2 * jnp.mean(q2 * x1, axis=-1, keepdims=True))
    second_gain_grad = jnp.sum(dxn2 * x1 * scale2, axis=0)
    dz = lax.all_gather(dx1.astype(LOW), "si", axis=0, tiled=True)
    do = dot(dz, wout)

    def mixer_reduce(term):
        cut = term.astype(LOW).reshape(shards, inner * shards, -1, width).transpose(1, 0, 2, 3)
        kept = lax.psum_scatter(cut, ("sj", "wt"), scatter_dimension=0, tiled=False)
        wide = lax.all_to_all(kept, "si", split_axis=0, concat_axis=2, tiled=True)
        return wide[0].astype(FULL)

    out_grad = mixer_reduce(dot(dz, o, 0, 0))
    dh = (do * gelu_y).astype(LOW)
    dy = (do * hr * grad_y).astype(LOW)
    branch_grad = mixer_reduce(dot(xn, dy, 0, 0))

    rem, e_loc = back_scan(dh, a, part_len)
    rem = rem.reshape(a3.shape)
    e_loc = e_loc.reshape(a3.shape)
    heads_out = jnp.stack([cum_a[:, -1], a3[:, 0] * e_loc[:, 0]])
    firsts = lax.all_gather(heads_out, "sj", axis=2).reshape(2, shards * inner, width)
    carry = jnp.zeros((width,), FULL)
    nexts = []
    for n in reversed(range(shards * inner)):
        nexts.append(carry)
        carry = firsts[0, n] * carry + firsts[1, n]
    e_in = lax.dynamic_index_in_dim(
        jnp.stack(nexts[::-1]).reshape(shards, inner, width), me_j, 1, keepdims=True
    )
    e = (e_loc + rem * e_in).reshape(rows, width)
    dla = (e * h_prev * a).astype(LOW).astype(FULL)
    dbr = e.astype(LOW).astype(FULL)
    dmult = jnp.where(reset, 0.0, -jnp.exp(2.0 * log_a) / mult)
    dlog_a = dla + dbr * c * ii * dmult
    dra_f = soft * dlog_a * r * (1.0 - r)
    dia_f = dbr * mult * c * ii * (1.0 - ii)
    recur_bias_grad = jnp.sum(dra_f, axis=0)
    input_bias_grad = jnp.sum(dia_f, axis=0)
    decay_grad = jnp.sum(-8.0 * dlog_a * r, axis=0) * jax.nn.sigmoid(rate)
    slopes = jnp.concatenate([dra_f.astype(LOW), dia_f.astype(LOW)], axis=0)
    slopes = edge_swap(slopes, edge)
    dra, dia = slopes[:rows], slopes[rows:]
    recur_gate_grad = heads_grad(c_ext, dra, head)
    input_gate_grad = heads_grad(c_ext, dia, head)
    mixed = heads_dot(dra, recur_table, True) + heads_dot(dia, input_table, True)
    dc = (dbr * mult * ii + own_part(mixed, edge)).reshape(shards, part_len, width)
    conv_grad = jnp.stack([jnp.sum(windows[k] * dc, axis=(0, 1)) for k in range(taps)], axis=-1)
    lead = lax.ppermute(dc[:, : taps - 1], "sj", [(j, (j - 1) % inner) for j in range(inner)])
    moved = jnp.concatenate([lead[1:], jnp.zeros_like(lead[:1])], axis=0)
    lead = jnp.where(me_j == inner - 1, moved, lead)
    next_j = (me_j + 1) % inner
    same_next = chunks_of(next_j)[:, : taps - 1]
    shifted = jnp.concatenate([same_next[1:], jnp.zeros_like(same_next[:1])], axis=0)
    same_next = jnp.where(me_j == inner - 1, shifted, same_next)
    dc_ext = jnp.concatenate([dc, lead], axis=1)
    same_ext = jnp.concatenate([same, same_next], axis=1)
    du = sum(
        (dc_ext * same_ext[:, :, k : k + 1])[:, k : k + part_len] * conv_mine[:, k]
        for k in range(taps)
    )
    du = du.reshape(rows, width).astype(LOW)
    dxn_part = (dot(du, win, 1, 1) + dot(dy, wbr, 1, 1)).astype(LOW)
    dxn = lax.psum_scatter(dxn_part, "si", scatter_dimension=0, tiled=True).astype(FULL)
    input_weight_grad = mixer_reduce(dot(xn, du, 0, 0))
    q1 = dxn * mixer_gain
    input_grad = dx1 + scale1 * (
        q1 - flat * scale1 * scale1 * jnp.mean(q1 * flat, axis=-1, keepdims=True)
    )
    mixer_gain_grad = jnp.sum(dxn * flat * scale1, axis=0)

    small = jnp.concatenate(
        [
            own_part(recur_gate_grad.T, edge).T,
            own_part(input_gate_grad.T, edge).T,
            conv_grad,
            recur_bias_grad[:, None],
            input_bias_grad[:, None],
            decay_grad[:, None],
        ],
        axis=1,
    )
    small = lax.psum_scatter(small, ("sj", "wt"), scatter_dimension=0, tiled=True)
    gains = jnp.stack([mixer_gain_grad, second_gain_grad], axis=1)
    gains = lax.psum_scatter(gains, ("si", "sj", "wt"), scatter_dimension=0, tiled=True)
    at = 2 * head + taps
    return (
        block_out,
        input_grad[None],
        gains[:, 0],
        input_weight_grad,
        branch_grad,
        small[:, 2 * head : at],
        small[:, :head],
        small[:, head : 2 * head],
        small[:, at],
        small[:, at + 1],
        small[:, at + 2],
        out_grad,
        gains[:, 1],
        gate_grad,
        up_grad,
        down_grad,
    )


def solution(mesh):
    shards = mesh.shape["wt"]
    inner = mesh.shape["seq"] // shards
    cut = Mesh(mesh.devices.reshape(shards, inner, shards), ("si", "sj", "wt"))
    seq = ("si", "sj")
    tokens = P("wt", seq, None)
    columns = P(None, "wt")
    row = P(("si", "sj", "wt"))
    flat_rows = P(("si", "sj", "wt"), None)
    return jax.shard_map(
        on_device,
        mesh=cut,
        in_specs=(
            tokens,
            P("wt", seq),
            P(),
            columns,
            columns,
            P(),
            P(),
            P(),
            P(),
            P(),
            P(),
            columns,
            P(),
            columns,
            columns,
            columns,
            tokens,
        ),
        out_specs=(
            tokens,
            tokens,
            row,
            flat_rows,
            flat_rows,
            flat_rows,
            flat_rows,
            flat_rows,
            row,
            row,
            row,
            flat_rows,
            row,
            flat_rows,
            flat_rows,
            flat_rows,
        ),
        check_vma=False,
    )
```

```python
import functools
import math

import jax
import jax.numpy as jnp
from jax import lax
from jax.experimental import pallas as pl
from jax.experimental.pallas import tpu as pltpu
from jax.sharding import PartitionSpec as P

EPSILON = 1e-06
LOW = jnp.bfloat16
FULL = jnp.float32


def dot(left, right, left_dim=1, right_dim=0):
    return lax.dot_general(
        left, right, (((left_dim,), (right_dim,)), ((), ())), preferred_element_type=FULL
    )


def gelu_both(values):
    slope = jnp.sqrt(2.0 / jnp.pi).astype(FULL)
    inner = jnp.tanh(slope * (values + 0.044715 * values * values * values))
    gelu = 0.5 * values * (1.0 + inner)
    grad = 0.5 * (1.0 + inner) + 0.5 * values * (1.0 - inner * inner) * slope * (
        1.0 + 3.0 * 0.044715 * values * values
    )
    return gelu, grad


def head_rows(gate_rows, shards):
    head = gate_rows.shape[1]
    width = gate_rows.shape[0] // shards
    heads = -(-width // head)
    first = (lax.axis_index("wt") * width) // head
    table = gate_rows.reshape(-1, head, head)
    return lax.dynamic_slice_in_dim(table, first, heads, 0)


def edge_swap(values, edge):
    me = lax.axis_index("wt")
    shards = lax.axis_size("wt")
    odd = me % 2 == 1
    mine = jnp.where(odd, values[:, :edge], values[:, -edge:])
    other = lax.ppermute(mine, "wt", [(i, i ^ 1) for i in range(shards)])
    return jnp.where(
        odd,
        jnp.concatenate([other, values], axis=1),
        jnp.concatenate([values, other], axis=1),
    )


def own_part(values, edge):
    odd = lax.axis_index("wt") % 2 == 1
    return jnp.where(odd, values[:, edge:], values[:, :-edge])


def heads_dot(values, table, transposed=False):
    heads, head, _ = table.shape
    return jnp.concatenate(
        [
            dot(values[:, n * head : (n + 1) * head], table[n], 1, 1 if transposed else 0)
            for n in range(heads)
        ],
        axis=1,
    )


def heads_grad(values, slopes, head):
    return jnp.concatenate(
        [
            dot(values[:, n * head : (n + 1) * head], slopes[:, n * head : (n + 1) * head], 0, 0)
            for n in range(values.shape[1] // head)
        ],
        axis=0,
    )


def scan_rows(coef, value, reverse):
    rows = coef.shape[0]
    place = lax.broadcasted_iota(jnp.int32, coef.shape, 0)
    step = 1
    while step < rows:
        if reverse:
            inside = place < rows - step
            by = rows - step
        else:
            inside = place >= step
            by = step
        far_coef = jnp.where(inside, pltpu.roll(coef, by, 0), 1.0)
        far_value = jnp.where(inside, pltpu.roll(value, by, 0), 0.0)
        value = coef * far_value + value
        coef = coef * far_coef
        step *= 2
    return coef, value


def gates_kernel(odd, c_ref, c_own, table_r, table_i, rows_ref, mask_ref, r_ref, ii_ref, a_ref, h_ref):
    c_head = c_ref[...]
    ra = jnp.dot(c_head, table_r[0], preferred_element_type=FULL)
    ia = jnp.dot(c_head, table_i[0], preferred_element_type=FULL)
    r = jax.nn.sigmoid(ra + rows_ref[0:1, :])
    ii = jax.nn.sigmoid(ia + rows_ref[1:2, :])
    keep = mask_ref[:, 0:1]
    log_a = rows_ref[2:3, :] * r
    decay = jnp.exp(2.0 * log_a)
    gap = jnp.where(2.0 * log_a > -0.01, -expm1_small(2.0 * log_a), 1.0 - decay)
    mult = jnp.where(keep == 0.0, 1.0, jnp.sqrt(gap))
    b = (mult * c_own[...].astype(FULL) * ii).astype(LOW).astype(FULL)
    a = jnp.exp(log_a.astype(LOW).astype(FULL)) * keep
    cum_a, h_loc = scan_rows(a, b, False)
    r_ref[...] = r
    ii_ref[...] = ii
    a_ref[...] = cum_a
    h_ref[...] = h_loc


def expm1_small(values):
    return values * (
        1.0 + values * (0.5 + values * (1.0 / 6.0 + values * (1.0 / 24.0 + values / 120.0)))
    )


def gates_scan(c_ext, table_r, table_i, rows8, mask, odd, part_len, width):
    rows = c_ext.shape[0]
    head = table_r.shape[1]
    half = 128
    per = head // half
    grid = (rows // part_len, width // half)
    spec = pltpu.PrefetchScalarGridSpec(
        num_scalar_prefetch=1,
        grid=grid,
        in_specs=[
            pl.BlockSpec((part_len, head), lambda m, n, s: (m, (n + s[0]) // per)),
            pl.BlockSpec((part_len, half), lambda m, n, s: (m, n + s[0])),
            pl.BlockSpec((1, head, half), lambda m, n, s: ((n + s[0]) // per, 0, (n + s[0]) % per)),
            pl.BlockSpec((1, head, half), lambda m, n, s: ((n + s[0]) // per, 0, (n + s[0]) % per)),
            pl.BlockSpec((8, half), lambda m, n, s: (0, n)),
            pl.BlockSpec((part_len, mask.shape[1]), lambda m, n, s: (m, 0)),
        ],
        out_specs=[pl.BlockSpec((part_len, half), lambda m, n, s: (m, n))] * 4,
    )
    return pl.pallas_call(
        gates_kernel,
        grid_spec=spec,
        out_shape=[jax.ShapeDtypeStruct((rows, width), FULL)] * 4,
    )(odd, c_ext, c_ext, table_r, table_i, rows8, mask)


def back_kernel(dh_ref, a_ref, rem_ref, e_ref):
    rows = dh_ref.shape[0]
    place = lax.broadcasted_iota(jnp.int32, dh_ref.shape, 0)
    a_next = jnp.where(place < rows - 1, pltpu.roll(a_ref[...], rows - 1, 0), 1.0)
    rem, e_loc = scan_rows(a_next, dh_ref[...].astype(FULL), True)
    rem_ref[...] = rem
    e_ref[...] = e_loc


def back_scan(dh, a, part_len):
    rows, width = a.shape
    half = 128
    block = pl.BlockSpec((part_len, half), lambda m, n: (m, n))
    return pl.pallas_call(
        back_kernel,
        grid=(rows // part_len, width // half),
        in_specs=[block, block],
        out_specs=[block, block],
        out_shape=[jax.ShapeDtypeStruct((rows, width), FULL)] * 2,
    )(dh, a)


MESH = pl.DeviceIdType.MESH


def remote(source, target, sent, landed, to):
    return pltpu.make_async_remote_copy(
        src_ref=source,
        dst_ref=target,
        send_sem=sent,
        recv_sem=landed,
        device_id={"wt": to},
        device_id_type=MESH,
    )


def greet(n, me, pair=False):
    barrier = pltpu.get_barrier_semaphore()

    @pl.when(me > 0)
    def _():
        pl.semaphore_signal(barrier, 1, device_id={"wt": me - 1}, device_id_type=MESH)

    @pl.when(me < n - 1)
    def _():
        pl.semaphore_signal(barrier, 1, device_id={"wt": me + 1}, device_id_type=MESH)

    peers = (me > 0).astype(jnp.int32) + (me < n - 1).astype(jnp.int32)
    if pair:
        place = lax.axis_index("seq")
        other = {"seq": place + 1 - 2 * lax.rem(place, 2)}
        pl.semaphore_signal(barrier, 1, device_id=other, device_id_type=MESH)
        peers = peers + 1
    pl.semaphore_wait(barrier, peers)


class LineGather:
    def __init__(self, n, me, blocks, sent, landed):
        self.n, self.me, self.blocks, self.sent, self.landed = n, me, blocks, sent, landed

    def rightward(self, d):
        block = self.blocks.at[self.me - d]
        return remote(block, block, self.sent.at[0, d], self.landed.at[0, d + 1], self.me + 1)

    def leftward(self, d):
        block = self.blocks.at[self.me + d]
        return remote(block, block, self.sent.at[1, d], self.landed.at[1, d + 1], self.me - 1)

    def start(self):
        @pl.when(self.me < self.n - 1)
        def _():
            self.rightward(0).start()

        @pl.when(self.me > 0)
        def _():
            self.leftward(0).start()

    def arrive(self, d):
        n, me = self.n, self.me

        @pl.when(me - d >= 0)
        def _():
            block = self.blocks.at[me - d]
            remote(block, block, self.sent.at[0, 0], self.landed.at[0, d], me).wait_recv()

            @pl.when(me < n - 1)
            def _():
                self.rightward(d).start()

        @pl.when(me + d < n)
        def _():
            block = self.blocks.at[me + d]
            remote(block, block, self.sent.at[1, 0], self.landed.at[1, d], me).wait_recv()

            @pl.when(me > 0)
            def _():
                self.leftward(d).start()

    def each(self, d, use):
        def side(k, carry):
            q = self.me + (2 * k - 1) * d

            @pl.when((q >= 0) & (q < self.n))
            def _():
                use(q)

            return carry

        lax.fori_loop(0, 2, side, 0)

    def finish(self):
        n, me = self.n, self.me
        for d in range(n - 1):

            @pl.when((me - d >= 0) & (me < n - 1))
            def _():
                self.rightward(d).wait_send()

            @pl.when((me + d < n) & (me > 0))
            def _():
                self.leftward(d).wait_send()


def line_gather(n, me, blocks, sent, landed, use, ready):
    line = LineGather(n, me, blocks, sent, landed)
    line.start()
    ready()
    use(me)

    def step(d, carry):
        line.arrive(d)
        line.each(d, use)
        return carry

    lax.fori_loop(1, n, step, 0)
    line.finish()


class LineReduce:
    def __init__(self, n, me, parts, slots, sent, landed):
        self.n, self.me, self.parts, self.slots = n, me, parts, slots
        self.sent, self.landed = sent, landed

    def rightward(self, k):
        source, target = self.parts.at[self.n - 1 - k], self.slots.at[0, k]
        return remote(source, target, self.sent.at[0, k], self.landed.at[0, k], self.me + 1)

    def leftward(self, k):
        source, target = self.parts.at[k], self.slots.at[1, k]
        return remote(source, target, self.sent.at[1, k], self.landed.at[1, k], self.me - 1)

    def arrived(self, side, k):
        slot = self.slots.at[side, k]
        remote(slot, slot, self.sent.at[side, k], self.landed.at[side, k], self.me).wait_recv()

    def add(self, q, side, k):
        total = self.parts[q].astype(FULL) + self.slots[side, k].astype(FULL)
        self.parts[q] = total.astype(LOW)

    def start(self, partial, early=True):
        n, me = self.n, self.me

        def first(k, carry):
            def side(which, inner):
                q = jnp.where(which == 0, n - 1 - k, k)

                @pl.when(jnp.where(which == 0, q > me, q < me))
                def _():
                    partial(q)

                return inner

            lax.fori_loop(0, 2, side, 0)

            @pl.when((k == 0) & (me == 0) & early)
            def _():
                self.rightward(0).start()

            @pl.when((k == 0) & (me == n - 1) & early)
            def _():
                self.leftward(0).start()

            return carry

        lax.fori_loop(0, n - 1, first, 0)
        partial(me)

    def relay(self, k):
        n, me = self.n, self.me

        @pl.when(n - 1 - k > me)
        def _():
            @pl.when(me > 0)
            def _():
                self.arrived(0, k)
                self.add(n - 1 - k, 0, k)

            if k > 0:
                self.rightward(k - 1).wait_send()

            @pl.when((me > 0) | (k > 0))
            def _():
                self.rightward(k).start()

        @pl.when(k < me)
        def _():
            @pl.when(me < n - 1)
            def _():
                self.arrived(1, k)
                self.add(k, 1, k)

            if k > 0:
                self.leftward(k - 1).wait_send()

            @pl.when((me < n - 1) | (k > 0))
            def _():
                self.leftward(k).start()

    def total(self):
        n, me = self.n, self.me

        @pl.when(me > 0)
        def _():
            self.arrived(0, n - 1 - me)

        @pl.when(me < n - 1)
        def _():
            self.arrived(1, me)

        total = self.parts[me].astype(FULL)
        other = self.slots[0, jnp.clip(n - 1 - me, 0, n - 2)].astype(FULL)
        total = total + jnp.where(me > 0, other, 0.0)
        other = self.slots[1, jnp.clip(me, 0, n - 2)].astype(FULL)
        return total + jnp.where(me < n - 1, other, 0.0)

    def finish(self):
        @pl.when(self.me < self.n - 1)
        def _():
            self.rightward(self.n - 2 - self.me).wait_send()

        @pl.when(self.me > 0)
        def _():
            self.leftward(self.me - 1).wait_send()


class LineBoth:
    def __init__(self, gather, back):
        self.gather, self.back = gather, back
        self.n, self.me = gather.n, gather.me

    def sends(self, side, t, act):
        n, me = self.n, self.me
        place = me if side == 0 else n - 1 - me
        spread = self.gather.rightward if side == 0 else self.gather.leftward
        pull = self.back.rightward if side == 0 else self.back.leftward

        @pl.when(place < n - 1)
        def _():
            @pl.when(t <= place)
            def _():
                act(spread(t))

            @pl.when(t > place)
            def _():
                act(pull(t - place - 1))

    def step(self, t):
        n, me = self.n, self.me
        for side in range(2):
            place = me if side == 0 else n - 1 - me
            if t > 0:

                @pl.when(t <= place)
                def _():
                    block = self.gather.blocks.at[me - t if side == 0 else me + t]
                    remote(
                        block, block, self.gather.sent.at[side, 0], self.gather.landed.at[side, t], me
                    ).wait_recv()

                @pl.when((t > place) & (place > 0))
                def _():
                    k = t - place - 1
                    self.back.arrived(side, k)
                    self.back.add(n - 1 - k if side == 0 else k, side, k)

                self.sends(side, t - 1, lambda copy: copy.wait_send())
            self.sends(side, t, lambda copy: copy.start())

    def finish(self):
        for side in range(2):
            self.sends(side, self.n - 1, lambda copy: copy.wait_send())


def line_reduce(n, me, parts, slots, sent, landed, partial, between, finish):
    line = LineReduce(n, me, parts, slots, sent, landed)
    line.start(partial)
    for k in range(n - 1):
        line.relay(k)
        between(k)
    finish(line.total())
    line.finish()


def tiles(count, size, body):
    def step(t, carry):
        body(pl.ds(pl.multiple_of(t * size, size), size))
        return carry

    lax.fori_loop(0, count // size, step, 0)


def tile_of(width, limit):
    size = limit
    while width % size:
        size -= 128
    return size


VMEM = pl.BlockSpec(memory_space=pltpu.VMEM)
ANY = pl.BlockSpec(memory_space=pl.ANY)


def gather_sems(n):
    return [pltpu.SemaphoreType.DMA((2, n)), pltpu.SemaphoreType.DMA((2, n + 1))]


def reduce_sems(n):
    return [pltpu.SemaphoreType.DMA((2, n)), pltpu.SemaphoreType.DMA((2, n))]


def lasting(micros):
    return pl.CostEstimate(
        flops=int(micros * 1.0e9), bytes_accessed=int(micros * 3.4e6), transcendentals=0
    )


def comm_params(number):
    return pltpu.CompilerParams(
        collective_id=number, has_side_effects=True, vmem_limit_bytes=64 * 1024 * 1024
    )


def enter_kernel(
    n, x_ref, gain_ref, doc_ref, win_hbm, wbr_hbm, xn_ref, u_ref, y_ref, docs_ref, win, wbr, docs, sent, landed, dsent, dlanded, local
):
    me = lax.axis_index("wt")
    loads = [
        pltpu.make_async_copy(win_hbm, win, local.at[0]),
        pltpu.make_async_copy(wbr_hbm, wbr, local.at[1]),
    ]
    for load in loads:
        load.start()
    docs[me] = jnp.broadcast_to(doc_ref[...], docs.shape[1:])
    flat = x_ref[...].astype(FULL)
    scale = lax.rsqrt(jnp.mean(flat * flat, axis=-1, keepdims=True) + EPSILON)
    xn_ref[me] = (flat * scale * gain_ref[...]).astype(LOW)
    greet(n, me)
    notes = LineGather(n, me, docs, dsent, dlanded)
    line = LineGather(n, me, xn_ref, sent, landed)
    notes.start()
    line.start()
    for load in loads:
        load.wait()

    def use(q):
        block = xn_ref[q]
        u_ref[q] = dot(block, win[...]).astype(LOW)
        y_ref[q] = dot(block, wbr[...])

    use(me)

    def step(d, carry):
        notes.arrive(d)
        line.arrive(d)
        line.each(d, use)
        return carry

    lax.fori_loop(1, n, step, 0)
    docs_ref[...] = docs[...]
    notes.finish()
    line.finish()


def enter(n, x, gain, doc, win, wbr):
    rows, model = x.shape
    width = win.shape[1]
    return pl.pallas_call(
        functools.partial(enter_kernel, n),
        out_shape=[
            jax.ShapeDtypeStruct((n, rows, model), LOW),
            jax.ShapeDtypeStruct((n, rows, width), LOW),
            jax.ShapeDtypeStruct((n, rows, width), FULL),
            jax.ShapeDtypeStruct((n, 8, rows), jnp.int32),
        ],
        in_specs=[VMEM, VMEM, VMEM, ANY, ANY],
        out_specs=[VMEM, VMEM, VMEM, VMEM],
        scratch_shapes=[
            pltpu.VMEM(win.shape, LOW),
            pltpu.VMEM(wbr.shape, LOW),
            pltpu.VMEM((n, 8, rows), jnp.int32),
        ]
        + gather_sems(n)
        + gather_sems(n)
        + [pltpu.SemaphoreType.DMA((2,))],
        compiler_params=comm_params(0),
        cost_estimate=lasting(50),
    )(x, gain, doc, win, wbr)


def close_kernel(
    n, o_ref, x_ref, gain_ref, w_ref, slope_ref, x1_ref, xn2_ref, dm_ref, parts, slots, sent, landed, gsent, glanded
):
    me = lax.axis_index("wt")
    dm_ref[me] = slope_ref[...].astype(LOW)
    greet(n, me)
    model = w_ref.shape[0]

    def partial(q):
        block = o_ref[q]

        def tile(at):
            parts[q, :, at] = dot(block, w_ref[at, :], 1, 1).astype(LOW)

        tiles(model, tile_of(model, 512), tile)

    def finish(total):
        x1 = x_ref[...].astype(FULL) + total
        x1_ref[...] = x1
        scale = lax.rsqrt(jnp.mean(x1 * x1, axis=-1, keepdims=True) + EPSILON)
        xn2_ref[...] = (x1 * scale * gain_ref[...]).astype(LOW)

    back = LineReduce(n, me, parts, slots, sent, landed)
    both = LineBoth(LineGather(n, me, dm_ref, gsent, glanded), back)
    both.step(0)
    back.start(partial, False)
    for t in range(1, n):
        both.step(t)
    finish(back.total())
    both.finish()


def close(n, o, x, gain, weight, slope):
    rows, model = x.shape
    return pl.pallas_call(
        functools.partial(close_kernel, n),
        out_shape=[
            jax.ShapeDtypeStruct((rows, model), FULL),
            jax.ShapeDtypeStruct((rows, model), LOW),
            jax.ShapeDtypeStruct((n, rows, model), LOW),
        ],
        in_specs=[VMEM] * 5,
        out_specs=[VMEM] * 3,
        scratch_shapes=[
            pltpu.VMEM((n, rows, model), LOW),
            pltpu.VMEM((2, n - 1, rows, model), LOW),
        ]
        + reduce_sems(n)
        + gather_sems(n),
        compiler_params=comm_params(1),
        cost_estimate=lasting(65),
    )(o, x, gain, weight, slope)


class PairSum:
    def __init__(self, part, halves, landing, sent, landed, free, flush, tag):
        self.me = lax.axis_index("seq")
        self.mine = lax.rem(self.me, 2)
        self.part, self.halves, self.landing = part, halves, landing
        self.sent, self.landed, self.free, self.flush = sent, landed, free, flush
        self.count = tag

    def other(self):
        return {"seq": self.me + 1 - 2 * self.mine}

    def send(self, slot):
        return pltpu.make_async_remote_copy(
            src_ref=self.halves.at[slot, 1 - self.mine],
            dst_ref=self.landing.at[slot],
            send_sem=self.sent.at[slot],
            recv_sem=self.landed.at[slot],
            device_id=self.other(),
            device_id_type=MESH,
        )

    def run(self, steps, compute, target):
        half = self.landing.shape[1]
        for t in range(steps):
            slot = self.count % 2

            def out(slot, t):
                return pltpu.make_async_copy(
                    self.halves.at[slot, self.mine],
                    target.at[pl.ds(t * half, half), :],
                    self.flush.at[slot],
                )

            if self.count >= 2:
                self.send(slot).wait_send()
                pltpu.make_async_copy(
                    self.halves.at[slot, self.mine], target.at[pl.ds(0, half), :], self.flush.at[slot]
                ).wait()
                pl.semaphore_wait(self.free, 1)
            compute(t, self.halves.at[slot])
            self.send(slot).start()
            self.send(slot).wait_recv()
            total = self.halves[slot, self.mine].astype(FULL) + self.landing[slot].astype(FULL)
            self.halves[slot, self.mine] = total.astype(LOW)
            pl.semaphore_signal(self.free, 1, device_id=self.other(), device_id_type=MESH)
            out(slot, t).start()
            self.count += 1

    def finish(self, target):
        half = self.landing.shape[1]
        for slot in range(2):
            self.send(slot).wait_send()
            pltpu.make_async_copy(
                self.halves.at[slot, self.mine], target.at[pl.ds(0, half), :], self.flush.at[slot]
            ).wait()
        pl.semaphore_wait(self.free, 2)


def pair_scratch(half, width):
    return [
        pltpu.VMEM((2, 2, half, width), LOW),
        pltpu.VMEM((2, half, width), LOW),
        pltpu.SemaphoreType.DMA((2,)),
        pltpu.SemaphoreType.DMA((2,)),
        pltpu.SemaphoreType.REGULAR,
        pltpu.SemaphoreType.DMA((2,)),
    ]


def pair_tile(model, places):
    size = 2 * model // places
    return size if size % 128 == 0 else size * 128 // math.gcd(size, 128)


def pair_dot(left, right, part, size):
    n, rows, _ = left.shape

    def compute(t, halves):
        lhs = left[:, :, pl.ds(t * size, size)].reshape(n * rows, size)
        width = right.shape[2]

        def tile(at):
            rhs = right[:, :, at].reshape(n * rows, -1)
            value = dot(lhs, rhs, 0, 0).astype(LOW)
            for k in range(size // (2 * part)):
                for side in range(2):
                    first = (2 * k + side) * part
                    halves[side, k * part : (k + 1) * part, at] = value[first : first + part]

        tiles(width, tile_of(width, 640), tile)

    return compute


def ffn_kernel(
    n,
    places,
    xn2_ref,
    dm_hbm,
    wg_hbm,
    wu_hbm,
    wd_hbm,
    dxn2_ref,
    hidden_hbm,
    gate_hbm,
    up_hbm,
    down_hbm,
    xall,
    dm,
    wg,
    wu,
    wd,
    hidden,
    dg,
    dv,
    parts,
    slots,
    halves,
    landing,
    psent,
    planded,
    free,
    pflush,
    gsent,
    glanded,
    rsent,
    rlanded,
    local,
    flush,
):
    me = lax.axis_index("wt")
    rows, model = xn2_ref.shape
    units = wg.shape[1]
    cut = tile_of(units, 640)
    span = tile_of(model, 512)
    loads = [
        pltpu.make_async_copy(source, target, local.at[k])
        for k, (source, target) in enumerate(
            [(wg_hbm, wg), (wu_hbm, wu), (wd_hbm, wd), (dm_hbm, dm)]
        )
    ]
    for load in loads:
        load.start()
    xall[me] = xn2_ref[...]
    greet(n, me, True)

    def ready():
        for load in loads:
            load.wait()

    def use(q):
        def tile(at):
            block = xall[q]
            g = dot(block, wg[:, at])
            v = dot(block, wu[:, at])
            back = dot(dm[q], wd[:, at])
            gelu, slope = gelu_both(g)
            hidden[q, :, at] = (gelu * v).astype(LOW)
            dg[q, :, at] = (back * v * slope).astype(LOW)
            dv[q, :, at] = (back * gelu).astype(LOW)

        tiles(units, cut, tile)

    line_gather(n, me, xall, gsent, glanded, use, ready)
    out = pltpu.make_async_copy(hidden, hidden_hbm, flush.at[0])
    out.start()

    def partial(q):
        def tile(at):
            total = dot(dg[q], wg[at, :], 1, 1) + dot(dv[q], wu[at, :], 1, 1)
            parts[q, :, at] = total.astype(LOW)

        tiles(model, span, tile)

    part = model // places
    size = pair_tile(model, places)
    pair = PairSum(part, halves, landing, psent, planded, free, pflush, 0)

    def between(k):
        if k == 0:
            pair.run(model // size, pair_dot(dm, hidden, part, size), down_hbm)
        if k == 1:
            pair.run(model // size, pair_dot(xall, dg, part, size), gate_hbm)
        if k == n - 2:
            pair.run(model // size, pair_dot(xall, dv, part, size), up_hbm)

    def finish(total):
        dxn2_ref[...] = total

    line_reduce(n, me, parts, slots, rsent, rlanded, partial, between, finish)
    pair.finish(up_hbm)
    out.wait()


def ffn(n, places, xn2, dm, wg, wu, wd):
    rows, model = xn2.shape
    units = wg.shape[1]
    grad = jax.ShapeDtypeStruct((model // 2, units), LOW)
    return pl.pallas_call(
        functools.partial(ffn_kernel, n, places),
        out_shape=[
            jax.ShapeDtypeStruct((rows, model), FULL),
            jax.ShapeDtypeStruct((n, rows, units), LOW),
            grad,
            grad,
            grad,
        ],
        in_specs=[VMEM, ANY, ANY, ANY, ANY],
        out_specs=[VMEM, ANY, ANY, ANY, ANY],
        scratch_shapes=[
            pltpu.VMEM((n, rows, model), LOW),
            pltpu.VMEM((n, rows, model), LOW),
            pltpu.VMEM((model, units), LOW),
            pltpu.VMEM((model, units), LOW),
            pltpu.VMEM((model, units), LOW),
            pltpu.VMEM((n, rows, units), LOW),
            pltpu.VMEM((n, rows, units), LOW),
            pltpu.VMEM((n, rows, units), LOW),
            pltpu.VMEM((n, rows, model), LOW),
            pltpu.VMEM((2, n - 1, rows, model), LOW),
        ]
        + pair_scratch(pair_tile(model, places) // 2, units)
        + gather_sems(n)
        + reduce_sems(n)
        + [pltpu.SemaphoreType.DMA((4,)), pltpu.SemaphoreType.DMA((1,))],
        compiler_params=comm_params(2),
        cost_estimate=lasting(125),
    )(xn2, dm, wg, wu, wd)


def back_in_kernel(
    n,
    dxn2_ref,
    x1_ref,
    slope_ref,
    gain_ref,
    w_hbm,
    hidden_hbm,
    wd_hbm,
    dx1_ref,
    dz_ref,
    do_ref,
    sum_ref,
    out_ref,
    w,
    hidden,
    wd,
    parts,
    slots,
    sent,
    landed,
    rsent,
    rlanded,
    local,
):
    me = lax.axis_index("wt")
    loads = [
        pltpu.make_async_copy(source, target, local.at[k])
        for k, (source, target) in enumerate([(w_hbm, w), (hidden_hbm, hidden), (wd_hbm, wd)])
    ]
    for load in loads:
        load.start()
    x1 = x1_ref[...]
    dxn2 = dxn2_ref[...]
    model = x1.shape[1]
    scale = lax.rsqrt(jnp.mean(x1 * x1, axis=-1, keepdims=True) + EPSILON)
    q2 = dxn2 * gain_ref[...]
    pull = jnp.mean(q2 * x1, axis=-1, keepdims=True)
    dx1 = slope_ref[...] + scale * (q2 - x1 * (scale * scale * pull))
    dx1_ref[...] = dx1
    dz_ref[me] = dx1.astype(LOW)
    greet(n, me)
    line = LineGather(n, me, dz_ref, sent, landed)
    back = LineReduce(n, me, parts, slots, rsent, rlanded)
    both = LineBoth(line, back)
    both.step(0)
    sum_ref[...] = jnp.sum(dxn2 * x1 * scale, axis=0, keepdims=True)
    for load in loads:
        load.wait()

    def use(q):
        do_ref[q] = dot(dz_ref[q], w[...])

    def partial(q):
        def tile(at):
            parts[q, :, at] = dot(hidden[q], wd[at, :], 1, 1).astype(LOW)

        tiles(model, tile_of(model, 512), tile)

    back.start(partial, False)
    use(me)
    for t in range(1, n):
        both.step(t)
        line.each(t, use)
    out_ref[...] = (x1_ref[...] + back.total()).astype(LOW)
    both.finish()


def back_in(n, dxn2, x1, slope, gain, weight, hidden, wd):
    rows, model = x1.shape
    return pl.pallas_call(
        functools.partial(back_in_kernel, n),
        out_shape=[
            jax.ShapeDtypeStruct((rows, model), FULL),
            jax.ShapeDtypeStruct((n, rows, model), LOW),
            jax.ShapeDtypeStruct((n, rows, weight.shape[1]), FULL),
            jax.ShapeDtypeStruct((1, model), FULL),
            jax.ShapeDtypeStruct((rows, model), LOW),
        ],
        in_specs=[VMEM] * 4 + [ANY] * 3,
        out_specs=[VMEM] * 5,
        scratch_shapes=[
            pltpu.VMEM(weight.shape, LOW),
            pltpu.VMEM(hidden.shape, LOW),
            pltpu.VMEM(wd.shape, LOW),
            pltpu.VMEM((n, rows, model), LOW),
            pltpu.VMEM((2, n - 1, rows, model), LOW),
        ]
        + gather_sems(n)
        + reduce_sems(n)
        + [pltpu.SemaphoreType.DMA((3,))],
        compiler_params=comm_params(3),
        cost_estimate=lasting(65),
    )(dxn2, x1, slope, gain, weight, hidden, wd)


def leave_kernel(
    n,
    places,
    du_ref,
    dy_ref,
    o_ref,
    x_ref,
    dx1_ref,
    gain_ref,
    xn_hbm,
    dz_hbm,
    win_hbm,
    wbr_hbm,
    grad_ref,
    sum_ref,
    mix_hbm,
    xn,
    dz,
    win,
    wbr,
    parts,
    slots,
    halves,
    landing,
    psent,
    planded,
    free,
    pflush,
    sent,
    landed,
    local,
):
    me = lax.axis_index("wt")
    loads = [
        pltpu.make_async_copy(source, target, local.at[k])
        for k, (source, target) in enumerate(
            [(win_hbm, win), (wbr_hbm, wbr), (xn_hbm, xn), (dz_hbm, dz)]
        )
    ]
    for load in loads:
        load.start()
    greet(n, me, True)
    for load in loads:
        load.wait()
    model = win.shape[0]

    def partial(q):
        def tile(at):
            total = dot(du_ref[q], win[at, :], 1, 1) + dot(dy_ref[q], wbr[at, :], 1, 1)
            parts[q, :, at] = total.astype(LOW)

        tiles(model, tile_of(model, 512), tile)

    part = model // places
    size = pair_tile(model, places)
    width = du_ref.shape[2]
    pair = PairSum(part, halves, landing, psent, planded, free, pflush, 0)

    def compute(t, target):
        for k, (left, right) in enumerate([(dz, o_ref), (xn, dy_ref), (xn, du_ref)]):
            columns = pl.ds(k * width, width)
            pair_dot(left, right, part, size)(t, target.at[:, :, columns])

    def between(k):
        if k == 0:
            pair.run(model // size, compute, mix_hbm)

    def finish(total):
        flat = x_ref[...].astype(FULL)
        scale = lax.rsqrt(jnp.mean(flat * flat, axis=-1, keepdims=True) + EPSILON)
        q1 = total * gain_ref[...]
        pull = jnp.mean(q1 * flat, axis=-1, keepdims=True)
        grad_ref[...] = dx1_ref[...] + scale * (q1 - flat * (scale * scale * pull))
        sum_ref[...] = jnp.sum(total * flat * scale, axis=0, keepdims=True)

    line_reduce(n, me, parts, slots, sent, landed, partial, between, finish)
    pair.finish(mix_hbm)


def leave(n, places, du, dy, o, x, dx1, gain, xn, dz, win, wbr):
    rows, model = x.shape
    width = win.shape[1]
    return pl.pallas_call(
        functools.partial(leave_kernel, n, places),
        out_shape=[
            jax.ShapeDtypeStruct((rows, model), FULL),
            jax.ShapeDtypeStruct((1, model), FULL),
            jax.ShapeDtypeStruct((model // 2, 3 * width), LOW),
        ],
        in_specs=[VMEM] * 6 + [ANY] * 4,
        out_specs=[VMEM, VMEM, ANY],
        scratch_shapes=[
            pltpu.VMEM((n, rows, model), LOW),
            pltpu.VMEM((n, rows, model), LOW),
            pltpu.VMEM(win.shape, LOW),
            pltpu.VMEM(wbr.shape, LOW),
            pltpu.VMEM((n, rows, model), LOW),
            pltpu.VMEM((2, n - 1, rows, model), LOW),
        ]
        + pair_scratch(pair_tile(model, places) // 2, 3 * width)
        + reduce_sems(n)
        + [pltpu.SemaphoreType.DMA((4,))],
        compiler_params=comm_params(4),
        cost_estimate=lasting(60),
    )(du, dy, o, x, dx1, gain, xn, dz, win, wbr)


def on_device(
    inputs,
    segment,
    mixer_gain,
    input_weight,
    branch_weight,
    conv_weight,
    recur_gate,
    input_gate,
    recur_bias,
    input_bias,
    decay_rate,
    output_weight,
    second_gain,
    gate_weight,
    up_weight,
    down_weight,
    cotangent,
):
    shards = lax.axis_size("wt")
    places = lax.axis_size("seq")
    me_w = lax.axis_index("wt")
    me_s = lax.axis_index("seq")
    part_len, model = inputs.shape[1:]
    lru = conv_weight.shape[0]
    taps = conv_weight.shape[1]
    width = lru // shards
    head = recur_gate.shape[1]
    edge = width % head
    rows = shards * part_len
    onward = [(s, s + 1) for s in range(places - 1)]
    backward = [(s + 1, s) for s in range(places - 1)]

    def mine(vector):
        return lax.dynamic_slice_in_dim(vector, me_w * width, width, 0)

    x = inputs[0]
    xn, u3, y, docs = enter(shards, x, mixer_gain[None], segment, input_weight, branch_weight)
    docs = docs[:, 0]
    reach = taps - 1
    lead = lax.ppermute(docs[:, -reach:], "seq", onward)
    trail = lax.ppermute(docs[:, :reach], "seq", backward)
    lead = jnp.where(me_s == 0, -1, lead)
    trail = jnp.where(me_s == places - 1, -1, trail)
    window = jnp.concatenate([lead, docs, trail], axis=1)
    same_wide = jnp.stack(
        [
            window[:, taps - 1 :] == window[:, taps - 1 - k : window.shape[1] - k]
            for k in range(taps)
        ],
        axis=-1,
    ).astype(FULL)
    same = same_wide[:, :part_len]
    keep = same[:, :, 1].reshape(rows, 1)
    reset = keep == 0.0

    y = y.reshape(rows, width)
    slope = cotangent[0]

    tail = u3[:, part_len - (taps - 1) :, :]
    before = lax.ppermute(tail, "seq", onward)
    extended = jnp.concatenate([before, u3], axis=1).astype(FULL)
    conv_mine = mine(conv_weight)
    windows = [
        extended[:, taps - 1 - k : taps - 1 - k + part_len, :] * same[:, :, k : k + 1]
        for k in range(taps)
    ]
    conv = sum(windows[k] * conv_mine[:, k] for k in range(taps))
    c_low = conv.reshape(rows, width).astype(LOW)
    c_ext = edge_swap(c_low, edge)
    recur_table = head_rows(recur_gate, shards)
    input_table = head_rows(input_gate, shards)
    c = c_low.astype(FULL)
    rate = mine(decay_rate)
    soft = -8.0 * jax.nn.softplus(rate)
    odd = (me_w % 2).astype(jnp.int32).reshape(1) * (edge // 128)
    rows8 = jnp.concatenate(
        [jnp.stack([mine(recur_bias), mine(input_bias), soft]), jnp.zeros((5, width), FULL)]
    )
    r, ii, cum_a, h_loc = gates_scan(
        c_ext, recur_table, input_table, rows8, keep, odd, part_len, width
    )
    log_a = soft * r
    mult = jnp.where(reset, 1.0, jnp.sqrt(-jnp.expm1(2.0 * log_a)))
    a = jnp.exp(log_a.astype(LOW).astype(FULL)) * keep
    a3 = a.reshape(shards, part_len, width)
    cum_a = cum_a.reshape(a3.shape)
    h_loc = h_loc.reshape(a3.shape)
    ends = lax.all_gather(jnp.stack([cum_a[:, -1], h_loc[:, -1]]), "seq", axis=0)
    carry = jnp.zeros((shards, width), FULL)
    h_in = carry
    for n in range(places):
        h_in = jnp.where(me_s == n, carry, h_in)
        carry = ends[n, 0] * carry + ends[n, 1]
    h_in = h_in[:, None]
    h = h_loc + cum_a * h_in
    h_prev = jnp.concatenate([h_in, h[:, :-1]], axis=1).reshape(rows, width)
    hr = h.reshape(rows, width).astype(LOW).astype(FULL)
    gelu_y, grad_y = gelu_both(y)
    o = (hr * gelu_y).astype(LOW)
    x1, xn2, dm = close(shards, o.reshape(u3.shape), x, second_gain[None], output_weight, slope)
    dxn2, hidden, gate_term, up_term, down_term = ffn(
        shards, places, xn2, dm, gate_weight, up_weight, down_weight
    )
    groups = [list(range(k, places, 2)) for k in range(2)]

    def reduce_pair(term):
        kept = lax.psum_scatter(
            term, "seq", scatter_dimension=0, tiled=True, axis_index_groups=groups
        )
        wide = lax.all_to_all(kept, "wt", split_axis=0, concat_axis=1, tiled=True)
        return wide.astype(FULL)

    def reduce(term):
        kept = lax.psum_scatter(term.astype(LOW), "seq", scatter_dimension=0, tiled=True)
        wide = lax.all_to_all(kept, "wt", split_axis=0, concat_axis=1, tiled=True)
        return wide.astype(FULL)

    gate_grad = reduce_pair(gate_term)
    up_grad = reduce_pair(up_term)
    down_grad = reduce_pair(down_term)

    dx1, dz, do, second_gain_grad, block_out = back_in(
        shards, dxn2, x1, slope, second_gain[None], output_weight, hidden, down_weight
    )
    do = do.reshape(rows, width)

    dh = (do * gelu_y).astype(LOW)
    dy = (do * hr * grad_y).astype(LOW)

    rem, e_loc = back_scan(dh, a, part_len)
    rem = rem.reshape(a3.shape)
    e_loc = e_loc.reshape(a3.shape)
    heads_out = jnp.stack([cum_a[:, -1], a3[:, 0] * e_loc[:, 0]])
    firsts = lax.all_gather(heads_out, "seq", axis=0)
    carry = jnp.zeros((shards, width), FULL)
    e_in = carry
    for n in reversed(range(places)):
        e_in = jnp.where(me_s == n, carry, e_in)
        carry = firsts[n, 0] * carry + firsts[n, 1]
    e_in = e_in[:, None]
    e = (e_loc + rem * e_in).reshape(rows, width)
    dla = (e * h_prev * a).astype(LOW).astype(FULL)
    dbr = e.astype(LOW).astype(FULL)
    dmult = jnp.where(reset, 0.0, -jnp.exp(2.0 * log_a) / mult)
    dlog_a = dla + dbr * c * ii * dmult
    dra_f = soft * dlog_a * r * (1.0 - r)
    dia_f = dbr * mult * c * ii * (1.0 - ii)
    recur_bias_grad = jnp.sum(dra_f, axis=0)
    input_bias_grad = jnp.sum(dia_f, axis=0)
    decay_grad = jnp.sum(-8.0 * dlog_a * r, axis=0) * jax.nn.sigmoid(rate)
    slopes = jnp.concatenate([dra_f.astype(LOW), dia_f.astype(LOW)], axis=0)
    slopes = edge_swap(slopes, edge)
    dra, dia = slopes[:rows], slopes[rows:]
    recur_gate_grad = heads_grad(c_ext, dra, head)
    input_gate_grad = heads_grad(c_ext, dia, head)
    mixed = heads_dot(dra, recur_table, True) + heads_dot(dia, input_table, True)
    dc = (dbr * mult * ii + own_part(mixed, edge)).reshape(shards, part_len, width)
    conv_grad = jnp.stack([jnp.sum(windows[k] * dc, axis=(0, 1)) for k in range(taps)], axis=-1)
    lead = lax.ppermute(dc[:, : taps - 1], "seq", backward)
    dc_ext = jnp.concatenate([dc, lead], axis=1)
    du = sum(
        (dc_ext * same_wide[:, :, k : k + 1])[:, k : k + part_len] * conv_mine[:, k]
        for k in range(taps)
    )
    du = du.reshape(rows, width).astype(LOW)
    input_grad, mixer_gain_grad, mix_term = leave(
        shards,
        places,
        du.reshape(u3.shape),
        dy.reshape(u3.shape),
        o.reshape(u3.shape),
        x,
        dx1,
        mixer_gain[None],
        xn,
        dz,
        input_weight,
        branch_weight,
    )
    mixed = reduce_pair(mix_term).reshape(-1, shards, 3, width)
    out_grad, branch_grad, input_weight_grad = [
        mixed[:, :, k].reshape(-1, lru) for k in range(3)
    ]

    small = jnp.concatenate(
        [
            own_part(recur_gate_grad.T, edge).T,
            own_part(input_gate_grad.T, edge).T,
            conv_grad,
            recur_bias_grad[:, None],
            input_bias_grad[:, None],
            decay_grad[:, None],
        ],
        axis=1,
    )
    small = lax.psum_scatter(small.astype(LOW), "seq", scatter_dimension=0, tiled=True)
    moves = [
        (s * shards + w, w * places + s) for s in range(places) for w in range(shards)
    ]
    small = lax.ppermute(small, ("seq", "wt"), moves).astype(FULL)
    share = model // (places * shards)
    gains = jnp.concatenate(
        [mixer_gain_grad.reshape(-1, share), second_gain_grad.reshape(-1, share)], axis=1
    )
    gains = lax.psum_scatter(gains, ("seq", "wt"), scatter_dimension=0, tiled=True)[0]
    at = 2 * head + taps
    return (
        block_out[None],
        input_grad[None],
        gains[:share],
        input_weight_grad,
        branch_grad,
        small[:, 2 * head : at],
        small[:, :head],
        small[:, head : 2 * head],
        small[:, at],
        small[:, at + 1],
        small[:, at + 2],
        out_grad,
        gains[share:],
        gate_grad,
        up_grad,
        down_grad,
    )


def solution(mesh):
    tokens = P("wt", "seq", None)
    columns = P(None, "wt")
    row = P(("seq", "wt"))
    flat_rows = P(("seq", "wt"), None)
    return jax.shard_map(
        on_device,
        mesh=mesh,
        in_specs=(
            tokens,
            P("wt", "seq"),
            P(),
            columns,
            columns,
            P(),
            P(),
            P(),
            P(),
            P(),
            P(),
            columns,
            P(),
            columns,
            columns,
            columns,
            tokens,
        ),
        out_specs=(
            tokens,
            tokens,
            row,
            flat_rows,
            flat_rows,
            flat_rows,
            flat_rows,
            flat_rows,
            row,
            row,
            row,
            flat_rows,
            row,
            flat_rows,
            flat_rows,
            flat_rows,
        ),
        check_vma=False,
    )
```

```python
import functools
import math

import jax
import jax.numpy as jnp
from jax import lax
from jax.experimental import pallas as pl
from jax.experimental.pallas import tpu as pltpu
from jax.sharding import PartitionSpec as P

EPSILON = 1e-06
LOW = jnp.bfloat16
FULL = jnp.float32


def dot(left, right, left_dim=1, right_dim=0):
    return lax.dot_general(
        left, right, (((left_dim,), (right_dim,)), ((), ())), preferred_element_type=FULL
    )


def gelu_both(values):
    slope = jnp.sqrt(2.0 / jnp.pi).astype(FULL)
    inner = jnp.tanh(slope * (values + 0.044715 * values * values * values))
    gelu = 0.5 * values * (1.0 + inner)
    grad = 0.5 * (1.0 + inner) + 0.5 * values * (1.0 - inner * inner) * slope * (
        1.0 + 3.0 * 0.044715 * values * values
    )
    return gelu, grad


def head_rows(gate_rows, shards):
    head = gate_rows.shape[1]
    width = gate_rows.shape[0] // shards
    heads = -(-width // head)
    first = (lax.axis_index("wt") * width) // head
    table = gate_rows.reshape(-1, head, head)
    return lax.dynamic_slice_in_dim(table, first, heads, 0)


def edge_swap(values, edge):
    me = lax.axis_index("wt")
    shards = lax.axis_size("wt")
    odd = me % 2 == 1
    mine = jnp.where(odd, values[:, :edge], values[:, -edge:])
    other = lax.ppermute(mine, "wt", [(i, i ^ 1) for i in range(shards)])
    return jnp.where(
        odd,
        jnp.concatenate([other, values], axis=1),
        jnp.concatenate([values, other], axis=1),
    )


def own_part(values, edge):
    odd = lax.axis_index("wt") % 2 == 1
    return jnp.where(odd, values[:, edge:], values[:, :-edge])


def heads_dot(values, table, transposed=False):
    heads, head, _ = table.shape
    return jnp.concatenate(
        [
            dot(values[:, n * head : (n + 1) * head], table[n], 1, 1 if transposed else 0)
            for n in range(heads)
        ],
        axis=1,
    )


def heads_grad(values, slopes, head):
    return jnp.concatenate(
        [
            dot(values[:, n * head : (n + 1) * head], slopes[:, n * head : (n + 1) * head], 0, 0)
            for n in range(values.shape[1] // head)
        ],
        axis=0,
    )


def scan_rows(coef, value, reverse):
    rows = coef.shape[0]
    place = lax.broadcasted_iota(jnp.int32, coef.shape, 0)
    step = 1
    while step < rows:
        if reverse:
            inside = place < rows - step
            by = rows - step
        else:
            inside = place >= step
            by = step
        far_coef = jnp.where(inside, pltpu.roll(coef, by, 0), 1.0)
        far_value = jnp.where(inside, pltpu.roll(value, by, 0), 0.0)
        value = coef * far_value + value
        coef = coef * far_coef
        step *= 2
    return coef, value


def gates_kernel(odd, c_ref, c_own, table_r, table_i, rows_ref, mask_ref, r_ref, ii_ref, a_ref, h_ref):
    c_head = c_ref[...]
    ra = jnp.dot(c_head, table_r[0], preferred_element_type=FULL)
    ia = jnp.dot(c_head, table_i[0], preferred_element_type=FULL)
    r = jax.nn.sigmoid(ra + rows_ref[0:1, :])
    ii = jax.nn.sigmoid(ia + rows_ref[1:2, :])
    keep = mask_ref[:, 0:1]
    log_a = rows_ref[2:3, :] * r
    decay = jnp.exp(2.0 * log_a)
    gap = jnp.where(2.0 * log_a > -0.01, -expm1_small(2.0 * log_a), 1.0 - decay)
    mult = jnp.where(keep == 0.0, 1.0, jnp.sqrt(gap))
    b = (mult * c_own[...].astype(FULL) * ii).astype(LOW).astype(FULL)
    a = jnp.exp(log_a.astype(LOW).astype(FULL)) * keep
    cum_a, h_loc = scan_rows(a, b, False)
    r_ref[...] = r
    ii_ref[...] = ii
    a_ref[...] = cum_a
    h_ref[...] = h_loc


def expm1_small(values):
    return values * (
        1.0 + values * (0.5 + values * (1.0 / 6.0 + values * (1.0 / 24.0 + values / 120.0)))
    )


def gates_scan(c_ext, table_r, table_i, rows8, mask, odd, part_len, width):
    rows = c_ext.shape[0]
    head = table_r.shape[1]
    half = 128
    per = head // half
    grid = (rows // part_len, width // half)
    spec = pltpu.PrefetchScalarGridSpec(
        num_scalar_prefetch=1,
        grid=grid,
        in_specs=[
            pl.BlockSpec((part_len, head), lambda m, n, s: (m, (n + s[0]) // per)),
            pl.BlockSpec((part_len, half), lambda m, n, s: (m, n + s[0])),
            pl.BlockSpec((1, head, half), lambda m, n, s: ((n + s[0]) // per, 0, (n + s[0]) % per)),
            pl.BlockSpec((1, head, half), lambda m, n, s: ((n + s[0]) // per, 0, (n + s[0]) % per)),
            pl.BlockSpec((8, half), lambda m, n, s: (0, n)),
            pl.BlockSpec((part_len, mask.shape[1]), lambda m, n, s: (m, 0)),
        ],
        out_specs=[pl.BlockSpec((part_len, half), lambda m, n, s: (m, n))] * 4,
    )
    return pl.pallas_call(
        gates_kernel,
        grid_spec=spec,
        out_shape=[jax.ShapeDtypeStruct((rows, width), FULL)] * 4,
    )(odd, c_ext, c_ext, table_r, table_i, rows8, mask)


def back_kernel(dh_ref, a_ref, rem_ref, e_ref):
    rows = dh_ref.shape[0]
    place = lax.broadcasted_iota(jnp.int32, dh_ref.shape, 0)
    a_next = jnp.where(place < rows - 1, pltpu.roll(a_ref[...], rows - 1, 0), 1.0)
    rem, e_loc = scan_rows(a_next, dh_ref[...].astype(FULL), True)
    rem_ref[...] = rem
    e_ref[...] = e_loc


def back_scan(dh, a, part_len):
    rows, width = a.shape
    half = 128
    block = pl.BlockSpec((part_len, half), lambda m, n: (m, n))
    return pl.pallas_call(
        back_kernel,
        grid=(rows // part_len, width // half),
        in_specs=[block, block],
        out_specs=[block, block],
        out_shape=[jax.ShapeDtypeStruct((rows, width), FULL)] * 2,
    )(dh, a)


MESH = pl.DeviceIdType.MESH


def remote(source, target, sent, landed, to):
    return pltpu.make_async_remote_copy(
        src_ref=source,
        dst_ref=target,
        send_sem=sent,
        recv_sem=landed,
        device_id={"wt": to},
        device_id_type=MESH,
    )


def greet(n, me, pair=False, bits=0, places=0):
    barrier = pltpu.get_barrier_semaphore()

    @pl.when(me > 0)
    def _():
        pl.semaphore_signal(barrier, 1, device_id={"wt": me - 1}, device_id_type=MESH)

    @pl.when(me < n - 1)
    def _():
        pl.semaphore_signal(barrier, 1, device_id={"wt": me + 1}, device_id_type=MESH)

    peers = (me > 0).astype(jnp.int32) + (me < n - 1).astype(jnp.int32)
    place = lax.axis_index("seq")
    if places:
        peers = peers + places - 1
        for by in range(1, places):
            other = {"seq": lax.rem(place + by, places)}
            pl.semaphore_signal(barrier, 1, device_id=other, device_id_type=MESH)
    if pair:
        other = {"seq": place + 1 - 2 * lax.rem(place, 2)}
        pl.semaphore_signal(barrier, 1, device_id=other, device_id_type=MESH)
        peers = peers + 1 + bits
        for k in range(1, bits + 1):
            step = 1 << k
            other = {"seq": place + step * (1 - 2 * lax.rem(place // step, 2))}
            pl.semaphore_signal(barrier, 1, device_id=other, device_id_type=MESH)
    pl.semaphore_wait(barrier, peers)


class LineGather:
    def __init__(self, n, me, blocks, sent, landed):
        self.n, self.me, self.blocks, self.sent, self.landed = n, me, blocks, sent, landed

    def rightward(self, d):
        block = self.blocks.at[self.me - d]
        return remote(block, block, self.sent.at[0, d], self.landed.at[0, d + 1], self.me + 1)

    def leftward(self, d):
        block = self.blocks.at[self.me + d]
        return remote(block, block, self.sent.at[1, d], self.landed.at[1, d + 1], self.me - 1)

    def start(self):
        @pl.when(self.me < self.n - 1)
        def _():
            self.rightward(0).start()

        @pl.when(self.me > 0)
        def _():
            self.leftward(0).start()

    def arrive(self, d):
        n, me = self.n, self.me

        @pl.when(me - d >= 0)
        def _():
            block = self.blocks.at[me - d]
            remote(block, block, self.sent.at[0, 0], self.landed.at[0, d], me).wait_recv()

            @pl.when(me < n - 1)
            def _():
                self.rightward(d).start()

        @pl.when(me + d < n)
        def _():
            block = self.blocks.at[me + d]
            remote(block, block, self.sent.at[1, 0], self.landed.at[1, d], me).wait_recv()

            @pl.when(me > 0)
            def _():
                self.leftward(d).start()

    def each(self, d, use):
        def side(k, carry):
            q = self.me + (2 * k - 1) * d

            @pl.when((q >= 0) & (q < self.n))
            def _():
                use(q)

            return carry

        lax.fori_loop(0, 2, side, 0)

    def finish(self):
        n, me = self.n, self.me
        for d in range(n - 1):

            @pl.when((me - d >= 0) & (me < n - 1))
            def _():
                self.rightward(d).wait_send()

            @pl.when((me + d < n) & (me > 0))
            def _():
                self.leftward(d).wait_send()


def line_gather(n, me, blocks, sent, landed, use, ready):
    line = LineGather(n, me, blocks, sent, landed)
    line.start()
    ready()
    use(me)

    def step(d, carry):
        line.arrive(d)
        line.each(d, use)
        return carry

    lax.fori_loop(1, n, step, 0)
    line.finish()


class LineReduce:
    def __init__(self, n, me, parts, slots, sent, landed):
        self.n, self.me, self.parts, self.slots = n, me, parts, slots
        self.sent, self.landed = sent, landed

    def rightward(self, k):
        source, target = self.parts.at[self.n - 1 - k], self.slots.at[0, k]
        return remote(source, target, self.sent.at[0, k], self.landed.at[0, k], self.me + 1)

    def leftward(self, k):
        source, target = self.parts.at[k], self.slots.at[1, k]
        return remote(source, target, self.sent.at[1, k], self.landed.at[1, k], self.me - 1)

    def arrived(self, side, k):
        slot = self.slots.at[side, k]
        remote(slot, slot, self.sent.at[side, k], self.landed.at[side, k], self.me).wait_recv()

    def add(self, q, side, k):
        total = self.parts[q].astype(FULL) + self.slots[side, k].astype(FULL)
        self.parts[q] = total.astype(LOW)

    def prepare(self, k, partial):
        def side(which, carry):
            q = jnp.where(which == 0, self.n - 1 - k, k)

            @pl.when(jnp.where(which == 0, q > self.me, q < self.me))
            def _():
                partial(q)

            return carry

        lax.fori_loop(0, 2, side, 0)

    def step(self, t):
        n = self.n
        for side in range(2):
            place = self.me if side == 0 else n - 1 - self.me
            k = t - place
            pull = self.rightward if side == 0 else self.leftward

            @pl.when((k >= 0) & (t <= n - 2))
            def _():
                @pl.when(place > 0)
                def _():
                    self.arrived(side, k)
                    self.add(n - 1 - k if side == 0 else k, side, k)

                @pl.when(k > 0)
                def _():
                    pull(k - 1).wait_send()

                pull(k).start()

    def total(self):
        n, me = self.n, self.me

        @pl.when(me > 0)
        def _():
            self.arrived(0, n - 1 - me)

        @pl.when(me < n - 1)
        def _():
            self.arrived(1, me)

        total = self.parts[me].astype(FULL)
        other = self.slots[0, jnp.clip(n - 1 - me, 0, n - 2)].astype(FULL)
        total = total + jnp.where(me > 0, other, 0.0)
        other = self.slots[1, jnp.clip(me, 0, n - 2)].astype(FULL)
        return total + jnp.where(me < n - 1, other, 0.0)

    def finish(self):
        @pl.when(self.me < self.n - 1)
        def _():
            self.rightward(self.n - 2 - self.me).wait_send()

        @pl.when(self.me > 0)
        def _():
            self.leftward(self.me - 1).wait_send()


class LineBoth:
    def __init__(self, gather, back):
        self.gather, self.back = gather, back
        self.n, self.me = gather.n, gather.me

    def sends(self, side, t, act):
        n, me = self.n, self.me
        place = me if side == 0 else n - 1 - me
        spread = self.gather.rightward if side == 0 else self.gather.leftward
        pull = self.back.rightward if side == 0 else self.back.leftward

        @pl.when(place < n - 1)
        def _():
            @pl.when(t <= place)
            def _():
                act(spread(t))

            @pl.when(t > place)
            def _():
                act(pull(t - place - 1))

    def step(self, t):
        n, me = self.n, self.me
        for side in range(2):
            place = me if side == 0 else n - 1 - me
            if t > 0:

                @pl.when(t <= place)
                def _():
                    block = self.gather.blocks.at[me - t if side == 0 else me + t]
                    remote(
                        block, block, self.gather.sent.at[side, 0], self.gather.landed.at[side, t], me
                    ).wait_recv()

                @pl.when((t > place) & (place > 0))
                def _():
                    k = t - place - 1
                    self.back.arrived(side, k)
                    self.back.add(n - 1 - k if side == 0 else k, side, k)

                self.sends(side, t - 1, lambda copy: copy.wait_send())
            self.sends(side, t, lambda copy: copy.start())

    def finish(self):
        for side in range(2):
            self.sends(side, self.n - 1, lambda copy: copy.wait_send())


def line_reduce(n, me, parts, slots, sent, landed, partial, work, finish):
    line = LineReduce(n, me, parts, slots, sent, landed)
    line.prepare(0, partial)
    line.step(0)
    for k in range(1, n - 1):
        line.prepare(k, partial)
    line.step(1)
    partial(me)
    share = -(-len(work) // (n - 2))
    for t in range(2, n):
        for task in work[(t - 2) * share : (t - 1) * share]:
            task()
        if t < n - 1:
            line.step(t)
    finish(line.total())
    line.finish()


def tiles(count, size, body):
    def step(t, carry):
        body(pl.ds(pl.multiple_of(t * size, size), size))
        return carry

    lax.fori_loop(0, count // size, step, 0)


def tile_of(width, limit):
    size = limit
    while width % size:
        size -= 128
    return size


VMEM = pl.BlockSpec(memory_space=pltpu.VMEM)
ANY = pl.BlockSpec(memory_space=pl.ANY)


def gather_sems(n):
    return [pltpu.SemaphoreType.DMA((2, n)), pltpu.SemaphoreType.DMA((2, n + 1))]


def reduce_sems(n):
    return [pltpu.SemaphoreType.DMA((2, n)), pltpu.SemaphoreType.DMA((2, n))]


def lasting(micros):
    return pl.CostEstimate(
        flops=int(micros * 1.0e9), bytes_accessed=int(micros * 3.4e6), transcendentals=0
    )


def comm_params(number):
    return pltpu.CompilerParams(
        collective_id=number, has_side_effects=True, vmem_limit_bytes=64 * 1024 * 1024
    )


def enter_kernel(
    n, x_ref, gain_ref, doc_ref, win_hbm, wbr_hbm, xn_ref, u_ref, y_ref, docs_ref, win, wbr, docs, sent, landed, dsent, dlanded, local
):
    me = lax.axis_index("wt")
    loads = [
        pltpu.make_async_copy(win_hbm, win, local.at[0]),
        pltpu.make_async_copy(wbr_hbm, wbr, local.at[1]),
    ]
    for load in loads:
        load.start()
    docs[me] = jnp.broadcast_to(doc_ref[...], docs.shape[1:])
    flat = x_ref[...].astype(FULL)
    scale = lax.rsqrt(jnp.mean(flat * flat, axis=-1, keepdims=True) + EPSILON)
    xn_ref[me] = (flat * scale * gain_ref[...]).astype(LOW)
    greet(n, me)
    notes = LineGather(n, me, docs, dsent, dlanded)
    line = LineGather(n, me, xn_ref, sent, landed)
    notes.start()
    line.start()
    for load in loads:
        load.wait()

    def use(q):
        block = xn_ref[q]
        u_ref[q] = dot(block, win[...]).astype(LOW)
        y_ref[q] = dot(block, wbr[...])

    use(me)

    def step(d, carry):
        notes.arrive(d)
        line.arrive(d)
        line.each(d, use)
        return carry

    lax.fori_loop(1, n, step, 0)
    docs_ref[...] = docs[...]
    notes.finish()
    line.finish()


def enter(n, x, gain, doc, win, wbr):
    rows, model = x.shape
    width = win.shape[1]
    return pl.pallas_call(
        functools.partial(enter_kernel, n),
        out_shape=[
            jax.ShapeDtypeStruct((n, rows, model), LOW),
            jax.ShapeDtypeStruct((n, rows, width), LOW),
            jax.ShapeDtypeStruct((n, rows, width), FULL),
            jax.ShapeDtypeStruct((n, 8, rows), jnp.int32),
        ],
        in_specs=[VMEM, VMEM, VMEM, ANY, ANY],
        out_specs=[VMEM, VMEM, VMEM, VMEM],
        scratch_shapes=[
            pltpu.VMEM(win.shape, LOW),
            pltpu.VMEM(wbr.shape, LOW),
            pltpu.VMEM((n, 8, rows), jnp.int32),
        ]
        + gather_sems(n)
        + gather_sems(n)
        + [pltpu.SemaphoreType.DMA((2,))],
        compiler_params=comm_params(0),
        cost_estimate=lasting(50),
    )(x, gain, doc, win, wbr)


def close_kernel(
    n, o_ref, x_ref, gain_ref, w_ref, slope_ref, x1_ref, xn2_ref, dm_ref, parts, slots, sent, landed, gsent, glanded
):
    me = lax.axis_index("wt")
    dm_ref[me] = slope_ref[...].astype(LOW)
    greet(n, me)
    model = w_ref.shape[0]

    def partial(q):
        block = o_ref[q]

        def tile(at):
            parts[q, :, at] = dot(block, w_ref[at, :], 1, 1).astype(LOW)

        tiles(model, tile_of(model, 512), tile)

    def finish(total):
        x1 = x_ref[...].astype(FULL) + total
        x1_ref[...] = x1
        scale = lax.rsqrt(jnp.mean(x1 * x1, axis=-1, keepdims=True) + EPSILON)
        xn2_ref[...] = (x1 * scale * gain_ref[...]).astype(LOW)

    back = LineReduce(n, me, parts, slots, sent, landed)
    both = LineBoth(LineGather(n, me, dm_ref, gsent, glanded), back)
    both.step(0)
    for k in range(n - 1):
        back.prepare(k, partial)
    for t in range(1, n):
        both.step(t)
        if t == 1:
            partial(me)
    finish(back.total())
    both.finish()


def close(n, o, x, gain, weight, slope):
    rows, model = x.shape
    return pl.pallas_call(
        functools.partial(close_kernel, n),
        out_shape=[
            jax.ShapeDtypeStruct((rows, model), FULL),
            jax.ShapeDtypeStruct((rows, model), LOW),
            jax.ShapeDtypeStruct((n, rows, model), LOW),
        ],
        in_specs=[VMEM] * 5,
        out_specs=[VMEM] * 3,
        scratch_shapes=[
            pltpu.VMEM((n, rows, model), LOW),
            pltpu.VMEM((2, n - 1, rows, model), LOW),
        ]
        + reduce_sems(n)
        + gather_sems(n),
        compiler_params=comm_params(1),
        cost_estimate=lasting(65),
    )(o, x, gain, weight, slope)


class PairSum:
    def __init__(self, part, halves, landing, sent, landed, free, flush):
        self.me = lax.axis_index("seq")
        self.mine = lax.rem(self.me, 2)
        self.part, self.halves, self.landing = part, halves, landing
        self.sent, self.landed, self.free, self.flush = sent, landed, free, flush
        self.count = 0
        self.pending = None

    def other(self):
        return {"seq": self.me + 1 - 2 * self.mine}

    def send(self, slot):
        return pltpu.make_async_remote_copy(
            src_ref=self.halves.at[slot, 1 - self.mine],
            dst_ref=self.landing.at[slot],
            send_sem=self.sent.at[slot],
            recv_sem=self.landed.at[slot],
            device_id=self.other(),
            device_id_type=MESH,
        )

    def out(self, slot, t, target):
        half = self.landing.shape[1]
        return pltpu.make_async_copy(
            self.halves.at[slot, self.mine],
            target.at[pl.ds(t * half, half), :],
            self.flush.at[slot],
        )

    def tasks(self, steps, compute, target):
        return [functools.partial(self.run, t, compute, target) for t in range(steps)]

    def run(self, t, compute, target):
        slot = self.count % 2
        if self.count >= 2:
            self.send(slot).wait_send()
            self.out(slot, 0, target).wait()
            pl.semaphore_wait(self.free, 1)
        compute(t, self.halves.at[slot])
        self.send(slot).start()
        self.settle()
        self.pending = (slot, t, target)
        self.count += 1

    def settle(self):
        if self.pending is None:
            return
        slot, t, target = self.pending
        self.send(slot).wait_recv()
        total = self.halves[slot, self.mine].astype(FULL) + self.landing[slot].astype(FULL)
        self.halves[slot, self.mine] = total.astype(LOW)
        pl.semaphore_signal(self.free, 1, device_id=self.other(), device_id_type=MESH)
        self.out(slot, t, target).start()
        self.pending = None

    def finish(self, target):
        self.settle()
        for slot in range(2):
            self.send(slot).wait_send()
            self.out(slot, 0, target).wait()
        pl.semaphore_wait(self.free, 2)


def pair_scratch(half, width):
    return [
        pltpu.VMEM((2, 2, half, width), LOW),
        pltpu.VMEM((2, half, width), LOW),
        pltpu.SemaphoreType.DMA((2,)),
        pltpu.SemaphoreType.DMA((2,)),
        pltpu.SemaphoreType.REGULAR,
        pltpu.SemaphoreType.DMA((2,)),
    ]


def pair_tile(model, places):
    size = 2 * model // places
    return size if size % 128 == 0 else size * 128 // math.gcd(size, 128)


def pair_dot(left, right, part, size):
    n, rows, _ = left.shape

    def compute(t, halves):
        lhs = left[:, :, pl.ds(t * size, size)].reshape(n * rows, size)
        width = right.shape[2]

        def tile(at):
            rhs = right[:, :, at].reshape(n * rows, -1)
            value = dot(lhs, rhs, 0, 0).astype(LOW)
            for k in range(size // (2 * part)):
                for side in range(2):
                    first = (2 * k + side) * part
                    halves[side, k * part : (k + 1) * part, at] = value[first : first + part]

        tiles(width, tile_of(width, 640), tile)

    return compute


def column_halves(width):
    first = -(-width // 256) * 128
    return [(0, first), (first, width - first)]


class PlaneReduce:
    def __init__(self, blocks, landings, sent, landed):
        self.blocks, self.landings, self.sent, self.landed = blocks, landings, sent, landed
        self.bits = len(blocks.shape) - 3
        self.me = lax.axis_index("seq")
        self.columns = column_halves(blocks.shape[-1])

    def bit(self, dim):
        return 1 << (self.bits - dim)

    def mine(self, dim):
        return lax.rem(self.me // self.bit(dim), 2)

    def order(self, side):
        dims = list(range(self.bits))
        return dims[::-1] if side == 0 else dims

    def peer(self, dim):
        return {"seq": self.me + self.bit(dim) * (1 - 2 * self.mine(dim))}

    def index(self, side, step, own):
        order = self.order(side)
        place = [slice(None)] * self.bits
        for dim in order[:step]:
            place[dim] = self.mine(dim)
        now = order[step]
        place[now] = self.mine(now) if own else 1 - self.mine(now)
        return tuple(place) + (slice(None), slice(None), pl.ds(*self.columns[side]))

    def send(self, side, step):
        return pltpu.make_async_remote_copy(
            src_ref=self.blocks.at[self.index(side, step, False)],
            dst_ref=self.landings[2 * step + side],
            send_sem=self.sent.at[side, step],
            recv_sem=self.landed.at[side, step],
            device_id=self.peer(self.order(side)[step]),
            device_id_type=MESH,
        )

    def begin(self):
        for side in range(2):
            self.send(side, 0).start()

    def advance(self, step):
        for side in range(2):
            self.send(side, step).wait_recv()
            at = self.index(side, step, True)
            total = self.blocks[at].astype(FULL) + self.landings[2 * step + side][...].astype(FULL)
            self.blocks[at] = total.astype(LOW)
            if step + 1 < self.bits:
                self.send(side, step + 1).start()

    def kept(self):
        return self.blocks.at[tuple(self.mine(dim) for dim in range(self.bits))]

    def finish(self):
        for step in range(self.bits):
            for side in range(2):
                self.send(side, step).wait_send()


def plane_scratch(shape):
    bits = len(shape) - 3
    landings = []
    for step in range(bits):
        for _, width in column_halves(shape[-1]):
            rest = [2] * (bits - 1 - step) + [shape[-3], shape[-2], width]
            landings.append(pltpu.VMEM(tuple(rest), LOW))
    return landings


def ffn_kernel(
    n,
    places,
    xn2_ref,
    dm_hbm,
    wg_hbm,
    wu_hbm,
    wd_hbm,
    dxn2_ref,
    hidden_hbm,
    dg_hbm,
    dv_hbm,
    xall_hbm,
    down_hbm,
    xall,
    dm,
    wg,
    wu,
    wd,
    hidden,
    dg,
    dv,
    parts,
    slots,
    halves,
    landing,
    psent,
    planded,
    free,
    pflush,
    gsent,
    glanded,
    rsent,
    rlanded,
    local,
    flush,
):
    me = lax.axis_index("wt")
    rows, model = xn2_ref.shape
    units = wg.shape[1]
    cut = tile_of(units, 640)
    span = tile_of(model, 512)
    loads = [
        pltpu.make_async_copy(source, target, local.at[k])
        for k, (source, target) in enumerate(
            [(wg_hbm, wg), (wu_hbm, wu), (wd_hbm, wd), (dm_hbm, dm)]
        )
    ]
    for load in loads:
        load.start()
    xall[me] = xn2_ref[...]
    greet(n, me, True)

    def ready():
        for load in loads:
            load.wait()

    def use(q):
        def tile(at):
            block = xall[q]
            g = dot(block, wg[:, at])
            v = dot(block, wu[:, at])
            back = dot(dm[q], wd[:, at])
            gelu, slope = gelu_both(g)
            hidden[q, :, at] = (gelu * v).astype(LOW)
            dg[q, :, at] = (back * v * slope).astype(LOW)
            dv[q, :, at] = (back * gelu).astype(LOW)

        tiles(units, cut, tile)

    line_gather(n, me, xall, gsent, glanded, use, ready)
    outs = [
        pltpu.make_async_copy(source, target, flush.at[k])
        for k, (source, target) in enumerate(
            [(hidden, hidden_hbm), (dg, dg_hbm), (dv, dv_hbm), (xall, xall_hbm)]
        )
    ]
    for out in outs:
        out.start()

    def partial(q):
        def tile(at):
            total = dot(dg[q], wg[at, :], 1, 1) + dot(dv[q], wu[at, :], 1, 1)
            parts[q, :, at] = total.astype(LOW)

        tiles(model, span, tile)

    part = model // places
    size = pair_tile(model, places)
    pair = PairSum(part, halves, landing, psent, planded, free, pflush)

    work = pair.tasks(model // size, pair_dot(dm, hidden, part, size), down_hbm)

    def finish(total):
        dxn2_ref[...] = total

    line_reduce(n, me, parts, slots, rsent, rlanded, partial, work, finish)
    pair.finish(down_hbm)
    for out in outs:
        out.wait()


def ffn(n, places, xn2, dm, wg, wu, wd):
    rows, model = xn2.shape
    units = wg.shape[1]
    grad = jax.ShapeDtypeStruct((model // 2, units), LOW)
    return pl.pallas_call(
        functools.partial(ffn_kernel, n, places),
        out_shape=[
            jax.ShapeDtypeStruct((rows, model), FULL),
            jax.ShapeDtypeStruct((n, rows, units), LOW),
            jax.ShapeDtypeStruct((n, rows, units), LOW),
            jax.ShapeDtypeStruct((n, rows, units), LOW),
            jax.ShapeDtypeStruct((n, rows, model), LOW),
            grad,
        ],
        in_specs=[VMEM, ANY, ANY, ANY, ANY],
        out_specs=[VMEM, ANY, ANY, ANY, ANY, ANY],
        scratch_shapes=[
            pltpu.VMEM((n, rows, model), LOW),
            pltpu.VMEM((n, rows, model), LOW),
            pltpu.VMEM((model, units), LOW),
            pltpu.VMEM((model, units), LOW),
            pltpu.VMEM((model, units), LOW),
            pltpu.VMEM((n, rows, units), LOW),
            pltpu.VMEM((n, rows, units), LOW),
            pltpu.VMEM((n, rows, units), LOW),
            pltpu.VMEM((n, rows, model), LOW),
            pltpu.VMEM((2, n - 1, rows, model), LOW),
        ]
        + pair_scratch(pair_tile(model, places) // 2, units)
        + gather_sems(n)
        + reduce_sems(n)
        + [pltpu.SemaphoreType.DMA((4,)), pltpu.SemaphoreType.DMA((4,))],
        compiler_params=comm_params(2),
        cost_estimate=lasting(125),
    )(xn2, dm, wg, wu, wd)


def back_in_kernel(n, places, bits, *refs):
    dxn2_ref, x1_ref, slope_ref, gain_ref, *sources = refs[:11]
    dx1_ref, dz_ref, do_ref, sum_ref, out_ref, kept_ref, gate_hbm, up_hbm = refs[11:19]
    w, hidden, wd, xall, dg, dv, blocks = refs[19:26]
    landings = refs[26 : 26 + 2 * bits]
    parts, slots, *sems = refs[26 + 2 * bits :]
    halves, landing, psent, planded, free, pflush, sent, landed, rsent, rlanded, bsent, blanded, local = sems
    me = lax.axis_index("wt")
    loads = [
        pltpu.make_async_copy(source, target, local.at[k])
        for k, (source, target) in enumerate(
            zip(sources, [blocks, w, wd, hidden, xall, dg, dv])
        )
    ]
    for load in loads:
        load.start()
    x1 = x1_ref[...]
    dxn2 = dxn2_ref[...]
    model = x1.shape[1]
    scale = lax.rsqrt(jnp.mean(x1 * x1, axis=-1, keepdims=True) + EPSILON)
    q2 = dxn2 * gain_ref[...]
    pull = jnp.mean(q2 * x1, axis=-1, keepdims=True)
    dx1 = slope_ref[...] + scale * (q2 - x1 * (scale * scale * pull))
    dx1_ref[...] = dx1
    dz_ref[me] = dx1.astype(LOW)
    greet(n, me, True, bits)
    line = LineGather(n, me, dz_ref, sent, landed)
    back = LineReduce(n, me, parts, slots, rsent, rlanded)
    both = LineBoth(line, back)
    both.step(0)
    loads[0].wait()
    plane = PlaneReduce(blocks, landings, bsent, blanded)
    plane.begin()
    sum_ref[...] = jnp.sum(dxn2 * x1 * scale, axis=0, keepdims=True)
    for load in loads[1:]:
        load.wait()

    def use(q):
        do_ref[q] = dot(dz_ref[q], w[...])

    def partial(q):
        def tile(at):
            parts[q, :, at] = dot(hidden[q], wd[at, :], 1, 1).astype(LOW)

        tiles(model, tile_of(model, 512), tile)

    part = model // places
    size = pair_tile(model, places)
    pair = PairSum(part, halves, landing, psent, planded, free, pflush)
    for k in range(n - 1):
        back.prepare(k, partial)
    partial(me)
    use(me)
    work = pair.tasks(model // size, pair_dot(xall, dg, part, size), gate_hbm)
    work += pair.tasks(model // size, pair_dot(xall, dv, part, size), up_hbm)
    share = -(-len(work) // (n - 1))
    for t in range(1, n):
        both.step(t)
        if t >= 2 and t - 2 < bits:
            plane.advance(t - 2)
        line.each(t, use)
        for task in work[(t - 1) * share : t * share]:
            task()
    for step in range(max(n - 2, 0), bits):
        plane.advance(step)
    out_ref[...] = (x1_ref[...] + back.total()).astype(LOW)
    kept_ref[...] = plane.kept()[...]
    pair.finish(up_hbm)
    both.finish()
    plane.finish()


def back_in(n, places, dxn2, x1, slope, gain, down, weight, wd, hidden, xall, dg, dv):
    rows, model = x1.shape
    bits = len(down.shape) - 3
    grad = jax.ShapeDtypeStruct((model // 2, wd.shape[1]), LOW)
    return pl.pallas_call(
        functools.partial(back_in_kernel, n, places, bits),
        out_shape=[
            jax.ShapeDtypeStruct((rows, model), FULL),
            jax.ShapeDtypeStruct((n, rows, model), LOW),
            jax.ShapeDtypeStruct((n, rows, weight.shape[1]), FULL),
            jax.ShapeDtypeStruct((1, model), FULL),
            jax.ShapeDtypeStruct((rows, model), LOW),
            jax.ShapeDtypeStruct(down.shape[bits:], LOW),
            grad,
            grad,
        ],
        in_specs=[VMEM] * 4 + [ANY] * 7,
        out_specs=[VMEM] * 6 + [ANY] * 2,
        scratch_shapes=[
            pltpu.VMEM(weight.shape, LOW),
            pltpu.VMEM(hidden.shape, LOW),
            pltpu.VMEM(wd.shape, LOW),
            pltpu.VMEM(xall.shape, LOW),
            pltpu.VMEM(dg.shape, LOW),
            pltpu.VMEM(dv.shape, LOW),
            pltpu.VMEM(down.shape, LOW),
        ]
        + plane_scratch(down.shape)
        + [
            pltpu.VMEM((n, rows, model), LOW),
            pltpu.VMEM((2, n - 1, rows, model), LOW),
        ]
        + pair_scratch(pair_tile(model, places) // 2, wd.shape[1])
        + gather_sems(n)
        + reduce_sems(n)
        + [
            pltpu.SemaphoreType.DMA((2, bits)),
            pltpu.SemaphoreType.DMA((2, bits)),
            pltpu.SemaphoreType.DMA((7,)),
        ],
        compiler_params=comm_params(3),
        cost_estimate=lasting(75),
    )(dxn2, x1, slope, gain, down, weight, wd, hidden, xall, dg, dv)


class PlaneShare:
    def __init__(self, places, source, lands, sent, landed):
        self.places, self.source, self.lands = places, source, lands
        self.sent, self.landed = sent, landed
        self.me = lax.axis_index("seq")

    def send(self, by):
        to = lax.rem(self.me + by, self.places)
        return pltpu.make_async_remote_copy(
            src_ref=self.source.at[to],
            dst_ref=self.lands.at[by],
            send_sem=self.sent.at[by],
            recv_sem=self.landed.at[by],
            device_id={"seq": to},
            device_id_type=MESH,
        )

    def start(self):
        self.lands[0] = self.source[self.me]
        for by in range(1, self.places):
            self.send(by).start()

    def finish(self, target):
        for by in range(1, self.places):
            self.send(by).wait_recv()
        target[...] = jnp.sum(self.lands[...].astype(FULL), axis=0)
        for by in range(1, self.places):
            self.send(by).wait_send()


def leave_kernel(
    n,
    places,
    du_ref,
    dy_ref,
    o_ref,
    x_ref,
    dx1_ref,
    gain_ref,
    xn_hbm,
    dz_hbm,
    win_hbm,
    wbr_hbm,
    after_hbm,
    small_ref,
    grad_ref,
    sum_ref,
    mix_hbm,
    passed_ref,
    xn,
    dz,
    win,
    wbr,
    parts,
    slots,
    halves,
    landing,
    psent,
    planded,
    free,
    pflush,
    sent,
    landed,
    lands,
    ssent,
    slanded,
    local,
):
    me = lax.axis_index("wt")
    loads = [
        pltpu.make_async_copy(source, target, local.at[k])
        for k, (source, target) in enumerate(
            [(win_hbm, win), (wbr_hbm, wbr), (xn_hbm, xn), (dz_hbm, dz)]
        )
    ]
    for load in loads:
        load.start()
    greet(n, me, False, 0, places)
    small = PlaneShare(places, small_ref, lands, ssent, slanded)
    small.start()
    for load in loads:
        load.wait()
    model = win.shape[0]

    def partial(q):
        def tile(at):
            total = dot(du_ref[q], win[at, :], 1, 1) + dot(dy_ref[q], wbr[at, :], 1, 1)
            parts[q, :, at] = total.astype(LOW)

        tiles(model, tile_of(model, 512), tile)

    part = model // places
    size = pair_tile(model, places)
    width = du_ref.shape[2]
    pair = PairSum(part, halves, landing, psent, planded, free, pflush)

    def compute(t, target):
        for k, (left, right) in enumerate([(dz, o_ref), (xn, dy_ref), (xn, du_ref)]):
            columns = pl.ds(k * width, width)
            pair_dot(left, right, part, size)(t, target.at[:, :, columns])

    work = pair.tasks(model // size, compute, mix_hbm)

    def finish(total):
        flat = x_ref[...].astype(FULL)
        scale = lax.rsqrt(jnp.mean(flat * flat, axis=-1, keepdims=True) + EPSILON)
        q1 = total * gain_ref[...]
        pull = jnp.mean(q1 * flat, axis=-1, keepdims=True)
        grad_ref[...] = dx1_ref[...] + scale * (q1 - flat * (scale * scale * pull))
        sum_ref[...] = jnp.sum(total * flat * scale, axis=0, keepdims=True)

    line_reduce(n, me, parts, slots, sent, landed, partial, work, finish)
    pair.finish(mix_hbm)
    small.finish(passed_ref)


def leave(n, places, du, dy, o, x, dx1, gain, xn, dz, win, wbr, after, small):
    rows, model = x.shape
    width = win.shape[1]
    return pl.pallas_call(
        functools.partial(leave_kernel, n, places),
        out_shape=[
            jax.ShapeDtypeStruct((rows, model), FULL),
            jax.ShapeDtypeStruct((1, model), FULL),
            jax.ShapeDtypeStruct((model // 2, 3 * width), LOW),
            jax.ShapeDtypeStruct(small.shape[1:], FULL),
        ],
        in_specs=[VMEM] * 6 + [ANY] * 5 + [VMEM],
        out_specs=[VMEM, VMEM, ANY, VMEM],
        scratch_shapes=[
            pltpu.VMEM((n, rows, model), LOW),
            pltpu.VMEM((n, rows, model), LOW),
            pltpu.VMEM(win.shape, LOW),
            pltpu.VMEM(wbr.shape, LOW),
            pltpu.VMEM((n, rows, model), LOW),
            pltpu.VMEM((2, n - 1, rows, model), LOW),
        ]
        + pair_scratch(pair_tile(model, places) // 2, 3 * width)
        + reduce_sems(n)
        + [
            pltpu.VMEM(small.shape, LOW),
            pltpu.SemaphoreType.DMA((places,)),
            pltpu.SemaphoreType.DMA((places,)),
            pltpu.SemaphoreType.DMA((4,)),
        ],
        compiler_params=comm_params(4),
        cost_estimate=lasting(60),
    )(du, dy, o, x, dx1, gain, xn, dz, win, wbr, after, small)


class LineSpread:
    def __init__(self, n, me, source, lands, sent, landed):
        self.n, self.me, self.source, self.lands = n, me, source, lands
        self.sent, self.landed = sent, landed

    def send(self, by):
        to = lax.rem(self.me + by, self.n)
        return remote(
            self.source.at[to], self.lands.at[self.me], self.sent.at[by], self.landed.at[by], to
        )

    def start(self):
        for by in range(1, self.n):
            self.send(by).start()

    def take(self, put, own):
        put(self.me, own[...])
        for by in range(1, self.n):
            slot = lax.rem(self.me + self.n - by, self.n)
            land = self.lands.at[slot]
            remote(land, land, self.sent.at[by], self.landed.at[by], self.me).wait_recv()
            put(slot, land[...])

    def finish(self):
        for by in range(1, self.n):
            self.send(by).wait_send()


def settle_kernel(n, places, bits, gate_hbm, up_hbm, mix_hbm, gains_ref, gate_ref, up_ref, out_ref, branch_ref, in_ref, total_ref, *scratch):
    blocks, landings, scratch = scratch[0], scratch[1 : 1 + 2 * bits], scratch[1 + 2 * bits :]
    lands, own, notes, around, psent, planded, ssent, slanded, gsent, glanded, local = scratch
    me = lax.axis_index("wt")
    seat = lax.axis_index("seq")
    loads = [
        pltpu.make_async_copy(mix_hbm, blocks, local.at[0]),
        pltpu.make_async_copy(gate_hbm.at[me], own.at[0], local.at[1]),
        pltpu.make_async_copy(up_hbm.at[me], own.at[1], local.at[2]),
    ]
    for load in loads:
        load.start()
    notes[me] = gains_ref[...]
    barrier = pltpu.get_barrier_semaphore()
    for by in range(1, n):
        pl.semaphore_signal(
            barrier, 1, device_id={"wt": lax.rem(me + by, n)}, device_id_type=MESH
        )
    for by in range(1, places):
        pl.semaphore_signal(
            barrier, 1, device_id={"seq": lax.rem(seat + by, places)}, device_id_type=MESH
        )
    pl.semaphore_wait(barrier, n + places - 2)
    loads[0].wait()
    plane = PlaneReduce(blocks, landings, psent, planded)
    plane.begin()
    spreads = [
        LineSpread(n, me, source, lands.at[k], ssent.at[k], slanded.at[k])
        for k, source in enumerate([gate_hbm, up_hbm])
    ]

    def note(by):
        to = lax.rem(me + by, n)
        return remote(notes.at[me], notes.at[me], gsent.at[0, by], glanded.at[0, by], to)

    for by in range(1, n):
        note(by).start()
    for spread in spreads:
        spread.start()
    for by in range(1, n):
        slot = notes.at[lax.rem(me + n - by, n)]
        remote(slot, slot, gsent.at[0, by], glanded.at[0, by], me).wait_recv()
    around[seat] = jnp.sum(notes[...], axis=0)

    def share(by):
        to = lax.rem(seat + by, places)
        return pltpu.make_async_remote_copy(
            src_ref=around.at[seat],
            dst_ref=around.at[seat],
            send_sem=gsent.at[1, by],
            recv_sem=glanded.at[1, by],
            device_id={"seq": to},
            device_id_type=MESH,
        )

    for by in range(1, places):
        share(by).start()
    for step in range(bits):
        plane.advance(step)
    kept = plane.kept()
    last = LineSpread(n, me, kept, lands.at[2], ssent.at[2], slanded.at[2])
    last.start()
    for by in range(1, places):
        slot = around.at[lax.rem(seat + places - by, places)]
        pltpu.make_async_remote_copy(
            src_ref=slot,
            dst_ref=slot,
            send_sem=gsent.at[1, by],
            recv_sem=glanded.at[1, by],
            device_id={"seq": seat},
            device_id_type=MESH,
        ).wait_recv()
    total_ref[...] = jnp.sum(around[...], axis=0)
    units = gate_hbm.shape[-1]
    for k, (spread, target) in enumerate(zip(spreads, [gate_ref, up_ref])):
        loads[1 + k].wait()

        def put(q, value, target=target):
            target[:, pl.ds(pl.multiple_of(q * units, 128), units)] = value.astype(FULL)

        spread.take(put, own.at[k])
    width = units // 3

    def put_mix(q, value):
        columns = pl.ds(pl.multiple_of(q * width, 128), width)
        for k, target in enumerate([out_ref, branch_ref, in_ref]):
            target[:, columns] = value[:, k * width : (k + 1) * width].astype(FULL)

    last.take(put_mix, kept.at[me])
    plane.finish()
    for spread in spreads + [last]:
        spread.finish()
    for by in range(1, n):
        note(by).wait_send()
    for by in range(1, places):
        share(by).wait_send()


def settle(n, places, gate, up, mix, gains):
    _, part, units = gate.shape
    bits = len(mix.shape) - 3
    wide = jax.ShapeDtypeStruct((part, n * units), FULL)
    thin = jax.ShapeDtypeStruct((part, n * units // 3), FULL)
    return pl.pallas_call(
        functools.partial(settle_kernel, n, places, bits),
        out_shape=[wide, wide, thin, thin, thin, jax.ShapeDtypeStruct(gains.shape, FULL)],
        in_specs=[ANY, ANY, ANY, VMEM],
        out_specs=[VMEM] * 6,
        scratch_shapes=[pltpu.VMEM(mix.shape, LOW)]
        + plane_scratch(mix.shape)
        + [
            pltpu.VMEM((3, n, part, units), LOW),
            pltpu.VMEM((2, part, units), LOW),
            pltpu.VMEM((n,) + gains.shape, FULL),
            pltpu.VMEM((places,) + gains.shape, FULL),
            pltpu.SemaphoreType.DMA((2, bits)),
            pltpu.SemaphoreType.DMA((2, bits)),
            pltpu.SemaphoreType.DMA((3, n)),
            pltpu.SemaphoreType.DMA((3, n)),
            pltpu.SemaphoreType.DMA((2, max(n, places))),
            pltpu.SemaphoreType.DMA((2, max(n, places))),
            pltpu.SemaphoreType.DMA((3,)),
        ],
        compiler_params=comm_params(5),
        cost_estimate=lasting(100),
    )(gate, up, mix, gains)


def on_device(
    inputs,
    segment,
    mixer_gain,
    input_weight,
    branch_weight,
    conv_weight,
    recur_gate,
    input_gate,
    recur_bias,
    input_bias,
    decay_rate,
    output_weight,
    second_gain,
    gate_weight,
    up_weight,
    down_weight,
    cotangent,
):
    shards = lax.axis_size("wt")
    places = lax.axis_size("seq")
    me_w = lax.axis_index("wt")
    me_s = lax.axis_index("seq")
    part_len, model = inputs.shape[1:]
    lru = conv_weight.shape[0]
    taps = conv_weight.shape[1]
    width = lru // shards
    head = recur_gate.shape[1]
    edge = width % head
    rows = shards * part_len
    onward = [(s, s + 1) for s in range(places - 1)]
    backward = [(s + 1, s) for s in range(places - 1)]

    def mine(vector):
        return lax.dynamic_slice_in_dim(vector, me_w * width, width, 0)

    x = inputs[0]
    xn, u3, y, docs = enter(shards, x, mixer_gain[None], segment, input_weight, branch_weight)
    docs = docs[:, 0]
    reach = taps - 1
    lead = lax.ppermute(docs[:, -reach:], "seq", onward)
    trail = lax.ppermute(docs[:, :reach], "seq", backward)
    lead = jnp.where(me_s == 0, -1, lead)
    trail = jnp.where(me_s == places - 1, -1, trail)
    window = jnp.concatenate([lead, docs, trail], axis=1)
    same_wide = jnp.stack(
        [
            window[:, taps - 1 :] == window[:, taps - 1 - k : window.shape[1] - k]
            for k in range(taps)
        ],
        axis=-1,
    ).astype(FULL)
    same = same_wide[:, :part_len]
    keep = same[:, :, 1].reshape(rows, 1)
    reset = keep == 0.0

    y = y.reshape(rows, width)
    slope = cotangent[0]

    tail = u3[:, part_len - (taps - 1) :, :]
    before = lax.ppermute(tail, "seq", onward)
    extended = jnp.concatenate([before, u3], axis=1).astype(FULL)
    conv_mine = mine(conv_weight)
    windows = [
        extended[:, taps - 1 - k : taps - 1 - k + part_len, :] * same[:, :, k : k + 1]
        for k in range(taps)
    ]
    conv = sum(windows[k] * conv_mine[:, k] for k in range(taps))
    c_low = conv.reshape(rows, width).astype(LOW)
    c_ext = edge_swap(c_low, edge)
    recur_table = head_rows(recur_gate, shards)
    input_table = head_rows(input_gate, shards)
    c = c_low.astype(FULL)
    rate = mine(decay_rate)
    soft = -8.0 * jax.nn.softplus(rate)
    odd = (me_w % 2).astype(jnp.int32).reshape(1) * (edge // 128)
    rows8 = jnp.concatenate(
        [jnp.stack([mine(recur_bias), mine(input_bias), soft]), jnp.zeros((5, width), FULL)]
    )
    r, ii, cum_a, h_loc = gates_scan(
        c_ext, recur_table, input_table, rows8, keep, odd, part_len, width
    )
    log_a = soft * r
    mult = jnp.where(reset, 1.0, jnp.sqrt(-jnp.expm1(2.0 * log_a)))
    a = jnp.exp(log_a.astype(LOW).astype(FULL)) * keep
    a3 = a.reshape(shards, part_len, width)
    cum_a = cum_a.reshape(a3.shape)
    h_loc = h_loc.reshape(a3.shape)
    ends = lax.all_gather(jnp.stack([cum_a[:, -1], h_loc[:, -1]]), "seq", axis=0)
    carry = jnp.zeros((shards, width), FULL)
    h_in = carry
    for n in range(places):
        h_in = jnp.where(me_s == n, carry, h_in)
        carry = ends[n, 0] * carry + ends[n, 1]
    h_in = h_in[:, None]
    h = h_loc + cum_a * h_in
    h_prev = jnp.concatenate([h_in, h[:, :-1]], axis=1).reshape(rows, width)
    hr = h.reshape(rows, width).astype(LOW).astype(FULL)
    gelu_y, grad_y = gelu_both(y)
    o = (hr * gelu_y).astype(LOW)
    x1, xn2, dm = close(shards, o.reshape(u3.shape), x, second_gain[None], output_weight, slope)
    dxn2, hidden, dg, dv, xn2, down_term = ffn(
        shards, places, xn2, dm, gate_weight, up_weight, down_weight
    )
    groups = [list(range(k, places, 2)) for k in range(2)]

    def summed(term):
        return lax.psum_scatter(
            term, "seq", scatter_dimension=0, tiled=True, axis_index_groups=groups
        )

    def spread(kept):
        return lax.all_to_all(kept, "wt", split_axis=0, concat_axis=1, tiled=True)

    part = model // (places * shards)
    bits = (places // 2 - 1).bit_length()
    dx1, dz, do, second_gain_grad, block_out, down_kept, gate_term, up_term = back_in(
        shards,
        places,
        dxn2,
        x1,
        slope,
        second_gain[None],
        down_term.reshape((2,) * bits + (shards, part, -1)),
        output_weight,
        down_weight,
        hidden,
        xn2,
        dg,
        dv,
    )
    down_wide = spread(down_kept.reshape(shards * part, -1))
    down_grad = down_wide.astype(FULL)
    gate_kept = summed(gate_term)
    up_kept = summed(up_term)
    do = do.reshape(rows, width)

    dh = (do * gelu_y).astype(LOW)
    dy = (do * hr * grad_y).astype(LOW)

    rem, e_loc = back_scan(dh, a, part_len)
    rem = rem.reshape(a3.shape)
    e_loc = e_loc.reshape(a3.shape)
    heads_out = jnp.stack([cum_a[:, -1], a3[:, 0] * e_loc[:, 0]])
    firsts = lax.all_gather(heads_out, "seq", axis=0)
    carry = jnp.zeros((shards, width), FULL)
    e_in = carry
    for n in reversed(range(places)):
        e_in = jnp.where(me_s == n, carry, e_in)
        carry = firsts[n, 0] * carry + firsts[n, 1]
    e_in = e_in[:, None]
    e = (e_loc + rem * e_in).reshape(rows, width)
    dla = (e * h_prev * a).astype(LOW).astype(FULL)
    dbr = e.astype(LOW).astype(FULL)
    dmult = jnp.where(reset, 0.0, -jnp.exp(2.0 * log_a) / mult)
    dlog_a = dla + dbr * c * ii * dmult
    dra_f = soft * dlog_a * r * (1.0 - r)
    dia_f = dbr * mult * c * ii * (1.0 - ii)
    recur_bias_grad = jnp.sum(dra_f, axis=0)
    input_bias_grad = jnp.sum(dia_f, axis=0)
    decay_grad = jnp.sum(-8.0 * dlog_a * r, axis=0) * jax.nn.sigmoid(rate)
    slopes = jnp.concatenate([dra_f.astype(LOW), dia_f.astype(LOW)], axis=0)
    slopes = edge_swap(slopes, edge)
    dra, dia = slopes[:rows], slopes[rows:]
    recur_gate_grad = heads_grad(c_ext, dra, head)
    input_gate_grad = heads_grad(c_ext, dia, head)
    mixed = heads_dot(dra, recur_table, True) + heads_dot(dia, input_table, True)
    dc = (dbr * mult * ii + own_part(mixed, edge)).reshape(shards, part_len, width)
    conv_grad = jnp.stack([jnp.sum(windows[k] * dc, axis=(0, 1)) for k in range(taps)], axis=-1)
    lead = lax.ppermute(dc[:, : taps - 1], "seq", backward)
    dc_ext = jnp.concatenate([dc, lead], axis=1)
    du = sum(
        (dc_ext * same_wide[:, :, k : k + 1])[:, k : k + part_len] * conv_mine[:, k]
        for k in range(taps)
    )
    du = du.reshape(rows, width).astype(LOW)
    small = jnp.concatenate(
        [
            own_part(recur_gate_grad.T, edge).T,
            own_part(input_gate_grad.T, edge).T,
            conv_grad,
            recur_bias_grad[:, None],
            input_bias_grad[:, None],
            decay_grad[:, None],
        ],
        axis=1,
    )
    input_grad, mixer_gain_grad, mix_term, small = leave(
        shards,
        places,
        du.reshape(u3.shape),
        dy.reshape(u3.shape),
        o.reshape(u3.shape),
        x,
        dx1,
        mixer_gain[None],
        xn,
        dz,
        input_weight,
        branch_weight,
        down_wide,
        jnp.pad(small, ((0, 0), (0, -small.shape[1] % 128))).astype(LOW).reshape(places, -1, -(-small.shape[1] // 128) * 128),
    )
    gains = jnp.concatenate(
        [mixer_gain_grad, second_gain_grad, jnp.zeros((6, model), FULL)], axis=0
    )
    gate_grad, up_grad, out_grad, branch_grad, input_weight_grad, gains = settle(
        shards,
        places,
        gate_kept.reshape(shards, part, -1),
        up_kept.reshape(shards, part, -1),
        mix_term.reshape((2,) * bits + (shards, part, -1)),
        gains,
    )
    gains = lax.dynamic_slice_in_dim(gains, (me_s * shards + me_w) * part, part, 1)

    moves = [
        (s * shards + w, w * places + s) for s in range(places) for w in range(shards)
    ]
    small = lax.ppermute(small, ("seq", "wt"), moves)
    at = 2 * head + taps
    return (
        block_out[None],
        input_grad[None],
        gains[0],
        input_weight_grad,
        branch_grad,
        small[:, 2 * head : at],
        small[:, :head],
        small[:, head : 2 * head],
        small[:, at],
        small[:, at + 1],
        small[:, at + 2],
        out_grad,
        gains[1],
        gate_grad,
        up_grad,
        down_grad,
    )


def solution(mesh):
    tokens = P("wt", "seq", None)
    columns = P(None, "wt")
    row = P(("seq", "wt"))
    flat_rows = P(("seq", "wt"), None)
    return jax.shard_map(
        on_device,
        mesh=mesh,
        in_specs=(
            tokens,
            P("wt", "seq"),
            P(),
            columns,
            columns,
            P(),
            P(),
            P(),
            P(),
            P(),
            P(),
            columns,
            P(),
            columns,
            columns,
            columns,
            tokens,
        ),
        out_specs=(
            tokens,
            tokens,
            row,
            flat_rows,
            flat_rows,
            flat_rows,
            flat_rows,
            flat_rows,
            row,
            row,
            row,
            flat_rows,
            row,
            flat_rows,
            flat_rows,
            flat_rows,
        ),
        check_vma=False,
    )
```

```python
import functools
import math

import jax
import jax.numpy as jnp
from jax import lax
from jax.experimental import pallas as pl
from jax.experimental.pallas import tpu as pltpu
from jax.sharding import PartitionSpec as P

EPSILON = 1e-06
LOW = jnp.bfloat16
FULL = jnp.float32


def dot(left, right, left_dim=1, right_dim=0):
    return lax.dot_general(
        left, right, (((left_dim,), (right_dim,)), ((), ())), preferred_element_type=FULL
    )


def gelu_both(values):
    slope = jnp.sqrt(2.0 / jnp.pi).astype(FULL)
    inner = jnp.tanh(slope * (values + 0.044715 * values * values * values))
    gelu = 0.5 * values * (1.0 + inner)
    grad = 0.5 * (1.0 + inner) + 0.5 * values * (1.0 - inner * inner) * slope * (
        1.0 + 3.0 * 0.044715 * values * values
    )
    return gelu, grad


def scan_rows(coef, value, reverse):
    rows = coef.shape[0]
    place = lax.broadcasted_iota(jnp.int32, coef.shape, 0)
    step = 1
    while step < rows:
        if reverse:
            inside = place < rows - step
            by = rows - step
        else:
            inside = place >= step
            by = step
        far_coef = jnp.where(inside, pltpu.roll(coef, by, 0), 1.0)
        far_value = jnp.where(inside, pltpu.roll(value, by, 0), 0.0)
        value = coef * far_value + value
        coef = coef * far_coef
        step *= 2
    return coef, value


def expm1_small(values):
    return values * (
        1.0 + values * (0.5 + values * (1.0 / 6.0 + values * (1.0 / 24.0 + values / 120.0)))
    )


MESH = pl.DeviceIdType.MESH


def remote(source, target, sent, landed, to):
    return pltpu.make_async_remote_copy(
        src_ref=source,
        dst_ref=target,
        send_sem=sent,
        recv_sem=landed,
        device_id={"wt": to},
        device_id_type=MESH,
    )


def greet(n, me, pair=False, bits=0, places=0):
    barrier = pltpu.get_barrier_semaphore()

    @pl.when(me > 0)
    def _():
        pl.semaphore_signal(barrier, 1, device_id={"wt": me - 1}, device_id_type=MESH)

    @pl.when(me < n - 1)
    def _():
        pl.semaphore_signal(barrier, 1, device_id={"wt": me + 1}, device_id_type=MESH)

    peers = (me > 0).astype(jnp.int32) + (me < n - 1).astype(jnp.int32)
    place = lax.axis_index("seq")
    if places:
        peers = peers + places - 1
        for by in range(1, places):
            other = {"seq": lax.rem(place + by, places)}
            pl.semaphore_signal(barrier, 1, device_id=other, device_id_type=MESH)
    if pair:
        other = {"seq": place + 1 - 2 * lax.rem(place, 2)}
        pl.semaphore_signal(barrier, 1, device_id=other, device_id_type=MESH)
        peers = peers + 1 + bits
        for k in range(1, bits + 1):
            step = 1 << k
            other = {"seq": place + step * (1 - 2 * lax.rem(place // step, 2))}
            pl.semaphore_signal(barrier, 1, device_id=other, device_id_type=MESH)
    pl.semaphore_wait(barrier, peers)


class LineGather:
    def __init__(self, n, me, blocks, sent, landed):
        self.n, self.me, self.blocks, self.sent, self.landed = n, me, blocks, sent, landed

    def rightward(self, d):
        block = self.blocks.at[self.me - d]
        return remote(block, block, self.sent.at[0, d], self.landed.at[0, d + 1], self.me + 1)

    def leftward(self, d):
        block = self.blocks.at[self.me + d]
        return remote(block, block, self.sent.at[1, d], self.landed.at[1, d + 1], self.me - 1)

    def start(self):
        @pl.when(self.me < self.n - 1)
        def _():
            self.rightward(0).start()

        @pl.when(self.me > 0)
        def _():
            self.leftward(0).start()

    def arrive(self, d):
        n, me = self.n, self.me

        @pl.when(me - d >= 0)
        def _():
            block = self.blocks.at[me - d]
            remote(block, block, self.sent.at[0, 0], self.landed.at[0, d], me).wait_recv()

            @pl.when(me < n - 1)
            def _():
                self.rightward(d).start()

        @pl.when(me + d < n)
        def _():
            block = self.blocks.at[me + d]
            remote(block, block, self.sent.at[1, 0], self.landed.at[1, d], me).wait_recv()

            @pl.when(me > 0)
            def _():
                self.leftward(d).start()

    def each(self, d, use):
        def side(k, carry):
            q = self.me + (2 * k - 1) * d

            @pl.when((q >= 0) & (q < self.n))
            def _():
                use(q)

            return carry

        lax.fori_loop(0, 2, side, 0)

    def finish(self):
        n, me = self.n, self.me
        for d in range(n - 1):

            @pl.when((me - d >= 0) & (me < n - 1))
            def _():
                self.rightward(d).wait_send()

            @pl.when((me + d < n) & (me > 0))
            def _():
                self.leftward(d).wait_send()


def line_gather(n, me, blocks, sent, landed, use, ready):
    line = LineGather(n, me, blocks, sent, landed)
    line.start()
    ready()
    use(me)

    def step(d, carry):
        line.arrive(d)
        line.each(d, use)
        return carry

    lax.fori_loop(1, n, step, 0)
    line.finish()


class LineReduce:
    def __init__(self, n, me, parts, slots, sent, landed):
        self.n, self.me, self.parts, self.slots = n, me, parts, slots
        self.sent, self.landed = sent, landed

    def rightward(self, k):
        source, target = self.parts.at[self.n - 1 - k], self.slots.at[0, k]
        return remote(source, target, self.sent.at[0, k], self.landed.at[0, k], self.me + 1)

    def leftward(self, k):
        source, target = self.parts.at[k], self.slots.at[1, k]
        return remote(source, target, self.sent.at[1, k], self.landed.at[1, k], self.me - 1)

    def arrived(self, side, k):
        slot = self.slots.at[side, k]
        remote(slot, slot, self.sent.at[side, k], self.landed.at[side, k], self.me).wait_recv()

    def add(self, q, side, k):
        total = self.parts[q].astype(FULL) + self.slots[side, k].astype(FULL)
        self.parts[q] = total.astype(LOW)

    def prepare(self, k, partial):
        def side(which, carry):
            q = jnp.where(which == 0, self.n - 1 - k, k)

            @pl.when(jnp.where(which == 0, q > self.me, q < self.me))
            def _():
                partial(q)

            return carry

        lax.fori_loop(0, 2, side, 0)

    def step(self, t):
        n = self.n
        for side in range(2):
            place = self.me if side == 0 else n - 1 - self.me
            k = t - place
            pull = self.rightward if side == 0 else self.leftward

            @pl.when((k >= 0) & (t <= n - 2))
            def _():
                @pl.when(place > 0)
                def _():
                    self.arrived(side, k)
                    self.add(n - 1 - k if side == 0 else k, side, k)

                @pl.when(k > 0)
                def _():
                    pull(k - 1).wait_send()

                pull(k).start()

    def total(self):
        n, me = self.n, self.me

        @pl.when(me > 0)
        def _():
            self.arrived(0, n - 1 - me)

        @pl.when(me < n - 1)
        def _():
            self.arrived(1, me)

        total = self.parts[me].astype(FULL)
        other = self.slots[0, jnp.clip(n - 1 - me, 0, n - 2)].astype(FULL)
        total = total + jnp.where(me > 0, other, 0.0)
        other = self.slots[1, jnp.clip(me, 0, n - 2)].astype(FULL)
        return total + jnp.where(me < n - 1, other, 0.0)

    def finish(self):
        @pl.when(self.me < self.n - 1)
        def _():
            self.rightward(self.n - 2 - self.me).wait_send()

        @pl.when(self.me > 0)
        def _():
            self.leftward(self.me - 1).wait_send()


class LineBoth:
    def __init__(self, gather, back, skip=0):
        self.gather, self.back, self.skip = gather, back, skip
        self.n, self.me = gather.n, gather.me

    def sends(self, side, t, act):
        n, me = self.n, self.me
        place = me if side == 0 else n - 1 - me
        spread = self.gather.rightward if side == 0 else self.gather.leftward
        pull = self.back.rightward if side == 0 else self.back.leftward
        d = t + self.skip

        @pl.when(place < n - 1)
        def _():
            @pl.when(d <= place)
            def _():
                act(spread(d))

            @pl.when(d > place)
            def _():
                act(pull(d - place - 1))

    def step(self, t):
        n, me = self.n, self.me
        d = t + self.skip
        for side in range(2):
            place = me if side == 0 else n - 1 - me
            if t > 0:

                @pl.when(d <= place)
                def _():
                    block = self.gather.blocks.at[me - d if side == 0 else me + d]
                    remote(
                        block, block, self.gather.sent.at[side, 0], self.gather.landed.at[side, d], me
                    ).wait_recv()

                @pl.when((d > place) & (place > 0))
                def _():
                    k = d - place - 1
                    self.back.arrived(side, k)
                    self.back.add(n - 1 - k if side == 0 else k, side, k)

                self.sends(side, t - 1, lambda copy: copy.wait_send())
            self.sends(side, t, lambda copy: copy.start())

    def finish(self):
        for side in range(2):
            self.sends(side, self.n - 1 - self.skip, lambda copy: copy.wait_send())


def line_reduce(n, me, parts, slots, sent, landed, partial, work, finish, early=None):
    line = LineReduce(n, me, parts, slots, sent, landed)
    line.prepare(0, partial)
    line.step(0)
    if early is not None:
        early()
    for k in range(1, n - 1):
        line.prepare(k, partial)
    line.step(1)
    partial(me)
    share = -(-len(work) // (n - 2))
    for t in range(2, n):
        for task in work[(t - 2) * share : (t - 1) * share]:
            task()
        if t < n - 1:
            line.step(t)
    finish(line.total())
    line.finish()


def tiles(count, size, body):
    def step(t, carry):
        body(pl.ds(pl.multiple_of(t * size, size), size))
        return carry

    lax.fori_loop(0, count // size, step, 0)


def tile_of(width, limit):
    size = limit
    while width % size:
        size -= 128
    return size


VMEM = pl.BlockSpec(memory_space=pltpu.VMEM)
ANY = pl.BlockSpec(memory_space=pl.ANY)


def gather_sems(n):
    return [pltpu.SemaphoreType.DMA((2, n)), pltpu.SemaphoreType.DMA((2, n + 1))]


def reduce_sems(n):
    return [pltpu.SemaphoreType.DMA((2, n)), pltpu.SemaphoreType.DMA((2, n))]


def lasting(micros):
    return pl.CostEstimate(
        flops=int(micros * 1.0e9), bytes_accessed=int(micros * 3.4e6), transcendentals=0
    )


def comm_params(number):
    return pltpu.CompilerParams(
        collective_id=number, has_side_effects=True, vmem_limit_bytes=64 * 1024 * 1024
    )


def enter_kernel(
    n, x_ref, gain_ref, doc_ref, win_hbm, wbr_hbm, xn_ref, u_ref, y_ref, docs_ref, win, wbr, docs, sent, landed, dsent, dlanded, local
):
    me = lax.axis_index("wt")
    loads = [
        pltpu.make_async_copy(win_hbm, win, local.at[0]),
        pltpu.make_async_copy(wbr_hbm, wbr, local.at[1]),
    ]
    for load in loads:
        load.start()
    docs[me] = jnp.broadcast_to(doc_ref[...], docs.shape[1:])
    flat = x_ref[...].astype(FULL)
    scale = lax.rsqrt(jnp.mean(flat * flat, axis=-1, keepdims=True) + EPSILON)
    xn_ref[me] = (flat * scale * gain_ref[...]).astype(LOW)
    greet(n, me)
    notes = LineGather(n, me, docs, dsent, dlanded)
    line = LineGather(n, me, xn_ref, sent, landed)
    notes.start()
    line.start()
    for load in loads:
        load.wait()

    def use(q):
        block = xn_ref[q]
        u_ref[q] = dot(block, win[...]).astype(LOW)
        y_ref[q] = dot(block, wbr[...])

    use(me)

    def step(d, carry):
        notes.arrive(d)
        line.arrive(d)
        line.each(d, use)
        return carry

    lax.fori_loop(1, n, step, 0)
    docs_ref[...] = docs[...]
    notes.finish()
    line.finish()


def enter(n, x, gain, doc, win, wbr):
    rows, model = x.shape
    width = win.shape[1]
    return pl.pallas_call(
        functools.partial(enter_kernel, n),
        out_shape=[
            jax.ShapeDtypeStruct((n, rows, model), LOW),
            jax.ShapeDtypeStruct((n, rows, width), LOW),
            jax.ShapeDtypeStruct((n, rows, width), FULL),
            jax.ShapeDtypeStruct((n, 8, rows), jnp.int32),
        ],
        in_specs=[VMEM, VMEM, VMEM, ANY, ANY],
        out_specs=[VMEM, VMEM, VMEM, VMEM],
        scratch_shapes=[
            pltpu.VMEM(win.shape, LOW),
            pltpu.VMEM(wbr.shape, LOW),
            pltpu.VMEM((n, 8, rows), jnp.int32),
        ]
        + gather_sems(n)
        + gather_sems(n)
        + [pltpu.SemaphoreType.DMA((2,))],
        compiler_params=comm_params(0),
        cost_estimate=lasting(50),
    )(x, gain, doc, win, wbr)


def close_kernel(
    n, o_ref, x_ref, gain_ref, w_ref, near_hbm, x1_ref, xn2_ref, dm_ref, parts, slots, sent, landed, gsent, glanded, local
):
    me = lax.axis_index("wt")
    model = w_ref.shape[0]

    def near(k, act):
        q = me + k - 1

        @pl.when((q >= 0) & (q < n))
        def _():
            act(pltpu.make_async_copy(near_hbm.at[k], dm_ref.at[q], local.at[k]))

    for k in range(3):
        near(k, lambda copy: copy.start())
    greet(n, me)

    def partial(q):
        block = o_ref[q]

        def tile(at):
            parts[q, :, at] = dot(block, w_ref[at, :], 1, 1).astype(LOW)

        tiles(model, tile_of(model, 512), tile)

    def finish(total):
        x1 = x_ref[...].astype(FULL) + total
        x1_ref[...] = x1
        scale = lax.rsqrt(jnp.mean(x1 * x1, axis=-1, keepdims=True) + EPSILON)
        xn2_ref[...] = (x1 * scale * gain_ref[...]).astype(LOW)

    back = LineReduce(n, me, parts, slots, sent, landed)
    both = LineBoth(LineGather(n, me, dm_ref, gsent, glanded), back, 1)
    for k in range(3):
        near(k, lambda copy: copy.wait())
    back.prepare(0, partial)
    both.step(0)
    for k in range(1, n - 1):
        back.prepare(k, partial)
    partial(me)
    for t in range(1, n - 1):
        both.step(t)
    finish(back.total())
    both.finish()


def close(n, o, x, gain, weight, near):
    rows, model = x.shape
    return pl.pallas_call(
        functools.partial(close_kernel, n),
        out_shape=[
            jax.ShapeDtypeStruct((rows, model), FULL),
            jax.ShapeDtypeStruct((rows, model), LOW),
            jax.ShapeDtypeStruct((n, rows, model), LOW),
        ],
        in_specs=[VMEM] * 4 + [ANY],
        out_specs=[VMEM] * 3,
        scratch_shapes=[
            pltpu.VMEM((n, rows, model), LOW),
            pltpu.VMEM((2, n - 1, rows, model), LOW),
        ]
        + reduce_sems(n)
        + gather_sems(n)
        + [pltpu.SemaphoreType.DMA((3,))],
        compiler_params=comm_params(1),
        cost_estimate=lasting(55),
    )(o, x, gain, weight, near)


class PairSum:
    def __init__(self, part, halves, landing, sent, landed, free, flush):
        self.me = lax.axis_index("seq")
        self.mine = lax.rem(self.me, 2)
        self.part, self.halves, self.landing = part, halves, landing
        self.sent, self.landed, self.free, self.flush = sent, landed, free, flush
        self.count = 0
        self.pending = None

    def other(self):
        return {"seq": self.me + 1 - 2 * self.mine}

    def send(self, slot):
        return pltpu.make_async_remote_copy(
            src_ref=self.halves.at[slot, 1 - self.mine],
            dst_ref=self.landing.at[slot],
            send_sem=self.sent.at[slot],
            recv_sem=self.landed.at[slot],
            device_id=self.other(),
            device_id_type=MESH,
        )

    def out(self, slot, t, target):
        half = self.landing.shape[1]
        return pltpu.make_async_copy(
            self.halves.at[slot, self.mine],
            target.at[pl.ds(t * half, half), :],
            self.flush.at[slot],
        )

    def tasks(self, steps, compute, target):
        return [functools.partial(self.run, t, compute, target) for t in range(steps)]

    def run(self, t, compute, target):
        slot = self.count % 2
        if self.count >= 2:
            self.send(slot).wait_send()
            self.out(slot, 0, target).wait()
            pl.semaphore_wait(self.free, 1)
        compute(t, self.halves.at[slot])
        self.send(slot).start()
        self.settle()
        self.pending = (slot, t, target)
        self.count += 1

    def settle(self):
        if self.pending is None:
            return
        slot, t, target = self.pending
        self.send(slot).wait_recv()
        total = self.halves[slot, self.mine].astype(FULL) + self.landing[slot].astype(FULL)
        self.halves[slot, self.mine] = total.astype(LOW)
        pl.semaphore_signal(self.free, 1, device_id=self.other(), device_id_type=MESH)
        self.out(slot, t, target).start()
        self.pending = None

    def finish(self, target):
        self.settle()
        for slot in range(2):
            self.send(slot).wait_send()
            self.out(slot, 0, target).wait()
        pl.semaphore_wait(self.free, 2)


def pair_scratch(half, width):
    return [
        pltpu.VMEM((2, 2, half, width), LOW),
        pltpu.VMEM((2, half, width), LOW),
        pltpu.SemaphoreType.DMA((2,)),
        pltpu.SemaphoreType.DMA((2,)),
        pltpu.SemaphoreType.REGULAR,
        pltpu.SemaphoreType.DMA((2,)),
    ]


def pair_tile(model, places):
    size = 2 * model // places
    return size if size % 128 == 0 else size * 128 // math.gcd(size, 128)


def pair_dot(left, right, part, size):
    n, rows, _ = left.shape

    def compute(t, halves):
        lhs = left[:, :, pl.ds(t * size, size)].reshape(n * rows, size)
        width = right.shape[2]

        def tile(at):
            rhs = right[:, :, at].reshape(n * rows, -1)
            value = dot(lhs, rhs, 0, 0).astype(LOW)
            for k in range(size // (2 * part)):
                for side in range(2):
                    first = (2 * k + side) * part
                    halves[side, k * part : (k + 1) * part, at] = value[first : first + part]

        tiles(width, tile_of(width, 640), tile)

    return compute


def column_halves(width):
    first = -(-width // 256) * 128
    return [(0, first), (first, width - first)]


class PlaneReduce:
    def __init__(self, blocks, landings, sent, landed):
        self.blocks, self.landings, self.sent, self.landed = blocks, landings, sent, landed
        self.bits = len(blocks.shape) - 3
        self.me = lax.axis_index("seq")
        self.columns = column_halves(blocks.shape[-1])

    def bit(self, dim):
        return 1 << (self.bits - dim)

    def mine(self, dim):
        return lax.rem(self.me // self.bit(dim), 2)

    def order(self, side):
        dims = list(range(self.bits))
        return dims[::-1] if side == 0 else dims

    def peer(self, dim):
        return {"seq": self.me + self.bit(dim) * (1 - 2 * self.mine(dim))}

    def index(self, side, step, own):
        order = self.order(side)
        place = [slice(None)] * self.bits
        for dim in order[:step]:
            place[dim] = self.mine(dim)
        now = order[step]
        place[now] = self.mine(now) if own else 1 - self.mine(now)
        return tuple(place) + (slice(None), slice(None), pl.ds(*self.columns[side]))

    def send(self, side, step, piece=0):
        at, landing = self.index(side, step, False), self.landings[2 * step + side]
        if step == 0:
            count = self.blocks.shape[-3] // 2
            rows = pl.ds(piece * count, count)
            at = at[: self.bits] + (rows,) + at[self.bits + 1 :]
            landing = landing.at[(slice(None),) * (self.bits - 1) + (rows,)]
        return pltpu.make_async_remote_copy(
            src_ref=self.blocks.at[at],
            dst_ref=landing,
            send_sem=self.sent.at[side, step + piece * self.bits],
            recv_sem=self.landed.at[side, step + piece * self.bits],
            device_id=self.peer(self.order(side)[step]),
            device_id_type=MESH,
        )

    def pieces(self, step):
        return (0, 1) if step == 0 else (0,)

    def begin(self, pieces=(0, 1)):
        for piece in pieces:
            for side in range(2):
                self.send(side, 0, piece).start()

    def advance(self, step):
        for side in range(2):
            for piece in self.pieces(step):
                self.send(side, step, piece).wait_recv()
            at = self.index(side, step, True)
            total = self.blocks[at].astype(FULL) + self.landings[2 * step + side][...].astype(FULL)
            self.blocks[at] = total.astype(LOW)
            if step + 1 < self.bits:
                self.send(side, step + 1).start()

    def kept(self):
        return self.blocks.at[tuple(self.mine(dim) for dim in range(self.bits))]

    def finish(self):
        for step in range(self.bits):
            for side in range(2):
                for piece in self.pieces(step):
                    self.send(side, step, piece).wait_send()


def plane_scratch(shape):
    bits = len(shape) - 3
    landings = []
    for step in range(bits):
        for _, width in column_halves(shape[-1]):
            rest = [2] * (bits - 1 - step) + [shape[-3], shape[-2], width]
            landings.append(pltpu.VMEM(tuple(rest), LOW))
    return landings


def ffn_kernel(
    n,
    places,
    xn2_ref,
    dm_hbm,
    wg_hbm,
    wu_hbm,
    wd_hbm,
    dxn2_ref,
    hidden_hbm,
    dg_hbm,
    dv_hbm,
    xall_hbm,
    down_hbm,
    xall,
    dm,
    wg,
    wu,
    wd,
    hidden,
    dg,
    dv,
    parts,
    slots,
    halves,
    landing,
    psent,
    planded,
    free,
    pflush,
    gsent,
    glanded,
    rsent,
    rlanded,
    local,
    flush,
):
    me = lax.axis_index("wt")
    rows, model = xn2_ref.shape
    units = wg.shape[1]
    cut = tile_of(units, 640)
    span = tile_of(model, 512)
    loads = [
        pltpu.make_async_copy(source, target, local.at[k])
        for k, (source, target) in enumerate(
            [(dm_hbm, dm), (wd_hbm, wd), (wg_hbm, wg), (wu_hbm, wu)]
        )
    ]
    for load in loads:
        load.start()
    xall[me] = xn2_ref[...]
    greet(n, me, True)

    def ready():
        for load in loads[:2]:
            load.wait()

        def tile(at):
            value = dot(dm[...].reshape(n * rows, model), wd[:, at])
            dg[:, :, at] = value.reshape(n, rows, -1).astype(LOW)

        tiles(units, cut, tile)
        for load in loads[2:]:
            load.wait()

    def use(q):
        def tile(at):
            block = xall[q]
            g = dot(block, wg[:, at])
            v = dot(block, wu[:, at])
            slopes = dg[q, :, at].astype(FULL)
            gelu, slope = gelu_both(g)
            hidden[q, :, at] = (gelu * v).astype(LOW)
            dg[q, :, at] = (slopes * v * slope).astype(LOW)
            dv[q, :, at] = (slopes * gelu).astype(LOW)

        tiles(units, cut, tile)

    line_gather(n, me, xall, gsent, glanded, use, ready)
    outs = [
        pltpu.make_async_copy(source, target, flush.at[k])
        for k, (source, target) in enumerate(
            [(hidden, hidden_hbm), (dg, dg_hbm), (dv, dv_hbm), (xall, xall_hbm)]
        )
    ]
    for out in outs:
        out.start()

    def partial(q):
        def tile(at):
            total = dot(dg[q], wg[at, :], 1, 1) + dot(dv[q], wu[at, :], 1, 1)
            parts[q, :, at] = total.astype(LOW)

        tiles(model, span, tile)

    part = model // places
    size = pair_tile(model, places)
    pair = PairSum(part, halves, landing, psent, planded, free, pflush)

    work = pair.tasks(model // size, pair_dot(dm, hidden, part, size), down_hbm)

    def finish(total):
        dxn2_ref[...] = total

    line_reduce(n, me, parts, slots, rsent, rlanded, partial, work, finish)
    pair.finish(down_hbm)
    for out in outs:
        out.wait()


def ffn(n, places, xn2, dm, wg, wu, wd):
    rows, model = xn2.shape
    units = wg.shape[1]
    grad = jax.ShapeDtypeStruct((model // 2, units), LOW)
    return pl.pallas_call(
        functools.partial(ffn_kernel, n, places),
        out_shape=[
            jax.ShapeDtypeStruct((rows, model), FULL),
            jax.ShapeDtypeStruct((n, rows, units), LOW),
            jax.ShapeDtypeStruct((n, rows, units), LOW),
            jax.ShapeDtypeStruct((n, rows, units), LOW),
            jax.ShapeDtypeStruct((n, rows, model), LOW),
            grad,
        ],
        in_specs=[VMEM, ANY, ANY, ANY, ANY],
        out_specs=[VMEM, ANY, ANY, ANY, ANY, ANY],
        scratch_shapes=[
            pltpu.VMEM((n, rows, model), LOW),
            pltpu.VMEM((n, rows, model), LOW),
            pltpu.VMEM((model, units), LOW),
            pltpu.VMEM((model, units), LOW),
            pltpu.VMEM((model, units), LOW),
            pltpu.VMEM((n, rows, units), LOW),
            pltpu.VMEM((n, rows, units), LOW),
            pltpu.VMEM((n, rows, units), LOW),
            pltpu.VMEM((n, rows, model), LOW),
            pltpu.VMEM((2, n - 1, rows, model), LOW),
        ]
        + pair_scratch(pair_tile(model, places) // 2, units)
        + gather_sems(n)
        + reduce_sems(n)
        + [pltpu.SemaphoreType.DMA((4,)), pltpu.SemaphoreType.DMA((4,))],
        compiler_params=comm_params(2),
        cost_estimate=lasting(105),
    )(xn2, dm, wg, wu, wd)


def back_in_kernel(n, places, bits, *refs):
    dxn2_ref, x1_ref, slope_ref, gain_ref, *sources = refs[:11]
    dx1_ref, dz_ref, do_ref, sum_ref, out_ref, kept_ref, gate_hbm, up_hbm = refs[11:19]
    w, hidden, wd, xall, dg, dv, blocks = refs[19:26]
    landings = refs[26 : 26 + 2 * bits]
    parts, slots, *sems = refs[26 + 2 * bits :]
    halves, landing, psent, planded, free, pflush, sent, landed, rsent, rlanded, bsent, blanded, local = sems
    me = lax.axis_index("wt")
    loads = [
        pltpu.make_async_copy(source, target, local.at[k])
        for k, (source, target) in enumerate(
            zip(sources, [blocks, w, wd, hidden, xall, dg, dv])
        )
    ]
    for load in loads:
        load.start()
    x1 = x1_ref[...]
    dxn2 = dxn2_ref[...]
    model = x1.shape[1]
    scale = lax.rsqrt(jnp.mean(x1 * x1, axis=-1, keepdims=True) + EPSILON)
    q2 = dxn2 * gain_ref[...]
    pull = jnp.mean(q2 * x1, axis=-1, keepdims=True)
    dx1 = slope_ref[...] + scale * (q2 - x1 * (scale * scale * pull))
    dx1_ref[...] = dx1
    dz_ref[me] = dx1.astype(LOW)
    greet(n, me, True, bits)
    line = LineGather(n, me, dz_ref, sent, landed)
    back = LineReduce(n, me, parts, slots, rsent, rlanded)
    both = LineBoth(line, back)
    both.step(0)
    loads[0].wait()
    plane = PlaneReduce(blocks, landings, bsent, blanded)
    plane.begin()
    sum_ref[...] = jnp.sum(dxn2 * x1 * scale, axis=0, keepdims=True)

    def use(q):
        do_ref[q] = dot(dz_ref[q], w[...])

    def partial(q):
        def tile(at):
            parts[q, :, at] = dot(hidden[q], wd[at, :], 1, 1).astype(LOW)

        tiles(model, tile_of(model, 512), tile)

    part = model // places
    size = pair_tile(model, places)
    pair = PairSum(part, halves, landing, psent, planded, free, pflush)
    loads[1].wait()
    use(me)
    for load in loads[2:4]:
        load.wait()
    back.prepare(0, partial)
    work = pair.tasks(model // size, pair_dot(xall, dg, part, size), gate_hbm)
    work += pair.tasks(model // size, pair_dot(xall, dv, part, size), up_hbm)
    share = -(-len(work) // (n - 1))
    for t in range(1, n):
        both.step(t)
        if t == 1:
            for k in range(1, n - 1):
                back.prepare(k, partial)
        if t >= 2 and t - 2 < bits:
            plane.advance(t - 2)
        line.each(t, use)
        if t == 1:
            partial(me)
            for load in loads[4:]:
                load.wait()
        for task in work[(t - 1) * share : t * share]:
            task()
    for step in range(max(n - 2, 0), bits):
        plane.advance(step)
    out_ref[...] = (x1_ref[...] + back.total()).astype(LOW)
    kept_ref[...] = plane.kept()[...]
    pair.finish(up_hbm)
    both.finish()
    plane.finish()


def back_in(n, places, dxn2, x1, slope, gain, down, weight, wd, hidden, xall, dg, dv):
    rows, model = x1.shape
    bits = len(down.shape) - 3
    grad = jax.ShapeDtypeStruct((model // 2, wd.shape[1]), LOW)
    return pl.pallas_call(
        functools.partial(back_in_kernel, n, places, bits),
        out_shape=[
            jax.ShapeDtypeStruct((rows, model), FULL),
            jax.ShapeDtypeStruct((n, rows, model), LOW),
            jax.ShapeDtypeStruct((n, rows, weight.shape[1]), FULL),
            jax.ShapeDtypeStruct((1, model), FULL),
            jax.ShapeDtypeStruct((rows, model), LOW),
            jax.ShapeDtypeStruct(down.shape[bits:], LOW),
            grad,
            grad,
        ],
        in_specs=[VMEM] * 4 + [ANY] * 7,
        out_specs=[VMEM] * 6 + [ANY] * 2,
        scratch_shapes=[
            pltpu.VMEM(weight.shape, LOW),
            pltpu.VMEM(hidden.shape, LOW),
            pltpu.VMEM(wd.shape, LOW),
            pltpu.VMEM(xall.shape, LOW),
            pltpu.VMEM(dg.shape, LOW),
            pltpu.VMEM(dv.shape, LOW),
            pltpu.VMEM(down.shape, LOW),
        ]
        + plane_scratch(down.shape)
        + [
            pltpu.VMEM((n, rows, model), LOW),
            pltpu.VMEM((2, n - 1, rows, model), LOW),
        ]
        + pair_scratch(pair_tile(model, places) // 2, wd.shape[1])
        + gather_sems(n)
        + reduce_sems(n)
        + [
            pltpu.SemaphoreType.DMA((2, 2 * bits)),
            pltpu.SemaphoreType.DMA((2, 2 * bits)),
            pltpu.SemaphoreType.DMA((7,)),
        ],
        compiler_params=comm_params(3),
        cost_estimate=lasting(75),
    )(dxn2, x1, slope, gain, down, weight, wd, hidden, xall, dg, dv)


class PlaneShare:
    def __init__(self, places, source, lands, sent, landed):
        self.places, self.source, self.lands = places, source, lands
        self.sent, self.landed = sent, landed
        self.me = lax.axis_index("seq")

    def send(self, by):
        to = lax.rem(self.me + by, self.places)
        return pltpu.make_async_remote_copy(
            src_ref=self.source.at[to],
            dst_ref=self.lands.at[by],
            send_sem=self.sent.at[by],
            recv_sem=self.landed.at[by],
            device_id={"seq": to},
            device_id_type=MESH,
        )

    def start(self):
        self.lands[0] = self.source[self.me]
        for by in range(1, self.places):
            self.send(by).start()

    def finish(self, target):
        for by in range(1, self.places):
            self.send(by).wait_recv()
        target[...] = jnp.sum(self.lands[...].astype(FULL), axis=0)
        for by in range(1, self.places):
            self.send(by).wait_send()


def leave_kernel(
    n,
    places,
    bits,
    du_ref,
    dy_ref,
    o_ref,
    x_ref,
    dx1_ref,
    gain_ref,
    xn_hbm,
    dz_hbm,
    win_hbm,
    wbr_hbm,
    up_hbm,
    small_ref,
    grad_ref,
    sum_ref,
    mix_hbm,
    passed_ref,
    kept_ref,
    xn,
    dz,
    win,
    wbr,
    parts,
    slots,
    halves,
    landing,
    psent,
    planded,
    free,
    pflush,
    sent,
    landed,
    lands,
    ssent,
    slanded,
    local,
    usent,
    ulanded,
    blocks,
    *landings,
):
    me = lax.axis_index("wt")
    loads = [
        pltpu.make_async_copy(source, target, local.at[k])
        for k, (source, target) in enumerate(
            [(win_hbm, win), (wbr_hbm, wbr), (up_hbm, blocks), (xn_hbm, xn), (dz_hbm, dz)]
        )
    ]
    for load in loads:
        load.start()
    greet(n, me, False, 0, places)
    small = PlaneShare(places, small_ref, lands, ssent, slanded)
    small.start()
    plane = PlaneReduce(blocks, landings, usent, ulanded)
    for load in loads[:2]:
        load.wait()

    def early():
        loads[2].wait()
        plane.begin()
        for load in loads[3:]:
            load.wait()

    model = win.shape[0]

    def partial(q):
        def tile(at):
            total = dot(du_ref[q], win[at, :], 1, 1) + dot(dy_ref[q], wbr[at, :], 1, 1)
            parts[q, :, at] = total.astype(LOW)

        tiles(model, tile_of(model, 512), tile)

    part = model // places
    size = pair_tile(model, places)
    width = du_ref.shape[2]
    pair = PairSum(part, halves, landing, psent, planded, free, pflush)

    def compute(t, target):
        for k, (left, right) in enumerate([(dz, o_ref), (xn, dy_ref), (xn, du_ref)]):
            columns = pl.ds(k * width, width)
            pair_dot(left, right, part, size)(t, target.at[:, :, columns])

    work = pair.tasks(model // size, compute, mix_hbm)

    def finish(total):
        flat = x_ref[...].astype(FULL)
        scale = lax.rsqrt(jnp.mean(flat * flat, axis=-1, keepdims=True) + EPSILON)
        q1 = total * gain_ref[...]
        pull = jnp.mean(q1 * flat, axis=-1, keepdims=True)
        grad_ref[...] = dx1_ref[...] + scale * (q1 - flat * (scale * scale * pull))
        sum_ref[...] = jnp.sum(total * flat * scale, axis=0, keepdims=True)

    tasks = work[:-1] + [lambda: (work[-1](), plane.advance(0))]
    line_reduce(n, me, parts, slots, sent, landed, partial, tasks, finish, early)
    pair.finish(mix_hbm)
    small.finish(passed_ref)
    for step in range(1, bits):
        plane.advance(step)
    kept_ref[...] = plane.kept()[...]
    plane.finish()


def leave(n, places, du, dy, o, x, dx1, gain, xn, dz, win, wbr, up, small):
    bits = len(up.shape) - 3
    rows, model = x.shape
    width = win.shape[1]
    return pl.pallas_call(
        functools.partial(leave_kernel, n, places, bits),
        out_shape=[
            jax.ShapeDtypeStruct((rows, model), FULL),
            jax.ShapeDtypeStruct((1, model), FULL),
            jax.ShapeDtypeStruct((model // 2, 3 * width), LOW),
            jax.ShapeDtypeStruct(small.shape[1:], FULL),
            jax.ShapeDtypeStruct(up.shape[bits:], LOW),
        ],
        in_specs=[VMEM] * 6 + [ANY] * 5 + [VMEM],
        out_specs=[VMEM, VMEM, ANY, VMEM, VMEM],
        scratch_shapes=[
            pltpu.VMEM((n, rows, model), LOW),
            pltpu.VMEM((n, rows, model), LOW),
            pltpu.VMEM(win.shape, LOW),
            pltpu.VMEM(wbr.shape, LOW),
            pltpu.VMEM((n, rows, model), LOW),
            pltpu.VMEM((2, n - 1, rows, model), LOW),
        ]
        + pair_scratch(pair_tile(model, places) // 2, 3 * width)
        + reduce_sems(n)
        + [
            pltpu.VMEM(small.shape, LOW),
            pltpu.SemaphoreType.DMA((places,)),
            pltpu.SemaphoreType.DMA((places,)),
            pltpu.SemaphoreType.DMA((5,)),
            pltpu.SemaphoreType.DMA((2, 2 * bits)),
            pltpu.SemaphoreType.DMA((2, 2 * bits)),
            pltpu.VMEM(up.shape, LOW),
        ]
        + plane_scratch(up.shape),
        compiler_params=comm_params(4),
        cost_estimate=lasting(60),
    )(du, dy, o, x, dx1, gain, xn, dz, win, wbr, up, small)


class LineSpread:
    def __init__(self, n, me, source, lands, sent, landed):
        self.n, self.me, self.source, self.lands = n, me, source, lands
        self.sent, self.landed = sent, landed

    def send(self, by):
        to = lax.rem(self.me + by, self.n)
        return remote(
            self.source.at[to], self.lands.at[self.me], self.sent.at[by], self.landed.at[by], to
        )

    def start(self):
        for by in range(1, self.n):
            self.send(by).start()

    def take(self, put, own):
        put(self.me, own[...])
        for by in range(1, self.n):
            slot = lax.rem(self.me + self.n - by, self.n)
            land = self.lands.at[slot]
            remote(land, land, self.sent.at[by], self.landed.at[by], self.me).wait_recv()
            put(slot, land[...])

    def finish(self):
        for by in range(1, self.n):
            self.send(by).wait_send()


def settle_kernel(n, places, bits, gate_hbm, up_hbm, mix_hbm, gains_ref, gate_ref, up_ref, out_ref, branch_ref, in_ref, total_ref, *scratch):
    blocks, landings, scratch = scratch[0], scratch[1 : 1 + 2 * bits], scratch[1 + 2 * bits :]
    lands, own, notes, around, psent, planded, ssent, slanded, gsent, glanded, local = scratch
    me = lax.axis_index("wt")
    seat = lax.axis_index("seq")
    loads = [
        pltpu.make_async_copy(mix_hbm, blocks, local.at[0]),
        pltpu.make_async_copy(gate_hbm.at[me], own.at[0], local.at[1]),
        pltpu.make_async_copy(up_hbm.at[me], own.at[1], local.at[2]),
    ]
    for load in loads:
        load.start()
    notes[me] = gains_ref[...]
    barrier = pltpu.get_barrier_semaphore()
    for by in range(1, n):
        pl.semaphore_signal(
            barrier, 1, device_id={"wt": lax.rem(me + by, n)}, device_id_type=MESH
        )
    for by in range(1, places):
        pl.semaphore_signal(
            barrier, 1, device_id={"seq": lax.rem(seat + by, places)}, device_id_type=MESH
        )
    pl.semaphore_wait(barrier, n + places - 2)
    loads[0].wait()
    plane = PlaneReduce(blocks, landings, psent, planded)
    plane.begin()
    spreads = [
        LineSpread(n, me, source, lands.at[k], ssent.at[k], slanded.at[k])
        for k, source in enumerate([gate_hbm, up_hbm])
    ]

    def note(by):
        to = lax.rem(me + by, n)
        return remote(notes.at[me], notes.at[me], gsent.at[0, by], glanded.at[0, by], to)

    for by in range(1, n):
        note(by).start()
    for spread in spreads:
        spread.start()
    for by in range(1, n):
        slot = notes.at[lax.rem(me + n - by, n)]
        remote(slot, slot, gsent.at[0, by], glanded.at[0, by], me).wait_recv()
    around[seat] = jnp.sum(notes[...], axis=0)

    def share(by):
        to = lax.rem(seat + by, places)
        return pltpu.make_async_remote_copy(
            src_ref=around.at[seat],
            dst_ref=around.at[seat],
            send_sem=gsent.at[1, by],
            recv_sem=glanded.at[1, by],
            device_id={"seq": to},
            device_id_type=MESH,
        )

    for by in range(1, places):
        share(by).start()
    for step in range(bits):
        plane.advance(step)
    kept = plane.kept()
    last = LineSpread(n, me, kept, lands.at[2], ssent.at[2], slanded.at[2])
    last.start()
    for by in range(1, places):
        slot = around.at[lax.rem(seat + places - by, places)]
        pltpu.make_async_remote_copy(
            src_ref=slot,
            dst_ref=slot,
            send_sem=gsent.at[1, by],
            recv_sem=glanded.at[1, by],
            device_id={"seq": seat},
            device_id_type=MESH,
        ).wait_recv()
    total_ref[...] = jnp.sum(around[...], axis=0)
    units = gate_hbm.shape[-1]
    for k, (spread, target) in enumerate(zip(spreads, [gate_ref, up_ref])):
        loads[1 + k].wait()

        def put(q, value, target=target):
            target[:, pl.ds(pl.multiple_of(q * units, 128), units)] = value.astype(FULL)

        spread.take(put, own.at[k])
    width = units // 3

    def put_mix(q, value):
        columns = pl.ds(pl.multiple_of(q * width, 128), width)
        for k, target in enumerate([out_ref, branch_ref, in_ref]):
            target[:, columns] = value[:, k * width : (k + 1) * width].astype(FULL)

    last.take(put_mix, kept.at[me])
    plane.finish()
    for spread in spreads + [last]:
        spread.finish()
    for by in range(1, n):
        note(by).wait_send()
    for by in range(1, places):
        share(by).wait_send()


def settle(n, places, gate, up, mix, gains):
    _, part, units = gate.shape
    bits = len(mix.shape) - 3
    wide = jax.ShapeDtypeStruct((part, n * units), FULL)
    thin = jax.ShapeDtypeStruct((part, n * units // 3), FULL)
    return pl.pallas_call(
        functools.partial(settle_kernel, n, places, bits),
        out_shape=[wide, wide, thin, thin, thin, jax.ShapeDtypeStruct(gains.shape, FULL)],
        in_specs=[ANY, ANY, ANY, VMEM],
        out_specs=[VMEM] * 6,
        scratch_shapes=[pltpu.VMEM(mix.shape, LOW)]
        + plane_scratch(mix.shape)
        + [
            pltpu.VMEM((3, n, part, units), LOW),
            pltpu.VMEM((2, part, units), LOW),
            pltpu.VMEM((n,) + gains.shape, FULL),
            pltpu.VMEM((places,) + gains.shape, FULL),
            pltpu.SemaphoreType.DMA((2, 2 * bits)),
            pltpu.SemaphoreType.DMA((2, 2 * bits)),
            pltpu.SemaphoreType.DMA((3, n)),
            pltpu.SemaphoreType.DMA((3, n)),
            pltpu.SemaphoreType.DMA((2, max(n, places))),
            pltpu.SemaphoreType.DMA((2, max(n, places))),
            pltpu.SemaphoreType.DMA((3,)),
        ],
        compiler_params=comm_params(5),
        cost_estimate=lasting(100),
    )(gate, up, mix, gains)


def conv_masks(own, before, after, taps):
    lane = lax.broadcasted_iota(jnp.int32, own.shape, 1)
    lines = []
    for here, back in ((own, before), (after, own)):
        for k in range(taps):
            shifted = jnp.where(lane >= k, pltpu.roll(here, k, 1), pltpu.roll(back, k, 1))
            lines.append((shifted == here).astype(FULL)[:1] if k else jnp.ones_like(here)[:1])
    lines.append(jnp.zeros((own.shape[1] - 2 * taps, own.shape[1]), FULL))
    return jnp.concatenate(lines, axis=0).T


def mid_kernel(
    n,
    places,
    taps,
    u_ref,
    y_ref,
    docs_ref,
    rows_ref,
    gr_hbm,
    gi_hbm,
    slope_ref,
    o_ref,
    c_ref,
    r_ref,
    ii_ref,
    h_ref,
    edge_ref,
    halo_ref,
    mask_ref,
    near_ref,
    tr,
    ti,
    cum,
    carry,
    before,
    after,
    hsent,
    hlanded,
    esent,
    elanded,
    csent,
    clanded,
    nsent,
    nlanded,
    local,
):
    me = lax.axis_index("wt")
    seat = lax.axis_index("seq")
    part_len, width = u_ref.shape[1:]
    head = gr_hbm.shape[1]
    ext = tr.shape[0]
    edge = ext - width
    odd = lax.rem(me, 2)
    shift = odd * edge
    block = 128
    first = pl.multiple_of((me * width) // head * head, head)
    loads = [
        pltpu.make_async_copy(source.at[pl.ds(first, ext), :], target, local.at[k])
        for k, (source, target) in enumerate([(gr_hbm, tr), (gi_hbm, ti)])
    ]
    for load in loads:
        load.start()
    partner = {"wt": me + 1 - 2 * odd}
    near_ref[1] = slope_ref[...].astype(LOW)
    greet(n, me, False, 0, places)

    def neighbours(act, out):
        for k, (to, there) in enumerate([(me + 1, 0), (me - 1, 2)]):
            copy = remote(near_ref.at[1], near_ref.at[there], nsent.at[k], nlanded.at[k], to)
            inside = (to >= 0) & (to < n)
            gives = (me > 0) if k == 0 else (me < n - 1)

            @pl.when(inside if out else gives)
            def _():
                act(copy)


    def hop(source, target, k, to):
        return pltpu.make_async_remote_copy(
            src_ref=source,
            dst_ref=target,
            send_sem=hsent.at[k],
            recv_sem=hlanded.at[k],
            device_id={"seq": to},
            device_id_type=MESH,
        )

    reach = halo_ref.shape[1]
    tails = u_ref.at[:, pl.ds(part_len - reach, reach), :]
    onward = [hop(tails, halo_ref, 0, seat + 1), hop(docs_ref, before, 1, seat + 1)]
    backward = [hop(docs_ref, after, 2, seat - 1)]

    @pl.when(seat < places - 1)
    def _():
        for copy in onward:
            copy.start()

    @pl.when(seat > 0)
    def _():
        for copy in backward:
            copy.start()

    @pl.when(seat == 0)
    def _():
        halo_ref[...] = jnp.zeros_like(halo_ref)
        before[...] = jnp.full_like(before, -1)

    @pl.when(seat == places - 1)
    def _():
        after[...] = jnp.full_like(after, -1)

    @pl.when(seat > 0)
    def _():
        for copy in onward:
            copy.wait_recv()

    @pl.when(seat < places - 1)
    def _():
        for copy in backward:
            copy.wait_recv()

    def columns(b):
        return pl.ds(pl.multiple_of(b * block, block), block)

    def ext_columns(b):
        return pl.ds(pl.multiple_of(b * block + shift, block), block)

    def each(body):
        def outer(q, carried):
            def inner(b, deeper):
                body(q, b)
                return deeper

            return lax.fori_loop(0, width // block, inner, carried)

        lax.fori_loop(0, n, outer, 0)

    def masks(q, carried):
        mask_ref[q] = conv_masks(
            docs_ref[q].astype(FULL), before[q].astype(FULL), after[q].astype(FULL), taps
        )
        return carried

    lax.fori_loop(0, n, masks, 0)

    def conv(q, b):
        at = columns(b)
        long = jnp.concatenate([halo_ref[q, :, at], u_ref[q, :, at]], axis=0).astype(FULL)
        total = long[reach:] * rows_ref[0:1, at]
        for k in range(1, taps):
            window = pltpu.roll(long, k, 0)[reach:]
            total = total + window * mask_ref[q, :, k : k + 1] * rows_ref[k : k + 1, at]
        c_ref[q, :, ext_columns(b)] = total.astype(LOW)

    each(conv)
    source = pl.ds(pl.multiple_of(jnp.where(odd == 1, edge, width - edge), edge), edge)
    target = pl.ds(pl.multiple_of(jnp.where(odd == 1, width, 0), edge), edge)
    swap = pltpu.make_async_remote_copy(
        src_ref=c_ref.at[:, :, source],
        dst_ref=c_ref.at[:, :, target],
        send_sem=esent.at[0],
        recv_sem=elanded.at[0],
        device_id=partner,
        device_id_type=MESH,
    )
    swap.start()
    for load in loads:
        load.wait()
    swap.wait_recv()
    neighbours(lambda copy: copy.start(), True)
    per = head // block

    def gates(q, b):
        at = columns(b)
        j = b + shift // block
        spot = j // per
        within = pl.ds(pl.multiple_of(lax.rem(j, per) * block, block), block)
        rows = pl.ds(pl.multiple_of(spot * head, head), head)
        c_head = c_ref[q, :, rows]
        c_own = c_ref[q, :, ext_columns(b)].astype(FULL)
        r = jax.nn.sigmoid(dot(c_head, tr[rows, within]) + rows_ref[taps : taps + 1, at])
        ii = jax.nn.sigmoid(dot(c_head, ti[rows, within]) + rows_ref[taps + 1 : taps + 2, at])
        keep = mask_ref[q, :, 1:2]
        log_a = rows_ref[taps + 2 : taps + 3, at] * r
        mult = mult_of(log_a, keep)
        b_low = (mult * c_own * ii).astype(LOW).astype(FULL)
        a = jnp.exp(log_a.astype(LOW).astype(FULL)) * keep
        cum_a, h_loc = scan_rows(a, b_low, False)
        r_ref[q, :, at] = r
        ii_ref[q, :, at] = ii
        cum[q, :, at] = cum_a
        h_ref[q, :, at] = h_loc

    each(gates)
    for q in range(n):
        carry[seat, q : q + 1, :] = cum[q, part_len - 1 : part_len, :]
        carry[seat, n + q : n + q + 1, :] = h_ref[q, part_len - 1 : part_len, :]

    def share(by):
        return pltpu.make_async_remote_copy(
            src_ref=carry.at[seat],
            dst_ref=carry.at[seat],
            send_sem=csent.at[by],
            recv_sem=clanded.at[by],
            device_id={"seq": lax.rem(seat + by, places)},
            device_id_type=MESH,
        )

    for by in range(1, places):
        share(by).start()
    for by in range(1, places):
        share(by).wait_recv()
    state = jnp.zeros((n, width), FULL)
    start = state
    for p in range(places):
        start = jnp.where(seat == p, state, start)
        state = carry[p, :n, :] * state + carry[p, n:, :]
    edge_ref[:n, :] = start
    edge_ref[n:, :] = carry[seat, :n, :]

    def finish(q, b):
        at = columns(b)
        h = h_ref[q, :, at] + cum[q, :, at] * pick_row(edge_ref[:, at], q)
        h_ref[q, :, at] = h
        gelu, _ = gelu_both(y_ref[q, :, at])
        o_ref[q, :, at] = (h.astype(LOW).astype(FULL) * gelu).astype(LOW)

    each(finish)
    neighbours(lambda copy: copy.wait_recv(), False)
    neighbours(lambda copy: copy.wait_send(), True)
    swap.wait_send()

    @pl.when(seat < places - 1)
    def _():
        for copy in onward:
            copy.wait_send()

    @pl.when(seat > 0)
    def _():
        for copy in backward:
            copy.wait_send()

    for by in range(1, places):
        share(by).wait_send()


def pick_row(table, q):
    place = lax.broadcasted_iota(jnp.int32, table.shape, 0)
    return jnp.sum(jnp.where(place == q, table, 0.0), axis=0, keepdims=True)


def mult_of(log_a, keep):
    twice = 2.0 * log_a
    gap = jnp.where(twice > -0.01, -expm1_small(twice), 1.0 - jnp.exp(twice))
    return jnp.where(keep == 0.0, 1.0, jnp.sqrt(gap))


def mid(n, places, taps, u, y, docs, rows8, gate_r, gate_i, slope):
    _, rows, width = u.shape
    head = gate_r.shape[1]
    ext = -(-width // head) * head
    full = jax.ShapeDtypeStruct(u.shape, FULL)
    return pl.pallas_call(
        functools.partial(mid_kernel, n, places, taps),
        out_shape=[
            jax.ShapeDtypeStruct(u.shape, LOW),
            jax.ShapeDtypeStruct((n, rows, ext), LOW),
            full,
            full,
            full,
            jax.ShapeDtypeStruct((2 * n, width), FULL),
            jax.ShapeDtypeStruct((n, 16, width), LOW),
            jax.ShapeDtypeStruct((n, rows, rows), FULL),
            jax.ShapeDtypeStruct((3,) + slope.shape, LOW),
        ],
        in_specs=[VMEM] * 4 + [ANY] * 2 + [VMEM],
        out_specs=[VMEM] * 9,
        scratch_shapes=[
            pltpu.VMEM((ext, head), LOW),
            pltpu.VMEM((ext, head), LOW),
            pltpu.VMEM(u.shape, FULL),
            pltpu.VMEM((places, 2 * n, width), FULL),
            pltpu.VMEM(docs.shape, jnp.int32),
            pltpu.VMEM(docs.shape, jnp.int32),
            pltpu.SemaphoreType.DMA((3,)),
            pltpu.SemaphoreType.DMA((3,)),
            pltpu.SemaphoreType.DMA((1,)),
            pltpu.SemaphoreType.DMA((1,)),
            pltpu.SemaphoreType.DMA((places,)),
            pltpu.SemaphoreType.DMA((places,)),
            pltpu.SemaphoreType.DMA((2,)),
            pltpu.SemaphoreType.DMA((2,)),
            pltpu.SemaphoreType.DMA((2,)),
        ],
        compiler_params=comm_params(6),
        cost_estimate=lasting(30),
    )(u, y, docs, rows8, gate_r, gate_i, slope)


def turn_kernel(
    n,
    places,
    taps,
    bits,
    do_ref,
    y_ref,
    r_ref,
    ii_ref,
    h_ref,
    edge_ref,
    c_ref,
    u_ref,
    halo_ref,
    mask_ref,
    rows_ref,
    gr_hbm,
    gi_hbm,
    down_hbm,
    gate_hbm,
    du_ref,
    dy_ref,
    small_ref,
    down_ref,
    kept_ref,
    tr,
    ti,
    rem,
    e_ref,
    dra,
    dia,
    dc,
    lead,
    carry,
    ein,
    sums,
    lands,
    own,
    hsent,
    hlanded,
    esent,
    elanded,
    csent,
    clanded,
    ssent,
    slanded,
    local,
    psent,
    planded,
    blocks,
    *landings,
):
    me = lax.axis_index("wt")
    seat = lax.axis_index("seq")
    part_len, width = u_ref.shape[1:]
    head = gr_hbm.shape[1]
    ext = tr.shape[0]
    edge = ext - width
    odd = lax.rem(me, 2)
    shift = odd * edge
    block = 128
    per = head // block
    reach = halo_ref.shape[1]
    first = pl.multiple_of((me * width) // head * head, head)
    loads = [
        pltpu.make_async_copy(gr_hbm.at[pl.ds(first, ext), :], tr, local.at[0]),
        pltpu.make_async_copy(gi_hbm.at[pl.ds(first, ext), :], ti, local.at[1]),
        pltpu.make_async_copy(down_hbm.at[me], own, local.at[2]),
        pltpu.make_async_copy(gate_hbm, blocks, local.at[3]),
    ]
    for load in loads:
        load.start()
    barrier = pltpu.get_barrier_semaphore()
    for by in range(1, places):
        other = {"seq": lax.rem(seat + by, places)}
        pl.semaphore_signal(barrier, 1, device_id=other, device_id_type=MESH)
    for by in range(1, n):
        other = {"wt": lax.rem(me + by, n)}
        pl.semaphore_signal(barrier, 1, device_id=other, device_id_type=MESH)
    pl.semaphore_wait(barrier, places + n - 2)
    spread = LineSpread(n, me, down_hbm, lands, ssent, slanded)
    spread.start()
    loads[3].wait()
    plane = PlaneReduce(blocks, landings, psent, planded)
    plane.begin((0,))

    def columns(b):
        return pl.ds(pl.multiple_of(b * block, block), block)

    def ext_columns(b):
        return pl.ds(pl.multiple_of(b * block + shift, block), block)

    def head_columns(b):
        spot = (b + shift // block) // per
        return pl.ds(pl.multiple_of(spot * head, head), head)

    def each(body):
        def outer(q, carried):
            def inner(b, deeper):
                body(q, b)
                return deeper

            return lax.fori_loop(0, width // block, inner, carried)

        lax.fori_loop(0, n, outer, 0)

    def decay(q, at, rows=slice(None)):
        log_a = rows_ref[taps + 2 : taps + 3, at] * r_ref[q, rows, at]
        return jnp.exp(log_a.astype(LOW).astype(FULL)) * mask_ref[q, rows, 1:2]

    place = lax.broadcasted_iota(jnp.int32, (part_len, block), 0)

    def scans(q, b):
        at = columns(b)
        gelu, slope = gelu_both(y_ref[q, :, at])
        back = do_ref[q, :, at]
        hr = h_ref[q, :, at].astype(LOW).astype(FULL)
        dy_ref[q, :, at] = (back * hr * slope).astype(LOW)
        dh = (back * gelu).astype(LOW).astype(FULL)
        a_next = jnp.where(
            place < part_len - 1, pltpu.roll(decay(q, at), part_len - 1, 0), 1.0
        )
        far, e_loc = scan_rows(a_next, dh, True)
        rem[q, :, at] = far
        e_ref[q, :, at] = e_loc

    each(scans)
    carry[seat, :n, :] = edge_ref[n:, :]
    for q in range(n):
        top = decay(q, slice(None), slice(0, 1)) * e_ref[q, 0:1, :]
        carry[seat, n + q : n + q + 1, :] = top

    def share(by):
        return pltpu.make_async_remote_copy(
            src_ref=carry.at[seat],
            dst_ref=carry.at[seat],
            send_sem=csent.at[by],
            recv_sem=clanded.at[by],
            device_id={"seq": lax.rem(seat + by, places)},
            device_id_type=MESH,
        )

    for by in range(1, places):
        share(by).start()
    sums[...] = jnp.zeros_like(sums)
    for by in range(1, places):
        share(by).wait_recv()
    plane.begin((1,))
    state = jnp.zeros((n, width), FULL)
    start = state
    for p in reversed(range(places)):
        start = jnp.where(seat == p, state, start)
        state = carry[p, :n, :] * state + carry[p, n:, :]
    ein[:n, :] = start
    ein[n:, :] = jnp.zeros_like(start)

    def slopes(q, b):
        at = columns(b)
        e = e_ref[q, :, at] + rem[q, :, at] * pick_row(ein[:, at], q)
        h_prev = jnp.where(
            place == 0, pick_row(edge_ref[:, at], q), pltpu.roll(h_ref[q, :, at], 1, 0)
        )
        r = r_ref[q, :, at]
        ii = ii_ref[q, :, at]
        keep = mask_ref[q, :, 1:2]
        soft = rows_ref[taps + 2 : taps + 3, at]
        log_a = soft * r
        mult = mult_of(log_a, keep)
        c = c_ref[q, :, ext_columns(b)].astype(FULL)
        dla = (e * h_prev * decay(q, at)).astype(LOW).astype(FULL)
        dbr = e.astype(LOW).astype(FULL)
        dmult = jnp.where(keep == 0.0, 0.0, -jnp.exp(2.0 * log_a) / mult)
        dlog_a = dla + dbr * c * ii * dmult
        dra_f = soft * dlog_a * r * (1.0 - r)
        direct = dbr * mult * ii
        dia_f = direct * c * (1.0 - ii)
        dra[q, :, ext_columns(b)] = dra_f.astype(LOW)
        dia[q, :, ext_columns(b)] = dia_f.astype(LOW)
        dc[q, :, at] = direct
        for k, value in enumerate([dra_f, dia_f, -8.0 * dlog_a * r]):
            sums[taps + k : taps + k + 1, at] += jnp.sum(value, axis=0, keepdims=True)

    each(slopes)
    source = pl.ds(pl.multiple_of(jnp.where(odd == 1, edge, width - edge), edge), edge)
    target = pl.ds(pl.multiple_of(jnp.where(odd == 1, width, 0), edge), edge)
    swaps = [
        pltpu.make_async_remote_copy(
            src_ref=ref.at[:, :, source],
            dst_ref=ref.at[:, :, target],
            send_sem=esent.at[k],
            recv_sem=elanded.at[k],
            device_id={"wt": me + 1 - 2 * odd},
            device_id_type=MESH,
        )
        for k, ref in enumerate([dra, dia])
    ]
    for swap in swaps:
        swap.start()
    for load in loads[:3]:
        load.wait()
    for swap in swaps:
        swap.wait_recv()

    def mix(q, b):
        at = columns(b)
        rows = head_columns(b)
        table = ext_columns(b)
        dc[q, :, at] += dot(dra[q, :, rows], tr[table, :], 1, 1) + dot(
            dia[q, :, rows], ti[table, :], 1, 1
        )

    each(mix)
    leads = pltpu.make_async_remote_copy(
        src_ref=dc.at[:, pl.ds(0, lead.shape[1]), :],
        dst_ref=lead,
        send_sem=hsent.at[0],
        recv_sem=hlanded.at[0],
        device_id={"seq": seat - 1},
        device_id_type=MESH,
    )

    @pl.when(seat > 0)
    def _():
        leads.start()

    @pl.when(seat == places - 1)
    def _():
        lead[...] = jnp.zeros_like(lead)

    def gate_grads(b, carried):
        left = c_ref[:, :, ext_columns(b)].reshape(n * part_len, block)
        rows = head_columns(b)
        for k, ref in enumerate([dra, dia]):
            right = ref[:, :, rows].reshape(n * part_len, head)
            small_ref[columns(b), k * head : (k + 1) * head] = dot(left, right, 0, 0).astype(LOW)
        return carried

    lax.fori_loop(0, width // block, gate_grads, 0)

    @pl.when(seat < places - 1)
    def _():
        leads.wait_recv()

    plane.advance(0)

    def conv(q, b):
        at = columns(b)
        slope = dc[q, :, at]
        next_rows = lead[q, :, at]
        long = jnp.concatenate([slope, next_rows], axis=0)
        total = slope * rows_ref[0:1, at]
        behind = jnp.concatenate([halo_ref[q, :, at], u_ref[q, :, at]], axis=0).astype(FULL)
        sums[0:1, at] += jnp.sum(behind[reach:] * slope, axis=0, keepdims=True)
        for k in range(1, taps):
            same = mask_ref[q, :, k : k + 1]
            same_next = mask_ref[q, : lead.shape[1], taps + k : taps + k + 1]
            masked = long * jnp.concatenate([same, same_next], axis=0)
            shifted = pltpu.roll(masked, long.shape[0] - k, 0)[:part_len]
            total = total + shifted * rows_ref[k : k + 1, at]
            window = pltpu.roll(behind, k, 0)[reach:] * same
            sums[k : k + 1, at] += jnp.sum(window * slope, axis=0, keepdims=True)
        du_ref[q, :, at] = total.astype(LOW)

    each(conv)
    row = taps + 2
    sums[row : row + 1, :] = sums[row : row + 1, :] * jax.nn.sigmoid(rows_ref[taps + 3 : taps + 4, :])

    def turn(b, carried):
        wide = jnp.concatenate(
            [sums[:, columns(b)], jnp.zeros((block - sums.shape[0], block), FULL)], axis=0
        )
        small_ref[columns(b), 2 * head : 2 * head + block] = wide.T.astype(LOW)
        return carried

    lax.fori_loop(0, width // block, turn, 0)
    units = down_hbm.shape[-1]

    def put(q, value):
        down_ref[:, pl.ds(pl.multiple_of(q * units, 128), units)] = value.astype(FULL)

    spread.take(put, own)
    for step in range(1, bits):
        plane.advance(step)
    kept_ref[...] = plane.kept()[...]
    plane.finish()
    spread.finish()
    for swap in swaps:
        swap.wait_send()
    for by in range(1, places):
        share(by).wait_send()

    @pl.when(seat > 0)
    def _():
        leads.wait_send()


def turn_back(
    n, places, taps, do, y, r, ii, h, edges, c, u, halo, mask, rows8, gate_r, gate_i, down, gate
):
    _, rows, width = u.shape
    head = gate_r.shape[1]
    ext = c.shape[2]
    _, part, units = down.shape
    bits = len(gate.shape) - 3
    low = jax.ShapeDtypeStruct(u.shape, LOW)
    return pl.pallas_call(
        functools.partial(turn_kernel, n, places, taps, bits),
        out_shape=[
            low,
            low,
            jax.ShapeDtypeStruct((width, 2 * head + 128), LOW),
            jax.ShapeDtypeStruct((part, n * units), FULL),
            jax.ShapeDtypeStruct(gate.shape[bits:], LOW),
        ],
        in_specs=[VMEM] * 11 + [ANY] * 4,
        out_specs=[VMEM] * 5,
        scratch_shapes=[
            pltpu.VMEM((ext, head), LOW),
            pltpu.VMEM((ext, head), LOW),
            pltpu.VMEM(u.shape, FULL),
            pltpu.VMEM(u.shape, FULL),
            pltpu.VMEM((n, rows, ext), LOW),
            pltpu.VMEM((n, rows, ext), LOW),
            pltpu.VMEM(u.shape, FULL),
            pltpu.VMEM((n, 8, width), FULL),
            pltpu.VMEM((places, 2 * n, width), FULL),
            pltpu.VMEM((2 * n, width), FULL),
            pltpu.VMEM((8, width), FULL),
            pltpu.VMEM(down.shape, LOW),
            pltpu.VMEM(down.shape[1:], LOW),
            pltpu.SemaphoreType.DMA((1,)),
            pltpu.SemaphoreType.DMA((1,)),
            pltpu.SemaphoreType.DMA((2,)),
            pltpu.SemaphoreType.DMA((2,)),
            pltpu.SemaphoreType.DMA((places,)),
            pltpu.SemaphoreType.DMA((places,)),
            pltpu.SemaphoreType.DMA((n,)),
            pltpu.SemaphoreType.DMA((n,)),
            pltpu.SemaphoreType.DMA((4,)),
            pltpu.SemaphoreType.DMA((2, 2 * bits)),
            pltpu.SemaphoreType.DMA((2, 2 * bits)),
            pltpu.VMEM(gate.shape, LOW),
        ]
        + plane_scratch(gate.shape),
        compiler_params=comm_params(7),
        cost_estimate=lasting(45),
    )(do, y, r, ii, h, edges, c, u, halo, mask, rows8, gate_r, gate_i, down, gate)


def on_device(
    inputs,
    segment,
    mixer_gain,
    input_weight,
    branch_weight,
    conv_weight,
    recur_gate,
    input_gate,
    recur_bias,
    input_bias,
    decay_rate,
    output_weight,
    second_gain,
    gate_weight,
    up_weight,
    down_weight,
    cotangent,
):
    shards = lax.axis_size("wt")
    places = lax.axis_size("seq")
    me_w = lax.axis_index("wt")
    me_s = lax.axis_index("seq")
    part_len, model = inputs.shape[1:]
    lru = conv_weight.shape[0]
    taps = conv_weight.shape[1]
    width = lru // shards
    head = recur_gate.shape[1]
    edge = width % head
    rows = shards * part_len

    def mine(vector):
        return lax.dynamic_slice_in_dim(vector, me_w * width, width, 0)

    x = inputs[0]
    slope = cotangent[0]
    xn, u3, y, docs = enter(shards, x, mixer_gain[None], segment, input_weight, branch_weight)
    rate = mine(decay_rate)
    soft = -8.0 * jax.nn.softplus(rate)
    conv_mine = mine(conv_weight)
    rows8 = jnp.concatenate(
        [conv_mine.T, jnp.stack([mine(recur_bias), mine(input_bias), soft, rate])], axis=0
    )
    y = y.reshape(u3.shape)
    o, c_ext, r, ii, h, ends, halo, mask, near = mid(
        shards, places, taps, u3, y, docs, rows8, recur_gate, input_gate, slope
    )
    x1, xn2, dm = close(shards, o, x, second_gain[None], output_weight, near)
    dxn2, hidden, dg, dv, xn2, down_term = ffn(
        shards, places, xn2, dm, gate_weight, up_weight, down_weight
    )
    part = model // (places * shards)
    bits = (places // 2 - 1).bit_length()
    cut = (2,) * bits + (shards, part, -1)
    dx1, dz, do, second_gain_grad, block_out, down_kept, gate_term, up_term = back_in(
        shards,
        places,
        dxn2,
        x1,
        slope,
        second_gain[None],
        down_term.reshape(cut),
        output_weight,
        down_weight,
        hidden,
        xn2,
        dg,
        dv,
    )
    du, dy, small, down_grad, gate_kept = turn_back(
        shards,
        places,
        taps,
        do,
        y,
        r,
        ii,
        h,
        ends,
        c_ext,
        u3,
        halo,
        mask,
        rows8,
        recur_gate,
        input_gate,
        down_kept,
        gate_term.reshape(cut),
    )
    input_grad, mixer_gain_grad, mix_term, small, up_kept = leave(
        shards,
        places,
        du,
        dy,
        o,
        x,
        dx1,
        mixer_gain[None],
        xn,
        dz,
        input_weight,
        branch_weight,
        up_term.reshape(cut),
        small.reshape(places, -1, small.shape[1]),
    )
    gains = jnp.concatenate(
        [mixer_gain_grad, second_gain_grad, jnp.zeros((6, model), FULL)], axis=0
    )
    gate_grad, up_grad, out_grad, branch_grad, input_weight_grad, gains = settle(
        shards,
        places,
        gate_kept,
        up_kept,
        mix_term.reshape(cut),
        gains,
    )
    gains = lax.dynamic_slice_in_dim(gains, (me_s * shards + me_w) * part, part, 1)

    moves = [
        (s * shards + w, w * places + s) for s in range(places) for w in range(shards)
    ]
    small = lax.ppermute(small, ("seq", "wt"), moves)
    at = 2 * head + taps
    return (
        block_out[None],
        input_grad[None],
        gains[0],
        input_weight_grad,
        branch_grad,
        small[:, 2 * head : at],
        small[:, :head],
        small[:, head : 2 * head],
        small[:, at],
        small[:, at + 1],
        small[:, at + 2],
        out_grad,
        gains[1],
        gate_grad,
        up_grad,
        down_grad,
    )


def solution(mesh):
    tokens = P("wt", "seq", None)
    columns = P(None, "wt")
    row = P(("seq", "wt"))
    flat_rows = P(("seq", "wt"), None)
    return jax.shard_map(
        on_device,
        mesh=mesh,
        in_specs=(
            tokens,
            P("wt", "seq"),
            P(),
            columns,
            columns,
            P(),
            P(),
            P(),
            P(),
            P(),
            P(),
            columns,
            P(),
            columns,
            columns,
            columns,
            tokens,
        ),
        out_specs=(
            tokens,
            tokens,
            row,
            flat_rows,
            flat_rows,
            flat_rows,
            flat_rows,
            flat_rows,
            row,
            row,
            row,
            flat_rows,
            row,
            flat_rows,
            flat_rows,
            flat_rows,
        ),
        check_vma=False,
    )
```

```python
import functools
import math

import jax
import jax.numpy as jnp
from jax import lax
from jax.experimental import pallas as pl
from jax.experimental.pallas import tpu as pltpu
from jax.sharding import PartitionSpec as P

EPSILON = 1e-06
LOW = jnp.bfloat16
FULL = jnp.float32


def dot(left, right, left_dim=1, right_dim=0):
    return lax.dot_general(
        left, right, (((left_dim,), (right_dim,)), ((), ())), preferred_element_type=FULL
    )


def gelu_both(values):
    slope = jnp.sqrt(2.0 / jnp.pi).astype(FULL)
    inner = jnp.tanh(slope * (values + 0.044715 * values * values * values))
    gelu = 0.5 * values * (1.0 + inner)
    grad = 0.5 * (1.0 + inner) + 0.5 * values * (1.0 - inner * inner) * slope * (
        1.0 + 3.0 * 0.044715 * values * values
    )
    return gelu, grad


def scan_rows(coef, value, reverse):
    rows = coef.shape[0]
    place = lax.broadcasted_iota(jnp.int32, coef.shape, 0)
    step = 1
    while step < rows:
        if reverse:
            inside = place < rows - step
            by = rows - step
        else:
            inside = place >= step
            by = step
        far_coef = jnp.where(inside, pltpu.roll(coef, by, 0), 1.0)
        far_value = jnp.where(inside, pltpu.roll(value, by, 0), 0.0)
        value = coef * far_value + value
        coef = coef * far_coef
        step *= 2
    return coef, value


def expm1_small(values):
    return values * (
        1.0 + values * (0.5 + values * (1.0 / 6.0 + values * (1.0 / 24.0 + values / 120.0)))
    )


MESH = pl.DeviceIdType.MESH


def remote(source, target, sent, landed, to):
    return pltpu.make_async_remote_copy(
        src_ref=source,
        dst_ref=target,
        send_sem=sent,
        recv_sem=landed,
        device_id={"wt": to},
        device_id_type=MESH,
    )


def greet(n, me, pair=False, bits=0, places=0):
    barrier = pltpu.get_barrier_semaphore()

    @pl.when(me > 0)
    def _():
        pl.semaphore_signal(barrier, 1, device_id={"wt": me - 1}, device_id_type=MESH)

    @pl.when(me < n - 1)
    def _():
        pl.semaphore_signal(barrier, 1, device_id={"wt": me + 1}, device_id_type=MESH)

    peers = (me > 0).astype(jnp.int32) + (me < n - 1).astype(jnp.int32)
    place = lax.axis_index("seq")
    if places:
        peers = peers + places - 1
        for by in range(1, places):
            other = {"seq": lax.rem(place + by, places)}
            pl.semaphore_signal(barrier, 1, device_id=other, device_id_type=MESH)
    if pair:
        other = {"seq": place + 1 - 2 * lax.rem(place, 2)}
        pl.semaphore_signal(barrier, 1, device_id=other, device_id_type=MESH)
        peers = peers + 1 + bits
        for k in range(1, bits + 1):
            step = 1 << k
            other = {"seq": place + step * (1 - 2 * lax.rem(place // step, 2))}
            pl.semaphore_signal(barrier, 1, device_id=other, device_id_type=MESH)
    pl.semaphore_wait(barrier, peers)


def greet_all(n, me, places, more, away):
    barrier = pltpu.get_barrier_semaphore()
    seat = lax.axis_index("seq")
    for by in range(1, n):
        other = {"wt": lax.rem(me + by, n)}
        pl.semaphore_signal(barrier, 1, device_id=other, device_id_type=MESH)
    for by in range(1, places):
        other = {"seq": lax.rem(seat + by, places)}
        pl.semaphore_signal(barrier, 1, device_id=other, device_id_type=MESH)

    @pl.when(away)
    def _():
        for other in more:
            pl.semaphore_signal(barrier, 1, device_id=other, device_id_type=MESH)

    peers = n + places - 2 + len(more) * away.astype(jnp.int32)
    pl.semaphore_wait(barrier, peers)


class LineGather:
    def __init__(self, n, me, blocks, sent, landed):
        self.n, self.me, self.blocks, self.sent, self.landed = n, me, blocks, sent, landed

    def rightward(self, d):
        block = self.blocks.at[self.me - d]
        return remote(block, block, self.sent.at[0, d], self.landed.at[0, d + 1], self.me + 1)

    def leftward(self, d):
        block = self.blocks.at[self.me + d]
        return remote(block, block, self.sent.at[1, d], self.landed.at[1, d + 1], self.me - 1)

    def start(self):
        @pl.when(self.me < self.n - 1)
        def _():
            self.rightward(0).start()

        @pl.when(self.me > 0)
        def _():
            self.leftward(0).start()

    def arrive(self, d):
        n, me = self.n, self.me

        @pl.when(me - d >= 0)
        def _():
            block = self.blocks.at[me - d]
            remote(block, block, self.sent.at[0, 0], self.landed.at[0, d], me).wait_recv()

            @pl.when(me < n - 1)
            def _():
                self.rightward(d).start()

        @pl.when(me + d < n)
        def _():
            block = self.blocks.at[me + d]
            remote(block, block, self.sent.at[1, 0], self.landed.at[1, d], me).wait_recv()

            @pl.when(me > 0)
            def _():
                self.leftward(d).start()

    def each(self, d, use):
        def side(k, carry):
            q = self.me + (2 * k - 1) * d

            @pl.when((q >= 0) & (q < self.n))
            def _():
                use(q)

            return carry

        lax.fori_loop(0, 2, side, 0)

    def finish(self):
        n, me = self.n, self.me
        for d in range(n - 1):

            @pl.when((me - d >= 0) & (me < n - 1))
            def _():
                self.rightward(d).wait_send()

            @pl.when((me + d < n) & (me > 0))
            def _():
                self.leftward(d).wait_send()


def line_gather(n, me, blocks, sent, landed, use, ready):
    line = LineGather(n, me, blocks, sent, landed)
    line.start()
    ready()
    use(me)

    def step(d, carry):
        line.arrive(d)
        line.each(d, use)
        return carry

    lax.fori_loop(1, n, step, 0)
    line.finish()


class LineReduce:
    def __init__(self, n, me, parts, slots, sent, landed):
        self.n, self.me, self.parts, self.slots = n, me, parts, slots
        self.sent, self.landed = sent, landed

    def rightward(self, k):
        source, target = self.parts.at[self.n - 1 - k], self.slots.at[0, k]
        return remote(source, target, self.sent.at[0, k], self.landed.at[0, k], self.me + 1)

    def leftward(self, k):
        source, target = self.parts.at[k], self.slots.at[1, k]
        return remote(source, target, self.sent.at[1, k], self.landed.at[1, k], self.me - 1)

    def arrived(self, side, k):
        slot = self.slots.at[side, k]
        remote(slot, slot, self.sent.at[side, k], self.landed.at[side, k], self.me).wait_recv()

    def add(self, q, side, k):
        total = self.parts[q].astype(FULL) + self.slots[side, k].astype(FULL)
        self.parts[q] = total.astype(LOW)

    def prepare(self, k, partial):
        def side(which, carry):
            q = jnp.where(which == 0, self.n - 1 - k, k)

            @pl.when(jnp.where(which == 0, q > self.me, q < self.me))
            def _():
                partial(q)

            return carry

        lax.fori_loop(0, 2, side, 0)

    def step(self, t):
        n = self.n
        for side in range(2):
            place = self.me if side == 0 else n - 1 - self.me
            k = t - place
            pull = self.rightward if side == 0 else self.leftward

            @pl.when((k >= 0) & (t <= n - 2))
            def _():
                @pl.when(place > 0)
                def _():
                    self.arrived(side, k)
                    self.add(n - 1 - k if side == 0 else k, side, k)

                @pl.when(k > 0)
                def _():
                    pull(k - 1).wait_send()

                pull(k).start()

    def total(self):
        n, me = self.n, self.me

        @pl.when(me > 0)
        def _():
            self.arrived(0, n - 1 - me)

        @pl.when(me < n - 1)
        def _():
            self.arrived(1, me)

        total = self.parts[me].astype(FULL)
        other = self.slots[0, jnp.clip(n - 1 - me, 0, n - 2)].astype(FULL)
        total = total + jnp.where(me > 0, other, 0.0)
        other = self.slots[1, jnp.clip(me, 0, n - 2)].astype(FULL)
        return total + jnp.where(me < n - 1, other, 0.0)

    def finish(self):
        @pl.when(self.me < self.n - 1)
        def _():
            self.rightward(self.n - 2 - self.me).wait_send()

        @pl.when(self.me > 0)
        def _():
            self.leftward(self.me - 1).wait_send()


class LineBoth:
    def __init__(self, gather, back, skip=0):
        self.gather, self.back, self.skip = gather, back, skip
        self.n, self.me = gather.n, gather.me

    def sends(self, side, t, act):
        n, me = self.n, self.me
        place = me if side == 0 else n - 1 - me
        spread = self.gather.rightward if side == 0 else self.gather.leftward
        pull = self.back.rightward if side == 0 else self.back.leftward
        d = t + self.skip

        @pl.when(place < n - 1)
        def _():
            @pl.when(d <= place)
            def _():
                act(spread(d))

            @pl.when(d > place)
            def _():
                act(pull(d - place - 1))

    def step(self, t):
        n, me = self.n, self.me
        d = t + self.skip
        for side in range(2):
            place = me if side == 0 else n - 1 - me
            if t > 0:

                @pl.when(d <= place)
                def _():
                    block = self.gather.blocks.at[me - d if side == 0 else me + d]
                    remote(
                        block, block, self.gather.sent.at[side, 0], self.gather.landed.at[side, d], me
                    ).wait_recv()

                @pl.when((d > place) & (place > 0))
                def _():
                    k = d - place - 1
                    self.back.arrived(side, k)
                    self.back.add(n - 1 - k if side == 0 else k, side, k)

                self.sends(side, t - 1, lambda copy: copy.wait_send())
            self.sends(side, t, lambda copy: copy.start())

    def finish(self):
        for side in range(2):
            self.sends(side, self.n - 1 - self.skip, lambda copy: copy.wait_send())


def line_reduce(n, me, parts, slots, sent, landed, partial, work, finish, early=None):
    line = LineReduce(n, me, parts, slots, sent, landed)
    line.prepare(0, partial)
    line.step(0)
    if early is not None:
        early()
    for k in range(1, n - 1):
        line.prepare(k, partial)
    line.step(1)
    partial(me)
    share = -(-len(work) // (n - 2))
    for t in range(2, n):
        for task in work[(t - 2) * share : (t - 1) * share]:
            task()
        if t < n - 1:
            line.step(t)
    finish(line.total())
    line.finish()


def tiles(count, size, body):
    def step(t, carry):
        body(pl.ds(pl.multiple_of(t * size, size), size))
        return carry

    lax.fori_loop(0, count // size, step, 0)


def tile_of(width, limit):
    size = limit
    while width % size:
        size -= 128
    return size


VMEM = pl.BlockSpec(memory_space=pltpu.VMEM)
ANY = pl.BlockSpec(memory_space=pl.ANY)


def gather_sems(n):
    return [pltpu.SemaphoreType.DMA((2, n)), pltpu.SemaphoreType.DMA((2, n + 1))]


def reduce_sems(n):
    return [pltpu.SemaphoreType.DMA((2, n)), pltpu.SemaphoreType.DMA((2, n))]


def lasting(micros):
    return pl.CostEstimate(
        flops=int(micros * 1.0e9), bytes_accessed=int(micros * 3.4e6), transcendentals=0
    )


def comm_params(number):
    return pltpu.CompilerParams(
        collective_id=number, has_side_effects=True, vmem_limit_bytes=64 * 1024 * 1024
    )


class PairSum:
    def __init__(self, part, halves, landing, sent, landed, free, flush):
        self.me = lax.axis_index("seq")
        self.mine = lax.rem(self.me, 2)
        self.part, self.halves, self.landing = part, halves, landing
        self.sent, self.landed, self.free, self.flush = sent, landed, free, flush
        self.count = 0
        self.pending = None

    def other(self):
        return {"seq": self.me + 1 - 2 * self.mine}

    def send(self, slot):
        return pltpu.make_async_remote_copy(
            src_ref=self.halves.at[slot, 1 - self.mine],
            dst_ref=self.landing.at[slot],
            send_sem=self.sent.at[slot],
            recv_sem=self.landed.at[slot],
            device_id=self.other(),
            device_id_type=MESH,
        )

    def out(self, slot, t, target):
        half = self.landing.shape[1]
        return pltpu.make_async_copy(
            self.halves.at[slot, self.mine],
            target.at[pl.ds(t * half, half), :],
            self.flush.at[slot],
        )

    def tasks(self, steps, compute, target):
        return [functools.partial(self.run, t, compute, target) for t in range(steps)]

    def run(self, t, compute, target):
        slot = self.count % 2
        if self.count >= 2:
            self.send(slot).wait_send()
            self.out(slot, 0, target).wait()
            pl.semaphore_wait(self.free, 1)
        compute(t, self.halves.at[slot])
        self.send(slot).start()
        self.settle()
        self.pending = (slot, t, target)
        self.count += 1

    def settle(self):
        if self.pending is None:
            return
        slot, t, target = self.pending
        self.send(slot).wait_recv()
        total = self.halves[slot, self.mine].astype(FULL) + self.landing[slot].astype(FULL)
        self.halves[slot, self.mine] = total.astype(LOW)
        pl.semaphore_signal(self.free, 1, device_id=self.other(), device_id_type=MESH)
        self.out(slot, t, target).start()
        self.pending = None

    def finish(self, target):
        self.settle()
        for slot in range(2):
            self.send(slot).wait_send()
            self.out(slot, 0, target).wait()
        pl.semaphore_wait(self.free, 2)


def pair_scratch(half, width):
    return [
        pltpu.VMEM((2, 2, half, width), LOW),
        pltpu.VMEM((2, half, width), LOW),
        pltpu.SemaphoreType.DMA((2,)),
        pltpu.SemaphoreType.DMA((2,)),
        pltpu.SemaphoreType.REGULAR,
        pltpu.SemaphoreType.DMA((2,)),
    ]


def pair_tile(model, places):
    size = 2 * model // places
    return size if size % 128 == 0 else size * 128 // math.gcd(size, 128)


def pair_dot(left, right, part, size):
    n, rows, _ = left.shape

    def compute(t, halves):
        lhs = left[:, :, pl.ds(t * size, size)].reshape(n * rows, size)
        width = right.shape[2]

        def tile(at):
            rhs = right[:, :, at].reshape(n * rows, -1)
            value = dot(lhs, rhs, 0, 0).astype(LOW)
            for k in range(size // (2 * part)):
                for side in range(2):
                    first = (2 * k + side) * part
                    halves[side, k * part : (k + 1) * part, at] = value[first : first + part]

        tiles(width, tile_of(width, 640), tile)

    return compute


def column_halves(width):
    first = -(-width // 256) * 128
    return [(0, first), (first, width - first)]


class PlaneReduce:
    def __init__(self, blocks, landings, sent, landed, tail=3):
        self.blocks, self.landings, self.sent, self.landed = blocks, landings, sent, landed
        self.bits = len(blocks.shape) - tail
        self.tail = tail
        self.me = lax.axis_index("seq")
        self.columns = column_halves(blocks.shape[-1])

    def bit(self, dim):
        return 1 << (self.bits - dim)

    def mine(self, dim):
        return lax.rem(self.me // self.bit(dim), 2)

    def order(self, side):
        dims = list(range(self.bits))
        return dims[::-1] if side == 0 else dims

    def peer(self, dim):
        return {"seq": self.me + self.bit(dim) * (1 - 2 * self.mine(dim))}

    def index(self, side, step, own):
        order = self.order(side)
        place = [slice(None)] * self.bits
        for dim in order[:step]:
            place[dim] = self.mine(dim)
        now = order[step]
        place[now] = self.mine(now) if own else 1 - self.mine(now)
        return tuple(place) + (slice(None),) * (self.tail - 1) + (pl.ds(*self.columns[side]),)

    def send(self, side, step, piece=0):
        at, landing = self.index(side, step, False), self.landings[2 * step + side]
        if step == 0:
            count = self.blocks.shape[self.bits]
            first = count // 2 if self.tail == 3 else count // 32 * 16
            rows = pl.ds(piece * first, count - first if piece else first)
            at = at[: self.bits] + (rows,) + at[self.bits + 1 :]
            landing = landing.at[(slice(None),) * (self.bits - 1) + (rows,)]
        return pltpu.make_async_remote_copy(
            src_ref=self.blocks.at[at],
            dst_ref=landing,
            send_sem=self.sent.at[side, step + piece * self.bits],
            recv_sem=self.landed.at[side, step + piece * self.bits],
            device_id=self.peer(self.order(side)[step]),
            device_id_type=MESH,
        )

    def pieces(self, step):
        return (0, 1) if step == 0 else (0,)

    def begin(self, pieces=(0, 1)):
        for piece in pieces:
            for side in range(2):
                self.send(side, 0, piece).start()

    def advance(self, step):
        for side in range(2):
            for piece in self.pieces(step):
                self.send(side, step, piece).wait_recv()
            at = self.index(side, step, True)
            total = self.blocks[at].astype(FULL) + self.landings[2 * step + side][...].astype(FULL)
            self.blocks[at] = total.astype(LOW)
            if step + 1 < self.bits:
                self.send(side, step + 1).start()

    def kept(self):
        return self.blocks.at[tuple(self.mine(dim) for dim in range(self.bits))]

    def finish(self):
        for step in range(self.bits):
            for side in range(2):
                for piece in self.pieces(step):
                    self.send(side, step, piece).wait_send()


def plane_scratch(shape, tail=3):
    bits = len(shape) - tail
    landings = []
    for step in range(bits):
        for _, width in column_halves(shape[-1]):
            rest = [2] * (bits - 1 - step) + list(shape[bits:-1]) + [width]
            landings.append(pltpu.VMEM(tuple(rest), LOW))
    return landings


def ffn_kernel(
    n,
    places,
    xn2_ref,
    dm_hbm,
    wg_hbm,
    wu_hbm,
    wd_hbm,
    dxn2_ref,
    hidden_hbm,
    dg_hbm,
    dv_hbm,
    xall_hbm,
    down_hbm,
    xall,
    dm,
    wg,
    wu,
    wd,
    hidden,
    dg,
    dv,
    parts,
    slots,
    halves,
    landing,
    psent,
    planded,
    free,
    pflush,
    gsent,
    glanded,
    rsent,
    rlanded,
    local,
    flush,
):
    me = lax.axis_index("wt")
    rows, model = xn2_ref.shape
    units = wg.shape[1]
    cut = tile_of(units, 640)
    span = tile_of(model, 512)
    loads = [
        pltpu.make_async_copy(source, target, local.at[k])
        for k, (source, target) in enumerate(
            [(dm_hbm, dm), (wd_hbm, wd), (wg_hbm, wg), (wu_hbm, wu)]
        )
    ]
    for load in loads:
        load.start()
    xall[me] = xn2_ref[...]
    greet(n, me, True)

    def ready():
        for load in loads[:2]:
            load.wait()

        def tile(at):
            value = dot(dm[...].reshape(n * rows, model), wd[:, at])
            dg[:, :, at] = value.reshape(n, rows, -1).astype(LOW)

        tiles(units, cut, tile)
        for load in loads[2:]:
            load.wait()

    def use(q):
        def tile(at):
            block = xall[q]
            g = dot(block, wg[:, at])
            v = dot(block, wu[:, at])
            slopes = dg[q, :, at].astype(FULL)
            gelu, slope = gelu_both(g)
            hidden[q, :, at] = (gelu * v).astype(LOW)
            dg[q, :, at] = (slopes * v * slope).astype(LOW)
            dv[q, :, at] = (slopes * gelu).astype(LOW)

        tiles(units, cut, tile)

    line_gather(n, me, xall, gsent, glanded, use, ready)
    outs = [
        pltpu.make_async_copy(source, target, flush.at[k])
        for k, (source, target) in enumerate(
            [(hidden, hidden_hbm), (dg, dg_hbm), (dv, dv_hbm), (xall, xall_hbm)]
        )
    ]
    for out in outs:
        out.start()

    def partial(q):
        def tile(at):
            total = dot(dg[q], wg[at, :], 1, 1) + dot(dv[q], wu[at, :], 1, 1)
            parts[q, :, at] = total.astype(LOW)

        tiles(model, span, tile)

    part = model // places
    size = pair_tile(model, places)
    pair = PairSum(part, halves, landing, psent, planded, free, pflush)

    work = pair.tasks(model // size, pair_dot(dm, hidden, part, size), down_hbm)

    def finish(total):
        dxn2_ref[...] = total

    line_reduce(n, me, parts, slots, rsent, rlanded, partial, work, finish)
    pair.finish(down_hbm)
    for out in outs:
        out.wait()


def ffn(n, places, xn2, dm, wg, wu, wd):
    rows, model = xn2.shape
    units = wg.shape[1]
    grad = jax.ShapeDtypeStruct((model // 2, units), LOW)
    return pl.pallas_call(
        functools.partial(ffn_kernel, n, places),
        out_shape=[
            jax.ShapeDtypeStruct((rows, model), FULL),
            jax.ShapeDtypeStruct((n, rows, units), LOW),
            jax.ShapeDtypeStruct((n, rows, units), LOW),
            jax.ShapeDtypeStruct((n, rows, units), LOW),
            jax.ShapeDtypeStruct((n, rows, model), LOW),
            grad,
        ],
        in_specs=[VMEM, ANY, ANY, ANY, ANY],
        out_specs=[VMEM, ANY, ANY, ANY, ANY, ANY],
        scratch_shapes=[
            pltpu.VMEM((n, rows, model), LOW),
            pltpu.VMEM((n, rows, model), LOW),
            pltpu.VMEM((model, units), LOW),
            pltpu.VMEM((model, units), LOW),
            pltpu.VMEM((model, units), LOW),
            pltpu.VMEM((n, rows, units), LOW),
            pltpu.VMEM((n, rows, units), LOW),
            pltpu.VMEM((n, rows, units), LOW),
            pltpu.VMEM((n, rows, model), LOW),
            pltpu.VMEM((2, n - 1, rows, model), LOW),
        ]
        + pair_scratch(pair_tile(model, places) // 2, units)
        + gather_sems(n)
        + reduce_sems(n)
        + [pltpu.SemaphoreType.DMA((4,)), pltpu.SemaphoreType.DMA((4,))],
        compiler_params=comm_params(2),
        cost_estimate=lasting(105),
    )(xn2, dm, wg, wu, wd)


def back_in_kernel(n, places, bits, *refs):
    dxn2_ref, x1_ref, slope_ref, gain_ref, *sources = refs[:11]
    dx1_ref, dz_ref, do_ref, sum_ref, out_ref, kept_ref, gate_hbm, up_hbm = refs[11:19]
    w, hidden, wd, xall, dg, dv, blocks = refs[19:26]
    landings = refs[26 : 26 + 2 * bits]
    parts, slots, *sems = refs[26 + 2 * bits :]
    halves, landing, psent, planded, free, pflush, sent, landed, rsent, rlanded, bsent, blanded, local = sems
    me = lax.axis_index("wt")
    loads = [
        pltpu.make_async_copy(source, target, local.at[k])
        for k, (source, target) in enumerate(
            zip(sources, [blocks, w, wd, hidden, xall, dg, dv])
        )
    ]
    for load in loads:
        load.start()
    x1 = x1_ref[...]
    dxn2 = dxn2_ref[...]
    model = x1.shape[1]
    scale = lax.rsqrt(jnp.mean(x1 * x1, axis=-1, keepdims=True) + EPSILON)
    q2 = dxn2 * gain_ref[...]
    pull = jnp.mean(q2 * x1, axis=-1, keepdims=True)
    dx1 = slope_ref[...] + scale * (q2 - x1 * (scale * scale * pull))
    dx1_ref[...] = dx1
    dz_ref[me] = dx1.astype(LOW)
    greet(n, me, True, bits)
    line = LineGather(n, me, dz_ref, sent, landed)
    back = LineReduce(n, me, parts, slots, rsent, rlanded)
    both = LineBoth(line, back)
    both.step(0)
    loads[0].wait()
    plane = PlaneReduce(blocks, landings, bsent, blanded)
    plane.begin()
    sum_ref[...] = jnp.sum(dxn2 * x1 * scale, axis=0, keepdims=True)

    def use(q):
        do_ref[q] = dot(dz_ref[q], w[...])

    def partial(q):
        def tile(at):
            parts[q, :, at] = dot(hidden[q], wd[at, :], 1, 1).astype(LOW)

        tiles(model, tile_of(model, 512), tile)

    part = model // places
    size = pair_tile(model, places)
    pair = PairSum(part, halves, landing, psent, planded, free, pflush)
    loads[1].wait()
    use(me)
    for load in loads[2:4]:
        load.wait()
    for k in range(n - 2):
        back.prepare(k, partial)
    work = pair.tasks(model // size, pair_dot(xall, dg, part, size), gate_hbm)
    work += pair.tasks(model // size, pair_dot(xall, dv, part, size), up_hbm)
    ends = [len(work) * max(4 * t - 1, 0) // (4 * (n - 1)) for t in range(n)]
    ends[-1] = len(work)
    for t in range(1, n):
        both.step(t)
        if t == 1:
            back.prepare(n - 2, partial)
        if t >= 2 and t - 2 < bits:
            plane.advance(t - 2)
        line.each(t, use)
        if t == 1:
            partial(me)
            for load in loads[4:]:
                load.wait()
        for task in work[ends[t - 1] : ends[t]]:
            task()
    for step in range(max(n - 2, 0), bits):
        plane.advance(step)
    out_ref[...] = (x1_ref[...] + back.total()).astype(LOW)
    kept_ref[...] = plane.kept()[...]
    pair.finish(up_hbm)
    both.finish()
    plane.finish()


def back_in(n, places, dxn2, x1, slope, gain, down, weight, wd, hidden, xall, dg, dv):
    rows, model = x1.shape
    bits = len(down.shape) - 3
    grad = jax.ShapeDtypeStruct((model // 2, wd.shape[1]), LOW)
    return pl.pallas_call(
        functools.partial(back_in_kernel, n, places, bits),
        out_shape=[
            jax.ShapeDtypeStruct((rows, model), FULL),
            jax.ShapeDtypeStruct((n, rows, model), LOW),
            jax.ShapeDtypeStruct((n, rows, weight.shape[1]), FULL),
            jax.ShapeDtypeStruct((1, model), FULL),
            jax.ShapeDtypeStruct((rows, model), LOW),
            jax.ShapeDtypeStruct(down.shape[bits:], LOW),
            grad,
            grad,
        ],
        in_specs=[VMEM] * 4 + [ANY] * 7,
        out_specs=[VMEM] * 6 + [ANY] * 2,
        scratch_shapes=[
            pltpu.VMEM(weight.shape, LOW),
            pltpu.VMEM(hidden.shape, LOW),
            pltpu.VMEM(wd.shape, LOW),
            pltpu.VMEM(xall.shape, LOW),
            pltpu.VMEM(dg.shape, LOW),
            pltpu.VMEM(dv.shape, LOW),
            pltpu.VMEM(down.shape, LOW),
        ]
        + plane_scratch(down.shape)
        + [
            pltpu.VMEM((n, rows, model), LOW),
            pltpu.VMEM((2, n - 1, rows, model), LOW),
        ]
        + pair_scratch(pair_tile(model, places) // 2, wd.shape[1])
        + gather_sems(n)
        + reduce_sems(n)
        + [
            pltpu.SemaphoreType.DMA((2, 2 * bits)),
            pltpu.SemaphoreType.DMA((2, 2 * bits)),
            pltpu.SemaphoreType.DMA((7,)),
        ],
        compiler_params=comm_params(3),
        cost_estimate=lasting(75),
    )(dxn2, x1, slope, gain, down, weight, wd, hidden, xall, dg, dv)


class PlaneShare:
    def __init__(self, places, source, lands, sent, landed):
        self.places, self.source, self.lands = places, source, lands
        self.sent, self.landed = sent, landed
        self.me = lax.axis_index("seq")

    def send(self, by):
        to = lax.rem(self.me + by, self.places)
        return pltpu.make_async_remote_copy(
            src_ref=self.source.at[to],
            dst_ref=self.lands.at[by],
            send_sem=self.sent.at[by],
            recv_sem=self.landed.at[by],
            device_id={"seq": to},
            device_id_type=MESH,
        )

    def start(self):
        self.lands[0] = self.source[self.me]
        for by in range(1, self.places):
            self.send(by).start()

    def finish(self, target):
        for by in range(1, self.places):
            self.send(by).wait_recv()
        target[...] = jnp.sum(self.lands[...].astype(FULL), axis=0)
        for by in range(1, self.places):
            self.send(by).wait_send()


class LineSpread:
    def __init__(self, n, me, source, lands, sent, landed):
        self.n, self.me, self.source, self.lands = n, me, source, lands
        self.sent, self.landed = sent, landed

    def send(self, by):
        to = lax.rem(self.me + by, self.n)
        return remote(
            self.source.at[to], self.lands.at[self.me], self.sent.at[by], self.landed.at[by], to
        )

    def start(self):
        for by in range(1, self.n):
            self.send(by).start()

    def take(self, put, own):
        put(self.me, own[...])
        for by in range(1, self.n):
            slot = lax.rem(self.me + self.n - by, self.n)
            land = self.lands.at[slot]
            remote(land, land, self.sent.at[by], self.landed.at[by], self.me).wait_recv()
            put(slot, land[...])

    def finish(self):
        for by in range(1, self.n):
            self.send(by).wait_send()


def leave_kernel(n, places, bits, *refs):
    du_ref, dy_ref, o_ref, x_ref, dx1_ref, gain_ref, second_ref, small_ref = refs[:8]
    xn_hbm, dz_hbm, win_hbm, wbr_hbm, up_hbm, gate_hbm = refs[8:14]
    grad_ref, total_ref, moved_ref, gate_ref, up_ref, out_ref, branch_ref, in_ref, mix_hbm = refs[14:23]
    xn, dz, win, wbr, parts, slots, blocks, kept, own, lands, notes, around, shares, passed = refs[23:37]
    landings = refs[37 : 37 + 2 * bits]
    others = refs[37 + 2 * bits : 37 + 4 * bits]
    sems = refs[37 + 4 * bits :]
    halves, landing, psent, planded, free, pflush, sent, landed, ssent, slanded = sems[:10]
    usent, ulanded, msent, mlanded, asent, alanded, gsent, glanded, hsent, hlanded, local, fill = sems[10:]
    me = lax.axis_index("wt")
    seat = lax.axis_index("seq")
    model, width = win.shape
    units = gate_hbm.shape[-1]
    part = kept.shape[1]
    rows = n * part

    def fills(source):
        copies = []
        for k in range(1 << bits):
            place = tuple((k >> (bits - 1 - dim)) & 1 for dim in range(bits))
            copies.append(
                pltpu.make_async_copy(
                    source.at[pl.ds(k * rows, rows), :], blocks.at[place], fill.at[k]
                )
            )
        return copies

    loads = [
        pltpu.make_async_copy(source, target, local.at[k])
        for k, (source, target) in enumerate(
            [(win_hbm, win), (wbr_hbm, wbr), (xn_hbm, xn), (dz_hbm, dz), (gate_hbm.at[me], own)]
        )
    ]
    for load in loads[:2] + fills(up_hbm) + loads[2:]:
        load.start()
    flat_to, flat_from = me * places + seat, seat * n + me
    goal = {"seq": flat_to // n, "wt": lax.rem(flat_to, n)}
    origin = {"seq": lax.rem(flat_from, places), "wt": flat_from // places}
    away = flat_to != flat_from
    greet_all(n, me, places, [goal, origin], away)
    small = PlaneShare(places, small_ref, shares, ssent, slanded)
    small.start()
    plane = PlaneReduce(blocks, landings, usent, ulanded, 2)
    for load in loads[:2]:
        load.wait()

    def partial(q):
        def tile(at):
            total = dot(du_ref[q], win[at, :], 1, 1) + dot(dy_ref[q], wbr[at, :], 1, 1)
            parts[q, :, at] = total.astype(LOW)

        tiles(model, tile_of(model, 512), tile)

    size = pair_tile(model, places)
    pair = PairSum(rows, halves, landing, psent, planded, free, pflush)

    def compute(t, target):
        for k, (left, right) in enumerate([(dz, o_ref), (xn, dy_ref), (xn, du_ref)]):
            columns = pl.ds(k * width, width)
            pair_dot(left, right, rows, size)(t, target.at[:, :, columns])

    def early():
        for copy in fills(up_hbm):
            copy.wait()
        plane.begin()
        for load in loads[2:]:
            load.wait()

    def finish(total):
        flat = x_ref[...].astype(FULL)
        scale = lax.rsqrt(jnp.mean(flat * flat, axis=-1, keepdims=True) + EPSILON)
        q1 = total * gain_ref[...]
        pull = jnp.mean(q1 * flat, axis=-1, keepdims=True)
        grad_ref[...] = dx1_ref[...] + scale * (q1 - flat * (scale * scale * pull))
        mine = jnp.sum(total * flat * scale, axis=0, keepdims=True)
        blank = jnp.zeros((notes.shape[1] - 2, model), FULL)
        notes[me] = jnp.concatenate([mine, second_ref[...], blank], axis=0)

    def keep(k, source):
        for q in range(n):
            kept[k * n + q] = source[q * part : (q + 1) * part, :]

    spreads = [
        LineSpread(n, me, source, lands.at[k], asent.at[k], alanded.at[k])
        for k, source in enumerate([gate_hbm, kept.at[pl.ds(0, n)], kept.at[pl.ds(n, n)]])
    ]
    work = pair.tasks(model // size, compute, mix_hbm)
    tasks = work[:-1] + [lambda: (work[-1](), plane.advance(0), spreads[0].start())]
    line_reduce(n, me, parts, slots, sent, landed, partial, tasks, finish, early)
    pair.finish(mix_hbm)

    def note(by):
        to = lax.rem(me + by, n)
        return remote(notes.at[me], notes.at[me], gsent.at[0, by], glanded.at[0, by], to)

    for by in range(1, n):
        note(by).start()
    for step in range(1, bits):
        plane.advance(step)
    keep(0, plane.kept())
    spreads[1].start()
    plane.finish()
    for copy in fills(mix_hbm):
        copy.start()
    for copy in fills(mix_hbm):
        copy.wait()
    mixing = PlaneReduce(blocks, others, msent, mlanded, 2)
    mixing.begin()
    small.finish(passed)
    move = pltpu.make_async_remote_copy(
        src_ref=passed,
        dst_ref=moved_ref,
        send_sem=hsent.at[0],
        recv_sem=hlanded.at[0],
        device_id=goal,
        device_id_type=MESH,
    )

    @pl.when(away)
    def _():
        move.start()

    @pl.when(jnp.logical_not(away))
    def _():
        moved_ref[...] = passed[...]

    for by in range(1, n):
        slot = notes.at[lax.rem(me + n - by, n)]
        remote(slot, slot, gsent.at[0, by], glanded.at[0, by], me).wait_recv()
    around[seat] = jnp.sum(notes[...], axis=0)

    def share(by):
        return pltpu.make_async_remote_copy(
            src_ref=around.at[seat],
            dst_ref=around.at[seat],
            send_sem=gsent.at[1, by],
            recv_sem=glanded.at[1, by],
            device_id={"seq": lax.rem(seat + by, places)},
            device_id_type=MESH,
        )

    for by in range(1, places):
        share(by).start()

    def put_into(target):
        def put(q, value):
            target[:, pl.ds(pl.multiple_of(q * units, 128), units)] = value

        return put

    spreads[0].take(put_into(gate_ref), own)
    for step in range(bits):
        mixing.advance(step)
    keep(1, mixing.kept())
    spreads[2].start()
    spreads[1].take(put_into(up_ref), kept.at[me])
    for by in range(1, places):
        slot = around.at[lax.rem(seat + places - by, places)]
        pltpu.make_async_remote_copy(
            src_ref=slot,
            dst_ref=slot,
            send_sem=gsent.at[1, by],
            recv_sem=glanded.at[1, by],
            device_id={"seq": seat},
            device_id_type=MESH,
        ).wait_recv()
    total_ref[...] = jnp.sum(around[...], axis=0)

    def put_mix(q, value):
        columns = pl.ds(pl.multiple_of(q * width, 128), width)
        for k, target in enumerate([out_ref, branch_ref, in_ref]):
            target[:, columns] = value[:, k * width : (k + 1) * width]

    spreads[2].take(put_mix, kept.at[n + me])
    mixing.finish()
    for spread in spreads:
        spread.finish()
    for by in range(1, n):
        note(by).wait_send()
    for by in range(1, places):
        share(by).wait_send()

    @pl.when(away)
    def _():
        move.wait()


def leave(n, places, du, dy, o, x, dx1, gain, second, small, xn, dz, win, wbr, up, gate):
    rows, model = x.shape
    width = win.shape[1]
    _, part, units = gate.shape
    bits = (model // 2 // (n * part)).bit_length() - 1
    blocks = (2,) * bits + (n * part, units)
    wide = jax.ShapeDtypeStruct((part, n * units), LOW)
    thin = jax.ShapeDtypeStruct((part, n * width), LOW)
    return pl.pallas_call(
        functools.partial(leave_kernel, n, places, bits),
        out_shape=[
            jax.ShapeDtypeStruct((rows, model), FULL),
            jax.ShapeDtypeStruct((8, model), FULL),
            jax.ShapeDtypeStruct(small.shape[1:], FULL),
            wide,
            wide,
            thin,
            thin,
            thin,
            jax.ShapeDtypeStruct(up.shape, LOW),
        ],
        in_specs=[VMEM] * 8 + [ANY] * 6,
        out_specs=[VMEM] * 8 + [ANY],
        scratch_shapes=[
            pltpu.VMEM((n, rows, model), LOW),
            pltpu.VMEM((n, rows, model), LOW),
            pltpu.VMEM(win.shape, LOW),
            pltpu.VMEM(wbr.shape, LOW),
            pltpu.VMEM((n, rows, model), LOW),
            pltpu.VMEM((2, n - 1, rows, model), LOW),
            pltpu.VMEM(blocks, LOW),
            pltpu.VMEM((2 * n, part, units), LOW),
            pltpu.VMEM((part, units), LOW),
            pltpu.VMEM((3, n, part, units), LOW),
            pltpu.VMEM((n, 8, model), FULL),
            pltpu.VMEM((places, 8, model), FULL),
            pltpu.VMEM(small.shape, LOW),
            pltpu.VMEM(small.shape[1:], FULL),
        ]
        + plane_scratch(blocks, 2)
        + plane_scratch(blocks, 2)
        + pair_scratch(pair_tile(model, places) // 2, 3 * width)
        + reduce_sems(n)
        + [
            pltpu.SemaphoreType.DMA((places,)),
            pltpu.SemaphoreType.DMA((places,)),
            pltpu.SemaphoreType.DMA((2, 2 * bits)),
            pltpu.SemaphoreType.DMA((2, 2 * bits)),
            pltpu.SemaphoreType.DMA((2, 2 * bits)),
            pltpu.SemaphoreType.DMA((2, 2 * bits)),
            pltpu.SemaphoreType.DMA((3, n)),
            pltpu.SemaphoreType.DMA((3, n)),
            pltpu.SemaphoreType.DMA((2, max(n, places))),
            pltpu.SemaphoreType.DMA((2, max(n, places))),
            pltpu.SemaphoreType.DMA((1,)),
            pltpu.SemaphoreType.DMA((1,)),
            pltpu.SemaphoreType.DMA((5,)),
            pltpu.SemaphoreType.DMA((1 << bits,)),
        ],
        compiler_params=comm_params(4),
        cost_estimate=lasting(140),
    )(du, dy, o, x, dx1, gain, second, small, xn, dz, win, wbr, up, gate)


def conv_masks(own, before, after, taps):
    lane = lax.broadcasted_iota(jnp.int32, own.shape, 1)
    lines = []
    for here, back in ((own, before), (after, own)):
        for k in range(taps):
            shifted = jnp.where(lane >= k, pltpu.roll(here, k, 1), pltpu.roll(back, k, 1))
            lines.append((shifted == here).astype(FULL)[:1] if k else jnp.ones_like(here)[:1])
    lines.append(jnp.zeros((own.shape[1] - 2 * taps, own.shape[1]), FULL))
    return jnp.concatenate(lines, axis=0).T


def pick_row(table, q):
    place = lax.broadcasted_iota(jnp.int32, table.shape, 0)
    return jnp.sum(jnp.where(place == q, table, 0.0), axis=0, keepdims=True)


def mult_of(log_a, keep):
    twice = 2.0 * log_a
    gap = jnp.where(twice > -0.01, -expm1_small(twice), 1.0 - jnp.exp(twice))
    return jnp.where(keep == 0.0, 1.0, jnp.sqrt(gap))


def enter_kernel(
    n, x_ref, gain_ref, doc_ref, win_hbm, wbr_hbm, xn_ref, u_ref, y_ref, docs_ref, win, wbr, docs, sent, landed, dsent, dlanded, local, places
):
    me = lax.axis_index("wt")
    loads = [
        pltpu.make_async_copy(win_hbm, win, local.at[0]),
        pltpu.make_async_copy(wbr_hbm, wbr, local.at[1]),
    ]
    for load in loads:
        load.start()
    docs[me] = jnp.broadcast_to(doc_ref[...], docs.shape[1:])
    flat = x_ref[...].astype(FULL)
    scale = lax.rsqrt(jnp.mean(flat * flat, axis=-1, keepdims=True) + EPSILON)
    xn_ref[me] = (flat * scale * gain_ref[...]).astype(LOW)
    greet(n, me, False, 0, places)
    notes = LineGather(n, me, docs, dsent, dlanded)
    line = LineGather(n, me, xn_ref, sent, landed)
    notes.start()
    line.start()
    for load in loads:
        load.wait()

    def use(q):
        block = xn_ref[q]
        u_ref[q] = dot(block, win[...]).astype(LOW)
        y_ref[q] = dot(block, wbr[...])

    use(me)

    def step(d, carry):
        notes.arrive(d)
        line.arrive(d)
        line.each(d, use)
        return carry

    lax.fori_loop(1, n, step, 0)
    docs_ref[...] = docs[...]
    notes.finish()
    line.finish()


def close_kernel(
    n, o_ref, x_ref, gain_ref, w_hbm, near_ref, x1_ref, xn2_ref, dm_ref, parts, slots, sent, landed, gsent, glanded, local, w_ref
):
    me = lax.axis_index("wt")
    model = w_ref.shape[0]

    def near(k, act):
        q = me + k - 1

        @pl.when((q >= 0) & (q < n))
        def _():
            act(pltpu.make_async_copy(near_ref.at[k], dm_ref.at[q], local.at[k]))

    for k in range(3):
        near(k, lambda copy: copy.start())

    def partial(q):
        block = o_ref[q]

        def tile(at):
            parts[q, :, at] = dot(block, w_ref[at, :], 1, 1).astype(LOW)

        tiles(model, tile_of(model, 512), tile)

    def finish(total):
        x1 = x_ref[...].astype(FULL) + total
        x1_ref[...] = x1
        scale = lax.rsqrt(jnp.mean(x1 * x1, axis=-1, keepdims=True) + EPSILON)
        xn2_ref[...] = (x1 * scale * gain_ref[...]).astype(LOW)

    back = LineReduce(n, me, parts, slots, sent, landed)
    both = LineBoth(LineGather(n, me, dm_ref, gsent, glanded), back, 1)
    for k in range(3):
        near(k, lambda copy: copy.wait())
    back.prepare(0, partial)
    both.step(0)
    for k in range(1, n - 1):
        back.prepare(k, partial)
    partial(me)
    for t in range(1, n - 1):
        both.step(t)
    finish(back.total())
    both.finish()


def mid_kernel(
    n,
    places,
    taps,
    u_ref,
    y_ref,
    docs_ref,
    rows_ref,
    gr_hbm,
    gi_hbm,
    slope_ref,
    o_ref,
    c_ref,
    r_ref,
    ii_ref,
    h_ref,
    edge_ref,
    halo_ref,
    mask_ref,
    near_ref,
    tr,
    ti,
    cum,
    carry,
    before,
    after,
    hsent,
    hlanded,
    esent,
    elanded,
    csent,
    clanded,
    nsent,
    nlanded,
    local,
):
    me = lax.axis_index("wt")
    seat = lax.axis_index("seq")
    part_len, width = u_ref.shape[1:]
    head = gr_hbm.shape[1]
    ext = tr.shape[0]
    edge = ext - width
    odd = lax.rem(me, 2)
    shift = odd * edge
    block = 128
    first = pl.multiple_of((me * width) // head * head, head)
    loads = [
        pltpu.make_async_copy(source.at[pl.ds(first, ext), :], target, local.at[k])
        for k, (source, target) in enumerate([(gr_hbm, tr), (gi_hbm, ti)])
    ]
    for load in loads:
        load.start()
    partner = {"wt": me + 1 - 2 * odd}
    near_ref[1] = slope_ref[...].astype(LOW)

    def neighbours(act, out):
        for k, (to, there) in enumerate([(me + 1, 0), (me - 1, 2)]):
            copy = remote(near_ref.at[1], near_ref.at[there], nsent.at[k], nlanded.at[k], to)
            inside = (to >= 0) & (to < n)
            gives = (me > 0) if k == 0 else (me < n - 1)

            @pl.when(inside if out else gives)
            def _():
                act(copy)


    def hop(source, target, k, to):
        return pltpu.make_async_remote_copy(
            src_ref=source,
            dst_ref=target,
            send_sem=hsent.at[k],
            recv_sem=hlanded.at[k],
            device_id={"seq": to},
            device_id_type=MESH,
        )

    reach = halo_ref.shape[1]
    tails = u_ref.at[:, pl.ds(part_len - reach, reach), :]
    onward = [hop(tails, halo_ref, 0, seat + 1), hop(docs_ref, before, 1, seat + 1)]
    backward = [hop(docs_ref, after, 2, seat - 1)]

    @pl.when(seat < places - 1)
    def _():
        for copy in onward:
            copy.start()

    @pl.when(seat > 0)
    def _():
        for copy in backward:
            copy.start()

    @pl.when(seat == 0)
    def _():
        halo_ref[...] = jnp.zeros_like(halo_ref)
        before[...] = jnp.full_like(before, -1)

    @pl.when(seat == places - 1)
    def _():
        after[...] = jnp.full_like(after, -1)

    @pl.when(seat > 0)
    def _():
        for copy in onward:
            copy.wait_recv()

    @pl.when(seat < places - 1)
    def _():
        for copy in backward:
            copy.wait_recv()

    def columns(b):
        return pl.ds(pl.multiple_of(b * block, block), block)

    def ext_columns(b):
        return pl.ds(pl.multiple_of(b * block + shift, block), block)

    def each(body):
        def outer(q, carried):
            def inner(b, deeper):
                body(q, b)
                return deeper

            return lax.fori_loop(0, width // block, inner, carried, unroll=True)

        lax.fori_loop(0, n, outer, 0)

    def masks(q, carried):
        mask_ref[q] = conv_masks(
            docs_ref[q].astype(FULL), before[q].astype(FULL), after[q].astype(FULL), taps
        )
        return carried

    lax.fori_loop(0, n, masks, 0)

    def conv(q, b):
        at = columns(b)
        long = jnp.concatenate([halo_ref[q, :, at], u_ref[q, :, at]], axis=0).astype(FULL)
        total = long[reach:] * rows_ref[0:1, at]
        for k in range(1, taps):
            window = pltpu.roll(long, k, 0)[reach:]
            total = total + window * mask_ref[q, :, k : k + 1] * rows_ref[k : k + 1, at]
        c_ref[q, :, ext_columns(b)] = total.astype(LOW)

    each(conv)
    source = pl.ds(pl.multiple_of(jnp.where(odd == 1, edge, width - edge), edge), edge)
    target = pl.ds(pl.multiple_of(jnp.where(odd == 1, width, 0), edge), edge)
    swap = pltpu.make_async_remote_copy(
        src_ref=c_ref.at[:, :, source],
        dst_ref=c_ref.at[:, :, target],
        send_sem=esent.at[0],
        recv_sem=elanded.at[0],
        device_id=partner,
        device_id_type=MESH,
    )
    swap.start()
    for load in loads:
        load.wait()
    swap.wait_recv()
    neighbours(lambda copy: copy.start(), True)
    per = head // block

    def gates(q, b):
        at = columns(b)
        j = b + shift // block
        spot = j // per
        within = pl.ds(pl.multiple_of(lax.rem(j, per) * block, block), block)
        rows = pl.ds(pl.multiple_of(spot * head, head), head)
        c_head = c_ref[q, :, rows]
        c_own = c_ref[q, :, ext_columns(b)].astype(FULL)
        r = jax.nn.sigmoid(dot(c_head, tr[rows, within]) + rows_ref[taps : taps + 1, at])
        ii = jax.nn.sigmoid(dot(c_head, ti[rows, within]) + rows_ref[taps + 1 : taps + 2, at])
        keep = mask_ref[q, :, 1:2]
        log_a = rows_ref[taps + 2 : taps + 3, at] * r
        mult = mult_of(log_a, keep)
        b_low = (mult * c_own * ii).astype(LOW).astype(FULL)
        a = jnp.exp(log_a.astype(LOW).astype(FULL)) * keep
        cum_a, h_loc = scan_rows(a, b_low, False)
        r_ref[q, :, at] = r
        ii_ref[q, :, at] = ii
        cum[q, :, at] = cum_a
        h_ref[q, :, at] = h_loc

    each(gates)
    for q in range(n):
        carry[seat, q : q + 1, :] = cum[q, part_len - 1 : part_len, :]
        carry[seat, n + q : n + q + 1, :] = h_ref[q, part_len - 1 : part_len, :]

    def share(by):
        return pltpu.make_async_remote_copy(
            src_ref=carry.at[seat],
            dst_ref=carry.at[seat],
            send_sem=csent.at[by],
            recv_sem=clanded.at[by],
            device_id={"seq": lax.rem(seat + by, places)},
            device_id_type=MESH,
        )

    for by in range(1, places):
        share(by).start()
    for by in range(1, places):
        share(by).wait_recv()
    state = jnp.zeros((n, width), FULL)
    start = state
    for p in range(places):
        start = jnp.where(seat == p, state, start)
        state = carry[p, :n, :] * state + carry[p, n:, :]
    edge_ref[:n, :] = start
    edge_ref[n:, :] = carry[seat, :n, :]

    def finish(q, b):
        at = columns(b)
        h = h_ref[q, :, at] + cum[q, :, at] * pick_row(edge_ref[:, at], q)
        h_ref[q, :, at] = h
        gelu, _ = gelu_both(y_ref[q, :, at])
        o_ref[q, :, at] = (h.astype(LOW).astype(FULL) * gelu).astype(LOW)

    each(finish)
    neighbours(lambda copy: copy.wait_recv(), False)
    neighbours(lambda copy: copy.wait_send(), True)
    swap.wait_send()

    @pl.when(seat < places - 1)
    def _():
        for copy in onward:
            copy.wait_send()

    @pl.when(seat > 0)
    def _():
        for copy in backward:
            copy.wait_send()

    for by in range(1, places):
        share(by).wait_send()


def head_kernel(n, places, taps, *refs):
    x, gain, doc, rows8, slope, second, win_hbm, wbr_hbm, gr_hbm, gi_hbm, w_hbm = refs[:11]
    xn, u, y, o, c, r, ii, h, edges, halo, mask, x1, xn2, dm = refs[11:25]
    win, wbr, docs, seen, near, tr, ti, cum, carry, before, after, parts, slots, w = refs[25:39]
    sems = refs[39:]
    load = pltpu.make_async_copy(w_hbm, w, sems[-1].at[0])
    load.start()
    enter_kernel(
        n, x, gain, doc, win_hbm, wbr_hbm, xn, u, y, seen, win, wbr, docs, *sems[:5], places
    )
    mid_kernel(
        n, places, taps, u, y, seen, rows8, gr_hbm, gi_hbm, slope, o, c, r, ii, h, edges, halo, mask, near,
        tr, ti, cum, carry, before, after, *sems[5:14]
    )
    load.wait()
    close_kernel(n, o, x, second, w_hbm, near, x1, xn2, dm, parts, slots, *sems[14:19], w)


def head_part(n, places, taps, x, gain, doc, rows8, slope, second, win, wbr, gate_r, gate_i, weight):
    rows, model = x.shape
    width = win.shape[1]
    head = gate_r.shape[1]
    ext = -(-width // head) * head
    full = jax.ShapeDtypeStruct((n, rows, width), FULL)
    low = jax.ShapeDtypeStruct((n, rows, width), LOW)
    long = jax.ShapeDtypeStruct((n, rows, model), LOW)
    docs = pltpu.VMEM((n, 8, rows), jnp.int32)
    pairs = [pltpu.SemaphoreType.DMA((count,)) for count in (3, 3, 1, 1, places, places, 2, 2, 2)]
    return pl.pallas_call(
        functools.partial(head_kernel, n, places, taps),
        out_shape=[
            long,
            low,
            full,
            low,
            jax.ShapeDtypeStruct((n, rows, ext), LOW),
            full,
            full,
            full,
            jax.ShapeDtypeStruct((2 * n, width), FULL),
            jax.ShapeDtypeStruct((n, 16, width), LOW),
            jax.ShapeDtypeStruct((n, rows, rows), FULL),
            jax.ShapeDtypeStruct((rows, model), FULL),
            jax.ShapeDtypeStruct((rows, model), LOW),
            long,
        ],
        in_specs=[VMEM] * 6 + [ANY] * 5,
        out_specs=[VMEM] * 14,
        scratch_shapes=[
            pltpu.VMEM(win.shape, LOW),
            pltpu.VMEM(wbr.shape, LOW),
            docs,
            docs,
            pltpu.VMEM((3, rows, model), LOW),
            pltpu.VMEM((ext, head), LOW),
            pltpu.VMEM((ext, head), LOW),
            pltpu.VMEM((n, rows, width), FULL),
            pltpu.VMEM((places, 2 * n, width), FULL),
            docs,
            docs,
            pltpu.VMEM((n, rows, model), LOW),
            pltpu.VMEM((2, n - 1, rows, model), LOW),
            pltpu.VMEM(weight.shape, LOW),
        ]
        + gather_sems(n)
        + gather_sems(n)
        + [pltpu.SemaphoreType.DMA((2,))]
        + pairs
        + reduce_sems(n)
        + gather_sems(n)
        + [pltpu.SemaphoreType.DMA((3,)), pltpu.SemaphoreType.DMA((1,))],
        compiler_params=comm_params(0),
        cost_estimate=lasting(135),
    )(x, gain, doc, rows8, slope, second, win, wbr, gate_r, gate_i, weight)


def turn_kernel(
    n,
    places,
    taps,
    bits,
    do_ref,
    y_ref,
    r_ref,
    ii_ref,
    h_ref,
    edge_ref,
    c_ref,
    u_ref,
    halo_ref,
    mask_ref,
    rows_ref,
    gr_hbm,
    gi_hbm,
    down_hbm,
    gate_hbm,
    du_ref,
    dy_ref,
    small_ref,
    down_ref,
    kept_ref,
    tr,
    ti,
    rem,
    e_ref,
    dra,
    dia,
    dc,
    lead,
    carry,
    ein,
    sums,
    lands,
    own,
    hsent,
    hlanded,
    esent,
    elanded,
    csent,
    clanded,
    ssent,
    slanded,
    local,
    psent,
    planded,
    blocks,
    *landings,
):
    me = lax.axis_index("wt")
    seat = lax.axis_index("seq")
    part_len, width = u_ref.shape[1:]
    head = gr_hbm.shape[1]
    ext = tr.shape[0]
    edge = ext - width
    odd = lax.rem(me, 2)
    shift = odd * edge
    block = 128
    per = head // block
    reach = halo_ref.shape[1]
    first = pl.multiple_of((me * width) // head * head, head)
    loads = [
        pltpu.make_async_copy(gr_hbm.at[pl.ds(first, ext), :], tr, local.at[0]),
        pltpu.make_async_copy(gi_hbm.at[pl.ds(first, ext), :], ti, local.at[1]),
        pltpu.make_async_copy(down_hbm.at[me], own, local.at[2]),
        pltpu.make_async_copy(gate_hbm, blocks, local.at[3]),
    ]
    for load in loads:
        load.start()
    barrier = pltpu.get_barrier_semaphore()
    for by in range(1, places):
        other = {"seq": lax.rem(seat + by, places)}
        pl.semaphore_signal(barrier, 1, device_id=other, device_id_type=MESH)
    for by in range(1, n):
        other = {"wt": lax.rem(me + by, n)}
        pl.semaphore_signal(barrier, 1, device_id=other, device_id_type=MESH)
    pl.semaphore_wait(barrier, places + n - 2)
    spread = LineSpread(n, me, down_hbm, lands, ssent, slanded)
    spread.start()
    loads[3].wait()
    plane = PlaneReduce(blocks, landings, psent, planded)
    plane.begin((0,))

    def columns(b):
        return pl.ds(pl.multiple_of(b * block, block), block)

    def ext_columns(b):
        return pl.ds(pl.multiple_of(b * block + shift, block), block)

    def head_columns(b):
        spot = (b + shift // block) // per
        return pl.ds(pl.multiple_of(spot * head, head), head)

    def each(body):
        def outer(q, carried):
            def inner(b, deeper):
                body(q, b)
                return deeper

            return lax.fori_loop(0, width // block, inner, carried, unroll=True)

        lax.fori_loop(0, n, outer, 0)

    def decay(q, at, rows=slice(None)):
        log_a = rows_ref[taps + 2 : taps + 3, at] * r_ref[q, rows, at]
        return jnp.exp(log_a.astype(LOW).astype(FULL)) * mask_ref[q, rows, 1:2]

    place = lax.broadcasted_iota(jnp.int32, (part_len, block), 0)

    def scans(q, b):
        at = columns(b)
        gelu, slope = gelu_both(y_ref[q, :, at])
        back = do_ref[q, :, at]
        hr = h_ref[q, :, at].astype(LOW).astype(FULL)
        dy_ref[q, :, at] = (back * hr * slope).astype(LOW)
        dh = (back * gelu).astype(LOW).astype(FULL)
        a_next = jnp.where(
            place < part_len - 1, pltpu.roll(decay(q, at), part_len - 1, 0), 1.0
        )
        far, e_loc = scan_rows(a_next, dh, True)
        rem[q, :, at] = far
        e_ref[q, :, at] = e_loc

    each(scans)
    carry[seat, :n, :] = edge_ref[n:, :]
    for q in range(n):
        top = decay(q, slice(None), slice(0, 1)) * e_ref[q, 0:1, :]
        carry[seat, n + q : n + q + 1, :] = top

    def share(by):
        return pltpu.make_async_remote_copy(
            src_ref=carry.at[seat],
            dst_ref=carry.at[seat],
            send_sem=csent.at[by],
            recv_sem=clanded.at[by],
            device_id={"seq": lax.rem(seat + by, places)},
            device_id_type=MESH,
        )

    for by in range(1, places):
        share(by).start()
    sums[...] = jnp.zeros_like(sums)
    for by in range(1, places):
        share(by).wait_recv()
    plane.begin((1,))
    state = jnp.zeros((n, width), FULL)
    start = state
    for p in reversed(range(places)):
        start = jnp.where(seat == p, state, start)
        state = carry[p, :n, :] * state + carry[p, n:, :]
    ein[:n, :] = start
    ein[n:, :] = jnp.zeros_like(start)

    def slopes(q, b):
        at = columns(b)
        e = e_ref[q, :, at] + rem[q, :, at] * pick_row(ein[:, at], q)
        h_prev = jnp.where(
            place == 0, pick_row(edge_ref[:, at], q), pltpu.roll(h_ref[q, :, at], 1, 0)
        )
        r = r_ref[q, :, at]
        ii = ii_ref[q, :, at]
        keep = mask_ref[q, :, 1:2]
        soft = rows_ref[taps + 2 : taps + 3, at]
        log_a = soft * r
        mult = mult_of(log_a, keep)
        c = c_ref[q, :, ext_columns(b)].astype(FULL)
        dla = (e * h_prev * decay(q, at)).astype(LOW).astype(FULL)
        dbr = e.astype(LOW).astype(FULL)
        dmult = jnp.where(keep == 0.0, 0.0, -jnp.exp(2.0 * log_a) / mult)
        dlog_a = dla + dbr * c * ii * dmult
        dra_f = soft * dlog_a * r * (1.0 - r)
        direct = dbr * mult * ii
        dia_f = direct * c * (1.0 - ii)
        dra[q, :, ext_columns(b)] = dra_f.astype(LOW)
        dia[q, :, ext_columns(b)] = dia_f.astype(LOW)
        dc[q, :, at] = direct
        for k, value in enumerate([dra_f, dia_f, -8.0 * dlog_a * r]):
            sums[taps + k : taps + k + 1, at] += jnp.sum(value, axis=0, keepdims=True)

    each(slopes)
    source = pl.ds(pl.multiple_of(jnp.where(odd == 1, edge, width - edge), edge), edge)
    target = pl.ds(pl.multiple_of(jnp.where(odd == 1, width, 0), edge), edge)
    swaps = [
        pltpu.make_async_remote_copy(
            src_ref=ref.at[:, :, source],
            dst_ref=ref.at[:, :, target],
            send_sem=esent.at[k],
            recv_sem=elanded.at[k],
            device_id={"wt": me + 1 - 2 * odd},
            device_id_type=MESH,
        )
        for k, ref in enumerate([dra, dia])
    ]
    for swap in swaps:
        swap.start()
    for load in loads[:3]:
        load.wait()
    for swap in swaps:
        swap.wait_recv()

    def mix(q, b):
        at = columns(b)
        rows = head_columns(b)
        table = ext_columns(b)
        dc[q, :, at] += dot(dra[q, :, rows], tr[table, :], 1, 1) + dot(
            dia[q, :, rows], ti[table, :], 1, 1
        )

    each(mix)
    leads = pltpu.make_async_remote_copy(
        src_ref=dc.at[:, pl.ds(0, lead.shape[1]), :],
        dst_ref=lead,
        send_sem=hsent.at[0],
        recv_sem=hlanded.at[0],
        device_id={"seq": seat - 1},
        device_id_type=MESH,
    )

    @pl.when(seat > 0)
    def _():
        leads.start()

    @pl.when(seat == places - 1)
    def _():
        lead[...] = jnp.zeros_like(lead)

    def gate_grads(b, carried):
        left = c_ref[:, :, ext_columns(b)].reshape(n * part_len, block)
        rows = head_columns(b)
        for k, ref in enumerate([dra, dia]):
            right = ref[:, :, rows].reshape(n * part_len, head)
            small_ref[columns(b), k * head : (k + 1) * head] = dot(left, right, 0, 0).astype(LOW)
        return carried

    lax.fori_loop(0, width // block, gate_grads, 0)

    @pl.when(seat < places - 1)
    def _():
        leads.wait_recv()

    plane.advance(0)

    def conv(q, b):
        at = columns(b)
        slope = dc[q, :, at]
        next_rows = lead[q, :, at]
        long = jnp.concatenate([slope, next_rows], axis=0)
        total = slope * rows_ref[0:1, at]
        behind = jnp.concatenate([halo_ref[q, :, at], u_ref[q, :, at]], axis=0).astype(FULL)
        sums[0:1, at] += jnp.sum(behind[reach:] * slope, axis=0, keepdims=True)
        for k in range(1, taps):
            same = mask_ref[q, :, k : k + 1]
            same_next = mask_ref[q, : lead.shape[1], taps + k : taps + k + 1]
            masked = long * jnp.concatenate([same, same_next], axis=0)
            shifted = pltpu.roll(masked, long.shape[0] - k, 0)[:part_len]
            total = total + shifted * rows_ref[k : k + 1, at]
            window = pltpu.roll(behind, k, 0)[reach:] * same
            sums[k : k + 1, at] += jnp.sum(window * slope, axis=0, keepdims=True)
        du_ref[q, :, at] = total.astype(LOW)

    each(conv)
    row = taps + 2
    sums[row : row + 1, :] = sums[row : row + 1, :] * jax.nn.sigmoid(rows_ref[taps + 3 : taps + 4, :])

    def turn(b, carried):
        wide = jnp.concatenate(
            [sums[:, columns(b)], jnp.zeros((block - sums.shape[0], block), FULL)], axis=0
        )
        small_ref[columns(b), 2 * head : 2 * head + block] = wide.T.astype(LOW)
        return carried

    lax.fori_loop(0, width // block, turn, 0)
    units = down_hbm.shape[-1]

    def put(q, value):
        down_ref[:, pl.ds(pl.multiple_of(q * units, 128), units)] = value

    spread.take(put, own)
    for step in range(1, bits):
        plane.advance(step)
    kept_ref[...] = plane.kept()[...]
    plane.finish()
    spread.finish()
    for swap in swaps:
        swap.wait_send()
    for by in range(1, places):
        share(by).wait_send()

    @pl.when(seat > 0)
    def _():
        leads.wait_send()


def turn_back(
    n, places, taps, do, y, r, ii, h, edges, c, u, halo, mask, rows8, gate_r, gate_i, down, gate
):
    _, rows, width = u.shape
    head = gate_r.shape[1]
    ext = c.shape[2]
    _, part, units = down.shape
    bits = len(gate.shape) - 3
    low = jax.ShapeDtypeStruct(u.shape, LOW)
    return pl.pallas_call(
        functools.partial(turn_kernel, n, places, taps, bits),
        out_shape=[
            low,
            low,
            jax.ShapeDtypeStruct((width, 2 * head + 128), LOW),
            jax.ShapeDtypeStruct((part, n * units), LOW),
            jax.ShapeDtypeStruct(gate.shape[bits:], LOW),
        ],
        in_specs=[VMEM] * 11 + [ANY] * 4,
        out_specs=[VMEM] * 5,
        scratch_shapes=[
            pltpu.VMEM((ext, head), LOW),
            pltpu.VMEM((ext, head), LOW),
            pltpu.VMEM(u.shape, FULL),
            pltpu.VMEM(u.shape, FULL),
            pltpu.VMEM((n, rows, ext), LOW),
            pltpu.VMEM((n, rows, ext), LOW),
            pltpu.VMEM(u.shape, FULL),
            pltpu.VMEM((n, 8, width), FULL),
            pltpu.VMEM((places, 2 * n, width), FULL),
            pltpu.VMEM((2 * n, width), FULL),
            pltpu.VMEM((8, width), FULL),
            pltpu.VMEM(down.shape, LOW),
            pltpu.VMEM(down.shape[1:], LOW),
            pltpu.SemaphoreType.DMA((1,)),
            pltpu.SemaphoreType.DMA((1,)),
            pltpu.SemaphoreType.DMA((2,)),
            pltpu.SemaphoreType.DMA((2,)),
            pltpu.SemaphoreType.DMA((places,)),
            pltpu.SemaphoreType.DMA((places,)),
            pltpu.SemaphoreType.DMA((n,)),
            pltpu.SemaphoreType.DMA((n,)),
            pltpu.SemaphoreType.DMA((4,)),
            pltpu.SemaphoreType.DMA((2, 2 * bits)),
            pltpu.SemaphoreType.DMA((2, 2 * bits)),
            pltpu.VMEM(gate.shape, LOW),
        ]
        + plane_scratch(gate.shape),
        compiler_params=comm_params(7),
        cost_estimate=lasting(45),
    )(do, y, r, ii, h, edges, c, u, halo, mask, rows8, gate_r, gate_i, down, gate)


def widen_kernel(count, *refs):
    for source, target in zip(refs[:count], refs[count:]):
        target[...] = source[...].astype(target.dtype)


def widen(n, terms, kept):
    arrays = terms + kept
    blocks = [
        pl.BlockSpec((term.shape[0], term.shape[1] // n), lambda k: (0, k)) for term in arrays
    ]
    return pl.pallas_call(
        functools.partial(widen_kernel, len(arrays)),
        grid=(n,),
        in_specs=blocks,
        out_specs=blocks,
        out_shape=[jax.ShapeDtypeStruct(term.shape, FULL) for term in terms]
        + [jax.ShapeDtypeStruct(term.shape, term.dtype) for term in kept],
    )(*arrays)


def on_device(
    inputs,
    segment,
    mixer_gain,
    input_weight,
    branch_weight,
    conv_weight,
    recur_gate,
    input_gate,
    recur_bias,
    input_bias,
    decay_rate,
    output_weight,
    second_gain,
    gate_weight,
    up_weight,
    down_weight,
    cotangent,
):
    shards = lax.axis_size("wt")
    places = lax.axis_size("seq")
    me_w = lax.axis_index("wt")
    me_s = lax.axis_index("seq")
    part_len, model = inputs.shape[1:]
    lru = conv_weight.shape[0]
    taps = conv_weight.shape[1]
    width = lru // shards
    head = recur_gate.shape[1]
    edge = width % head
    rows = shards * part_len

    def mine(vector):
        return lax.dynamic_slice_in_dim(vector, me_w * width, width, 0)

    x = inputs[0]
    slope = cotangent[0]
    rate = mine(decay_rate)
    soft = -8.0 * jax.nn.softplus(rate)
    conv_mine = mine(conv_weight)
    rows8 = jnp.concatenate(
        [conv_mine.T, jnp.stack([mine(recur_bias), mine(input_bias), soft, rate])], axis=0
    )
    xn, u3, y, o, c_ext, r, ii, h, ends, halo, mask, x1, xn2, dm = head_part(
        shards,
        places,
        taps,
        x,
        mixer_gain[None],
        segment,
        rows8,
        slope,
        second_gain[None],
        input_weight,
        branch_weight,
        recur_gate,
        input_gate,
        output_weight,
    )
    dxn2, hidden, dg, dv, xn2, down_term = ffn(
        shards, places, xn2, dm, gate_weight, up_weight, down_weight
    )
    part = model // (places * shards)
    bits = (places // 2 - 1).bit_length()
    cut = (2,) * bits + (shards, part, -1)
    dx1, dz, do, second_gain_grad, block_out, down_kept, gate_term, up_term = back_in(
        shards,
        places,
        dxn2,
        x1,
        slope,
        second_gain[None],
        down_term.reshape(cut),
        output_weight,
        down_weight,
        hidden,
        xn2,
        dg,
        dv,
    )
    du, dy, small, down_grad, gate_kept = turn_back(
        shards,
        places,
        taps,
        do,
        y,
        r,
        ii,
        h,
        ends,
        c_ext,
        u3,
        halo,
        mask,
        rows8,
        recur_gate,
        input_gate,
        down_kept,
        gate_term.reshape(cut),
    )
    input_grad, gains, small, gate_grad, up_grad, out_grad, branch_grad, input_weight_grad, _ = leave(
        shards,
        places,
        du,
        dy,
        o,
        x,
        dx1,
        mixer_gain[None],
        second_gain_grad,
        small.reshape(places, -1, small.shape[1]),
        xn,
        dz,
        input_weight,
        branch_weight,
        up_term,
        gate_kept,
    )
    terms = [down_grad, gate_grad, up_grad, out_grad, branch_grad, input_weight_grad]
    (
        down_grad,
        gate_grad,
        up_grad,
        out_grad,
        branch_grad,
        input_weight_grad,
        input_grad,
        block_out,
    ) = widen(shards, terms, [input_grad, block_out])
    gains = lax.dynamic_slice_in_dim(gains, (me_s * shards + me_w) * part, part, 1)

    at = 2 * head + taps
    return (
        block_out[None],
        input_grad[None],
        gains[0],
        input_weight_grad,
        branch_grad,
        small[:, 2 * head : at],
        small[:, :head],
        small[:, head : 2 * head],
        small[:, at],
        small[:, at + 1],
        small[:, at + 2],
        out_grad,
        gains[1],
        gate_grad,
        up_grad,
        down_grad,
    )


def solution(mesh):
    tokens = P("wt", "seq", None)
    columns = P(None, "wt")
    row = P(("seq", "wt"))
    flat_rows = P(("seq", "wt"), None)
    return jax.shard_map(
        on_device,
        mesh=mesh,
        in_specs=(
            tokens,
            P("wt", "seq"),
            P(),
            columns,
            columns,
            P(),
            P(),
            P(),
            P(),
            P(),
            P(),
            columns,
            P(),
            columns,
            columns,
            columns,
            tokens,
        ),
        out_specs=(
            tokens,
            tokens,
            row,
            flat_rows,
            flat_rows,
            flat_rows,
            flat_rows,
            flat_rows,
            row,
            row,
            row,
            flat_rows,
            row,
            flat_rows,
            flat_rows,
            flat_rows,
        ),
        check_vma=False,
    )
```

```python
import functools
import math

import jax
import jax.numpy as jnp
from jax import lax
from jax.experimental import pallas as pl
from jax.experimental.pallas import tpu as pltpu
from jax.sharding import PartitionSpec as P

EPSILON = 1e-06
LOW = jnp.bfloat16
FULL = jnp.float32


def dot(left, right, left_dim=1, right_dim=0):
    return lax.dot_general(
        left, right, (((left_dim,), (right_dim,)), ((), ())), preferred_element_type=FULL
    )


def gelu_both(values):
    slope = jnp.sqrt(2.0 / jnp.pi).astype(FULL)
    inner = jnp.tanh(slope * (values + 0.044715 * values * values * values))
    gelu = 0.5 * values * (1.0 + inner)
    grad = 0.5 * (1.0 + inner) + 0.5 * values * (1.0 - inner * inner) * slope * (
        1.0 + 3.0 * 0.044715 * values * values
    )
    return gelu, grad


def scan_rows(coef, value, reverse):
    rows = coef.shape[0]
    place = lax.broadcasted_iota(jnp.int32, coef.shape, 0)
    step = 1
    while step < rows:
        if reverse:
            inside = place < rows - step
            by = rows - step
        else:
            inside = place >= step
            by = step
        far_coef = jnp.where(inside, pltpu.roll(coef, by, 0), 1.0)
        far_value = jnp.where(inside, pltpu.roll(value, by, 0), 0.0)
        value = coef * far_value + value
        coef = coef * far_coef
        step *= 2
    return coef, value


def expm1_small(values):
    return values * (
        1.0 + values * (0.5 + values * (1.0 / 6.0 + values * (1.0 / 24.0 + values / 120.0)))
    )


MESH = pl.DeviceIdType.MESH


def remote(source, target, sent, landed, to):
    return pltpu.make_async_remote_copy(
        src_ref=source,
        dst_ref=target,
        send_sem=sent,
        recv_sem=landed,
        device_id={"wt": to},
        device_id_type=MESH,
    )


def greet(n, me, pair=False, bits=0, places=0):
    barrier = pltpu.get_barrier_semaphore()

    @pl.when(me > 0)
    def _():
        pl.semaphore_signal(barrier, 1, device_id={"wt": me - 1}, device_id_type=MESH)

    @pl.when(me < n - 1)
    def _():
        pl.semaphore_signal(barrier, 1, device_id={"wt": me + 1}, device_id_type=MESH)

    peers = (me > 0).astype(jnp.int32) + (me < n - 1).astype(jnp.int32)
    place = lax.axis_index("seq")
    if places:
        peers = peers + places - 1
        for by in range(1, places):
            other = {"seq": lax.rem(place + by, places)}
            pl.semaphore_signal(barrier, 1, device_id=other, device_id_type=MESH)
    if pair:
        other = {"seq": place + 1 - 2 * lax.rem(place, 2)}
        pl.semaphore_signal(barrier, 1, device_id=other, device_id_type=MESH)
        peers = peers + 1 + bits
        for k in range(1, bits + 1):
            step = 1 << k
            other = {"seq": place + step * (1 - 2 * lax.rem(place // step, 2))}
            pl.semaphore_signal(barrier, 1, device_id=other, device_id_type=MESH)
    pl.semaphore_wait(barrier, peers)


def greet_all(n, me, places, more, away):
    barrier = pltpu.get_barrier_semaphore()
    seat = lax.axis_index("seq")
    for by in range(1, n):
        other = {"wt": lax.rem(me + by, n)}
        pl.semaphore_signal(barrier, 1, device_id=other, device_id_type=MESH)
    for by in range(1, places):
        other = {"seq": lax.rem(seat + by, places)}
        pl.semaphore_signal(barrier, 1, device_id=other, device_id_type=MESH)

    @pl.when(away)
    def _():
        for other in more:
            pl.semaphore_signal(barrier, 1, device_id=other, device_id_type=MESH)

    peers = n + places - 2 + len(more) * away.astype(jnp.int32)
    pl.semaphore_wait(barrier, peers)


class LineGather:
    def __init__(self, n, me, blocks, sent, landed):
        self.n, self.me, self.blocks, self.sent, self.landed = n, me, blocks, sent, landed

    def rightward(self, d):
        block = self.blocks.at[self.me - d]
        return remote(block, block, self.sent.at[0, d], self.landed.at[0, d + 1], self.me + 1)

    def leftward(self, d):
        block = self.blocks.at[self.me + d]
        return remote(block, block, self.sent.at[1, d], self.landed.at[1, d + 1], self.me - 1)

    def start(self):
        @pl.when(self.me < self.n - 1)
        def _():
            self.rightward(0).start()

        @pl.when(self.me > 0)
        def _():
            self.leftward(0).start()

    def arrive(self, d):
        n, me = self.n, self.me

        @pl.when(me - d >= 0)
        def _():
            block = self.blocks.at[me - d]
            remote(block, block, self.sent.at[0, 0], self.landed.at[0, d], me).wait_recv()

            @pl.when(me < n - 1)
            def _():
                self.rightward(d).start()

        @pl.when(me + d < n)
        def _():
            block = self.blocks.at[me + d]
            remote(block, block, self.sent.at[1, 0], self.landed.at[1, d], me).wait_recv()

            @pl.when(me > 0)
            def _():
                self.leftward(d).start()

    def each(self, d, use):
        def side(k, carry):
            q = self.me + (2 * k - 1) * d

            @pl.when((q >= 0) & (q < self.n))
            def _():
                use(q)

            return carry

        lax.fori_loop(0, 2, side, 0)

    def finish(self):
        n, me = self.n, self.me
        for d in range(n - 1):

            @pl.when((me - d >= 0) & (me < n - 1))
            def _():
                self.rightward(d).wait_send()

            @pl.when((me + d < n) & (me > 0))
            def _():
                self.leftward(d).wait_send()


def line_gather(n, me, blocks, sent, landed, use, ready):
    line = LineGather(n, me, blocks, sent, landed)
    line.start()
    ready()
    use(me)

    def step(d, carry):
        line.arrive(d)
        line.each(d, use)
        return carry

    lax.fori_loop(1, n, step, 0)
    line.finish()


class LineReduce:
    def __init__(self, n, me, parts, slots, sent, landed):
        self.n, self.me, self.parts, self.slots = n, me, parts, slots
        self.sent, self.landed = sent, landed

    def rightward(self, k):
        source, target = self.parts.at[self.n - 1 - k], self.slots.at[0, k]
        return remote(source, target, self.sent.at[0, k], self.landed.at[0, k], self.me + 1)

    def leftward(self, k):
        source, target = self.parts.at[k], self.slots.at[1, k]
        return remote(source, target, self.sent.at[1, k], self.landed.at[1, k], self.me - 1)

    def arrived(self, side, k):
        slot = self.slots.at[side, k]
        remote(slot, slot, self.sent.at[side, k], self.landed.at[side, k], self.me).wait_recv()

    def add(self, q, side, k):
        total = self.parts[q].astype(FULL) + self.slots[side, k].astype(FULL)
        self.parts[q] = total.astype(LOW)

    def prepare(self, k, partial):
        def side(which, carry):
            q = jnp.where(which == 0, self.n - 1 - k, k)

            @pl.when(jnp.where(which == 0, q > self.me, q < self.me))
            def _():
                partial(q)

            return carry

        lax.fori_loop(0, 2, side, 0)

    def step(self, t):
        n = self.n
        for side in range(2):
            place = self.me if side == 0 else n - 1 - self.me
            k = t - place
            pull = self.rightward if side == 0 else self.leftward

            @pl.when((k >= 0) & (t <= n - 2))
            def _():
                @pl.when(place > 0)
                def _():
                    self.arrived(side, k)
                    self.add(n - 1 - k if side == 0 else k, side, k)

                @pl.when(k > 0)
                def _():
                    pull(k - 1).wait_send()

                pull(k).start()

    def total(self):
        n, me = self.n, self.me

        @pl.when(me > 0)
        def _():
            self.arrived(0, n - 1 - me)

        @pl.when(me < n - 1)
        def _():
            self.arrived(1, me)

        total = self.parts[me].astype(FULL)
        other = self.slots[0, jnp.clip(n - 1 - me, 0, n - 2)].astype(FULL)
        total = total + jnp.where(me > 0, other, 0.0)
        other = self.slots[1, jnp.clip(me, 0, n - 2)].astype(FULL)
        return total + jnp.where(me < n - 1, other, 0.0)

    def finish(self):
        @pl.when(self.me < self.n - 1)
        def _():
            self.rightward(self.n - 2 - self.me).wait_send()

        @pl.when(self.me > 0)
        def _():
            self.leftward(self.me - 1).wait_send()


class LineBoth:
    def __init__(self, gather, back, skip=0):
        self.gather, self.back, self.skip = gather, back, skip
        self.n, self.me = gather.n, gather.me

    def sends(self, side, t, act):
        n, me = self.n, self.me
        place = me if side == 0 else n - 1 - me
        spread = self.gather.rightward if side == 0 else self.gather.leftward
        pull = self.back.rightward if side == 0 else self.back.leftward
        d = t + self.skip

        @pl.when(place < n - 1)
        def _():
            @pl.when(d <= place)
            def _():
                act(spread(d))

            @pl.when(d > place)
            def _():
                act(pull(d - place - 1))

    def step(self, t):
        n, me = self.n, self.me
        d = t + self.skip
        for side in range(2):
            place = me if side == 0 else n - 1 - me
            if t > 0:

                @pl.when(d <= place)
                def _():
                    block = self.gather.blocks.at[me - d if side == 0 else me + d]
                    remote(
                        block, block, self.gather.sent.at[side, 0], self.gather.landed.at[side, d], me
                    ).wait_recv()

                @pl.when((d > place) & (place > 0))
                def _():
                    k = d - place - 1
                    self.back.arrived(side, k)
                    self.back.add(n - 1 - k if side == 0 else k, side, k)

                self.sends(side, t - 1, lambda copy: copy.wait_send())
            self.sends(side, t, lambda copy: copy.start())

    def finish(self):
        for side in range(2):
            self.sends(side, self.n - 1 - self.skip, lambda copy: copy.wait_send())


def line_reduce(n, me, parts, slots, sent, landed, partial, work, finish, early=None):
    line = LineReduce(n, me, parts, slots, sent, landed)
    line.prepare(0, partial)
    line.step(0)
    if early is not None:
        early()
    for k in range(1, n - 1):
        line.prepare(k, partial)
    line.step(1)
    partial(me)
    share = -(-len(work) // (n - 2))
    for t in range(2, n):
        for task in work[(t - 2) * share : (t - 1) * share]:
            task()
        if t < n - 1:
            line.step(t)
    finish(line.total())
    line.finish()


def tiles(count, size, body):
    def step(t, carry):
        body(pl.ds(pl.multiple_of(t * size, size), size))
        return carry

    lax.fori_loop(0, count // size, step, 0)


def tile_of(width, limit):
    size = limit
    while width % size:
        size -= 128
    return size


VMEM = pl.BlockSpec(memory_space=pltpu.VMEM)
ANY = pl.BlockSpec(memory_space=pl.ANY)


def gather_sems(n):
    return [pltpu.SemaphoreType.DMA((2, n)), pltpu.SemaphoreType.DMA((2, n + 1))]


def reduce_sems(n):
    return [pltpu.SemaphoreType.DMA((2, n)), pltpu.SemaphoreType.DMA((2, n))]


def lasting(micros):
    return pl.CostEstimate(
        flops=int(micros * 1.0e9), bytes_accessed=int(micros * 3.4e6), transcendentals=0
    )


def comm_params(number):
    return pltpu.CompilerParams(
        collective_id=number, has_side_effects=True, vmem_limit_bytes=64 * 1024 * 1024
    )


class PairSum:
    def __init__(self, part, halves, landing, sent, landed, free, flush):
        self.me = lax.axis_index("seq")
        self.mine = lax.rem(self.me, 2)
        self.part, self.halves, self.landing = part, halves, landing
        self.sent, self.landed, self.free, self.flush = sent, landed, free, flush
        self.count = 0
        self.pending = None

    def other(self):
        return {"seq": self.me + 1 - 2 * self.mine}

    def send(self, slot):
        return pltpu.make_async_remote_copy(
            src_ref=self.halves.at[slot, 1 - self.mine],
            dst_ref=self.landing.at[slot],
            send_sem=self.sent.at[slot],
            recv_sem=self.landed.at[slot],
            device_id=self.other(),
            device_id_type=MESH,
        )

    def out(self, slot, t, target):
        half = self.landing.shape[1]
        return pltpu.make_async_copy(
            self.halves.at[slot, self.mine],
            target.at[pl.ds(t * half, half), :],
            self.flush.at[slot],
        )

    def tasks(self, steps, compute, target):
        return [functools.partial(self.run, t, compute, target) for t in range(steps)]

    def run(self, t, compute, target):
        slot = self.count % 2
        if self.count >= 2:
            self.send(slot).wait_send()
            self.out(slot, 0, target).wait()
            pl.semaphore_wait(self.free, 1)
        compute(t, self.halves.at[slot])
        self.send(slot).start()
        self.settle()
        self.pending = (slot, t, target)
        self.count += 1

    def settle(self):
        if self.pending is None:
            return
        slot, t, target = self.pending
        self.send(slot).wait_recv()
        total = self.halves[slot, self.mine].astype(FULL) + self.landing[slot].astype(FULL)
        self.halves[slot, self.mine] = total.astype(LOW)
        pl.semaphore_signal(self.free, 1, device_id=self.other(), device_id_type=MESH)
        self.out(slot, t, target).start()
        self.pending = None

    def finish(self, target):
        self.settle()
        for slot in range(2):
            self.send(slot).wait_send()
            self.out(slot, 0, target).wait()
        pl.semaphore_wait(self.free, 2)


def pair_scratch(half, width):
    return [
        pltpu.VMEM((2, 2, half, width), LOW),
        pltpu.VMEM((2, half, width), LOW),
        pltpu.SemaphoreType.DMA((2,)),
        pltpu.SemaphoreType.DMA((2,)),
        pltpu.SemaphoreType.REGULAR,
        pltpu.SemaphoreType.DMA((2,)),
    ]


def pair_tile(model, places):
    size = 2 * model // places
    return size if size % 128 == 0 else size * 128 // math.gcd(size, 128)


def pair_dot(left, right, part, size):
    n, rows, _ = left.shape

    def compute(t, halves):
        lhs = left[:, :, pl.ds(t * size, size)].reshape(n * rows, size)
        width = right.shape[2]

        def tile(at):
            rhs = right[:, :, at].reshape(n * rows, -1)
            value = dot(lhs, rhs, 0, 0).astype(LOW)
            for k in range(size // (2 * part)):
                for side in range(2):
                    first = (2 * k + side) * part
                    halves[side, k * part : (k + 1) * part, at] = value[first : first + part]

        tiles(width, tile_of(width, 640), tile)

    return compute


def column_halves(width):
    first = -(-width // 256) * 128
    return [(0, first), (first, width - first)]


class PlaneReduce:
    def __init__(self, blocks, landings, sent, landed, tail=3):
        self.blocks, self.landings, self.sent, self.landed = blocks, landings, sent, landed
        self.bits = len(blocks.shape) - tail
        self.tail = tail
        self.me = lax.axis_index("seq")
        self.columns = column_halves(blocks.shape[-1])

    def bit(self, dim):
        return 1 << (self.bits - dim)

    def mine(self, dim):
        return lax.rem(self.me // self.bit(dim), 2)

    def order(self, side):
        dims = list(range(self.bits))
        return dims[::-1] if side == 0 else dims

    def peer(self, dim):
        return {"seq": self.me + self.bit(dim) * (1 - 2 * self.mine(dim))}

    def index(self, side, step, own):
        order = self.order(side)
        place = [slice(None)] * self.bits
        for dim in order[:step]:
            place[dim] = self.mine(dim)
        now = order[step]
        place[now] = self.mine(now) if own else 1 - self.mine(now)
        return tuple(place) + (slice(None),) * (self.tail - 1) + (pl.ds(*self.columns[side]),)

    def send(self, side, step, piece=0):
        at, landing = self.index(side, step, False), self.landings[2 * step + side]
        if step == 0:
            count = self.blocks.shape[self.bits]
            first = count // 2 if self.tail == 3 else count // 32 * 16
            rows = pl.ds(piece * first, count - first if piece else first)
            at = at[: self.bits] + (rows,) + at[self.bits + 1 :]
            landing = landing.at[(slice(None),) * (self.bits - 1) + (rows,)]
        return pltpu.make_async_remote_copy(
            src_ref=self.blocks.at[at],
            dst_ref=landing,
            send_sem=self.sent.at[side, step + piece * self.bits],
            recv_sem=self.landed.at[side, step + piece * self.bits],
            device_id=self.peer(self.order(side)[step]),
            device_id_type=MESH,
        )

    def pieces(self, step):
        return (0, 1) if step == 0 else (0,)

    def begin(self, pieces=(0, 1)):
        for piece in pieces:
            for side in range(2):
                self.send(side, 0, piece).start()

    def advance(self, step):
        for side in range(2):
            for piece in self.pieces(step):
                self.send(side, step, piece).wait_recv()
            at = self.index(side, step, True)
            total = self.blocks[at].astype(FULL) + self.landings[2 * step + side][...].astype(FULL)
            self.blocks[at] = total.astype(LOW)
            if step + 1 < self.bits:
                self.send(side, step + 1).start()

    def kept(self):
        return self.blocks.at[tuple(self.mine(dim) for dim in range(self.bits))]

    def finish(self):
        for step in range(self.bits):
            for side in range(2):
                for piece in self.pieces(step):
                    self.send(side, step, piece).wait_send()


def plane_scratch(shape, tail=3):
    bits = len(shape) - tail
    landings = []
    for step in range(bits):
        for _, width in column_halves(shape[-1]):
            rest = [2] * (bits - 1 - step) + list(shape[bits:-1]) + [width]
            landings.append(pltpu.VMEM(tuple(rest), LOW))
    return landings


def ffn_kernel(
    n,
    places,
    xn2_ref,
    dm_hbm,
    wg_hbm,
    wu_hbm,
    wd_hbm,
    dxn2_ref,
    hidden_hbm,
    dg_hbm,
    dv_hbm,
    xall_hbm,
    down_hbm,
    xall,
    dm,
    wg,
    wu,
    wd,
    hidden,
    dg,
    dv,
    parts,
    slots,
    halves,
    landing,
    psent,
    planded,
    free,
    pflush,
    gsent,
    glanded,
    rsent,
    rlanded,
    local,
    flush,
):
    me = lax.axis_index("wt")
    rows, model = xn2_ref.shape
    units = wg.shape[1]
    cut = tile_of(units, 640)
    span = tile_of(model, 512)
    loads = [
        pltpu.make_async_copy(source, target, local.at[k])
        for k, (source, target) in enumerate(
            [(dm_hbm, dm), (wd_hbm, wd), (wg_hbm, wg), (wu_hbm, wu)]
        )
    ]
    for load in loads:
        load.start()
    xall[me] = xn2_ref[...]
    greet(n, me, True)

    def ready():
        for load in loads[:2]:
            load.wait()

        def tile(at):
            value = dot(dm[...].reshape(n * rows, model), wd[:, at])
            dg[:, :, at] = value.reshape(n, rows, -1).astype(LOW)

        tiles(units, cut, tile)
        for load in loads[2:]:
            load.wait()

    def use(q):
        def tile(at):
            block = xall[q]
            g = dot(block, wg[:, at])
            v = dot(block, wu[:, at])
            slopes = dg[q, :, at].astype(FULL)
            gelu, slope = gelu_both(g)
            hidden[q, :, at] = (gelu * v).astype(LOW)
            dg[q, :, at] = (slopes * v * slope).astype(LOW)
            dv[q, :, at] = (slopes * gelu).astype(LOW)

        tiles(units, cut, tile)

    line_gather(n, me, xall, gsent, glanded, use, ready)
    outs = [
        pltpu.make_async_copy(source, target, flush.at[k])
        for k, (source, target) in enumerate(
            [(hidden, hidden_hbm), (dg, dg_hbm), (dv, dv_hbm), (xall, xall_hbm)]
        )
    ]
    for out in outs:
        out.start()

    def partial(q):
        def tile(at):
            total = dot(dg[q], wg[at, :], 1, 1) + dot(dv[q], wu[at, :], 1, 1)
            parts[q, :, at] = total.astype(LOW)

        tiles(model, span, tile)

    part = model // places
    size = pair_tile(model, places)
    pair = PairSum(part, halves, landing, psent, planded, free, pflush)

    work = pair.tasks(model // size, pair_dot(dm, hidden, part, size), down_hbm)

    def finish(total):
        dxn2_ref[...] = total

    line_reduce(n, me, parts, slots, rsent, rlanded, partial, work, finish)
    pair.finish(down_hbm)
    for out in outs:
        out.wait()


def ffn(n, places, xn2, dm, wg, wu, wd):
    rows, model = xn2.shape
    units = wg.shape[1]
    grad = jax.ShapeDtypeStruct((model // 2, units), LOW)
    return pl.pallas_call(
        functools.partial(ffn_kernel, n, places),
        out_shape=[
            jax.ShapeDtypeStruct((rows, model), FULL),
            jax.ShapeDtypeStruct((n, rows, units), LOW),
            jax.ShapeDtypeStruct((n, rows, units), LOW),
            jax.ShapeDtypeStruct((n, rows, units), LOW),
            jax.ShapeDtypeStruct((n, rows, model), LOW),
            grad,
        ],
        in_specs=[VMEM, ANY, ANY, ANY, ANY],
        out_specs=[VMEM, ANY, ANY, ANY, ANY, ANY],
        scratch_shapes=[
            pltpu.VMEM((n, rows, model), LOW),
            pltpu.VMEM((n, rows, model), LOW),
            pltpu.VMEM((model, units), LOW),
            pltpu.VMEM((model, units), LOW),
            pltpu.VMEM((model, units), LOW),
            pltpu.VMEM((n, rows, units), LOW),
            pltpu.VMEM((n, rows, units), LOW),
            pltpu.VMEM((n, rows, units), LOW),
            pltpu.VMEM((n, rows, model), LOW),
            pltpu.VMEM((2, n - 1, rows, model), LOW),
        ]
        + pair_scratch(pair_tile(model, places) // 2, units)
        + gather_sems(n)
        + reduce_sems(n)
        + [pltpu.SemaphoreType.DMA((4,)), pltpu.SemaphoreType.DMA((4,))],
        compiler_params=comm_params(2),
        cost_estimate=lasting(105),
    )(xn2, dm, wg, wu, wd)


def back_in_kernel(n, places, bits, *refs):
    dxn2_ref, x1_ref, slope_ref, gain_ref, *sources = refs[:11]
    dx1_ref, dz_ref, do_ref, sum_ref, out_ref, kept_ref, gate_hbm, up_hbm = refs[11:19]
    w, hidden, wd, xall, dg, dv, blocks = refs[19:26]
    landings = refs[26 : 26 + 2 * bits]
    parts, slots, *sems = refs[26 + 2 * bits :]
    halves, landing, psent, planded, free, pflush, sent, landed, rsent, rlanded, bsent, blanded, local = sems
    me = lax.axis_index("wt")
    loads = [
        pltpu.make_async_copy(source, target, local.at[k])
        for k, (source, target) in enumerate(
            zip(sources, [blocks, w, wd, hidden, xall, dg, dv])
        )
    ]
    for load in loads:
        load.start()
    x1 = x1_ref[...]
    dxn2 = dxn2_ref[...]
    model = x1.shape[1]
    scale = lax.rsqrt(jnp.mean(x1 * x1, axis=-1, keepdims=True) + EPSILON)
    q2 = dxn2 * gain_ref[gain_ref.shape[0] - 1 :, :]
    pull = jnp.mean(q2 * x1, axis=-1, keepdims=True)
    dx1 = slope_ref[...] + scale * (q2 - x1 * (scale * scale * pull))
    dx1_ref[...] = dx1
    dz_ref[me] = dx1.astype(LOW)
    greet(n, me, True, bits)
    line = LineGather(n, me, dz_ref, sent, landed)
    back = LineReduce(n, me, parts, slots, rsent, rlanded)
    both = LineBoth(line, back)
    both.step(0)
    loads[0].wait()
    plane = PlaneReduce(blocks, landings, bsent, blanded)
    plane.begin()
    sum_ref[...] = jnp.sum(dxn2 * x1 * scale, axis=0, keepdims=True)

    def use(q):
        do_ref[q] = dot(dz_ref[q], w[...])

    def partial(q):
        def tile(at):
            parts[q, :, at] = dot(hidden[q], wd[at, :], 1, 1).astype(LOW)

        tiles(model, tile_of(model, 512), tile)

    part = model // places
    size = pair_tile(model, places)
    pair = PairSum(part, halves, landing, psent, planded, free, pflush)
    loads[1].wait()
    use(me)
    for load in loads[2:4]:
        load.wait()
    for k in range(n - 2):
        back.prepare(k, partial)
    work = pair.tasks(model // size, pair_dot(xall, dg, part, size), gate_hbm)
    work += pair.tasks(model // size, pair_dot(xall, dv, part, size), up_hbm)
    ends = [len(work) * max(4 * t - 1, 0) // (4 * (n - 1)) for t in range(n)]
    ends[-1] = len(work)
    for t in range(1, n):
        both.step(t)
        if t == 1:
            back.prepare(n - 2, partial)
        if t >= 2 and t - 2 < bits:
            plane.advance(t - 2)
        line.each(t, use)
        if t == 1:
            partial(me)
            for load in loads[4:]:
                load.wait()
        for task in work[ends[t - 1] : ends[t]]:
            task()
    for step in range(max(n - 2, 0), bits):
        plane.advance(step)
    out_ref[...] = (x1_ref[...] + back.total()).astype(LOW)
    kept_ref[...] = plane.kept()[...]
    pair.finish(up_hbm)
    both.finish()
    plane.finish()


def back_in(n, places, dxn2, x1, slope, gain, down, weight, wd, hidden, xall, dg, dv):
    rows, model = x1.shape
    bits = len(down.shape) - 3
    grad = jax.ShapeDtypeStruct((model // 2, wd.shape[1]), LOW)
    return pl.pallas_call(
        functools.partial(back_in_kernel, n, places, bits),
        out_shape=[
            jax.ShapeDtypeStruct((rows, model), FULL),
            jax.ShapeDtypeStruct((n, rows, model), LOW),
            jax.ShapeDtypeStruct((n, rows, weight.shape[1]), FULL),
            jax.ShapeDtypeStruct((1, model), FULL),
            jax.ShapeDtypeStruct((rows, model), LOW),
            jax.ShapeDtypeStruct(down.shape[bits:], LOW),
            grad,
            grad,
        ],
        in_specs=[VMEM] * 4 + [ANY] * 7,
        out_specs=[VMEM] * 6 + [ANY] * 2,
        scratch_shapes=[
            pltpu.VMEM(weight.shape, LOW),
            pltpu.VMEM(hidden.shape, LOW),
            pltpu.VMEM(wd.shape, LOW),
            pltpu.VMEM(xall.shape, LOW),
            pltpu.VMEM(dg.shape, LOW),
            pltpu.VMEM(dv.shape, LOW),
            pltpu.VMEM(down.shape, LOW),
        ]
        + plane_scratch(down.shape)
        + [
            pltpu.VMEM((n, rows, model), LOW),
            pltpu.VMEM((2, n - 1, rows, model), LOW),
        ]
        + pair_scratch(pair_tile(model, places) // 2, wd.shape[1])
        + gather_sems(n)
        + reduce_sems(n)
        + [
            pltpu.SemaphoreType.DMA((2, 2 * bits)),
            pltpu.SemaphoreType.DMA((2, 2 * bits)),
            pltpu.SemaphoreType.DMA((7,)),
        ],
        compiler_params=comm_params(3),
        cost_estimate=lasting(75),
    )(dxn2, x1, slope, gain, down, weight, wd, hidden, xall, dg, dv)


class PlaneShare:
    def __init__(self, places, source, lands, sent, landed):
        self.places, self.source, self.lands = places, source, lands
        self.sent, self.landed = sent, landed
        self.me = lax.axis_index("seq")

    def send(self, by):
        to = lax.rem(self.me + by, self.places)
        return pltpu.make_async_remote_copy(
            src_ref=self.source.at[to],
            dst_ref=self.lands.at[by],
            send_sem=self.sent.at[by],
            recv_sem=self.landed.at[by],
            device_id={"seq": to},
            device_id_type=MESH,
        )

    def start(self):
        self.lands[0] = self.source[self.me]
        for by in range(1, self.places):
            self.send(by).start()

    def finish(self, target):
        for by in range(1, self.places):
            self.send(by).wait_recv()
        target[...] = jnp.sum(self.lands[...].astype(FULL), axis=0)
        for by in range(1, self.places):
            self.send(by).wait_send()


class LineSpread:
    def __init__(self, n, me, source, lands, sent, landed):
        self.n, self.me, self.source, self.lands = n, me, source, lands
        self.sent, self.landed = sent, landed

    def send(self, by):
        to = lax.rem(self.me + by, self.n)
        return remote(
            self.source.at[to], self.lands.at[self.me], self.sent.at[by], self.landed.at[by], to
        )

    def start(self):
        for by in range(1, self.n):
            self.send(by).start()

    def take(self, put, own):
        put(self.me, own[...])
        for by in range(1, self.n):
            slot = lax.rem(self.me + self.n - by, self.n)
            land = self.lands.at[slot]
            remote(land, land, self.sent.at[by], self.landed.at[by], self.me).wait_recv()
            put(slot, land[...])

    def finish(self):
        for by in range(1, self.n):
            self.send(by).wait_send()


def leave_kernel(n, places, bits, *refs):
    du_ref, dy_ref, o_ref, x_ref, dx1_ref, gain_ref, second_ref, small_ref = refs[:8]
    xn_hbm, dz_hbm, win_hbm, wbr_hbm, up_hbm, gate_hbm = refs[8:14]
    grad_ref, total_ref, moved_ref, gate_ref, up_ref, out_ref, branch_ref, in_ref, mix_hbm = refs[14:23]
    xn, dz, win, wbr, parts, slots, blocks, kept, own, lands, notes, around, shares, passed = refs[23:37]
    landings = refs[37 : 37 + 2 * bits]
    others = refs[37 + 2 * bits : 37 + 4 * bits]
    sems = refs[37 + 4 * bits :]
    halves, landing, psent, planded, free, pflush, sent, landed, ssent, slanded = sems[:10]
    usent, ulanded, msent, mlanded, asent, alanded, gsent, glanded, hsent, hlanded, local, fill = sems[10:]
    me = lax.axis_index("wt")
    seat = lax.axis_index("seq")
    model, width = win.shape
    units = gate_hbm.shape[-1]
    part = kept.shape[1]
    rows = n * part

    def fills(source):
        copies = []
        for k in range(1 << bits):
            place = tuple((k >> (bits - 1 - dim)) & 1 for dim in range(bits))
            copies.append(
                pltpu.make_async_copy(
                    source.at[pl.ds(k * rows, rows), :], blocks.at[place], fill.at[k]
                )
            )
        return copies

    loads = [
        pltpu.make_async_copy(source, target, local.at[k])
        for k, (source, target) in enumerate(
            [(win_hbm, win), (wbr_hbm, wbr), (xn_hbm, xn), (dz_hbm, dz), (gate_hbm.at[me], own)]
        )
    ]
    for load in loads[:2] + fills(up_hbm) + loads[2:]:
        load.start()
    flat_to, flat_from = me * places + seat, seat * n + me
    goal = {"seq": flat_to // n, "wt": lax.rem(flat_to, n)}
    origin = {"seq": lax.rem(flat_from, places), "wt": flat_from // places}
    away = flat_to != flat_from
    greet_all(n, me, places, [goal, origin], away)
    small = PlaneShare(places, small_ref, shares, ssent, slanded)
    small.start()
    plane = PlaneReduce(blocks, landings, usent, ulanded, 2)
    for load in loads[:2]:
        load.wait()

    def partial(q):
        def tile(at):
            total = dot(du_ref[q], win[at, :], 1, 1) + dot(dy_ref[q], wbr[at, :], 1, 1)
            parts[q, :, at] = total.astype(LOW)

        tiles(model, tile_of(model, 512), tile)

    size = pair_tile(model, places)
    pair = PairSum(rows, halves, landing, psent, planded, free, pflush)

    def compute(t, target):
        for k, (left, right) in enumerate([(dz, o_ref), (xn, dy_ref), (xn, du_ref)]):
            columns = pl.ds(k * width, width)
            pair_dot(left, right, rows, size)(t, target.at[:, :, columns])

    def early():
        for copy in fills(up_hbm):
            copy.wait()
        plane.begin()
        for load in loads[2:]:
            load.wait()

    def finish(total):
        flat = x_ref[...].astype(FULL)
        scale = lax.rsqrt(jnp.mean(flat * flat, axis=-1, keepdims=True) + EPSILON)
        q1 = total * gain_ref[gain_ref.shape[0] - 2 : gain_ref.shape[0] - 1, :]
        pull = jnp.mean(q1 * flat, axis=-1, keepdims=True)
        grad_ref[...] = dx1_ref[...] + scale * (q1 - flat * (scale * scale * pull))
        mine = jnp.sum(total * flat * scale, axis=0, keepdims=True)
        blank = jnp.zeros((notes.shape[1] - 2, model), FULL)
        notes[me] = jnp.concatenate([mine, second_ref[...], blank], axis=0)

    def keep(k, source):
        for q in range(n):
            kept[k * n + q] = source[q * part : (q + 1) * part, :]

    spreads = [
        LineSpread(n, me, source, lands.at[k], asent.at[k], alanded.at[k])
        for k, source in enumerate([gate_hbm, kept.at[pl.ds(0, n)], kept.at[pl.ds(n, n)]])
    ]
    work = pair.tasks(model // size, compute, mix_hbm)
    tasks = work[:-1] + [lambda: (work[-1](), plane.advance(0), spreads[0].start())]
    line_reduce(n, me, parts, slots, sent, landed, partial, tasks, finish, early)
    pair.finish(mix_hbm)

    def note(by):
        to = lax.rem(me + by, n)
        return remote(notes.at[me], notes.at[me], gsent.at[0, by], glanded.at[0, by], to)

    for by in range(1, n):
        note(by).start()
    for step in range(1, bits):
        plane.advance(step)
    keep(0, plane.kept())
    spreads[1].start()
    plane.finish()
    for copy in fills(mix_hbm):
        copy.start()
    for copy in fills(mix_hbm):
        copy.wait()
    mixing = PlaneReduce(blocks, others, msent, mlanded, 2)
    mixing.begin()
    small.finish(passed)
    move = pltpu.make_async_remote_copy(
        src_ref=passed,
        dst_ref=moved_ref,
        send_sem=hsent.at[0],
        recv_sem=hlanded.at[0],
        device_id=goal,
        device_id_type=MESH,
    )

    @pl.when(away)
    def _():
        move.start()

    @pl.when(jnp.logical_not(away))
    def _():
        moved_ref[...] = passed[...]

    for by in range(1, n):
        slot = notes.at[lax.rem(me + n - by, n)]
        remote(slot, slot, gsent.at[0, by], glanded.at[0, by], me).wait_recv()
    around[seat] = jnp.sum(notes[...], axis=0)

    def share(by):
        return pltpu.make_async_remote_copy(
            src_ref=around.at[seat],
            dst_ref=around.at[seat],
            send_sem=gsent.at[1, by],
            recv_sem=glanded.at[1, by],
            device_id={"seq": lax.rem(seat + by, places)},
            device_id_type=MESH,
        )

    for by in range(1, places):
        share(by).start()

    def put_into(target):
        def put(q, value):
            target[:, pl.ds(pl.multiple_of(q * units, 128), units)] = value

        return put

    spreads[0].take(put_into(gate_ref), own)
    for step in range(bits):
        mixing.advance(step)
    keep(1, mixing.kept())
    spreads[2].start()
    spreads[1].take(put_into(up_ref), kept.at[me])
    for by in range(1, places):
        slot = around.at[lax.rem(seat + places - by, places)]
        pltpu.make_async_remote_copy(
            src_ref=slot,
            dst_ref=slot,
            send_sem=gsent.at[1, by],
            recv_sem=glanded.at[1, by],
            device_id={"seq": seat},
            device_id_type=MESH,
        ).wait_recv()
    total_ref[...] = jnp.sum(around[...], axis=0)

    def put_mix(q, value):
        columns = pl.ds(pl.multiple_of(q * width, 128), width)
        for k, target in enumerate([out_ref, branch_ref, in_ref]):
            target[:, columns] = value[:, k * width : (k + 1) * width]

    spreads[2].take(put_mix, kept.at[n + me])
    mixing.finish()
    for spread in spreads:
        spread.finish()
    for by in range(1, n):
        note(by).wait_send()
    for by in range(1, places):
        share(by).wait_send()

    @pl.when(away)
    def _():
        move.wait()


def leave(n, places, du, dy, o, x, dx1, gain, second, small, xn, dz, win, wbr, up, gate):
    rows, model = x.shape
    width = win.shape[1]
    _, part, units = gate.shape
    bits = (model // 2 // (n * part)).bit_length() - 1
    blocks = (2,) * bits + (n * part, units)
    wide = jax.ShapeDtypeStruct((part, n * units), LOW)
    thin = jax.ShapeDtypeStruct((part, n * width), LOW)
    return pl.pallas_call(
        functools.partial(leave_kernel, n, places, bits),
        out_shape=[
            jax.ShapeDtypeStruct((rows, model), FULL),
            jax.ShapeDtypeStruct((8, model), FULL),
            jax.ShapeDtypeStruct(small.shape[1:], FULL),
            wide,
            wide,
            thin,
            thin,
            thin,
            jax.ShapeDtypeStruct(up.shape, LOW),
        ],
        in_specs=[VMEM] * 8 + [ANY] * 6,
        out_specs=[VMEM] * 8 + [ANY],
        scratch_shapes=[
            pltpu.VMEM((n, rows, model), LOW),
            pltpu.VMEM((n, rows, model), LOW),
            pltpu.VMEM(win.shape, LOW),
            pltpu.VMEM(wbr.shape, LOW),
            pltpu.VMEM((n, rows, model), LOW),
            pltpu.VMEM((2, n - 1, rows, model), LOW),
            pltpu.VMEM(blocks, LOW),
            pltpu.VMEM((2 * n, part, units), LOW),
            pltpu.VMEM((part, units), LOW),
            pltpu.VMEM((3, n, part, units), LOW),
            pltpu.VMEM((n, 8, model), FULL),
            pltpu.VMEM((places, 8, model), FULL),
            pltpu.VMEM(small.shape, LOW),
            pltpu.VMEM(small.shape[1:], FULL),
        ]
        + plane_scratch(blocks, 2)
        + plane_scratch(blocks, 2)
        + pair_scratch(pair_tile(model, places) // 2, 3 * width)
        + reduce_sems(n)
        + [
            pltpu.SemaphoreType.DMA((places,)),
            pltpu.SemaphoreType.DMA((places,)),
            pltpu.SemaphoreType.DMA((2, 2 * bits)),
            pltpu.SemaphoreType.DMA((2, 2 * bits)),
            pltpu.SemaphoreType.DMA((2, 2 * bits)),
            pltpu.SemaphoreType.DMA((2, 2 * bits)),
            pltpu.SemaphoreType.DMA((3, n)),
            pltpu.SemaphoreType.DMA((3, n)),
            pltpu.SemaphoreType.DMA((2, max(n, places))),
            pltpu.SemaphoreType.DMA((2, max(n, places))),
            pltpu.SemaphoreType.DMA((1,)),
            pltpu.SemaphoreType.DMA((1,)),
            pltpu.SemaphoreType.DMA((5,)),
            pltpu.SemaphoreType.DMA((1 << bits,)),
        ],
        compiler_params=comm_params(4),
        cost_estimate=lasting(140),
    )(du, dy, o, x, dx1, gain, second, small, xn, dz, win, wbr, up, gate)


def conv_masks(own, before, after, taps):
    lane = lax.broadcasted_iota(jnp.int32, own.shape, 1)
    lines = []
    for here, back in ((own, before), (after, own)):
        for k in range(taps):
            shifted = jnp.where(lane >= k, pltpu.roll(here, k, 1), pltpu.roll(back, k, 1))
            lines.append((shifted == here).astype(FULL)[:1] if k else jnp.ones_like(here)[:1])
    lines.append(jnp.zeros((own.shape[1] - 2 * taps, own.shape[1]), FULL))
    return jnp.concatenate(lines, axis=0).T


def pick_row(table, q):
    place = lax.broadcasted_iota(jnp.int32, table.shape, 0)
    return jnp.sum(jnp.where(place == q, table, 0.0), axis=0, keepdims=True)


def mult_of(log_a, keep):
    twice = 2.0 * log_a
    gap = jnp.where(twice > -0.01, -expm1_small(twice), 1.0 - jnp.exp(twice))
    return jnp.where(keep == 0.0, 1.0, jnp.sqrt(gap))


def enter_kernel(
    n, x_ref, gain_ref, doc_ref, win_hbm, wbr_hbm, xn_ref, u_ref, y_ref, docs_ref, win, wbr, docs, sent, landed, dsent, dlanded, local, places
):
    me = lax.axis_index("wt")
    loads = [
        pltpu.make_async_copy(win_hbm, win, local.at[0]),
        pltpu.make_async_copy(wbr_hbm, wbr, local.at[1]),
    ]
    for load in loads:
        load.start()
    docs[me] = jnp.broadcast_to(doc_ref[...], docs.shape[1:])
    flat = x_ref[...].astype(FULL)
    scale = lax.rsqrt(jnp.mean(flat * flat, axis=-1, keepdims=True) + EPSILON)
    xn_ref[me] = (flat * scale * gain_ref[...]).astype(LOW)
    greet(n, me, False, 0, places)
    notes = LineGather(n, me, docs, dsent, dlanded)
    line = LineGather(n, me, xn_ref, sent, landed)
    notes.start()
    line.start()
    for load in loads:
        load.wait()

    def use(q):
        block = xn_ref[q]
        u_ref[q] = dot(block, win[...]).astype(LOW)
        y_ref[q] = dot(block, wbr[...])

    use(me)

    def step(d, carry):
        notes.arrive(d)
        line.arrive(d)
        line.each(d, use)
        return carry

    lax.fori_loop(1, n, step, 0)
    docs_ref[...] = docs[...]
    notes.finish()
    line.finish()


def close_kernel(
    n, o_ref, x_ref, gain_ref, w_hbm, near_ref, x1_ref, xn2_ref, dm_ref, parts, slots, sent, landed, gsent, glanded, local, w_ref
):
    me = lax.axis_index("wt")
    model = w_ref.shape[0]

    def near(k, act):
        q = me + k - 1

        @pl.when((q >= 0) & (q < n))
        def _():
            act(pltpu.make_async_copy(near_ref.at[k], dm_ref.at[q], local.at[k]))

    for k in range(3):
        near(k, lambda copy: copy.start())

    def partial(q):
        block = o_ref[q]

        def tile(at):
            parts[q, :, at] = dot(block, w_ref[at, :], 1, 1).astype(LOW)

        tiles(model, tile_of(model, 512), tile)

    def finish(total):
        x1 = x_ref[...].astype(FULL) + total
        x1_ref[...] = x1
        scale = lax.rsqrt(jnp.mean(x1 * x1, axis=-1, keepdims=True) + EPSILON)
        xn2_ref[...] = (x1 * scale * gain_ref[...]).astype(LOW)

    back = LineReduce(n, me, parts, slots, sent, landed)
    both = LineBoth(LineGather(n, me, dm_ref, gsent, glanded), back, 1)
    for k in range(3):
        near(k, lambda copy: copy.wait())
    back.prepare(0, partial)
    both.step(0)
    for k in range(1, n - 1):
        back.prepare(k, partial)
    partial(me)
    for t in range(1, n - 1):
        both.step(t)
    finish(back.total())
    both.finish()


def mid_kernel(
    n,
    places,
    taps,
    u_ref,
    y_ref,
    docs_ref,
    rows_ref,
    gr_hbm,
    gi_hbm,
    slope_ref,
    o_ref,
    c_ref,
    r_ref,
    ii_ref,
    h_ref,
    edge_ref,
    halo_ref,
    mask_ref,
    near_ref,
    tr,
    ti,
    cum,
    carry,
    before,
    after,
    hsent,
    hlanded,
    esent,
    elanded,
    csent,
    clanded,
    nsent,
    nlanded,
    local,
):
    me = lax.axis_index("wt")
    seat = lax.axis_index("seq")
    part_len, width = u_ref.shape[1:]
    head = gr_hbm.shape[1]
    ext = tr.shape[0]
    edge = ext - width
    odd = lax.rem(me, 2)
    shift = odd * edge
    block = 128
    first = pl.multiple_of((me * width) // head * head, head)
    loads = [
        pltpu.make_async_copy(source.at[pl.ds(first, ext), :], target, local.at[k])
        for k, (source, target) in enumerate([(gr_hbm, tr), (gi_hbm, ti)])
    ]
    for load in loads:
        load.start()
    partner = {"wt": me + 1 - 2 * odd}
    near_ref[1] = slope_ref[...].astype(LOW)

    def neighbours(act, out):
        for k, (to, there) in enumerate([(me + 1, 0), (me - 1, 2)]):
            copy = remote(near_ref.at[1], near_ref.at[there], nsent.at[k], nlanded.at[k], to)
            inside = (to >= 0) & (to < n)
            gives = (me > 0) if k == 0 else (me < n - 1)

            @pl.when(inside if out else gives)
            def _():
                act(copy)


    def hop(source, target, k, to):
        return pltpu.make_async_remote_copy(
            src_ref=source,
            dst_ref=target,
            send_sem=hsent.at[k],
            recv_sem=hlanded.at[k],
            device_id={"seq": to},
            device_id_type=MESH,
        )

    reach = halo_ref.shape[1]
    tails = u_ref.at[:, pl.ds(part_len - reach, reach), :]
    onward = [hop(tails, halo_ref, 0, seat + 1), hop(docs_ref, before, 1, seat + 1)]
    backward = [hop(docs_ref, after, 2, seat - 1)]

    @pl.when(seat < places - 1)
    def _():
        for copy in onward:
            copy.start()

    @pl.when(seat > 0)
    def _():
        for copy in backward:
            copy.start()

    @pl.when(seat == 0)
    def _():
        halo_ref[...] = jnp.zeros_like(halo_ref)
        before[...] = jnp.full_like(before, -1)

    @pl.when(seat == places - 1)
    def _():
        after[...] = jnp.full_like(after, -1)

    @pl.when(seat > 0)
    def _():
        for copy in onward:
            copy.wait_recv()

    @pl.when(seat < places - 1)
    def _():
        for copy in backward:
            copy.wait_recv()

    def columns(b):
        return pl.ds(pl.multiple_of(b * block, block), block)

    def ext_columns(b):
        return pl.ds(pl.multiple_of(b * block + shift, block), block)

    def each(body):
        def outer(q, carried):
            def inner(b, deeper):
                body(q, b)
                return deeper

            return lax.fori_loop(0, width // block, inner, carried, unroll=True)

        lax.fori_loop(0, n, outer, 0)

    def masks(q, carried):
        mask_ref[q] = conv_masks(
            docs_ref[q].astype(FULL), before[q].astype(FULL), after[q].astype(FULL), taps
        )
        return carried

    lax.fori_loop(0, n, masks, 0)

    def conv(q, b):
        at = columns(b)
        long = jnp.concatenate([halo_ref[q, :, at], u_ref[q, :, at]], axis=0).astype(FULL)
        total = long[reach:] * rows_ref[0:1, at]
        for k in range(1, taps):
            window = pltpu.roll(long, k, 0)[reach:]
            total = total + window * mask_ref[q, :, k : k + 1] * rows_ref[k : k + 1, at]
        c_ref[q, :, ext_columns(b)] = total.astype(LOW)

    each(conv)
    source = pl.ds(pl.multiple_of(jnp.where(odd == 1, edge, width - edge), edge), edge)
    target = pl.ds(pl.multiple_of(jnp.where(odd == 1, width, 0), edge), edge)
    swap = pltpu.make_async_remote_copy(
        src_ref=c_ref.at[:, :, source],
        dst_ref=c_ref.at[:, :, target],
        send_sem=esent.at[0],
        recv_sem=elanded.at[0],
        device_id=partner,
        device_id_type=MESH,
    )
    swap.start()
    for load in loads:
        load.wait()
    swap.wait_recv()
    neighbours(lambda copy: copy.start(), True)
    per = head // block

    def gates(q, b):
        at = columns(b)
        j = b + shift // block
        spot = j // per
        within = pl.ds(pl.multiple_of(lax.rem(j, per) * block, block), block)
        rows = pl.ds(pl.multiple_of(spot * head, head), head)
        c_head = c_ref[q, :, rows]
        c_own = c_ref[q, :, ext_columns(b)].astype(FULL)
        r = jax.nn.sigmoid(dot(c_head, tr[rows, within]) + rows_ref[taps : taps + 1, at])
        ii = jax.nn.sigmoid(dot(c_head, ti[rows, within]) + rows_ref[taps + 1 : taps + 2, at])
        keep = mask_ref[q, :, 1:2]
        log_a = rows_ref[taps + 2 : taps + 3, at] * r
        mult = mult_of(log_a, keep)
        b_low = (mult * c_own * ii).astype(LOW).astype(FULL)
        a = jnp.exp(log_a.astype(LOW).astype(FULL)) * keep
        cum_a, h_loc = scan_rows(a, b_low, False)
        r_ref[q, :, at] = r
        ii_ref[q, :, at] = ii
        cum[q, :, at] = cum_a
        h_ref[q, :, at] = h_loc

    each(gates)
    for q in range(n):
        carry[seat, q : q + 1, :] = cum[q, part_len - 1 : part_len, :]
        carry[seat, n + q : n + q + 1, :] = h_ref[q, part_len - 1 : part_len, :]

    def share(by):
        return pltpu.make_async_remote_copy(
            src_ref=carry.at[seat],
            dst_ref=carry.at[seat],
            send_sem=csent.at[by],
            recv_sem=clanded.at[by],
            device_id={"seq": lax.rem(seat + by, places)},
            device_id_type=MESH,
        )

    for by in range(1, places):
        share(by).start()
    for by in range(1, places):
        share(by).wait_recv()
    state = jnp.zeros((n, width), FULL)
    start = state
    for p in range(places):
        start = jnp.where(seat == p, state, start)
        state = carry[p, :n, :] * state + carry[p, n:, :]
    edge_ref[:n, :] = start
    edge_ref[n:, :] = carry[seat, :n, :]

    def finish(q, b):
        at = columns(b)
        h = h_ref[q, :, at] + cum[q, :, at] * pick_row(edge_ref[:, at], q)
        h_ref[q, :, at] = h
        gelu, _ = gelu_both(y_ref[q, :, at])
        o_ref[q, :, at] = (h.astype(LOW).astype(FULL) * gelu).astype(LOW)

    each(finish)
    neighbours(lambda copy: copy.wait_recv(), False)
    neighbours(lambda copy: copy.wait_send(), True)
    swap.wait_send()

    @pl.when(seat < places - 1)
    def _():
        for copy in onward:
            copy.wait_send()

    @pl.when(seat > 0)
    def _():
        for copy in backward:
            copy.wait_send()

    for by in range(1, places):
        share(by).wait_send()


def head_kernel(n, places, taps, *refs):
    x, doc, table, slope, win_hbm, wbr_hbm, gr_hbm, gi_hbm, w_hbm = refs[:9]
    xn, u, y, o, c, r, ii, h, edges, halo, mask, x1, xn2, dm, rows8 = refs[9:24]
    win, wbr, docs, seen, near, tr, ti, cum, carry, before, after, parts, slots, w = refs[24:38]
    sems = refs[38:]
    width = u.shape[2]
    first = pl.multiple_of(lax.axis_index("wt") * width, 128)
    rows8[...] = table[: taps + 4, pl.ds(first, width)]
    gain, second = table.at[pl.ds(taps + 4, 1)], table.at[pl.ds(taps + 5, 1)]
    load = pltpu.make_async_copy(w_hbm, w, sems[-1].at[0])
    load.start()
    enter_kernel(
        n, x, gain, doc, win_hbm, wbr_hbm, xn, u, y, seen, win, wbr, docs, *sems[:5], places
    )
    mid_kernel(
        n, places, taps, u, y, seen, rows8, gr_hbm, gi_hbm, slope, o, c, r, ii, h, edges, halo, mask, near,
        tr, ti, cum, carry, before, after, *sems[5:14]
    )
    load.wait()
    close_kernel(n, o, x, second, w_hbm, near, x1, xn2, dm, parts, slots, *sems[14:19], w)


def head_part(n, places, taps, x, doc, table, slope, win, wbr, gate_r, gate_i, weight):
    rows, model = x.shape
    width = win.shape[1]
    head = gate_r.shape[1]
    ext = -(-width // head) * head
    full = jax.ShapeDtypeStruct((n, rows, width), FULL)
    low = jax.ShapeDtypeStruct((n, rows, width), LOW)
    long = jax.ShapeDtypeStruct((n, rows, model), LOW)
    docs = pltpu.VMEM((n, 8, rows), jnp.int32)
    pairs = [pltpu.SemaphoreType.DMA((count,)) for count in (3, 3, 1, 1, places, places, 2, 2, 2)]
    return pl.pallas_call(
        functools.partial(head_kernel, n, places, taps),
        out_shape=[
            long,
            low,
            full,
            low,
            jax.ShapeDtypeStruct((n, rows, ext), LOW),
            full,
            full,
            full,
            jax.ShapeDtypeStruct((2 * n, width), FULL),
            jax.ShapeDtypeStruct((n, 16, width), LOW),
            jax.ShapeDtypeStruct((n, rows, rows), FULL),
            jax.ShapeDtypeStruct((rows, model), FULL),
            jax.ShapeDtypeStruct((rows, model), LOW),
            long,
            jax.ShapeDtypeStruct((taps + 4, width), FULL),
        ],
        in_specs=[VMEM] * 4 + [ANY] * 5,
        out_specs=[VMEM] * 15,
        scratch_shapes=[
            pltpu.VMEM(win.shape, LOW),
            pltpu.VMEM(wbr.shape, LOW),
            docs,
            docs,
            pltpu.VMEM((3, rows, model), LOW),
            pltpu.VMEM((ext, head), LOW),
            pltpu.VMEM((ext, head), LOW),
            pltpu.VMEM((n, rows, width), FULL),
            pltpu.VMEM((places, 2 * n, width), FULL),
            docs,
            docs,
            pltpu.VMEM((n, rows, model), LOW),
            pltpu.VMEM((2, n - 1, rows, model), LOW),
            pltpu.VMEM(weight.shape, LOW),
        ]
        + gather_sems(n)
        + gather_sems(n)
        + [pltpu.SemaphoreType.DMA((2,))]
        + pairs
        + reduce_sems(n)
        + gather_sems(n)
        + [pltpu.SemaphoreType.DMA((3,)), pltpu.SemaphoreType.DMA((1,))],
        compiler_params=comm_params(0),
        cost_estimate=lasting(135),
    )(x, doc, table, slope, win, wbr, gate_r, gate_i, weight)


def turn_kernel(
    n,
    places,
    taps,
    bits,
    do_ref,
    y_ref,
    r_ref,
    ii_ref,
    h_ref,
    edge_ref,
    c_ref,
    u_ref,
    halo_ref,
    mask_ref,
    rows_ref,
    gr_hbm,
    gi_hbm,
    down_hbm,
    gate_hbm,
    du_ref,
    dy_ref,
    small_ref,
    down_ref,
    kept_ref,
    tr,
    ti,
    rem,
    e_ref,
    dra,
    dia,
    dc,
    lead,
    carry,
    ein,
    sums,
    lands,
    own,
    hsent,
    hlanded,
    esent,
    elanded,
    csent,
    clanded,
    ssent,
    slanded,
    local,
    psent,
    planded,
    blocks,
    *landings,
):
    me = lax.axis_index("wt")
    seat = lax.axis_index("seq")
    part_len, width = u_ref.shape[1:]
    head = gr_hbm.shape[1]
    ext = tr.shape[0]
    edge = ext - width
    odd = lax.rem(me, 2)
    shift = odd * edge
    block = 128
    per = head // block
    reach = halo_ref.shape[1]
    first = pl.multiple_of((me * width) // head * head, head)
    loads = [
        pltpu.make_async_copy(gr_hbm.at[pl.ds(first, ext), :], tr, local.at[0]),
        pltpu.make_async_copy(gi_hbm.at[pl.ds(first, ext), :], ti, local.at[1]),
        pltpu.make_async_copy(down_hbm.at[me], own, local.at[2]),
        pltpu.make_async_copy(gate_hbm, blocks, local.at[3]),
    ]
    for load in loads:
        load.start()
    barrier = pltpu.get_barrier_semaphore()
    for by in range(1, places):
        other = {"seq": lax.rem(seat + by, places)}
        pl.semaphore_signal(barrier, 1, device_id=other, device_id_type=MESH)
    for by in range(1, n):
        other = {"wt": lax.rem(me + by, n)}
        pl.semaphore_signal(barrier, 1, device_id=other, device_id_type=MESH)
    pl.semaphore_wait(barrier, places + n - 2)
    spread = LineSpread(n, me, down_hbm, lands, ssent, slanded)
    spread.start()
    loads[3].wait()
    plane = PlaneReduce(blocks, landings, psent, planded)
    plane.begin((0,))

    def columns(b):
        return pl.ds(pl.multiple_of(b * block, block), block)

    def ext_columns(b):
        return pl.ds(pl.multiple_of(b * block + shift, block), block)

    def head_columns(b):
        spot = (b + shift // block) // per
        return pl.ds(pl.multiple_of(spot * head, head), head)

    def each(body):
        def outer(q, carried):
            def inner(b, deeper):
                body(q, b)
                return deeper

            return lax.fori_loop(0, width // block, inner, carried, unroll=True)

        lax.fori_loop(0, n, outer, 0)

    def decay(q, at, rows=slice(None)):
        log_a = rows_ref[taps + 2 : taps + 3, at] * r_ref[q, rows, at]
        return jnp.exp(log_a.astype(LOW).astype(FULL)) * mask_ref[q, rows, 1:2]

    place = lax.broadcasted_iota(jnp.int32, (part_len, block), 0)

    def scans(q, b):
        at = columns(b)
        gelu, slope = gelu_both(y_ref[q, :, at])
        back = do_ref[q, :, at]
        hr = h_ref[q, :, at].astype(LOW).astype(FULL)
        dy_ref[q, :, at] = (back * hr * slope).astype(LOW)
        dh = (back * gelu).astype(LOW).astype(FULL)
        a_next = jnp.where(
            place < part_len - 1, pltpu.roll(decay(q, at), part_len - 1, 0), 1.0
        )
        far, e_loc = scan_rows(a_next, dh, True)
        rem[q, :, at] = far
        e_ref[q, :, at] = e_loc

    each(scans)
    carry[seat, :n, :] = edge_ref[n:, :]
    for q in range(n):
        top = decay(q, slice(None), slice(0, 1)) * e_ref[q, 0:1, :]
        carry[seat, n + q : n + q + 1, :] = top

    def share(by):
        return pltpu.make_async_remote_copy(
            src_ref=carry.at[seat],
            dst_ref=carry.at[seat],
            send_sem=csent.at[by],
            recv_sem=clanded.at[by],
            device_id={"seq": lax.rem(seat + by, places)},
            device_id_type=MESH,
        )

    for by in range(1, places):
        share(by).start()
    sums[...] = jnp.zeros_like(sums)
    for by in range(1, places):
        share(by).wait_recv()
    plane.begin((1,))
    state = jnp.zeros((n, width), FULL)
    start = state
    for p in reversed(range(places)):
        start = jnp.where(seat == p, state, start)
        state = carry[p, :n, :] * state + carry[p, n:, :]
    ein[:n, :] = start
    ein[n:, :] = jnp.zeros_like(start)

    def slopes(q, b):
        at = columns(b)
        e = e_ref[q, :, at] + rem[q, :, at] * pick_row(ein[:, at], q)
        h_prev = jnp.where(
            place == 0, pick_row(edge_ref[:, at], q), pltpu.roll(h_ref[q, :, at], 1, 0)
        )
        r = r_ref[q, :, at]
        ii = ii_ref[q, :, at]
        keep = mask_ref[q, :, 1:2]
        soft = rows_ref[taps + 2 : taps + 3, at]
        log_a = soft * r
        mult = mult_of(log_a, keep)
        c = c_ref[q, :, ext_columns(b)].astype(FULL)
        dla = (e * h_prev * decay(q, at)).astype(LOW).astype(FULL)
        dbr = e.astype(LOW).astype(FULL)
        dmult = jnp.where(keep == 0.0, 0.0, -jnp.exp(2.0 * log_a) / mult)
        dlog_a = dla + dbr * c * ii * dmult
        dra_f = soft * dlog_a * r * (1.0 - r)
        direct = dbr * mult * ii
        dia_f = direct * c * (1.0 - ii)
        dra[q, :, ext_columns(b)] = dra_f.astype(LOW)
        dia[q, :, ext_columns(b)] = dia_f.astype(LOW)
        dc[q, :, at] = direct
        for k, value in enumerate([dra_f, dia_f, -8.0 * dlog_a * r]):
            sums[taps + k : taps + k + 1, at] += jnp.sum(value, axis=0, keepdims=True)

    each(slopes)
    source = pl.ds(pl.multiple_of(jnp.where(odd == 1, edge, width - edge), edge), edge)
    target = pl.ds(pl.multiple_of(jnp.where(odd == 1, width, 0), edge), edge)
    swaps = [
        pltpu.make_async_remote_copy(
            src_ref=ref.at[:, :, source],
            dst_ref=ref.at[:, :, target],
            send_sem=esent.at[k],
            recv_sem=elanded.at[k],
            device_id={"wt": me + 1 - 2 * odd},
            device_id_type=MESH,
        )
        for k, ref in enumerate([dra, dia])
    ]
    for swap in swaps:
        swap.start()
    for load in loads[:3]:
        load.wait()
    for swap in swaps:
        swap.wait_recv()

    def mix(q, b):
        at = columns(b)
        rows = head_columns(b)
        table = ext_columns(b)
        dc[q, :, at] += dot(dra[q, :, rows], tr[table, :], 1, 1) + dot(
            dia[q, :, rows], ti[table, :], 1, 1
        )

    each(mix)
    leads = pltpu.make_async_remote_copy(
        src_ref=dc.at[:, pl.ds(0, lead.shape[1]), :],
        dst_ref=lead,
        send_sem=hsent.at[0],
        recv_sem=hlanded.at[0],
        device_id={"seq": seat - 1},
        device_id_type=MESH,
    )

    @pl.when(seat > 0)
    def _():
        leads.start()

    @pl.when(seat == places - 1)
    def _():
        lead[...] = jnp.zeros_like(lead)

    def gate_grads(b, carried):
        left = c_ref[:, :, ext_columns(b)].reshape(n * part_len, block)
        rows = head_columns(b)
        for k, ref in enumerate([dra, dia]):
            right = ref[:, :, rows].reshape(n * part_len, head)
            small_ref[columns(b), k * head : (k + 1) * head] = dot(left, right, 0, 0).astype(LOW)
        return carried

    lax.fori_loop(0, width // block, gate_grads, 0)

    @pl.when(seat < places - 1)
    def _():
        leads.wait_recv()

    plane.advance(0)

    def conv(q, b):
        at = columns(b)
        slope = dc[q, :, at]
        next_rows = lead[q, :, at]
        long = jnp.concatenate([slope, next_rows], axis=0)
        total = slope * rows_ref[0:1, at]
        behind = jnp.concatenate([halo_ref[q, :, at], u_ref[q, :, at]], axis=0).astype(FULL)
        sums[0:1, at] += jnp.sum(behind[reach:] * slope, axis=0, keepdims=True)
        for k in range(1, taps):
            same = mask_ref[q, :, k : k + 1]
            same_next = mask_ref[q, : lead.shape[1], taps + k : taps + k + 1]
            masked = long * jnp.concatenate([same, same_next], axis=0)
            shifted = pltpu.roll(masked, long.shape[0] - k, 0)[:part_len]
            total = total + shifted * rows_ref[k : k + 1, at]
            window = pltpu.roll(behind, k, 0)[reach:] * same
            sums[k : k + 1, at] += jnp.sum(window * slope, axis=0, keepdims=True)
        du_ref[q, :, at] = total.astype(LOW)

    each(conv)
    row = taps + 2
    sums[row : row + 1, :] = sums[row : row + 1, :] * jax.nn.sigmoid(rows_ref[taps + 3 : taps + 4, :])

    def turn(b, carried):
        wide = jnp.concatenate(
            [sums[:, columns(b)], jnp.zeros((block - sums.shape[0], block), FULL)], axis=0
        )
        small_ref[columns(b), 2 * head : 2 * head + block] = wide.T.astype(LOW)
        return carried

    lax.fori_loop(0, width // block, turn, 0)
    units = down_hbm.shape[-1]

    def put(q, value):
        down_ref[:, pl.ds(pl.multiple_of(q * units, 128), units)] = value

    spread.take(put, own)
    for step in range(1, bits):
        plane.advance(step)
    kept_ref[...] = plane.kept()[...]
    plane.finish()
    spread.finish()
    for swap in swaps:
        swap.wait_send()
    for by in range(1, places):
        share(by).wait_send()

    @pl.when(seat > 0)
    def _():
        leads.wait_send()


def turn_back(
    n, places, taps, do, y, r, ii, h, edges, c, u, halo, mask, rows8, gate_r, gate_i, down, gate
):
    _, rows, width = u.shape
    head = gate_r.shape[1]
    ext = c.shape[2]
    _, part, units = down.shape
    bits = len(gate.shape) - 3
    low = jax.ShapeDtypeStruct(u.shape, LOW)
    return pl.pallas_call(
        functools.partial(turn_kernel, n, places, taps, bits),
        out_shape=[
            low,
            low,
            jax.ShapeDtypeStruct((width, 2 * head + 128), LOW),
            jax.ShapeDtypeStruct((part, n * units), LOW),
            jax.ShapeDtypeStruct(gate.shape[bits:], LOW),
        ],
        in_specs=[VMEM] * 11 + [ANY] * 4,
        out_specs=[VMEM] * 5,
        scratch_shapes=[
            pltpu.VMEM((ext, head), LOW),
            pltpu.VMEM((ext, head), LOW),
            pltpu.VMEM(u.shape, FULL),
            pltpu.VMEM(u.shape, FULL),
            pltpu.VMEM((n, rows, ext), LOW),
            pltpu.VMEM((n, rows, ext), LOW),
            pltpu.VMEM(u.shape, FULL),
            pltpu.VMEM((n, 8, width), FULL),
            pltpu.VMEM((places, 2 * n, width), FULL),
            pltpu.VMEM((2 * n, width), FULL),
            pltpu.VMEM((8, width), FULL),
            pltpu.VMEM(down.shape, LOW),
            pltpu.VMEM(down.shape[1:], LOW),
            pltpu.SemaphoreType.DMA((1,)),
            pltpu.SemaphoreType.DMA((1,)),
            pltpu.SemaphoreType.DMA((2,)),
            pltpu.SemaphoreType.DMA((2,)),
            pltpu.SemaphoreType.DMA((places,)),
            pltpu.SemaphoreType.DMA((places,)),
            pltpu.SemaphoreType.DMA((n,)),
            pltpu.SemaphoreType.DMA((n,)),
            pltpu.SemaphoreType.DMA((4,)),
            pltpu.SemaphoreType.DMA((2, 2 * bits)),
            pltpu.SemaphoreType.DMA((2, 2 * bits)),
            pltpu.VMEM(gate.shape, LOW),
        ]
        + plane_scratch(gate.shape),
        compiler_params=comm_params(7),
        cost_estimate=lasting(45),
    )(do, y, r, ii, h, edges, c, u, halo, mask, rows8, gate_r, gate_i, down, gate)


def widen_kernel(count, head, *refs):
    sources, targets = refs[: count + 1], refs[count + 1 :]
    for source, target in zip(sources[:count], targets[:count]):
        target[...] = source[...].astype(target.dtype)
    targets[count][...] = sources[count][:, :head]
    targets[count + 1][...] = sources[count][:, head : 2 * head]


def widen(n, head, terms, kept, small):
    arrays = terms + kept
    part = small.shape[0]
    gate = jax.ShapeDtypeStruct((part, head), FULL)
    blocks = [
        pl.BlockSpec((term.shape[0], term.shape[1] // n), lambda k: (0, k)) for term in arrays
    ]
    return pl.pallas_call(
        functools.partial(widen_kernel, len(arrays), head),
        grid=(n,),
        in_specs=blocks + [pl.BlockSpec(small.shape, lambda k: (0, 0))],
        out_specs=blocks + [pl.BlockSpec((part, head), lambda k: (0, 0))] * 2,
        out_shape=[jax.ShapeDtypeStruct(term.shape, FULL) for term in terms]
        + [jax.ShapeDtypeStruct(term.shape, term.dtype) for term in kept]
        + [gate, gate],
    )(*arrays, small)


def on_device(
    inputs,
    segment,
    mixer_gain,
    input_weight,
    branch_weight,
    conv_weight,
    recur_gate,
    input_gate,
    recur_bias,
    input_bias,
    decay_rate,
    output_weight,
    second_gain,
    gate_weight,
    up_weight,
    down_weight,
    cotangent,
):
    shards = lax.axis_size("wt")
    places = lax.axis_size("seq")
    me_w = lax.axis_index("wt")
    me_s = lax.axis_index("seq")
    part_len, model = inputs.shape[1:]
    lru = conv_weight.shape[0]
    taps = conv_weight.shape[1]
    width = lru // shards
    head = recur_gate.shape[1]
    edge = width % head
    rows = shards * part_len

    x = inputs[0]
    slope = cotangent[0]
    soft = -8.0 * jax.nn.softplus(decay_rate)
    vectors = [recur_bias, input_bias, soft, decay_rate, mixer_gain, second_gain]
    table = jnp.concatenate([conv_weight.T, jnp.stack(vectors)], axis=0)
    xn, u3, y, o, c_ext, r, ii, h, ends, halo, mask, x1, xn2, dm, rows8 = head_part(
        shards,
        places,
        taps,
        x,
        segment,
        table,
        slope,
        input_weight,
        branch_weight,
        recur_gate,
        input_gate,
        output_weight,
    )
    dxn2, hidden, dg, dv, xn2, down_term = ffn(
        shards, places, xn2, dm, gate_weight, up_weight, down_weight
    )
    part = model // (places * shards)
    bits = (places // 2 - 1).bit_length()
    cut = (2,) * bits + (shards, part, -1)
    dx1, dz, do, second_gain_grad, block_out, down_kept, gate_term, up_term = back_in(
        shards,
        places,
        dxn2,
        x1,
        slope,
        table,
        down_term.reshape(cut),
        output_weight,
        down_weight,
        hidden,
        xn2,
        dg,
        dv,
    )
    du, dy, small, down_grad, gate_kept = turn_back(
        shards,
        places,
        taps,
        do,
        y,
        r,
        ii,
        h,
        ends,
        c_ext,
        u3,
        halo,
        mask,
        rows8,
        recur_gate,
        input_gate,
        down_kept,
        gate_term.reshape(cut),
    )
    input_grad, gains, small, gate_grad, up_grad, out_grad, branch_grad, input_weight_grad, _ = leave(
        shards,
        places,
        du,
        dy,
        o,
        x,
        dx1,
        table,
        second_gain_grad,
        small.reshape(places, -1, small.shape[1]),
        xn,
        dz,
        input_weight,
        branch_weight,
        up_term,
        gate_kept,
    )
    terms = [down_grad, gate_grad, up_grad, out_grad, branch_grad, input_weight_grad]
    (
        down_grad,
        gate_grad,
        up_grad,
        out_grad,
        branch_grad,
        input_weight_grad,
        input_grad,
        block_out,
        recur_grad,
        gate_in_grad,
    ) = widen(shards, head, terms, [input_grad, block_out], small)
    gains = lax.dynamic_slice_in_dim(gains, (me_s * shards + me_w) * part, part, 1)

    at = 2 * head + taps
    return (
        block_out[None],
        input_grad[None],
        gains[0],
        input_weight_grad,
        branch_grad,
        small[:, 2 * head : at],
        recur_grad,
        gate_in_grad,
        small[:, at],
        small[:, at + 1],
        small[:, at + 2],
        out_grad,
        gains[1],
        gate_grad,
        up_grad,
        down_grad,
    )


def solution(mesh):
    tokens = P("wt", "seq", None)
    columns = P(None, "wt")
    row = P(("seq", "wt"))
    flat_rows = P(("seq", "wt"), None)
    return jax.shard_map(
        on_device,
        mesh=mesh,
        in_specs=(
            tokens,
            P("wt", "seq"),
            P(),
            columns,
            columns,
            P(),
            P(),
            P(),
            P(),
            P(),
            P(),
            columns,
            P(),
            columns,
            columns,
            columns,
            tokens,
        ),
        out_specs=(
            tokens,
            tokens,
            row,
            flat_rows,
            flat_rows,
            flat_rows,
            flat_rows,
            flat_rows,
            row,
            row,
            row,
            flat_rows,
            row,
            flat_rows,
            flat_rows,
            flat_rows,
        ),
        check_vma=False,
    )
```

```python
import functools
import math

import jax
import jax.numpy as jnp
from jax import lax
from jax.experimental import pallas as pl
from jax.experimental.pallas import tpu as pltpu
from jax.sharding import PartitionSpec as P

EPSILON = 1e-06
LOW = jnp.bfloat16
FULL = jnp.float32


def dot(left, right, left_dim=1, right_dim=0):
    return lax.dot_general(
        left, right, (((left_dim,), (right_dim,)), ((), ())), preferred_element_type=FULL
    )


def gelu_both(values):
    slope = jnp.sqrt(2.0 / jnp.pi).astype(FULL)
    inner = jnp.tanh(slope * (values + 0.044715 * values * values * values))
    gelu = 0.5 * values * (1.0 + inner)
    grad = 0.5 * (1.0 + inner) + 0.5 * values * (1.0 - inner * inner) * slope * (
        1.0 + 3.0 * 0.044715 * values * values
    )
    return gelu, grad


def scan_rows(coef, value, reverse):
    rows = coef.shape[0]
    place = lax.broadcasted_iota(jnp.int32, coef.shape, 0)
    step = 1
    while step < rows:
        if reverse:
            inside = place < rows - step
            by = rows - step
        else:
            inside = place >= step
            by = step
        far_coef = jnp.where(inside, pltpu.roll(coef, by, 0), 1.0)
        far_value = jnp.where(inside, pltpu.roll(value, by, 0), 0.0)
        value = coef * far_value + value
        coef = coef * far_coef
        step *= 2
    return coef, value


def expm1_small(values):
    return values * (
        1.0 + values * (0.5 + values * (1.0 / 6.0 + values * (1.0 / 24.0 + values / 120.0)))
    )


MESH = pl.DeviceIdType.MESH


def remote(source, target, sent, landed, to):
    return pltpu.make_async_remote_copy(
        src_ref=source,
        dst_ref=target,
        send_sem=sent,
        recv_sem=landed,
        device_id={"wt": to},
        device_id_type=MESH,
    )


def greet(n, me, pair=False, bits=0, places=0):
    barrier = pltpu.get_barrier_semaphore()

    @pl.when(me > 0)
    def _():
        pl.semaphore_signal(barrier, 1, device_id={"wt": me - 1}, device_id_type=MESH)

    @pl.when(me < n - 1)
    def _():
        pl.semaphore_signal(barrier, 1, device_id={"wt": me + 1}, device_id_type=MESH)

    peers = (me > 0).astype(jnp.int32) + (me < n - 1).astype(jnp.int32)
    place = lax.axis_index("seq")
    if places:
        peers = peers + places - 1
        for by in range(1, places):
            other = {"seq": lax.rem(place + by, places)}
            pl.semaphore_signal(barrier, 1, device_id=other, device_id_type=MESH)
    if pair:
        other = {"seq": place + 1 - 2 * lax.rem(place, 2)}
        pl.semaphore_signal(barrier, 1, device_id=other, device_id_type=MESH)
        peers = peers + 1 + bits
        for k in range(1, bits + 1):
            step = 1 << k
            other = {"seq": place + step * (1 - 2 * lax.rem(place // step, 2))}
            pl.semaphore_signal(barrier, 1, device_id=other, device_id_type=MESH)
    pl.semaphore_wait(barrier, peers)


def greet_all(n, me, places, more, away):
    barrier = pltpu.get_barrier_semaphore()
    seat = lax.axis_index("seq")
    for by in range(1, n):
        other = {"wt": lax.rem(me + by, n)}
        pl.semaphore_signal(barrier, 1, device_id=other, device_id_type=MESH)
    for by in range(1, places):
        other = {"seq": lax.rem(seat + by, places)}
        pl.semaphore_signal(barrier, 1, device_id=other, device_id_type=MESH)

    @pl.when(away)
    def _():
        for other in more:
            pl.semaphore_signal(barrier, 1, device_id=other, device_id_type=MESH)

    peers = n + places - 2 + len(more) * away.astype(jnp.int32)
    pl.semaphore_wait(barrier, peers)


class LineGather:
    def __init__(self, n, me, blocks, sent, landed):
        self.n, self.me, self.blocks, self.sent, self.landed = n, me, blocks, sent, landed

    def rightward(self, d):
        block = self.blocks.at[self.me - d]
        return remote(block, block, self.sent.at[0, d], self.landed.at[0, d + 1], self.me + 1)

    def leftward(self, d):
        block = self.blocks.at[self.me + d]
        return remote(block, block, self.sent.at[1, d], self.landed.at[1, d + 1], self.me - 1)

    def start(self):
        @pl.when(self.me < self.n - 1)
        def _():
            self.rightward(0).start()

        @pl.when(self.me > 0)
        def _():
            self.leftward(0).start()

    def arrive(self, d):
        n, me = self.n, self.me

        @pl.when(me - d >= 0)
        def _():
            block = self.blocks.at[me - d]
            remote(block, block, self.sent.at[0, 0], self.landed.at[0, d], me).wait_recv()

            @pl.when(me < n - 1)
            def _():
                self.rightward(d).start()

        @pl.when(me + d < n)
        def _():
            block = self.blocks.at[me + d]
            remote(block, block, self.sent.at[1, 0], self.landed.at[1, d], me).wait_recv()

            @pl.when(me > 0)
            def _():
                self.leftward(d).start()

    def each(self, d, use):
        def side(k, carry):
            q = self.me + (2 * k - 1) * d

            @pl.when((q >= 0) & (q < self.n))
            def _():
                use(q)

            return carry

        lax.fori_loop(0, 2, side, 0)

    def finish(self):
        n, me = self.n, self.me
        for d in range(n - 1):

            @pl.when((me - d >= 0) & (me < n - 1))
            def _():
                self.rightward(d).wait_send()

            @pl.when((me + d < n) & (me > 0))
            def _():
                self.leftward(d).wait_send()


def line_gather(n, me, blocks, sent, landed, use, ready):
    line = LineGather(n, me, blocks, sent, landed)
    line.start()
    ready()
    use(me)

    def step(d, carry):
        line.arrive(d)
        line.each(d, use)
        return carry

    lax.fori_loop(1, n, step, 0)
    line.finish()


class LineReduce:
    def __init__(self, n, me, parts, slots, sent, landed):
        self.n, self.me, self.parts, self.slots = n, me, parts, slots
        self.sent, self.landed = sent, landed

    def rightward(self, k):
        source, target = self.parts.at[self.n - 1 - k], self.slots.at[0, k]
        return remote(source, target, self.sent.at[0, k], self.landed.at[0, k], self.me + 1)

    def leftward(self, k):
        source, target = self.parts.at[k], self.slots.at[1, k]
        return remote(source, target, self.sent.at[1, k], self.landed.at[1, k], self.me - 1)

    def arrived(self, side, k):
        slot = self.slots.at[side, k]
        remote(slot, slot, self.sent.at[side, k], self.landed.at[side, k], self.me).wait_recv()

    def add(self, q, side, k):
        total = self.parts[q].astype(FULL) + self.slots[side, k].astype(FULL)
        self.parts[q] = total.astype(LOW)

    def prepare(self, k, partial):
        def side(which, carry):
            q = jnp.where(which == 0, self.n - 1 - k, k)

            @pl.when(jnp.where(which == 0, q > self.me, q < self.me))
            def _():
                partial(q)

            return carry

        lax.fori_loop(0, 2, side, 0)

    def step(self, t):
        n = self.n
        for side in range(2):
            place = self.me if side == 0 else n - 1 - self.me
            k = t - place
            pull = self.rightward if side == 0 else self.leftward

            @pl.when((k >= 0) & (t <= n - 2))
            def _():
                @pl.when(place > 0)
                def _():
                    self.arrived(side, k)
                    self.add(n - 1 - k if side == 0 else k, side, k)

                @pl.when(k > 0)
                def _():
                    pull(k - 1).wait_send()

                pull(k).start()

    def total(self):
        n, me = self.n, self.me

        @pl.when(me > 0)
        def _():
            self.arrived(0, n - 1 - me)

        @pl.when(me < n - 1)
        def _():
            self.arrived(1, me)

        total = self.parts[me].astype(FULL)
        other = self.slots[0, jnp.clip(n - 1 - me, 0, n - 2)].astype(FULL)
        total = total + jnp.where(me > 0, other, 0.0)
        other = self.slots[1, jnp.clip(me, 0, n - 2)].astype(FULL)
        return total + jnp.where(me < n - 1, other, 0.0)

    def finish(self):
        @pl.when(self.me < self.n - 1)
        def _():
            self.rightward(self.n - 2 - self.me).wait_send()

        @pl.when(self.me > 0)
        def _():
            self.leftward(self.me - 1).wait_send()


class LineBoth:
    def __init__(self, gather, back, skip=0):
        self.gather, self.back, self.skip = gather, back, skip
        self.n, self.me = gather.n, gather.me

    def sends(self, side, t, act):
        n, me = self.n, self.me
        place = me if side == 0 else n - 1 - me
        spread = self.gather.rightward if side == 0 else self.gather.leftward
        pull = self.back.rightward if side == 0 else self.back.leftward
        d = t + self.skip

        @pl.when(place < n - 1)
        def _():
            @pl.when(d <= place)
            def _():
                act(spread(d))

            @pl.when(d > place)
            def _():
                act(pull(d - place - 1))

    def step(self, t):
        n, me = self.n, self.me
        d = t + self.skip
        for side in range(2):
            place = me if side == 0 else n - 1 - me
            if t > 0:

                @pl.when(d <= place)
                def _():
                    block = self.gather.blocks.at[me - d if side == 0 else me + d]
                    remote(
                        block, block, self.gather.sent.at[side, 0], self.gather.landed.at[side, d], me
                    ).wait_recv()

                @pl.when((d > place) & (place > 0))
                def _():
                    k = d - place - 1
                    self.back.arrived(side, k)
                    self.back.add(n - 1 - k if side == 0 else k, side, k)

                self.sends(side, t - 1, lambda copy: copy.wait_send())
            self.sends(side, t, lambda copy: copy.start())

    def finish(self):
        for side in range(2):
            self.sends(side, self.n - 1 - self.skip, lambda copy: copy.wait_send())


def line_reduce(n, me, parts, slots, sent, landed, partial, work, finish, early=None):
    line = LineReduce(n, me, parts, slots, sent, landed)
    line.prepare(0, partial)
    line.step(0)
    if early is not None:
        early()
    for k in range(1, n - 1):
        line.prepare(k, partial)
    line.step(1)
    partial(me)
    share = -(-len(work) // (n - 2))
    for t in range(2, n):
        for task in work[(t - 2) * share : (t - 1) * share]:
            task()
        if t < n - 1:
            line.step(t)
    finish(line.total())
    line.finish()


def tiles(count, size, body):
    def step(t, carry):
        body(pl.ds(pl.multiple_of(t * size, size), size))
        return carry

    lax.fori_loop(0, count // size, step, 0)


def tile_of(width, limit):
    size = limit
    while width % size:
        size -= 128
    return size


VMEM = pl.BlockSpec(memory_space=pltpu.VMEM)
ANY = pl.BlockSpec(memory_space=pl.ANY)


def gather_sems(n):
    return [pltpu.SemaphoreType.DMA((2, n)), pltpu.SemaphoreType.DMA((2, n + 1))]


def reduce_sems(n):
    return [pltpu.SemaphoreType.DMA((2, n)), pltpu.SemaphoreType.DMA((2, n))]


def lasting(micros):
    return pl.CostEstimate(
        flops=int(micros * 1.0e9), bytes_accessed=int(micros * 3.4e6), transcendentals=0
    )


def comm_params(number):
    return pltpu.CompilerParams(
        collective_id=number, has_side_effects=True, vmem_limit_bytes=64 * 1024 * 1024
    )


class PairSum:
    def __init__(self, part, halves, landing, sent, landed, free, flush):
        self.me = lax.axis_index("seq")
        self.mine = lax.rem(self.me, 2)
        self.part, self.halves, self.landing = part, halves, landing
        self.sent, self.landed, self.free, self.flush = sent, landed, free, flush
        self.count = 0
        self.pending = None

    def other(self):
        return {"seq": self.me + 1 - 2 * self.mine}

    def send(self, slot):
        return pltpu.make_async_remote_copy(
            src_ref=self.halves.at[slot, 1 - self.mine],
            dst_ref=self.landing.at[slot],
            send_sem=self.sent.at[slot],
            recv_sem=self.landed.at[slot],
            device_id=self.other(),
            device_id_type=MESH,
        )

    def out(self, slot, t, target):
        half = self.landing.shape[1]
        return pltpu.make_async_copy(
            self.halves.at[slot, self.mine],
            target.at[pl.ds(t * half, half), :],
            self.flush.at[slot],
        )

    def tasks(self, steps, compute, target):
        return [functools.partial(self.run, t, compute, target) for t in range(steps)]

    def run(self, t, compute, target):
        slot = self.count % 2
        if self.count >= 2:
            self.send(slot).wait_send()
            self.out(slot, 0, target).wait()
            pl.semaphore_wait(self.free, 1)
        compute(t, self.halves.at[slot])
        self.send(slot).start()
        self.settle()
        self.pending = (slot, t, target)
        self.count += 1

    def settle(self):
        if self.pending is None:
            return
        slot, t, target = self.pending
        self.send(slot).wait_recv()
        total = self.halves[slot, self.mine].astype(FULL) + self.landing[slot].astype(FULL)
        self.halves[slot, self.mine] = total.astype(LOW)
        pl.semaphore_signal(self.free, 1, device_id=self.other(), device_id_type=MESH)
        self.out(slot, t, target).start()
        self.pending = None

    def finish(self, target):
        self.settle()
        for slot in range(2):
            self.send(slot).wait_send()
            self.out(slot, 0, target).wait()
        pl.semaphore_wait(self.free, 2)


def pair_scratch(half, width):
    return [
        pltpu.VMEM((2, 2, half, width), LOW),
        pltpu.VMEM((2, half, width), LOW),
        pltpu.SemaphoreType.DMA((2,)),
        pltpu.SemaphoreType.DMA((2,)),
        pltpu.SemaphoreType.REGULAR,
        pltpu.SemaphoreType.DMA((2,)),
    ]


def pair_tile(model, places):
    size = 2 * model // places
    return size if size % 128 == 0 else size * 128 // math.gcd(size, 128)


def pair_dot(left, right, part, size):
    n, rows, _ = left.shape

    def compute(t, halves):
        lhs = left[:, :, pl.ds(t * size, size)].reshape(n * rows, size)
        width = right.shape[2]

        def tile(at):
            rhs = right[:, :, at].reshape(n * rows, -1)
            value = dot(lhs, rhs, 0, 0).astype(LOW)
            for k in range(size // (2 * part)):
                for side in range(2):
                    first = (2 * k + side) * part
                    halves[side, k * part : (k + 1) * part, at] = value[first : first + part]

        tiles(width, tile_of(width, 640), tile)

    return compute


def column_halves(width):
    first = -(-width // 256) * 128
    return [(0, first), (first, width - first)]


class PlaneReduce:
    def __init__(self, blocks, landings, sent, landed, tail=3):
        self.blocks, self.landings, self.sent, self.landed = blocks, landings, sent, landed
        self.bits = len(blocks.shape) - tail
        self.tail = tail
        self.me = lax.axis_index("seq")
        self.columns = column_halves(blocks.shape[-1])

    def bit(self, dim):
        return 1 << (self.bits - dim)

    def mine(self, dim):
        return lax.rem(self.me // self.bit(dim), 2)

    def order(self, side):
        dims = list(range(self.bits))
        return dims[::-1] if side == 0 else dims

    def peer(self, dim):
        return {"seq": self.me + self.bit(dim) * (1 - 2 * self.mine(dim))}

    def index(self, side, step, own):
        order = self.order(side)
        place = [slice(None)] * self.bits
        for dim in order[:step]:
            place[dim] = self.mine(dim)
        now = order[step]
        place[now] = self.mine(now) if own else 1 - self.mine(now)
        return tuple(place) + (slice(None),) * (self.tail - 1) + (pl.ds(*self.columns[side]),)

    def send(self, side, step, piece=0):
        at, landing = self.index(side, step, False), self.landings[2 * step + side]
        if step == 0:
            count = self.blocks.shape[self.bits]
            first = count // 2 if self.tail == 3 else count // 32 * 16
            rows = pl.ds(piece * first, count - first if piece else first)
            at = at[: self.bits] + (rows,) + at[self.bits + 1 :]
            landing = landing.at[(slice(None),) * (self.bits - 1) + (rows,)]
        return pltpu.make_async_remote_copy(
            src_ref=self.blocks.at[at],
            dst_ref=landing,
            send_sem=self.sent.at[side, step + piece * self.bits],
            recv_sem=self.landed.at[side, step + piece * self.bits],
            device_id=self.peer(self.order(side)[step]),
            device_id_type=MESH,
        )

    def pieces(self, step):
        return (0, 1) if step == 0 else (0,)

    def begin(self, pieces=(0, 1)):
        for piece in pieces:
            for side in range(2):
                self.send(side, 0, piece).start()

    def advance(self, step):
        for side in range(2):
            for piece in self.pieces(step):
                self.send(side, step, piece).wait_recv()
            at = self.index(side, step, True)
            total = self.blocks[at].astype(FULL) + self.landings[2 * step + side][...].astype(FULL)
            self.blocks[at] = total.astype(LOW)
            if step + 1 < self.bits:
                self.send(side, step + 1).start()

    def kept(self):
        return self.blocks.at[tuple(self.mine(dim) for dim in range(self.bits))]

    def finish(self):
        for step in range(self.bits):
            for side in range(2):
                for piece in self.pieces(step):
                    self.send(side, step, piece).wait_send()


def plane_scratch(shape, tail=3):
    bits = len(shape) - tail
    landings = []
    for step in range(bits):
        for _, width in column_halves(shape[-1]):
            rest = [2] * (bits - 1 - step) + list(shape[bits:-1]) + [width]
            landings.append(pltpu.VMEM(tuple(rest), LOW))
    return landings


def ffn_kernel(
    n,
    places,
    xn2_ref,
    dm_hbm,
    wg_hbm,
    wu_hbm,
    wd_hbm,
    dxn2_ref,
    hidden_hbm,
    dg_hbm,
    dv_hbm,
    xall_hbm,
    down_hbm,
    xall,
    dm,
    wg,
    wu,
    wd,
    hidden,
    dg,
    dv,
    parts,
    slots,
    halves,
    landing,
    psent,
    planded,
    free,
    pflush,
    gsent,
    glanded,
    rsent,
    rlanded,
    local,
    flush,
):
    me = lax.axis_index("wt")
    rows, model = xn2_ref.shape
    units = wg.shape[1]
    cut = tile_of(units, 640)
    span = tile_of(model, 512)
    loads = [
        pltpu.make_async_copy(source, target, local.at[k])
        for k, (source, target) in enumerate(
            [(dm_hbm, dm), (wd_hbm, wd), (wg_hbm, wg), (wu_hbm, wu)]
        )
    ]
    for load in loads:
        load.start()
    xall[me] = xn2_ref[...]
    greet(n, me, True)

    def ready():
        for load in loads[:2]:
            load.wait()

        def tile(at):
            value = dot(dm[...].reshape(n * rows, model), wd[:, at])
            dg[:, :, at] = value.reshape(n, rows, -1).astype(LOW)

        tiles(units, cut, tile)
        for load in loads[2:]:
            load.wait()

    def use(q):
        def tile(at):
            block = xall[q]
            g = dot(block, wg[:, at])
            v = dot(block, wu[:, at])
            slopes = dg[q, :, at].astype(FULL)
            gelu, slope = gelu_both(g)
            hidden[q, :, at] = (gelu * v).astype(LOW)
            dg[q, :, at] = (slopes * v * slope).astype(LOW)
            dv[q, :, at] = (slopes * gelu).astype(LOW)

        tiles(units, cut, tile)

    line_gather(n, me, xall, gsent, glanded, use, ready)
    outs = [
        pltpu.make_async_copy(source, target, flush.at[k])
        for k, (source, target) in enumerate(
            [(hidden, hidden_hbm), (dg, dg_hbm), (dv, dv_hbm), (xall, xall_hbm)]
        )
    ]
    for out in outs:
        out.start()

    def partial(q):
        def tile(at):
            total = dot(dg[q], wg[at, :], 1, 1) + dot(dv[q], wu[at, :], 1, 1)
            parts[q, :, at] = total.astype(LOW)

        tiles(model, span, tile)

    part = model // places
    size = pair_tile(model, places)
    pair = PairSum(part, halves, landing, psent, planded, free, pflush)

    work = pair.tasks(model // size, pair_dot(dm, hidden, part, size), down_hbm)

    def finish(total):
        dxn2_ref[...] = total

    line_reduce(n, me, parts, slots, rsent, rlanded, partial, work, finish)
    pair.finish(down_hbm)
    for out in outs:
        out.wait()


def ffn(n, places, xn2, dm, wg, wu, wd):
    rows, model = xn2.shape
    units = wg.shape[1]
    grad = jax.ShapeDtypeStruct((model // 2, units), LOW)
    return pl.pallas_call(
        functools.partial(ffn_kernel, n, places),
        out_shape=[
            jax.ShapeDtypeStruct((rows, model), FULL),
            jax.ShapeDtypeStruct((n, rows, units), LOW),
            jax.ShapeDtypeStruct((n, rows, units), LOW),
            jax.ShapeDtypeStruct((n, rows, units), LOW),
            jax.ShapeDtypeStruct((n, rows, model), LOW),
            grad,
        ],
        in_specs=[VMEM, ANY, ANY, ANY, ANY],
        out_specs=[VMEM, ANY, ANY, ANY, ANY, ANY],
        scratch_shapes=[
            pltpu.VMEM((n, rows, model), LOW),
            pltpu.VMEM((n, rows, model), LOW),
            pltpu.VMEM((model, units), LOW),
            pltpu.VMEM((model, units), LOW),
            pltpu.VMEM((model, units), LOW),
            pltpu.VMEM((n, rows, units), LOW),
            pltpu.VMEM((n, rows, units), LOW),
            pltpu.VMEM((n, rows, units), LOW),
            pltpu.VMEM((n, rows, model), LOW),
            pltpu.VMEM((2, n - 1, rows, model), LOW),
        ]
        + pair_scratch(pair_tile(model, places) // 2, units)
        + gather_sems(n)
        + reduce_sems(n)
        + [pltpu.SemaphoreType.DMA((4,)), pltpu.SemaphoreType.DMA((4,))],
        compiler_params=comm_params(2),
        cost_estimate=lasting(105),
    )(xn2, dm, wg, wu, wd)


def back_in_kernel(n, places, bits, *refs):
    dxn2_ref, x1_ref, slope_ref, gain_ref, *sources = refs[:11]
    dx1_ref, dz_ref, do_ref, sum_ref, out_ref, kept_ref, gate_hbm, up_hbm = refs[11:19]
    w, hidden, wd, xall, dg, dv, blocks = refs[19:26]
    landings = refs[26 : 26 + 2 * bits]
    parts, slots, *sems = refs[26 + 2 * bits :]
    halves, landing, psent, planded, free, pflush, sent, landed, rsent, rlanded, bsent, blanded, local = sems
    me = lax.axis_index("wt")
    loads = [
        pltpu.make_async_copy(source, target, local.at[k])
        for k, (source, target) in enumerate(
            zip(sources, [blocks, w, wd, hidden, xall, dg, dv])
        )
    ]
    for load in loads:
        load.start()
    x1 = x1_ref[...]
    dxn2 = dxn2_ref[...]
    model = x1.shape[1]
    scale = lax.rsqrt(jnp.mean(x1 * x1, axis=-1, keepdims=True) + EPSILON)
    q2 = dxn2 * gain_ref[gain_ref.shape[0] - 1 :, :]
    pull = jnp.mean(q2 * x1, axis=-1, keepdims=True)
    dx1 = slope_ref[...] + scale * (q2 - x1 * (scale * scale * pull))
    dx1_ref[...] = dx1
    dz_ref[me] = dx1.astype(LOW)
    greet(n, me, True, bits)
    line = LineGather(n, me, dz_ref, sent, landed)
    back = LineReduce(n, me, parts, slots, rsent, rlanded)
    both = LineBoth(line, back)
    both.step(0)
    loads[0].wait()
    plane = PlaneReduce(blocks, landings, bsent, blanded)
    plane.begin()
    sum_ref[...] = jnp.sum(dxn2 * x1 * scale, axis=0, keepdims=True)

    def use(q):
        do_ref[q] = dot(dz_ref[q], w[...])

    def partial(q):
        def tile(at):
            parts[q, :, at] = dot(hidden[q], wd[at, :], 1, 1).astype(LOW)

        tiles(model, tile_of(model, 512), tile)

    part = model // places
    size = pair_tile(model, places)
    pair = PairSum(part, halves, landing, psent, planded, free, pflush)
    loads[1].wait()
    use(me)
    for load in loads[2:4]:
        load.wait()
    for k in range(n - 2):
        back.prepare(k, partial)
    work = pair.tasks(model // size, pair_dot(xall, dg, part, size), gate_hbm)
    work += pair.tasks(model // size, pair_dot(xall, dv, part, size), up_hbm)
    ends = [len(work) * max(4 * t - 1, 0) // (4 * (n - 1)) for t in range(n)]
    ends[-1] = len(work)
    for t in range(1, n):
        both.step(t)
        if t == 1:
            back.prepare(n - 2, partial)
        if t >= 2 and t - 2 < bits:
            plane.advance(t - 2)
        line.each(t, use)
        if t == 1:
            partial(me)
            for load in loads[4:]:
                load.wait()
        for task in work[ends[t - 1] : ends[t]]:
            task()
    for step in range(max(n - 2, 0), bits):
        plane.advance(step)
    out_ref[...] = (x1_ref[...] + back.total()).astype(LOW)
    kept_ref[...] = plane.kept()[...]
    pair.finish(up_hbm)
    both.finish()
    plane.finish()


def back_in(n, places, dxn2, x1, slope, gain, down, weight, wd, hidden, xall, dg, dv):
    rows, model = x1.shape
    bits = len(down.shape) - 3
    grad = jax.ShapeDtypeStruct((model // 2, wd.shape[1]), LOW)
    return pl.pallas_call(
        functools.partial(back_in_kernel, n, places, bits),
        out_shape=[
            jax.ShapeDtypeStruct((rows, model), FULL),
            jax.ShapeDtypeStruct((n, rows, model), LOW),
            jax.ShapeDtypeStruct((n, rows, weight.shape[1]), FULL),
            jax.ShapeDtypeStruct((1, model), FULL),
            jax.ShapeDtypeStruct((rows, model), LOW),
            jax.ShapeDtypeStruct(down.shape[bits:], LOW),
            grad,
            grad,
        ],
        in_specs=[VMEM] * 4 + [ANY] * 7,
        out_specs=[VMEM] * 6 + [ANY] * 2,
        scratch_shapes=[
            pltpu.VMEM(weight.shape, LOW),
            pltpu.VMEM(hidden.shape, LOW),
            pltpu.VMEM(wd.shape, LOW),
            pltpu.VMEM(xall.shape, LOW),
            pltpu.VMEM(dg.shape, LOW),
            pltpu.VMEM(dv.shape, LOW),
            pltpu.VMEM(down.shape, LOW),
        ]
        + plane_scratch(down.shape)
        + [
            pltpu.VMEM((n, rows, model), LOW),
            pltpu.VMEM((2, n - 1, rows, model), LOW),
        ]
        + pair_scratch(pair_tile(model, places) // 2, wd.shape[1])
        + gather_sems(n)
        + reduce_sems(n)
        + [
            pltpu.SemaphoreType.DMA((2, 2 * bits)),
            pltpu.SemaphoreType.DMA((2, 2 * bits)),
            pltpu.SemaphoreType.DMA((7,)),
        ],
        compiler_params=comm_params(3),
        cost_estimate=lasting(75),
    )(dxn2, x1, slope, gain, down, weight, wd, hidden, xall, dg, dv)


class PlaneShare:
    def __init__(self, places, source, lands, sent, landed):
        self.places, self.source, self.lands = places, source, lands
        self.sent, self.landed = sent, landed
        self.me = lax.axis_index("seq")

    def send(self, by):
        to = lax.rem(self.me + by, self.places)
        return pltpu.make_async_remote_copy(
            src_ref=self.source.at[to],
            dst_ref=self.lands.at[by],
            send_sem=self.sent.at[by],
            recv_sem=self.landed.at[by],
            device_id={"seq": to},
            device_id_type=MESH,
        )

    def start(self):
        self.lands[0] = self.source[self.me]
        for by in range(1, self.places):
            self.send(by).start()

    def finish(self, target):
        for by in range(1, self.places):
            self.send(by).wait_recv()
        target[...] = jnp.sum(self.lands[...].astype(FULL), axis=0)
        for by in range(1, self.places):
            self.send(by).wait_send()


class LineSpread:
    def __init__(self, n, me, source, lands, sent, landed):
        self.n, self.me, self.source, self.lands = n, me, source, lands
        self.sent, self.landed = sent, landed

    def send(self, by):
        to = lax.rem(self.me + by, self.n)
        return remote(
            self.source.at[to], self.lands.at[self.me], self.sent.at[by], self.landed.at[by], to
        )

    def start(self):
        for by in range(1, self.n):
            self.send(by).start()

    def take(self, put, own):
        put(self.me, own[...])
        for by in range(1, self.n):
            slot = lax.rem(self.me + self.n - by, self.n)
            land = self.lands.at[slot]
            remote(land, land, self.sent.at[by], self.landed.at[by], self.me).wait_recv()
            put(slot, land[...])

    def finish(self):
        for by in range(1, self.n):
            self.send(by).wait_send()


def leave_kernel(n, places, bits, *refs):
    du_ref, dy_ref, o_ref, x_ref, dx1_ref, gain_ref, second_ref, small_ref = refs[:8]
    xn_hbm, dz_hbm, win_hbm, wbr_hbm, up_hbm, gate_hbm = refs[8:14]
    grad_ref, total_ref, moved_ref, gate_ref, up_ref, out_ref, branch_ref, in_ref, mix_hbm = refs[14:23]
    xn, dz, win, wbr, parts, slots, blocks, kept, own, lands, notes, around, shares, passed = refs[23:37]
    landings = refs[37 : 37 + 2 * bits]
    others = refs[37 + 2 * bits : 37 + 4 * bits]
    sems = refs[37 + 4 * bits :]
    halves, landing, psent, planded, free, pflush, sent, landed, ssent, slanded = sems[:10]
    usent, ulanded, msent, mlanded, asent, alanded, gsent, glanded, hsent, hlanded, local, fill = sems[10:]
    me = lax.axis_index("wt")
    seat = lax.axis_index("seq")
    model, width = win.shape
    units = gate_hbm.shape[-1]
    part = kept.shape[1]
    rows = n * part

    def fills(source):
        copies = []
        for k in range(1 << bits):
            place = tuple((k >> (bits - 1 - dim)) & 1 for dim in range(bits))
            copies.append(
                pltpu.make_async_copy(
                    source.at[pl.ds(k * rows, rows), :], blocks.at[place], fill.at[k]
                )
            )
        return copies

    loads = [
        pltpu.make_async_copy(source, target, local.at[k])
        for k, (source, target) in enumerate(
            [(win_hbm, win), (wbr_hbm, wbr), (xn_hbm, xn), (dz_hbm, dz), (gate_hbm.at[me], own)]
        )
    ]
    for load in loads[:2] + fills(up_hbm) + loads[2:]:
        load.start()
    flat_to, flat_from = me * places + seat, seat * n + me
    goal = {"seq": flat_to // n, "wt": lax.rem(flat_to, n)}
    origin = {"seq": lax.rem(flat_from, places), "wt": flat_from // places}
    away = flat_to != flat_from
    greet_all(n, me, places, [goal, origin], away)
    small = PlaneShare(places, small_ref, shares, ssent, slanded)
    small.start()
    plane = PlaneReduce(blocks, landings, usent, ulanded, 2)
    for load in loads[:2]:
        load.wait()

    def partial(q):
        def tile(at):
            total = dot(du_ref[q], win[at, :], 1, 1) + dot(dy_ref[q], wbr[at, :], 1, 1)
            parts[q, :, at] = total.astype(LOW)

        tiles(model, tile_of(model, 512), tile)

    size = pair_tile(model, places)
    pair = PairSum(rows, halves, landing, psent, planded, free, pflush)

    def compute(t, target):
        for k, (left, right) in enumerate([(dz, o_ref), (xn, dy_ref), (xn, du_ref)]):
            columns = pl.ds(k * width, width)
            pair_dot(left, right, rows, size)(t, target.at[:, :, columns])

    def early():
        for copy in fills(up_hbm):
            copy.wait()
        plane.begin()
        for load in loads[2:]:
            load.wait()

    def finish(total):
        flat = x_ref[...].astype(FULL)
        scale = lax.rsqrt(jnp.mean(flat * flat, axis=-1, keepdims=True) + EPSILON)
        q1 = total * gain_ref[gain_ref.shape[0] - 2 : gain_ref.shape[0] - 1, :]
        pull = jnp.mean(q1 * flat, axis=-1, keepdims=True)
        grad_ref[...] = dx1_ref[...] + scale * (q1 - flat * (scale * scale * pull))
        mine = jnp.sum(total * flat * scale, axis=0, keepdims=True)
        blank = jnp.zeros((notes.shape[1] - 2, model), FULL)
        notes[me] = jnp.concatenate([mine, second_ref[...], blank], axis=0)

    def keep(k, source):
        for q in range(n):
            kept[k * n + q] = source[q * part : (q + 1) * part, :]

    spreads = [
        LineSpread(n, me, source, lands.at[k], asent.at[k], alanded.at[k])
        for k, source in enumerate([gate_hbm, kept.at[pl.ds(0, n)], kept.at[pl.ds(n, n)]])
    ]
    work = pair.tasks(model // size, compute, mix_hbm)
    tasks = work[:-2] + [
        lambda: (plane.advance(0), work[-2]()),
        lambda: (work[-1](), spreads[0].start()),
    ]
    line_reduce(n, me, parts, slots, sent, landed, partial, tasks, finish, early)
    pair.finish(mix_hbm)

    def note(by):
        to = lax.rem(me + by, n)
        return remote(notes.at[me], notes.at[me], gsent.at[0, by], glanded.at[0, by], to)

    for by in range(1, n):
        note(by).start()
    for step in range(1, bits):
        plane.advance(step)
    keep(0, plane.kept())
    spreads[1].start()
    plane.finish()
    for copy in fills(mix_hbm):
        copy.start()
    for copy in fills(mix_hbm):
        copy.wait()
    mixing = PlaneReduce(blocks, others, msent, mlanded, 2)
    mixing.begin()
    small.finish(passed)
    move = pltpu.make_async_remote_copy(
        src_ref=passed,
        dst_ref=moved_ref,
        send_sem=hsent.at[0],
        recv_sem=hlanded.at[0],
        device_id=goal,
        device_id_type=MESH,
    )

    @pl.when(away)
    def _():
        move.start()

    @pl.when(jnp.logical_not(away))
    def _():
        moved_ref[...] = passed[...]

    for by in range(1, n):
        slot = notes.at[lax.rem(me + n - by, n)]
        remote(slot, slot, gsent.at[0, by], glanded.at[0, by], me).wait_recv()
    around[seat] = jnp.sum(notes[...], axis=0)

    def share(by):
        return pltpu.make_async_remote_copy(
            src_ref=around.at[seat],
            dst_ref=around.at[seat],
            send_sem=gsent.at[1, by],
            recv_sem=glanded.at[1, by],
            device_id={"seq": lax.rem(seat + by, places)},
            device_id_type=MESH,
        )

    for by in range(1, places):
        share(by).start()

    def put_into(target):
        def put(q, value):
            target[:, pl.ds(pl.multiple_of(q * units, 128), units)] = value

        return put

    spreads[0].take(put_into(gate_ref), own)
    for step in range(bits):
        mixing.advance(step)
    keep(1, mixing.kept())
    spreads[2].start()
    spreads[1].take(put_into(up_ref), kept.at[me])
    for by in range(1, places):
        slot = around.at[lax.rem(seat + places - by, places)]
        pltpu.make_async_remote_copy(
            src_ref=slot,
            dst_ref=slot,
            send_sem=gsent.at[1, by],
            recv_sem=glanded.at[1, by],
            device_id={"seq": seat},
            device_id_type=MESH,
        ).wait_recv()
    total_ref[...] = jnp.sum(around[...], axis=0)

    def put_mix(q, value):
        columns = pl.ds(pl.multiple_of(q * width, 128), width)
        for k, target in enumerate([out_ref, branch_ref, in_ref]):
            target[:, columns] = value[:, k * width : (k + 1) * width]

    spreads[2].take(put_mix, kept.at[n + me])
    mixing.finish()
    for spread in spreads:
        spread.finish()
    for by in range(1, n):
        note(by).wait_send()
    for by in range(1, places):
        share(by).wait_send()

    @pl.when(away)
    def _():
        move.wait()


def leave(n, places, du, dy, o, x, dx1, gain, second, small, xn, dz, win, wbr, up, gate):
    rows, model = x.shape
    width = win.shape[1]
    _, part, units = gate.shape
    bits = (model // 2 // (n * part)).bit_length() - 1
    blocks = (2,) * bits + (n * part, units)
    wide = jax.ShapeDtypeStruct((part, n * units), LOW)
    thin = jax.ShapeDtypeStruct((part, n * width), LOW)
    return pl.pallas_call(
        functools.partial(leave_kernel, n, places, bits),
        out_shape=[
            jax.ShapeDtypeStruct((rows, model), FULL),
            jax.ShapeDtypeStruct((8, model), FULL),
            jax.ShapeDtypeStruct(small.shape[1:], FULL),
            wide,
            wide,
            thin,
            thin,
            thin,
            jax.ShapeDtypeStruct(up.shape, LOW),
        ],
        in_specs=[VMEM] * 8 + [ANY] * 6,
        out_specs=[VMEM] * 8 + [ANY],
        scratch_shapes=[
            pltpu.VMEM((n, rows, model), LOW),
            pltpu.VMEM((n, rows, model), LOW),
            pltpu.VMEM(win.shape, LOW),
            pltpu.VMEM(wbr.shape, LOW),
            pltpu.VMEM((n, rows, model), LOW),
            pltpu.VMEM((2, n - 1, rows, model), LOW),
            pltpu.VMEM(blocks, LOW),
            pltpu.VMEM((2 * n, part, units), LOW),
            pltpu.VMEM((part, units), LOW),
            pltpu.VMEM((3, n, part, units), LOW),
            pltpu.VMEM((n, 8, model), FULL),
            pltpu.VMEM((places, 8, model), FULL),
            pltpu.VMEM(small.shape, LOW),
            pltpu.VMEM(small.shape[1:], FULL),
        ]
        + plane_scratch(blocks, 2)
        + plane_scratch(blocks, 2)
        + pair_scratch(pair_tile(model, places) // 2, 3 * width)
        + reduce_sems(n)
        + [
            pltpu.SemaphoreType.DMA((places,)),
            pltpu.SemaphoreType.DMA((places,)),
            pltpu.SemaphoreType.DMA((2, 2 * bits)),
            pltpu.SemaphoreType.DMA((2, 2 * bits)),
            pltpu.SemaphoreType.DMA((2, 2 * bits)),
            pltpu.SemaphoreType.DMA((2, 2 * bits)),
            pltpu.SemaphoreType.DMA((3, n)),
            pltpu.SemaphoreType.DMA((3, n)),
            pltpu.SemaphoreType.DMA((2, max(n, places))),
            pltpu.SemaphoreType.DMA((2, max(n, places))),
            pltpu.SemaphoreType.DMA((1,)),
            pltpu.SemaphoreType.DMA((1,)),
            pltpu.SemaphoreType.DMA((5,)),
            pltpu.SemaphoreType.DMA((1 << bits,)),
        ],
        compiler_params=comm_params(4),
        cost_estimate=lasting(140),
    )(du, dy, o, x, dx1, gain, second, small, xn, dz, win, wbr, up, gate)


def conv_masks(own, before, after, taps):
    lane = lax.broadcasted_iota(jnp.int32, own.shape, 1)
    lines = []
    for here, back in ((own, before), (after, own)):
        for k in range(taps):
            shifted = jnp.where(lane >= k, pltpu.roll(here, k, 1), pltpu.roll(back, k, 1))
            lines.append((shifted == here).astype(FULL)[:1] if k else jnp.ones_like(here)[:1])
    lines.append(jnp.zeros((own.shape[1] - 2 * taps, own.shape[1]), FULL))
    return jnp.concatenate(lines, axis=0).T


def pick_row(table, q):
    place = lax.broadcasted_iota(jnp.int32, table.shape, 0)
    return jnp.sum(jnp.where(place == q, table, 0.0), axis=0, keepdims=True)


def mult_of(log_a, keep):
    twice = 2.0 * log_a
    gap = jnp.where(twice > -0.01, -expm1_small(twice), 1.0 - jnp.exp(twice))
    return jnp.where(keep == 0.0, 1.0, jnp.sqrt(gap))


def enter_kernel(
    n, x_ref, gain_ref, doc_ref, win_hbm, wbr_hbm, xn_ref, u_ref, y_ref, docs_ref, win, wbr, docs, sent, landed, dsent, dlanded, local, places
):
    me = lax.axis_index("wt")
    loads = [
        pltpu.make_async_copy(win_hbm, win, local.at[0]),
        pltpu.make_async_copy(wbr_hbm, wbr, local.at[1]),
    ]
    for load in loads:
        load.start()
    docs[me] = jnp.broadcast_to(doc_ref[...], docs.shape[1:])
    flat = x_ref[...].astype(FULL)
    scale = lax.rsqrt(jnp.mean(flat * flat, axis=-1, keepdims=True) + EPSILON)
    xn_ref[me] = (flat * scale * gain_ref[...]).astype(LOW)
    greet(n, me, False, 0, places)
    notes = LineGather(n, me, docs, dsent, dlanded)
    line = LineGather(n, me, xn_ref, sent, landed)
    notes.start()
    line.start()
    for load in loads:
        load.wait()

    def use(q):
        block = xn_ref[q]
        u_ref[q] = dot(block, win[...]).astype(LOW)
        y_ref[q] = dot(block, wbr[...])

    use(me)

    def step(d, carry):
        notes.arrive(d)
        line.arrive(d)
        line.each(d, use)
        return carry

    lax.fori_loop(1, n, step, 0)
    docs_ref[...] = docs[...]
    notes.finish()
    line.finish()


def close_kernel(
    n, o_ref, x_ref, gain_ref, w_hbm, near_ref, x1_ref, xn2_ref, dm_ref, parts, slots, sent, landed, gsent, glanded, local, w_ref
):
    me = lax.axis_index("wt")
    model = w_ref.shape[0]

    def near(k, act):
        q = me + k - 1

        @pl.when((q >= 0) & (q < n))
        def _():
            act(pltpu.make_async_copy(near_ref.at[k], dm_ref.at[q], local.at[k]))

    for k in range(3):
        near(k, lambda copy: copy.start())

    def partial(q):
        block = o_ref[q]

        def tile(at):
            parts[q, :, at] = dot(block, w_ref[at, :], 1, 1).astype(LOW)

        tiles(model, tile_of(model, 512), tile)

    def finish(total):
        x1 = x_ref[...].astype(FULL) + total
        x1_ref[...] = x1
        scale = lax.rsqrt(jnp.mean(x1 * x1, axis=-1, keepdims=True) + EPSILON)
        xn2_ref[...] = (x1 * scale * gain_ref[...]).astype(LOW)

    back = LineReduce(n, me, parts, slots, sent, landed)
    both = LineBoth(LineGather(n, me, dm_ref, gsent, glanded), back, 1)
    for k in range(3):
        near(k, lambda copy: copy.wait())
    back.prepare(0, partial)
    both.step(0)
    for k in range(1, n - 1):
        back.prepare(k, partial)
    partial(me)
    for t in range(1, n - 1):
        both.step(t)
    finish(back.total())
    both.finish()


def mid_kernel(
    n,
    places,
    taps,
    u_ref,
    y_ref,
    docs_ref,
    rows_ref,
    gr_hbm,
    gi_hbm,
    slope_ref,
    o_ref,
    c_ref,
    r_ref,
    ii_ref,
    h_ref,
    edge_ref,
    halo_ref,
    mask_ref,
    near_ref,
    tr,
    ti,
    cum,
    carry,
    before,
    after,
    hsent,
    hlanded,
    esent,
    elanded,
    csent,
    clanded,
    nsent,
    nlanded,
    local,
):
    me = lax.axis_index("wt")
    seat = lax.axis_index("seq")
    part_len, width = u_ref.shape[1:]
    head = gr_hbm.shape[1]
    ext = tr.shape[0]
    edge = ext - width
    odd = lax.rem(me, 2)
    shift = odd * edge
    block = 128
    first = pl.multiple_of((me * width) // head * head, head)
    loads = [
        pltpu.make_async_copy(source.at[pl.ds(first, ext), :], target, local.at[k])
        for k, (source, target) in enumerate([(gr_hbm, tr), (gi_hbm, ti)])
    ]
    for load in loads:
        load.start()
    partner = {"wt": me + 1 - 2 * odd}
    near_ref[1] = slope_ref[...].astype(LOW)

    def neighbours(act, out):
        for k, (to, there) in enumerate([(me + 1, 0), (me - 1, 2)]):
            copy = remote(near_ref.at[1], near_ref.at[there], nsent.at[k], nlanded.at[k], to)
            inside = (to >= 0) & (to < n)
            gives = (me > 0) if k == 0 else (me < n - 1)

            @pl.when(inside if out else gives)
            def _():
                act(copy)


    def hop(source, target, k, to):
        return pltpu.make_async_remote_copy(
            src_ref=source,
            dst_ref=target,
            send_sem=hsent.at[k],
            recv_sem=hlanded.at[k],
            device_id={"seq": to},
            device_id_type=MESH,
        )

    reach = halo_ref.shape[1]
    tails = u_ref.at[:, pl.ds(part_len - reach, reach), :]
    onward = [hop(tails, halo_ref, 0, seat + 1), hop(docs_ref, before, 1, seat + 1)]
    backward = [hop(docs_ref, after, 2, seat - 1)]

    @pl.when(seat < places - 1)
    def _():
        for copy in onward:
            copy.start()

    @pl.when(seat > 0)
    def _():
        for copy in backward:
            copy.start()

    @pl.when(seat == 0)
    def _():
        halo_ref[...] = jnp.zeros_like(halo_ref)
        before[...] = jnp.full_like(before, -1)

    @pl.when(seat == places - 1)
    def _():
        after[...] = jnp.full_like(after, -1)

    @pl.when(seat > 0)
    def _():
        for copy in onward:
            copy.wait_recv()

    @pl.when(seat < places - 1)
    def _():
        for copy in backward:
            copy.wait_recv()

    def columns(b):
        return pl.ds(pl.multiple_of(b * block, block), block)

    def ext_columns(b):
        return pl.ds(pl.multiple_of(b * block + shift, block), block)

    def each(body):
        def outer(q, carried):
            def inner(b, deeper):
                body(q, b)
                return deeper

            return lax.fori_loop(0, width // block, inner, carried, unroll=True)

        lax.fori_loop(0, n, outer, 0)

    def masks(q, carried):
        mask_ref[q] = conv_masks(
            docs_ref[q].astype(FULL), before[q].astype(FULL), after[q].astype(FULL), taps
        )
        return carried

    lax.fori_loop(0, n, masks, 0)

    def conv(q, b):
        at = columns(b)
        long = jnp.concatenate([halo_ref[q, :, at], u_ref[q, :, at]], axis=0).astype(FULL)
        total = long[reach:] * rows_ref[0:1, at]
        for k in range(1, taps):
            window = pltpu.roll(long, k, 0)[reach:]
            total = total + window * mask_ref[q, :, k : k + 1] * rows_ref[k : k + 1, at]
        c_ref[q, :, ext_columns(b)] = total.astype(LOW)

    each(conv)
    source = pl.ds(pl.multiple_of(jnp.where(odd == 1, edge, width - edge), edge), edge)
    target = pl.ds(pl.multiple_of(jnp.where(odd == 1, width, 0), edge), edge)
    swap = pltpu.make_async_remote_copy(
        src_ref=c_ref.at[:, :, source],
        dst_ref=c_ref.at[:, :, target],
        send_sem=esent.at[0],
        recv_sem=elanded.at[0],
        device_id=partner,
        device_id_type=MESH,
    )
    swap.start()
    for load in loads:
        load.wait()
    swap.wait_recv()
    neighbours(lambda copy: copy.start(), True)
    per = head // block

    def gates(q, b):
        at = columns(b)
        j = b + shift // block
        spot = j // per
        within = pl.ds(pl.multiple_of(lax.rem(j, per) * block, block), block)
        rows = pl.ds(pl.multiple_of(spot * head, head), head)
        c_head = c_ref[q, :, rows]
        c_own = c_ref[q, :, ext_columns(b)].astype(FULL)
        r = jax.nn.sigmoid(dot(c_head, tr[rows, within]) + rows_ref[taps : taps + 1, at])
        ii = jax.nn.sigmoid(dot(c_head, ti[rows, within]) + rows_ref[taps + 1 : taps + 2, at])
        keep = mask_ref[q, :, 1:2]
        log_a = rows_ref[taps + 2 : taps + 3, at] * r
        mult = mult_of(log_a, keep)
        b_low = (mult * c_own * ii).astype(LOW).astype(FULL)
        a = jnp.exp(log_a.astype(LOW).astype(FULL)) * keep
        cum_a, h_loc = scan_rows(a, b_low, False)
        r_ref[q, :, at] = r
        ii_ref[q, :, at] = ii
        cum[q, :, at] = cum_a
        h_ref[q, :, at] = h_loc

    each(gates)
    for q in range(n):
        carry[seat, q : q + 1, :] = cum[q, part_len - 1 : part_len, :]
        carry[seat, n + q : n + q + 1, :] = h_ref[q, part_len - 1 : part_len, :]

    def share(by):
        return pltpu.make_async_remote_copy(
            src_ref=carry.at[seat],
            dst_ref=carry.at[seat],
            send_sem=csent.at[by],
            recv_sem=clanded.at[by],
            device_id={"seq": lax.rem(seat + by, places)},
            device_id_type=MESH,
        )

    for by in range(1, places):
        share(by).start()
    for by in range(1, places):
        share(by).wait_recv()
    state = jnp.zeros((n, width), FULL)
    start = state
    for p in range(places):
        start = jnp.where(seat == p, state, start)
        state = carry[p, :n, :] * state + carry[p, n:, :]
    edge_ref[:n, :] = start
    edge_ref[n:, :] = carry[seat, :n, :]

    def finish(q, b):
        at = columns(b)
        h = h_ref[q, :, at] + cum[q, :, at] * pick_row(edge_ref[:, at], q)
        h_ref[q, :, at] = h
        gelu, _ = gelu_both(y_ref[q, :, at])
        o_ref[q, :, at] = (h.astype(LOW).astype(FULL) * gelu).astype(LOW)

    each(finish)
    neighbours(lambda copy: copy.wait_recv(), False)
    neighbours(lambda copy: copy.wait_send(), True)
    swap.wait_send()

    @pl.when(seat < places - 1)
    def _():
        for copy in onward:
            copy.wait_send()

    @pl.when(seat > 0)
    def _():
        for copy in backward:
            copy.wait_send()

    for by in range(1, places):
        share(by).wait_send()


def head_kernel(n, places, taps, *refs):
    x, doc, table, slope, win_hbm, wbr_hbm, gr_hbm, gi_hbm, w_hbm = refs[:9]
    xn, u, y, o, c, r, ii, h, edges, halo, mask, x1, xn2, dm, rows8 = refs[9:24]
    win, wbr, docs, seen, near, tr, ti, cum, carry, before, after, parts, slots, w = refs[24:38]
    sems = refs[38:]
    width = u.shape[2]
    first = pl.multiple_of(lax.axis_index("wt") * width, 128)
    rows8[...] = table[: taps + 4, pl.ds(first, width)]
    gain, second = table.at[pl.ds(taps + 4, 1)], table.at[pl.ds(taps + 5, 1)]
    load = pltpu.make_async_copy(w_hbm, w, sems[-1].at[0])
    load.start()
    enter_kernel(
        n, x, gain, doc, win_hbm, wbr_hbm, xn, u, y, seen, win, wbr, docs, *sems[:5], places
    )
    mid_kernel(
        n, places, taps, u, y, seen, rows8, gr_hbm, gi_hbm, slope, o, c, r, ii, h, edges, halo, mask, near,
        tr, ti, cum, carry, before, after, *sems[5:14]
    )
    load.wait()
    close_kernel(n, o, x, second, w_hbm, near, x1, xn2, dm, parts, slots, *sems[14:19], w)


def head_part(n, places, taps, x, doc, table, slope, win, wbr, gate_r, gate_i, weight):
    rows, model = x.shape
    width = win.shape[1]
    head = gate_r.shape[1]
    ext = -(-width // head) * head
    full = jax.ShapeDtypeStruct((n, rows, width), FULL)
    low = jax.ShapeDtypeStruct((n, rows, width), LOW)
    long = jax.ShapeDtypeStruct((n, rows, model), LOW)
    docs = pltpu.VMEM((n, 8, rows), jnp.int32)
    pairs = [pltpu.SemaphoreType.DMA((count,)) for count in (3, 3, 1, 1, places, places, 2, 2, 2)]
    return pl.pallas_call(
        functools.partial(head_kernel, n, places, taps),
        out_shape=[
            long,
            low,
            full,
            low,
            jax.ShapeDtypeStruct((n, rows, ext), LOW),
            full,
            full,
            full,
            jax.ShapeDtypeStruct((2 * n, width), FULL),
            jax.ShapeDtypeStruct((n, 16, width), LOW),
            jax.ShapeDtypeStruct((n, rows, rows), FULL),
            jax.ShapeDtypeStruct((rows, model), FULL),
            jax.ShapeDtypeStruct((rows, model), LOW),
            long,
            jax.ShapeDtypeStruct((taps + 4, width), FULL),
        ],
        in_specs=[VMEM] * 4 + [ANY] * 5,
        out_specs=[VMEM] * 15,
        scratch_shapes=[
            pltpu.VMEM(win.shape, LOW),
            pltpu.VMEM(wbr.shape, LOW),
            docs,
            docs,
            pltpu.VMEM((3, rows, model), LOW),
            pltpu.VMEM((ext, head), LOW),
            pltpu.VMEM((ext, head), LOW),
            pltpu.VMEM((n, rows, width), FULL),
            pltpu.VMEM((places, 2 * n, width), FULL),
            docs,
            docs,
            pltpu.VMEM((n, rows, model), LOW),
            pltpu.VMEM((2, n - 1, rows, model), LOW),
            pltpu.VMEM(weight.shape, LOW),
        ]
        + gather_sems(n)
        + gather_sems(n)
        + [pltpu.SemaphoreType.DMA((2,))]
        + pairs
        + reduce_sems(n)
        + gather_sems(n)
        + [pltpu.SemaphoreType.DMA((3,)), pltpu.SemaphoreType.DMA((1,))],
        compiler_params=comm_params(0),
        cost_estimate=lasting(135),
    )(x, doc, table, slope, win, wbr, gate_r, gate_i, weight)


def turn_kernel(
    n,
    places,
    taps,
    bits,
    do_ref,
    y_ref,
    r_ref,
    ii_ref,
    h_ref,
    edge_ref,
    c_ref,
    u_ref,
    halo_ref,
    mask_ref,
    rows_ref,
    gr_hbm,
    gi_hbm,
    down_hbm,
    gate_hbm,
    du_ref,
    dy_ref,
    small_ref,
    down_ref,
    kept_ref,
    tr,
    ti,
    rem,
    e_ref,
    dra,
    dia,
    dc,
    lead,
    carry,
    ein,
    sums,
    lands,
    own,
    hsent,
    hlanded,
    esent,
    elanded,
    csent,
    clanded,
    ssent,
    slanded,
    local,
    psent,
    planded,
    blocks,
    *landings,
):
    me = lax.axis_index("wt")
    seat = lax.axis_index("seq")
    part_len, width = u_ref.shape[1:]
    head = gr_hbm.shape[1]
    ext = tr.shape[0]
    edge = ext - width
    odd = lax.rem(me, 2)
    shift = odd * edge
    block = 128
    per = head // block
    reach = halo_ref.shape[1]
    first = pl.multiple_of((me * width) // head * head, head)
    loads = [
        pltpu.make_async_copy(gr_hbm.at[pl.ds(first, ext), :], tr, local.at[0]),
        pltpu.make_async_copy(gi_hbm.at[pl.ds(first, ext), :], ti, local.at[1]),
        pltpu.make_async_copy(down_hbm.at[me], own, local.at[2]),
        pltpu.make_async_copy(gate_hbm, blocks, local.at[3]),
    ]
    for load in loads:
        load.start()
    barrier = pltpu.get_barrier_semaphore()
    for by in range(1, places):
        other = {"seq": lax.rem(seat + by, places)}
        pl.semaphore_signal(barrier, 1, device_id=other, device_id_type=MESH)
    for by in range(1, n):
        other = {"wt": lax.rem(me + by, n)}
        pl.semaphore_signal(barrier, 1, device_id=other, device_id_type=MESH)
    pl.semaphore_wait(barrier, places + n - 2)
    spread = LineSpread(n, me, down_hbm, lands, ssent, slanded)
    spread.start()
    loads[3].wait()
    plane = PlaneReduce(blocks, landings, psent, planded)
    plane.begin((0,))

    def columns(b):
        return pl.ds(pl.multiple_of(b * block, block), block)

    def ext_columns(b):
        return pl.ds(pl.multiple_of(b * block + shift, block), block)

    def head_columns(b):
        spot = (b + shift // block) // per
        return pl.ds(pl.multiple_of(spot * head, head), head)

    def each(body):
        def outer(q, carried):
            def inner(b, deeper):
                body(q, b)
                return deeper

            return lax.fori_loop(0, width // block, inner, carried, unroll=True)

        lax.fori_loop(0, n, outer, 0)

    def decay(q, at, rows=slice(None)):
        log_a = rows_ref[taps + 2 : taps + 3, at] * r_ref[q, rows, at]
        return jnp.exp(log_a.astype(LOW).astype(FULL)) * mask_ref[q, rows, 1:2]

    place = lax.broadcasted_iota(jnp.int32, (part_len, block), 0)

    def scans(q, b):
        at = columns(b)
        gelu, slope = gelu_both(y_ref[q, :, at])
        back = do_ref[q, :, at]
        hr = h_ref[q, :, at].astype(LOW).astype(FULL)
        dy_ref[q, :, at] = (back * hr * slope).astype(LOW)
        dh = (back * gelu).astype(LOW).astype(FULL)
        a_next = jnp.where(
            place < part_len - 1, pltpu.roll(decay(q, at), part_len - 1, 0), 1.0
        )
        far, e_loc = scan_rows(a_next, dh, True)
        rem[q, :, at] = far
        e_ref[q, :, at] = e_loc

    each(scans)
    carry[seat, :n, :] = edge_ref[n:, :]
    for q in range(n):
        top = decay(q, slice(None), slice(0, 1)) * e_ref[q, 0:1, :]
        carry[seat, n + q : n + q + 1, :] = top

    def share(by):
        return pltpu.make_async_remote_copy(
            src_ref=carry.at[seat],
            dst_ref=carry.at[seat],
            send_sem=csent.at[by],
            recv_sem=clanded.at[by],
            device_id={"seq": lax.rem(seat + by, places)},
            device_id_type=MESH,
        )

    for by in range(1, places):
        share(by).start()
    sums[...] = jnp.zeros_like(sums)
    for by in range(1, places):
        share(by).wait_recv()
    plane.begin((1,))
    state = jnp.zeros((n, width), FULL)
    start = state
    for p in reversed(range(places)):
        start = jnp.where(seat == p, state, start)
        state = carry[p, :n, :] * state + carry[p, n:, :]
    ein[:n, :] = start
    ein[n:, :] = jnp.zeros_like(start)

    def slopes(q, b):
        at = columns(b)
        e = e_ref[q, :, at] + rem[q, :, at] * pick_row(ein[:, at], q)
        h_prev = jnp.where(
            place == 0, pick_row(edge_ref[:, at], q), pltpu.roll(h_ref[q, :, at], 1, 0)
        )
        r = r_ref[q, :, at]
        ii = ii_ref[q, :, at]
        keep = mask_ref[q, :, 1:2]
        soft = rows_ref[taps + 2 : taps + 3, at]
        log_a = soft * r
        mult = mult_of(log_a, keep)
        c = c_ref[q, :, ext_columns(b)].astype(FULL)
        dla = (e * h_prev * decay(q, at)).astype(LOW).astype(FULL)
        dbr = e.astype(LOW).astype(FULL)
        dmult = jnp.where(keep == 0.0, 0.0, -jnp.exp(2.0 * log_a) / mult)
        dlog_a = dla + dbr * c * ii * dmult
        dra_f = soft * dlog_a * r * (1.0 - r)
        direct = dbr * mult * ii
        dia_f = direct * c * (1.0 - ii)
        dra[q, :, ext_columns(b)] = dra_f.astype(LOW)
        dia[q, :, ext_columns(b)] = dia_f.astype(LOW)
        dc[q, :, at] = direct
        for k, value in enumerate([dra_f, dia_f, -8.0 * dlog_a * r]):
            sums[taps + k : taps + k + 1, at] += jnp.sum(value, axis=0, keepdims=True)

    each(slopes)
    source = pl.ds(pl.multiple_of(jnp.where(odd == 1, edge, width - edge), edge), edge)
    target = pl.ds(pl.multiple_of(jnp.where(odd == 1, width, 0), edge), edge)
    swaps = [
        pltpu.make_async_remote_copy(
            src_ref=ref.at[:, :, source],
            dst_ref=ref.at[:, :, target],
            send_sem=esent.at[k],
            recv_sem=elanded.at[k],
            device_id={"wt": me + 1 - 2 * odd},
            device_id_type=MESH,
        )
        for k, ref in enumerate([dra, dia])
    ]
    for swap in swaps:
        swap.start()
    for load in loads[:3]:
        load.wait()
    for swap in swaps:
        swap.wait_recv()

    def mix(q, b):
        at = columns(b)
        rows = head_columns(b)
        table = ext_columns(b)
        dc[q, :, at] += dot(dra[q, :, rows], tr[table, :], 1, 1) + dot(
            dia[q, :, rows], ti[table, :], 1, 1
        )

    each(mix)
    leads = pltpu.make_async_remote_copy(
        src_ref=dc.at[:, pl.ds(0, lead.shape[1]), :],
        dst_ref=lead,
        send_sem=hsent.at[0],
        recv_sem=hlanded.at[0],
        device_id={"seq": seat - 1},
        device_id_type=MESH,
    )

    @pl.when(seat > 0)
    def _():
        leads.start()

    @pl.when(seat == places - 1)
    def _():
        lead[...] = jnp.zeros_like(lead)

    def gate_grads(b, carried):
        left = c_ref[:, :, ext_columns(b)].reshape(n * part_len, block)
        rows = head_columns(b)
        for k, ref in enumerate([dra, dia]):
            right = ref[:, :, rows].reshape(n * part_len, head)
            small_ref[columns(b), k * head : (k + 1) * head] = dot(left, right, 0, 0).astype(LOW)
        return carried

    lax.fori_loop(0, width // block, gate_grads, 0)

    @pl.when(seat < places - 1)
    def _():
        leads.wait_recv()

    plane.advance(0)

    def conv(q, b):
        at = columns(b)
        slope = dc[q, :, at]
        next_rows = lead[q, :, at]
        long = jnp.concatenate([slope, next_rows], axis=0)
        total = slope * rows_ref[0:1, at]
        behind = jnp.concatenate([halo_ref[q, :, at], u_ref[q, :, at]], axis=0).astype(FULL)
        sums[0:1, at] += jnp.sum(behind[reach:] * slope, axis=0, keepdims=True)
        for k in range(1, taps):
            same = mask_ref[q, :, k : k + 1]
            same_next = mask_ref[q, : lead.shape[1], taps + k : taps + k + 1]
            masked = long * jnp.concatenate([same, same_next], axis=0)
            shifted = pltpu.roll(masked, long.shape[0] - k, 0)[:part_len]
            total = total + shifted * rows_ref[k : k + 1, at]
            window = pltpu.roll(behind, k, 0)[reach:] * same
            sums[k : k + 1, at] += jnp.sum(window * slope, axis=0, keepdims=True)
        du_ref[q, :, at] = total.astype(LOW)

    each(conv)
    row = taps + 2
    sums[row : row + 1, :] = sums[row : row + 1, :] * jax.nn.sigmoid(rows_ref[taps + 3 : taps + 4, :])

    def turn(b, carried):
        wide = jnp.concatenate(
            [sums[:, columns(b)], jnp.zeros((block - sums.shape[0], block), FULL)], axis=0
        )
        small_ref[columns(b), 2 * head : 2 * head + block] = wide.T.astype(LOW)
        return carried

    lax.fori_loop(0, width // block, turn, 0)
    units = down_hbm.shape[-1]

    def put(q, value):
        down_ref[:, pl.ds(pl.multiple_of(q * units, 128), units)] = value

    spread.take(put, own)
    for step in range(1, bits):
        plane.advance(step)
    kept_ref[...] = plane.kept()[...]
    plane.finish()
    spread.finish()
    for swap in swaps:
        swap.wait_send()
    for by in range(1, places):
        share(by).wait_send()

    @pl.when(seat > 0)
    def _():
        leads.wait_send()


def turn_back(
    n, places, taps, do, y, r, ii, h, edges, c, u, halo, mask, rows8, gate_r, gate_i, down, gate
):
    _, rows, width = u.shape
    head = gate_r.shape[1]
    ext = c.shape[2]
    _, part, units = down.shape
    bits = len(gate.shape) - 3
    low = jax.ShapeDtypeStruct(u.shape, LOW)
    return pl.pallas_call(
        functools.partial(turn_kernel, n, places, taps, bits),
        out_shape=[
            low,
            low,
            jax.ShapeDtypeStruct((width, 2 * head + 128), LOW),
            jax.ShapeDtypeStruct((part, n * units), LOW),
            jax.ShapeDtypeStruct(gate.shape[bits:], LOW),
        ],
        in_specs=[VMEM] * 11 + [ANY] * 4,
        out_specs=[VMEM] * 5,
        scratch_shapes=[
            pltpu.VMEM((ext, head), LOW),
            pltpu.VMEM((ext, head), LOW),
            pltpu.VMEM(u.shape, FULL),
            pltpu.VMEM(u.shape, FULL),
            pltpu.VMEM((n, rows, ext), LOW),
            pltpu.VMEM((n, rows, ext), LOW),
            pltpu.VMEM(u.shape, FULL),
            pltpu.VMEM((n, 8, width), FULL),
            pltpu.VMEM((places, 2 * n, width), FULL),
            pltpu.VMEM((2 * n, width), FULL),
            pltpu.VMEM((8, width), FULL),
            pltpu.VMEM(down.shape, LOW),
            pltpu.VMEM(down.shape[1:], LOW),
            pltpu.SemaphoreType.DMA((1,)),
            pltpu.SemaphoreType.DMA((1,)),
            pltpu.SemaphoreType.DMA((2,)),
            pltpu.SemaphoreType.DMA((2,)),
            pltpu.SemaphoreType.DMA((places,)),
            pltpu.SemaphoreType.DMA((places,)),
            pltpu.SemaphoreType.DMA((n,)),
            pltpu.SemaphoreType.DMA((n,)),
            pltpu.SemaphoreType.DMA((4,)),
            pltpu.SemaphoreType.DMA((2, 2 * bits)),
            pltpu.SemaphoreType.DMA((2, 2 * bits)),
            pltpu.VMEM(gate.shape, LOW),
        ]
        + plane_scratch(gate.shape),
        compiler_params=comm_params(7),
        cost_estimate=lasting(45),
    )(do, y, r, ii, h, edges, c, u, halo, mask, rows8, gate_r, gate_i, down, gate)


def widen_kernel(count, head, *refs):
    sources, targets = refs[: count + 1], refs[count + 1 :]
    for source, target in zip(sources[:count], targets[:count]):
        target[...] = source[...].astype(target.dtype)
    targets[count][...] = sources[count][:, :head]
    targets[count + 1][...] = sources[count][:, head : 2 * head]


def widen(n, head, terms, kept, small):
    arrays = terms + kept
    part = small.shape[0]
    gate = jax.ShapeDtypeStruct((part, head), FULL)
    blocks = [
        pl.BlockSpec((term.shape[0], term.shape[1] // n), lambda k: (0, k)) for term in arrays
    ]
    return pl.pallas_call(
        functools.partial(widen_kernel, len(arrays), head),
        grid=(n,),
        in_specs=blocks + [pl.BlockSpec(small.shape, lambda k: (0, 0))],
        out_specs=blocks + [pl.BlockSpec((part, head), lambda k: (0, 0))] * 2,
        out_shape=[jax.ShapeDtypeStruct(term.shape, FULL) for term in terms]
        + [jax.ShapeDtypeStruct(term.shape, term.dtype) for term in kept]
        + [gate, gate],
    )(*arrays, small)


def on_device(
    inputs,
    segment,
    mixer_gain,
    input_weight,
    branch_weight,
    conv_weight,
    recur_gate,
    input_gate,
    recur_bias,
    input_bias,
    decay_rate,
    output_weight,
    second_gain,
    gate_weight,
    up_weight,
    down_weight,
    cotangent,
):
    shards = lax.axis_size("wt")
    places = lax.axis_size("seq")
    me_w = lax.axis_index("wt")
    me_s = lax.axis_index("seq")
    part_len, model = inputs.shape[1:]
    lru = conv_weight.shape[0]
    taps = conv_weight.shape[1]
    width = lru // shards
    head = recur_gate.shape[1]
    edge = width % head
    rows = shards * part_len

    x = inputs[0]
    slope = cotangent[0]
    soft = -8.0 * jax.nn.softplus(decay_rate)
    vectors = [recur_bias, input_bias, soft, decay_rate, mixer_gain, second_gain]
    table = jnp.concatenate([conv_weight.T, jnp.stack(vectors)], axis=0)
    xn, u3, y, o, c_ext, r, ii, h, ends, halo, mask, x1, xn2, dm, rows8 = head_part(
        shards,
        places,
        taps,
        x,
        segment,
        table,
        slope,
        input_weight,
        branch_weight,
        recur_gate,
        input_gate,
        output_weight,
    )
    dxn2, hidden, dg, dv, xn2, down_term = ffn(
        shards, places, xn2, dm, gate_weight, up_weight, down_weight
    )
    part = model // (places * shards)
    bits = (places // 2 - 1).bit_length()
    cut = (2,) * bits + (shards, part, -1)
    dx1, dz, do, second_gain_grad, block_out, down_kept, gate_term, up_term = back_in(
        shards,
        places,
        dxn2,
        x1,
        slope,
        table,
        down_term.reshape(cut),
        output_weight,
        down_weight,
        hidden,
        xn2,
        dg,
        dv,
    )
    du, dy, small, down_grad, gate_kept = turn_back(
        shards,
        places,
        taps,
        do,
        y,
        r,
        ii,
        h,
        ends,
        c_ext,
        u3,
        halo,
        mask,
        rows8,
        recur_gate,
        input_gate,
        down_kept,
        gate_term.reshape(cut),
    )
    input_grad, gains, small, gate_grad, up_grad, out_grad, branch_grad, input_weight_grad, _ = leave(
        shards,
        places,
        du,
        dy,
        o,
        x,
        dx1,
        table,
        second_gain_grad,
        small.reshape(places, -1, small.shape[1]),
        xn,
        dz,
        input_weight,
        branch_weight,
        up_term,
        gate_kept,
    )
    terms = [down_grad, gate_grad, up_grad, out_grad, branch_grad, input_weight_grad]
    (
        down_grad,
        gate_grad,
        up_grad,
        out_grad,
        branch_grad,
        input_weight_grad,
        input_grad,
        block_out,
        recur_grad,
        gate_in_grad,
    ) = widen(shards, head, terms, [input_grad, block_out], small)
    gains = lax.dynamic_slice_in_dim(gains, (me_s * shards + me_w) * part, part, 1)

    at = 2 * head + taps
    return (
        block_out[None],
        input_grad[None],
        gains[0],
        input_weight_grad,
        branch_grad,
        small[:, 2 * head : at],
        recur_grad,
        gate_in_grad,
        small[:, at],
        small[:, at + 1],
        small[:, at + 2],
        out_grad,
        gains[1],
        gate_grad,
        up_grad,
        down_grad,
    )


def solution(mesh):
    tokens = P("wt", "seq", None)
    columns = P(None, "wt")
    row = P(("seq", "wt"))
    flat_rows = P(("seq", "wt"), None)
    return jax.shard_map(
        on_device,
        mesh=mesh,
        in_specs=(
            tokens,
            P("wt", "seq"),
            P(),
            columns,
            columns,
            P(),
            P(),
            P(),
            P(),
            P(),
            P(),
            columns,
            P(),
            columns,
            columns,
            columns,
            tokens,
        ),
        out_specs=(
            tokens,
            tokens,
            row,
            flat_rows,
            flat_rows,
            flat_rows,
            flat_rows,
            flat_rows,
            row,
            row,
            row,
            flat_rows,
            row,
            flat_rows,
            flat_rows,
            flat_rows,
        ),
        check_vma=False,
    )
```
